32 devices in a mesh: rows: 4 (over x, core), chan: 8 (over z, y).
Axes of the slice: x: 2, y: 2, z: 4, core: 2. Of those that a mesh axis runs over, the one named last changes fastest.
Arguments:
- inputs: bfloat16 [8192, 1024], P(('rows', 'chan')), may hold values from -6 to 6
- mix_gain: float32 [1024], replicated, may hold values from 0.5 to 1.5
- gate_proj: bfloat16 [1024, 1536], P(None, 'chan'), may hold values from -0.1875 to 0.1875
- gate_bias: float32 [1536], replicated, may hold values from -3 to 3
- lift_proj: bfloat16 [1024, 1536], P(None, 'chan'), may hold values from -0.1875 to 0.1875
- lift_bias: float32 [1536], replicated, may hold values from -3 to 3
- conv_taps: float32 [4, 1536], replicated, may hold values from -3 to 3
- conv_bias: float32 [1536], replicated, may hold values from -2 to 2
- recur_gate: float32 [8, 192, 192], replicated, may hold values from -0.4375 to 0.4375
- recur_bias: float32 [1536], replicated, may hold values from -3 to 3
- input_gate: float32 [8, 192, 192], replicated, may hold values from -0.4375 to 0.4375
- input_bias: float32 [1536], replicated, may hold values from -3 to 3
- decay_param: float32 [1536], replicated, may hold values from 2.2 to 6.9
- out_proj: bfloat16 [1536, 1024], P('chan'), may hold values from -0.15625 to 0.15625
- out_bias: float32 [1024], replicated, may hold values from -2 to 2
- mlp_gain: float32 [1024], replicated, may hold values from 0.5 to 1.5
- mlp_gate: bfloat16 [1024, 3072], P(None, 'chan'), may hold values from -0.1875 to 0.1875
- mlp_up: bfloat16 [1024, 3072], P(None, 'chan'), may hold values from -0.1875 to 0.1875
- mlp_down: bfloat16 [3072, 1024], P('chan'), may hold values from -0.109375 to 0.109375
- doc_starts: int32 [4, 8], P('rows'), may hold values from 0 to 2048, as said below
- cotangent: bfloat16 [8192, 1024], P(('rows', 'chan')), may hold values from -6 to 6
Outputs:
- output: bfloat16 [8192, 1024], P(('rows', 'chan'))
- grad_inputs: bfloat16 [8192, 1024], P(('rows', 'chan'))
- grad_mix_gain: float32 [1024], P('chan')
- grad_gate_proj: float32 [1024, 1536], P(None, 'chan')
- grad_gate_bias: float32 [1536], P('chan')
- grad_lift_proj: float32 [1024, 1536], P(None, 'chan')
- grad_lift_bias: float32 [1536], P('chan')
- grad_conv_taps: float32 [4, 1536], P(None, 'chan')
- grad_conv_bias: float32 [1536], P('chan')
- grad_recur_gate: float32 [8, 192, 192], P(None, 'chan')
- grad_recur_bias: float32 [1536], P('chan')
- grad_input_gate: float32 [8, 192, 192], P(None, 'chan')
- grad_input_bias: float32 [1536], P('chan')
- grad_decay_param: float32 [1536], P('chan')
- grad_out_proj: float32 [1536, 1024], P('chan')
- grad_out_bias: float32 [1024], P('chan')
- grad_mlp_gain: float32 [1024], P('chan')
- grad_mlp_gate: float32 [1024, 3072], P(None, 'chan')
- grad_mlp_up: float32 [1024, 3072], P(None, 'chan')
- grad_mlp_down: float32 [3072, 1024], P('chan')
The draws below stay inside these ranges and needn't reach their ends.
Inputs may be any that keep to these rules, and one draw needn't show every extreme that they name: `doc_starts`: each row is non-decreasing, begins with 0 and ends with 2048; entries equal to 2048 mark no document and stand only at the row's end.
All inputs are finite; a program needn't handle non-finite values.
Results may differ from the reference program's by a relative error of at most 0.0085.
Values may be sent and summed in bfloat16 or wider, within the bound.
A program may use at most 320 MiB of HBM per device.

```python
import jax
import jax.numpy as jnp
from jax import lax

D = 1024
LRU = 1536
FF = 3072
HEADS = 8
MAXD = 8
SEQ_LEN = 2048
GB = 192
NSEQ = 4
TOKENS = 8192


def draw_doc_starts(key, part):
    key = jax.random.fold_in(key, 7)
    pos_key, count_key = jax.random.split(key)
    inner_pos = jnp.sort(jax.random.randint(pos_key, (NSEQ, MAXD - 1), 1, SEQ_LEN), axis=1)
    doc_count = jax.random.randint(count_key, (NSEQ, 1), 1, MAXD)
    keep_mask = jnp.arange(1, MAXD, dtype=jnp.int32)[None, :] < doc_count
    inner_pos = jnp.where(keep_mask, inner_pos, SEQ_LEN)
    return jnp.concatenate([jnp.zeros((NSEQ, 1), jnp.int32), inner_pos.astype(jnp.int32)], axis=1)


def shard_levels(rng, dims, cuts, low, high):
    def one(axis_at, shards_of):
        draws = jax.random.uniform(jax.random.fold_in(jax.random.fold_in(rng, 6), axis_at), (shards_of,), jnp.float32, low / len(cuts), high / len(cuts))
        return jnp.repeat(jnp.exp(draws), dims[axis_at] // shards_of).reshape((-1,) + (1,) * (len(dims) - axis_at - 1))

    factor_of = one(*cuts[0])
    for cut in cuts[1:]:
        factor_of = factor_of * one(*cut)
    return factor_of


def bell_draw(own_key, dims, spread, reach, cuts=(), kind=jnp.bfloat16):
    level = shard_levels(own_key, dims, cuts, -0.22, 0.18) if cuts else 1.0
    array = jax.random.normal(own_key, dims, jnp.float32) * spread * level
    return jnp.minimum(jnp.maximum(array, -reach), reach).astype(kind)


def setup_inputs(seed: int = 0) -> dict:
    key_list = jax.random.split(jax.random.key(seed), 22)
    inputs = bell_draw(key_list[0], (TOKENS, D), 1.0, 6.0, ((0, 32),))
    mix_gain = jnp.clip(1.0 + 0.1 * jax.random.normal(key_list[1], (D,), jnp.float32), 0.5, 1.5)
    gate_proj = bell_draw(key_list[2], (D, LRU), D ** -0.5, 0.1875, ((1, 8),))
    gate_bias = bell_draw(key_list[3], (LRU,), 0.5, 3.0, (), jnp.float32)
    lift_proj = bell_draw(key_list[4], (D, LRU), D ** -0.5, 0.1875, ((1, 8),))
    lift_bias = bell_draw(key_list[5], (LRU,), 0.5, 3.0, (), jnp.float32)
    conv_taps = bell_draw(key_list[6], (4, LRU), 4 ** -0.5, 3.0, (), jnp.float32)
    conv_bias = bell_draw(key_list[7], (LRU,), 0.3, 2.0, (), jnp.float32)
    recur_gate = bell_draw(key_list[8], (HEADS, GB, GB), GB ** -0.5, 0.4375, (), jnp.float32)
    recur_bias = bell_draw(key_list[9], (LRU,), 0.5, 3.0, (), jnp.float32)
    input_gate = bell_draw(key_list[10], (HEADS, GB, GB), GB ** -0.5, 0.4375, (), jnp.float32)
    input_bias = bell_draw(key_list[11], (LRU,), 0.5, 3.0, (), jnp.float32)
    decay_param = jnp.clip(jax.random.uniform(key_list[12], (LRU,), jnp.float32, 2.2, 6.9), 2.2, 6.9)
    out_proj = bell_draw(key_list[13], (LRU, D), LRU ** -0.5, 0.15625, ((0, 8),))
    out_bias = bell_draw(key_list[14], (D,), 0.3, 2.0, (), jnp.float32)
    mlp_gain = jnp.clip(1.0 + 0.1 * jax.random.normal(key_list[15], (D,), jnp.float32), 0.5, 1.5)
    mlp_gate = bell_draw(key_list[16], (D, FF), D ** -0.5, 0.1875, ((1, 8),))
    mlp_up = bell_draw(key_list[17], (D, FF), D ** -0.5, 0.1875, ((1, 8),))
    mlp_down = bell_draw(key_list[18], (FF, D), FF ** -0.5, 0.109375, ((0, 8),))
    doc_starts = draw_doc_starts(jax.random.fold_in(key_list[21], 71), 0)
    cotangent = bell_draw(key_list[20], (TOKENS, D), 1.0, 6.0, ((0, 32),))
    return dict(inputs=inputs, mix_gain=mix_gain, gate_proj=gate_proj, gate_bias=gate_bias, lift_proj=lift_proj, lift_bias=lift_bias, conv_taps=conv_taps, conv_bias=conv_bias, recur_gate=recur_gate, recur_bias=recur_bias, input_gate=input_gate, input_bias=input_bias, decay_param=decay_param, out_proj=out_proj, out_bias=out_bias, mlp_gain=mlp_gain, mlp_gate=mlp_gate, mlp_up=mlp_up, mlp_down=mlp_down, doc_starts=doc_starts, cotangent=cotangent)


EPSILON = 1e-06
precise = lax.Precision.HIGHEST

@jax.custom_vjp
def low(v):
    return lax.optimization_barrier(v.astype(jnp.bfloat16)).astype(jnp.float32)

@jax.custom_vjp
def low_back(v):
    return v

def low_keep(v):
    return (low(v), None)

def low_pass(kept, grad):
    return (grad,)

def back_keep(v):
    return (v, None)

def back_low(kept, grad):
    return (low(grad),)
low.defvjp(low_keep, low_pass)
low_back.defvjp(back_keep, back_low)

def matmul(left_mat, right_mat):
    return jnp.dot(left_mat, right_mat, precision=precise)

def rms_scale(values, gain_vec):
    return values * lax.rsqrt(lax.optimization_barrier(jnp.mean(values * values, axis=-1, keepdims=True)) + EPSILON) * gain_vec

def affine(earlier, later_map):
    return (earlier[0] * later_map[0], later_map[0] * earlier[1] + later_map[1])

def forward(params, seq_rows, starts):
    mix_gain, gate_proj, gate_bias, lift_proj, lift_bias, conv_taps, conv_bias, recur_gate, recur_bias, input_gate, input_bias, decay_param, out_proj, out_bias, mlp_gain, mlp_gate, mlp_up, mlp_down = params
    length = seq_rows.shape[0]
    channels = gate_proj.shape[1]
    gate_block = recur_gate.shape[1]
    within = jnp.arange(length, dtype=jnp.int32)
    doc_tally = lax.optimization_barrier(jnp.sum((starts[None, :] <= within[:, None]).astype(jnp.int32), axis=1))
    prior_tally = jnp.concatenate([jnp.full((1,), -1, jnp.int32), doc_tally[:-1]])
    is_reset = (doc_tally != prior_tally)[:, None]
    normed = low(rms_scale(seq_rows, mix_gain))
    gate_pre = low_back(matmul(normed, gate_proj)) + gate_bias
    lifted = low_back(matmul(normed, lift_proj)) + lift_bias
    conv_out = conv_bias + conv_taps[0] * lifted
    for offset in range(1, 4):
        shifted = jnp.concatenate([jnp.zeros((offset, channels), jnp.float32), lifted[:length - offset]], axis=0)
        earlier_tally = jnp.concatenate([jnp.full((offset,), -1, jnp.int32), doc_tally[:length - offset]])
        same_doc = (earlier_tally == doc_tally).astype(jnp.float32)[:, None]
        conv_out = conv_out + conv_taps[offset] * shifted * same_doc
    grouped = conv_out.reshape(length, channels // gate_block, gate_block)
    recurrence = jax.nn.sigmoid(jnp.einsum('thi,hio->tho', grouped, recur_gate, precision=precise).reshape(length, channels) + recur_bias)
    opening = jax.nn.sigmoid(jnp.einsum('thi,hio->tho', grouped, input_gate, precision=precise).reshape(length, channels) + input_bias)
    log_decay = -8.0 * recurrence * jax.nn.softplus(-decay_param)
    decay_rate = jnp.where(is_reset, 0.0, jnp.exp(log_decay))
    scaling = jnp.where(is_reset, 1.0, jnp.sqrt(-jnp.expm1(2.0 * log_decay)))
    lru_input = scaling * opening * conv_out
    _, lru_state = lax.associative_scan(affine, (decay_rate, lru_input), axis=0)
    mixed_out = low(lru_state * jax.nn.gelu(gate_pre))
    resid = seq_rows + low_back(matmul(mixed_out, out_proj)) + out_bias
    normed2 = low(rms_scale(resid, mlp_gain))
    hidden = low(jax.nn.gelu(low_back(matmul(normed2, mlp_gate))) * low_back(matmul(normed2, mlp_up)))
    return resid + matmul(hidden, mlp_down)

def reference(inputs, mix_gain, gate_proj, gate_bias, lift_proj, lift_bias, conv_taps, conv_bias, recur_gate, recur_bias, input_gate, input_bias, decay_param, out_proj, out_bias, mlp_gain, mlp_gate, mlp_up, mlp_down, doc_starts, cotangent):
    params = tuple((source.astype(jnp.float32) for source in (mix_gain, gate_proj, gate_bias, lift_proj, lift_bias, conv_taps, conv_bias, recur_gate, recur_bias, input_gate, input_bias, decay_param, out_proj, out_bias, mlp_gain, mlp_gate, mlp_up, mlp_down)))
    seq_count = doc_starts.shape[0]
    all_rows = inputs.astype(jnp.float32).reshape(seq_count, SEQ_LEN, D)
    all_cots = cotangent.astype(jnp.float32).reshape(seq_count, SEQ_LEN, D)

    def one_seq(grad_sums, seq_item):
        rows_one, cot_one, starts_one = seq_item
        result, pull_back = jax.vjp(lambda weights, values: forward(weights, values, starts_one), params, rows_one)
        param_grads, row_grads = pull_back(cot_one)
        grad_sums = jax.tree.map(jnp.add, grad_sums, param_grads)
        return (grad_sums, (result.astype(jnp.bfloat16), row_grads.astype(jnp.bfloat16)))
    start_sums = jax.tree.map(jnp.zeros_like, params)
    summed, (results, row_grads) = lax.scan(one_seq, start_sums, (all_rows, all_cots, doc_starts))
    return (results.reshape(TOKENS, D), row_grads.reshape(TOKENS, D), summed[0], summed[1], summed[2], summed[3], summed[4], summed[5], summed[6], summed[7], summed[8], summed[9], summed[10], summed[11], summed[12], summed[13], summed[14], summed[15], summed[16], summed[17])
```

```python
from functools import partial
import math

import jax
import jax.numpy as jnp
from jax import lax
from jax.experimental import pallas as pl
from jax.experimental.pallas import tpu as pltpu
from jax.sharding import PartitionSpec as P

D = 1024
LRU = 1536
FF = 3072
HEADS = 8
GB = 192


EPSILON = 1e-06
precise = lax.Precision.HIGHEST


def from_behind(block, axis, distance):
    devices = range(lax.axis_size(axis))
    route = [(i - distance, i) for i in devices if i - distance in devices]
    return lax.ppermute(block, axis, route)


def prefix(value, axis, join, neutral, backward):
    count, mine = (lax.axis_size(axis), lax.axis_index(axis))
    pieces = jax.tree.map(lambda part: lax.all_gather(part, axis), value)
    if backward:
        pieces = jax.tree.map(lambda part: part[::-1], pieces)
        mine = count - 1 - mine
    subtotal = jax.tree.map(
        lambda part, zero: jnp.full_like(part, 0) + jnp.asarray(zero, part.dtype), value, neutral
    )

    def hop(position, subtotal):
        longer = join(subtotal, jax.tree.map(lambda part: part[position], pieces))
        return jax.tree.map(lambda new, old: jnp.where(position < mine, new, old), longer, subtotal)

    return lax.fori_loop(0, count - 1, hop, subtotal)


def rms_scale(values, gain_vec):
    return (
        values * lax.rsqrt(jnp.mean(values * values, axis=-1, keepdims=True) + EPSILON) * gain_vec
    )


def gated_unit(gate_pre, up_vals):
    return jax.nn.gelu(gate_pre) * up_vals


def affine(earlier, later_map):
    return (earlier[0] * later_map[0], later_map[0] * earlier[1] + later_map[1])


def segment_ids(starts, start_pos, pos_count, seq_len):
    where_at = start_pos + jnp.arange(pos_count, dtype=jnp.int32)
    seq_of = jnp.floor_divide(where_at, seq_len)
    within = where_at - seq_of * seq_len
    owner = seq_of[:, None] == jnp.arange(starts.shape[0], dtype=jnp.int32)[None, :]
    passed = starts[None, :, :] <= within[:, None, None]
    doc_tally = jnp.sum(jnp.logical_and(owner[:, :, None], passed).astype(jnp.int32), axis=(1, 2))
    return seq_of * (starts.shape[1] + 1) + doc_tally


def project(normed, weights, first_bias, second_bias):
    product = jnp.einsum("td,dc->ct", normed, weights, preferred_element_type=jnp.float32)
    channels = first_bias.shape[0]
    return (product[:channels] + first_bias[:, None], product[channels:] + second_bias[:, None])


def conv_forward(lifted, tail_rows, segments, tap_vals, bias_vec):
    length = lifted.shape[1]
    extended = jnp.concatenate([tail_rows, lifted], axis=1)
    own_seg = segments[3 : 3 + length]
    result = bias_vec[:, None] + tap_vals[0][:, None] * lifted
    for offset in range(1, 4):
        same_doc = (segments[3 - offset : 3 - offset + length] == own_seg).astype(jnp.float32)
        result = (
            result
            + tap_vals[offset][:, None]
            * extended[:, 3 - offset : 3 - offset + length]
            * same_doc[None, :]
        )
    return result


def conv_backward(grad_conv, head_rows, segments, lifted, tail_rows, tap_vals):
    length = grad_conv.shape[1]
    ahead_grad = jnp.concatenate([grad_conv, head_rows], axis=1)
    behind = jnp.concatenate([tail_rows, lifted], axis=1)
    own_seg = segments[3 : 3 + length]
    grad_lifted = tap_vals[0][:, None] * grad_conv
    tap_grads = [jnp.sum(grad_conv * lifted, axis=1)]
    for offset in range(1, 4):
        later_same = (segments[3 + offset : 3 + offset + length] == own_seg).astype(jnp.float32)
        grad_lifted = (
            grad_lifted
            + tap_vals[offset][:, None]
            * ahead_grad[:, offset : offset + length]
            * later_same[None, :]
        )
        earlier = (segments[3 - offset : 3 - offset + length] == own_seg).astype(jnp.float32)
        tap_grads.append(
            jnp.sum(
                grad_conv * behind[:, 3 - offset : 3 - offset + length] * earlier[None, :], axis=1
            )
        )
    return (grad_lifted, jnp.stack(tap_grads, axis=1), jnp.sum(grad_conv, axis=1))


def coefficients(is_reset, conv_out, recur_gate, recur_bias, input_gate, input_bias, decay_param):
    channels, length = conv_out.shape
    gate_block = recur_gate.shape[1]
    grouped = conv_out.reshape(channels // gate_block, gate_block, length)
    recurrence = jax.nn.sigmoid(
        jnp.einsum("hit,hio->hot", grouped, recur_gate, precision=precise).reshape(channels, length)
        + recur_bias[:, None]
    )
    opening = jax.nn.sigmoid(
        jnp.einsum("hit,hio->hot", grouped, input_gate, precision=precise).reshape(channels, length)
        + input_bias[:, None]
    )
    log_decay = -8.0 * recurrence * jax.nn.softplus(-decay_param)[:, None]
    decay_rate = jnp.where(is_reset[None, :], 0.0, jnp.exp(log_decay))
    scaling = jnp.where(is_reset[None, :], 1.0, jnp.sqrt(-jnp.expm1(2.0 * log_decay)))
    return (decay_rate, scaling * opening * conv_out)


def reverse_local(decay_rate, grad_state):
    ones_col = jnp.ones_like(decay_rate[:, :1])
    factor = jnp.flip(jnp.concatenate([decay_rate[:, 1:], ones_col], axis=1), axis=1)
    product, carried = lax.associative_scan(affine, (factor, jnp.flip(grad_state, axis=1)), axis=1)
    return (jnp.flip(product, axis=1), jnp.flip(carried, axis=1))


def finish_state(lru_state, start_state, carried, pull_coef):
    previous = jnp.concatenate([start_state[:, None], lru_state[:, :-1]], axis=1)
    return pull_coef((carried * previous, carried))


def flatten_rows(pieces, row_count):
    return jnp.concatenate([source.reshape(row_count, -1) for source in pieces], axis=1)


def body(
    inputs,
    mix_gain,
    gate_proj,
    gate_bias,
    lift_proj,
    lift_bias,
    conv_taps,
    conv_bias,
    recur_gate,
    recur_bias,
    input_gate,
    input_bias,
    decay_param,
    out_proj,
    out_bias,
    mlp_gain,
    mlp_gate,
    mlp_up,
    mlp_down,
    doc_starts,
    cotangent,
):
    chan_count = lax.axis_size("chan")
    chan_place = lax.axis_index("chan")
    local_rows = inputs.shape[0]
    seq_length = local_rows * chan_count
    rows_f32 = inputs.astype(jnp.float32)
    cot_f32 = cotangent.astype(jnp.float32)
    normed, pull_norm = jax.vjp(rms_scale, rows_f32, mix_gain)
    normed_low = normed.astype(jnp.bfloat16)
    gate_full, lift_full, out_full, mlp_gate_full, mlp_up_full, mlp_down_full = (
        lax.all_gather(gate_proj, "chan", axis=1, tiled=True),
        lax.all_gather(lift_proj, "chan", axis=1, tiled=True),
        lax.all_gather(out_proj, "chan", axis=0, tiled=True),
        lax.all_gather(mlp_gate, "chan", axis=1, tiled=True),
        lax.all_gather(mlp_up, "chan", axis=1, tiled=True),
        lax.all_gather(mlp_down, "chan", axis=0, tiled=True),
    )
    channels = LRU
    hidden_cut = FF
    segments = segment_ids(doc_starts, chan_place * local_rows - 3, local_rows + 6, seq_length)
    mix_proj = jnp.concatenate([gate_full, lift_full], axis=1)
    gate_pre, lifted = project(normed_low, mix_proj, gate_bias, lift_bias)
    tail_rows = from_behind(lifted[:, -3:], "chan", 1)
    conv_out = conv_forward(lifted, tail_rows, segments, conv_taps, conv_bias)
    is_reset = segments[3 : 3 + local_rows] != segments[2 : 2 + local_rows]
    (decay_rate, lru_input), pull_coef = jax.vjp(
        partial(coefficients, is_reset),
        conv_out,
        recur_gate,
        recur_bias,
        input_gate,
        input_bias,
        decay_param,
    )
    running, local_state = lax.associative_scan(affine, (decay_rate, lru_input), axis=1)
    ones_vec = jnp.ones((channels,), jnp.float32)
    zeros_vec = jnp.zeros((channels,), jnp.float32)
    _, start_state = prefix(
        (running[:, -1], local_state[:, -1]), "chan", affine, (ones_vec, zeros_vec), False
    )
    lru_state = local_state + running * start_state[:, None]
    gate_val, pull_gelu = jax.vjp(jax.nn.gelu, gate_pre)
    mixed_out = (lru_state * gate_val).astype(jnp.bfloat16)
    resid = (
        rows_f32
        + jnp.einsum("ct,cd->td", mixed_out, out_full, preferred_element_type=jnp.float32)
        + out_bias
    )
    normed2, pull_norm2 = jax.vjp(rms_scale, resid, mlp_gain)
    normed2_low = normed2.astype(jnp.bfloat16)
    mlp_proj = jnp.concatenate([mlp_gate_full, mlp_up_full], axis=1)
    mlp_pre = jnp.einsum("td,df->ft", normed2_low, mlp_proj, preferred_element_type=jnp.float32)
    hidden, pull_mlp = jax.vjp(gated_unit, mlp_pre[:hidden_cut], mlp_pre[hidden_cut:])
    hidden_low = hidden.astype(jnp.bfloat16)
    output = (
        resid
        + jnp.einsum("ft,fd->td", hidden_low, mlp_down_full, preferred_element_type=jnp.float32)
    ).astype(jnp.bfloat16)
    grad_down = jnp.einsum("ft,td->fd", hidden_low, cotangent, preferred_element_type=jnp.float32)
    grad_gate_m, grad_up_m = pull_mlp(
        jnp.einsum("td,fd->ft", cotangent, mlp_down_full, preferred_element_type=jnp.float32)
    )
    grad_pre = jnp.concatenate([grad_gate_m, grad_up_m], axis=0).astype(jnp.bfloat16)
    grad_mlp_in = jnp.einsum("ft,td->fd", grad_pre, normed2_low, preferred_element_type=jnp.float32)
    grad_resid_part, grad_gain2 = pull_norm2(
        jnp.einsum("ft,df->td", grad_pre, mlp_proj, preferred_element_type=jnp.float32)
    )
    grad_resid = cot_f32 + grad_resid_part
    grad_branch = grad_resid.astype(jnp.bfloat16)
    grad_out_proj = jnp.einsum(
        "ct,td->cd", mixed_out, grad_branch, preferred_element_type=jnp.float32
    )
    grad_mixed = jnp.einsum("td,cd->ct", grad_branch, out_full, preferred_element_type=jnp.float32)
    product, carried = reverse_local(decay_rate, grad_mixed * gate_val)
    _, incoming = prefix(
        (decay_rate[:, 0] * product[:, 0], decay_rate[:, 0] * carried[:, 0]),
        "chan",
        affine,
        (ones_vec, zeros_vec),
        True,
    )
    carried = carried + product * incoming[:, None]
    coef_grads = finish_state(lru_state, start_state, carried, pull_coef)
    head_rows = from_behind(coef_grads[0][:, :3], "chan", -1)
    grad_lifted, grad_taps, grad_conv_bias = conv_backward(
        coef_grads[0], head_rows, segments, lifted, tail_rows, conv_taps
    )
    (grad_gate_pre,) = pull_gelu(grad_mixed * lru_state)
    grad_front = jnp.concatenate([grad_gate_pre, grad_lifted], axis=0).astype(jnp.bfloat16)
    grad_mix_proj = jnp.einsum(
        "ct,td->cd", grad_front, normed_low, preferred_element_type=jnp.float32
    )
    grad_normed = jnp.einsum("ct,dc->td", grad_front, mix_proj, preferred_element_type=jnp.float32)
    grad_x_part, grad_gain1 = pull_norm(grad_normed)
    grad_inputs = (grad_resid + grad_x_part).astype(jnp.bfloat16)
    grad_out_bias = jnp.sum(grad_resid, axis=0)
    pieces = [
        grad_mix_proj[:channels],
        grad_mix_proj[channels:],
        jnp.sum(grad_gate_pre, axis=1),
        jnp.sum(grad_lifted, axis=1),
        grad_taps,
        grad_conv_bias,
        jnp.transpose(coef_grads[1], (1, 0, 2)),
        coef_grads[2],
        jnp.transpose(coef_grads[3], (1, 0, 2)),
        coef_grads[4],
        coef_grads[5],
        grad_out_proj,
        grad_mlp_in[:hidden_cut],
        grad_mlp_in[hidden_cut:],
        grad_down,
        grad_gain1,
        grad_out_bias,
        grad_gain2,
    ]
    spread = flatten_rows(pieces, chan_count)
    shared = lax.psum_scatter(spread, "chan", scatter_dimension=0, tiled=True)
    summed = lax.psum(shared.reshape(-1), "rows")
    channels_dev = LRU // chan_count
    hidden_dev = FF // chan_count
    width_dev = D // chan_count
    block_dev = GB // chan_count
    shapes = [
        (channels_dev, D),
        (channels_dev, D),
        (channels_dev,),
        (channels_dev,),
        (channels_dev, 4),
        (channels_dev,),
        (block_dev, HEADS, GB),
        (channels_dev,),
        (block_dev, HEADS, GB),
        (channels_dev,),
        (channels_dev,),
        (channels_dev, D),
        (hidden_dev, D),
        (hidden_dev, D),
        (hidden_dev, D),
        (width_dev,),
        (width_dev,),
        (width_dev,),
    ]
    unpacked = []
    offset = 0
    for piece_shape in shapes:
        piece_size = math.prod(piece_shape)
        unpacked.append(summed[offset : offset + piece_size].reshape(piece_shape))
        offset = offset + piece_size
    return (
        output,
        grad_inputs,
        unpacked[15],
        unpacked[0].T,
        unpacked[2],
        unpacked[1].T,
        unpacked[3],
        unpacked[4].T,
        unpacked[5],
        jnp.transpose(unpacked[6], (1, 0, 2)),
        unpacked[7],
        jnp.transpose(unpacked[8], (1, 0, 2)),
        unpacked[9],
        unpacked[10],
        unpacked[11],
        unpacked[16],
        unpacked[17],
        unpacked[12].T,
        unpacked[13].T,
        unpacked[14],
    )


MESH = pl.DeviceIdType.MESH
LOW = jnp.bfloat16
F32 = jnp.float32
VMEM_BYTES = 60 * 2**20
TILE = 8
GELU_A = math.sqrt(2.0 / math.pi)
GELU_B = 0.044715


def nt(left, right):
    return lax.dot_general(left, right, (((1,), (1,)), ((), ())), preferred_element_type=F32)


def nn(left, right):
    return lax.dot_general(left, right, (((1,), (0,)), ((), ())), preferred_element_type=F32)


def tn(left, right):
    return lax.dot_general(left, right, (((0,), (0,)), ((), ())), preferred_element_type=F32)


def gelu_pair(values):
    squared = values * values
    bend = jnp.tanh(GELU_A * values * (1.0 + GELU_B * squared))
    half = 0.5 * (1.0 + bend)
    slope = half + 0.5 * values * (1.0 - bend * bend) * GELU_A * (1.0 + 3.0 * GELU_B * squared)
    return values * half, slope


class Spot:
    def __init__(self):
        self.r = lax.axis_index("rows")
        self.c = lax.axis_index("chan")
        self.z = lax.div(self.c, 2)
        self.y = lax.rem(self.c, 2)
        self.r_core = self.r + 1 - 2 * lax.rem(self.r, 2)
        self.r_x = lax.rem(self.r + 2, 4)
        self.core = (self.r_core, self.c)
        self.x = (self.r_x, self.c)
        self.c_y = self.c + 1 - 2 * self.y
        self.ymate = (self.r, self.c_y)
        self.up = (self.r, lax.rem(self.c + 2, 8))
        self.dn = (self.r, lax.rem(self.c + 6, 8))


def greet(always, maybe=()):
    barrier = pltpu.get_barrier_semaphore()
    count = len(always)
    for device in always:
        pl.semaphore_signal(barrier, inc=1, device_id=device, device_id_type=MESH)
    for device, there in maybe:

        @pl.when(there)
        def _(device=device):
            pl.semaphore_signal(barrier, inc=1, device_id=device, device_id_type=MESH)

        count = count + jnp.where(there, 1, 0)
    pl.semaphore_wait(barrier, count)


def push(source, target, sems, index, device):
    return pltpu.make_async_remote_copy(
        src_ref=source,
        dst_ref=target,
        send_sem=sems[0].at[index],
        recv_sem=sems[1].at[index],
        device_id=device,
        device_id_type=MESH,
    )


def landed(me, target, sems, index):
    push(target, target, sems, index, me.ymate).wait_recv()


def sem_pair(count):
    return [pltpu.SemaphoreType.DMA((count,)), pltpu.SemaphoreType.DMA((count,))]


def comm_params(collective_id):
    return pltpu.CompilerParams(
        collective_id=collective_id, has_side_effects=True, vmem_limit_bytes=VMEM_BYTES
    )


def plain_params():
    return pltpu.CompilerParams(
        dimension_semantics=("arbitrary",), vmem_limit_bytes=VMEM_BYTES
    )


ANYWHERE = pl.BlockSpec(memory_space=pl.ANY)
IN_VMEM = pl.BlockSpec(memory_space=pltpu.VMEM)


def gather_kernel(
    wm, nrm, cot, starts, wq, nall, call, halo, starts_all,
    loc, xs, xr, cs, cr, hs, hr, ss, sr, ys, yr, us, ds, zr,
):
    me = Spot()
    r, c, z, y = me.r, me.c, me.z, me.y
    rows = wm.shape[1]
    piece = 48
    per = rows // piece
    greet(
        [me.core, me.x, (me.r_x + 1 - 2 * lax.rem(me.r_x, 2), c), me.ymate],
        [(me.up, z < 3), (me.dn, z > 0)]
        + [((row, lax.rem(c + 1, 8)), c < 7) for row in range(4)]
        + [((row, lax.rem(c + 7, 8)), c > 0) for row in range(4)],
    )
    tail = nrm.shape[0] - halo.shape[1]
    own = pltpu.make_async_copy(wm, wq.at[:, pl.ds(y * rows, rows)], loc.at[0])

    @pl.when(z == r)
    def _():
        own.start()

    x_n = push(nrm, nall.at[r], (xs, xr), 0, me.x)
    x_n.start()
    c_n = push(nrm, nall.at[r], (cs, cr), 0, me.core)
    c_n.start()
    diag = (me.r_x + 1 - 2 * lax.rem(me.r_x, 2), c)
    s_copies = [
        push(starts, starts_all.at[r], (ss, sr), i, device)
        for i, device in enumerate((me.core, me.x, diag))
    ]
    for copy in s_copies:
        copy.start()
    halo_copies = [
        push(nrm.at[pl.ds(tail, halo.shape[1])], halo.at[r], (hs, hr), i, (lax.rem(r + i, 4), lax.rem(c + 1, 8)))
        for i in range(4)
    ]

    @pl.when(c < 7)
    def _():
        for copy in halo_copies:
            copy.start()

    here_n = pltpu.make_async_copy(nrm, nall.at[r], loc.at[1])
    here_n.start()
    here_c = pltpu.make_async_copy(cot, call.at[r], loc.at[2])
    here_c.start()
    here_s = pltpu.make_async_copy(starts, starts_all.at[r], loc.at[3])
    here_s.start()
    halo_fill = [
        pltpu.make_async_copy(nrm.at[pl.ds(tail, halo.shape[1])], halo.at[i], loc.at[4 + i])
        for i in range(4)
    ]

    @pl.when(c == 0)
    def _():
        for copy in halo_fill:
            copy.start()

    c_c = push(cot, call.at[r], (cs, cr), 1, me.core)
    c_c.start()
    x_c = push(cot, call.at[r], (xs, xr), 1, me.x)
    fwd_n = push(nall.at[me.r_x], nall.at[me.r_x], (cs, cr), 2, me.core)
    fwd_c = push(call.at[me.r_x], call.at[me.r_x], (cs, cr), 3, me.core)

    @pl.when(z == r)
    def _():
        own.wait()

    count = 3 * per
    go_up = jnp.logical_and(z >= r, z < 3)
    go_dn = jnp.logical_and(z <= r, z > 0)

    def slab(k, half):
        return wq.at[k // per, pl.ds(half * rows + (k % per) * piece, piece)]

    y_copies = [push(slab(k, y), slab(k, y), (ys, yr), k, me.ymate) for k in range(count)]
    up_copies = [push(slab(k, y), slab(k, y), (us, zr), k, me.up) for k in range(count)]
    dn_copies = [push(slab(k, y), slab(k, y), (ds, zr), k, me.dn) for k in range(count)]

    def sent(k):
        y_copies[k].wait_send()

        @pl.when(go_up)
        def _():
            up_copies[k].wait_send()

        @pl.when(go_dn)
        def _():
            dn_copies[k].wait_send()

    for k in range(count):

        @pl.when(z != r)
        def _(k=k):
            landed(me, slab(k, y), (us, zr), k)

        y_copies[k].start()

        @pl.when(go_up)
        def _(k=k):
            up_copies[k].start()

        @pl.when(go_dn)
        def _(k=k):
            dn_copies[k].start()

        if k == per:
            x_c.start()
        if k == 2 * per:
            x_n.wait_recv()
            fwd_n.start()
        if k >= 3:
            sent(k - 3)
    for k in range(count - 3, count):
        sent(k)
    x_c.wait_recv()
    fwd_c.start()
    for k in range(count):
        y_copies[k].wait_recv()
    x_n.wait_send()
    x_c.wait_send()
    for copy in [c_n, c_c, fwd_n, fwd_c]:
        copy.wait_send()
        copy.wait_recv()
    for copy in s_copies:
        copy.wait_send()
        copy.wait_recv()

    @pl.when(c < 7)
    def _():
        for copy in halo_copies:
            copy.wait_send()

    @pl.when(c > 0)
    def _():
        for i in range(4):
            landed(me, halo.at[i], (hs, hr), i)

    @pl.when(c == 0)
    def _():
        for copy in halo_fill:
            copy.wait()

    here_n.wait()
    here_c.wait()
    here_s.wait()


def gather(wm, nrm, cot, starts):
    rows = wm.shape[1]
    count = 3 * rows // 48
    sd = jax.ShapeDtypeStruct
    return pl.pallas_call(
        gather_kernel,
        name="gather_front",
        out_shape=[
            sd((3, 2 * rows, D), LOW),
            sd((4,) + nrm.shape, LOW),
            sd((4,) + cot.shape, LOW),
            sd((4, 16, D), LOW),
            sd((4,) + starts.shape, starts.dtype),
        ],
        in_specs=[ANYWHERE] * 4,
        out_specs=[ANYWHERE] * 5,
        scratch_shapes=[pltpu.SemaphoreType.DMA((8,))]
        + sem_pair(2) + sem_pair(4) + sem_pair(4) + sem_pair(3) + sem_pair(count)
        + [pltpu.SemaphoreType.DMA((count,))] * 3,
        compiler_params=comm_params(1),
    )(wm, nrm, cot, starts)


def decay_terms(rec, softplus_row, reset):
    log_decay = -8.0 * rec * softplus_row
    decay = jnp.exp(log_decay)
    twice = 2.0 * log_decay
    series = twice * (
        1.0
        + twice * (1 / 2 + twice * (1 / 6 + twice * (1 / 24 + twice * (1 / 120 + twice * (1 / 720)))))
    )
    gap = jnp.where(twice > -0.25, -series, 1.0 - jnp.exp(twice))
    return decay, jnp.where(reset, 1.0, jnp.sqrt(gap))


def mixer_one_kernel(
    nrm, halo, wg, wl, vec, taps, rgate, igate, mask,
    gate_pre, lext, conv_o, rec_o, open_o, a_o, b_o, tot,
):
    length = nrm.shape[1]
    wide = wg.shape[1]
    tokens = nrm[0]
    gate_pre[0] = nt(tokens, wg[0]) + vec[0:1]
    lifted = nt(tokens, wl[0]) + vec[1:2]
    lext[0, 0:8] = (nt(halo[0], wl[0]) + vec[1:2])[8:16]
    lext[0, pl.ds(8, length)] = lifted
    conv = vec[2:3] + taps[0:1] * lifted
    for k in range(1, 4):
        conv = conv + taps[k : k + 1] * lext[0, pl.ds(8 - k, length)] * mask[0, :, k - 1 : k]
    conv_o[0] = conv
    conv_low = conv.astype(LOW)
    rec = jax.nn.sigmoid(nn(conv_low, rgate[...]) + vec[3:4])
    opening = jax.nn.sigmoid(nn(conv_low, igate[...]) + vec[4:5])
    rec_o[0] = rec
    open_o[0] = opening
    reset = mask[0, :, 3:4] > 0.5
    decay, scaling = decay_terms(rec, vec[5:6], reset)
    decay = jnp.where(reset, 0.0, decay)
    a = decay.reshape(length // TILE, TILE, wide)
    b = (scaling * opening * conv).reshape(length // TILE, TILE, wide)
    row = lax.broadcasted_iota(jnp.int32, a.shape, 1)
    for step in (1, 2, 4):
        earlier = row >= step
        b = b + a * jnp.where(earlier, pltpu.roll(b, step, 1), 0.0)
        a = a * jnp.where(earlier, pltpu.roll(a, step, 1), 1.0)
    a_o[0] = a.reshape(length, wide)
    b_o[0] = b.reshape(length, wide)
    product = jnp.ones((1, wide), F32)
    state = jnp.zeros((1, wide), F32)
    for t in range(length // TILE):
        last = t * TILE + TILE - 1
        a_last = a_o[0, last : last + 1]
        state = b_o[0, last : last + 1] + a_last * state
        product = product * a_last
    tot[0, 0:1] = product
    tot[0, 1:2] = state


def whole(shape):
    return pl.BlockSpec(shape, lambda s: (0,) * len(shape))


def per_seq(shape):
    return pl.BlockSpec((1,) + shape, lambda s: (s,) + (0,) * len(shape))


def mixer_one(nall, halo, wq, vec, taps, rgate, igate, mask):
    seqs, length, width = nall.shape
    wide = wq.shape[1]
    sd = jax.ShapeDtypeStruct
    full = sd((seqs, length, wide), F32)
    return pl.pallas_call(
        mixer_one_kernel,
        name="mixer_forward_gates",
        grid=(seqs,),
        in_specs=[
            per_seq((length, width)),
            per_seq((16, width)),
            pl.BlockSpec((1, wide, width), lambda s: (0, 0, 0)),
            pl.BlockSpec((1, wide, width), lambda s: (1, 0, 0)),
            whole(vec.shape),
            whole(taps.shape),
            whole(rgate.shape),
            whole(igate.shape),
            per_seq((length, 8)),
        ],
        out_specs=[per_seq((length, wide)), per_seq((length + 8, wide))]
        + [per_seq((length, wide))] * 5
        + [per_seq((2, wide))],
        out_shape=[full, sd((seqs, length + 8, wide), F32), full, full, full, full, full,
                   sd((seqs, 2, wide), F32)],
        compiler_params=plain_params(),
    )(nall, halo, wq, wq, vec, taps, rgate, igate, mask)


def prefix_kernel(backward, totals, start, slots, send, recv):
    me = Spot()
    r, c = me.r, me.c
    sign = -1 if backward else 1
    steps = c if backward else 7 - c
    behind = (7 - c) if backward else c
    greet(
        [],
        [((r, lax.rem(c + 8 + sign * d, 8)), d <= steps) for d in range(1, 8)]
        + [((r, lax.rem(c + 8 - sign * d, 8)), d <= behind) for d in range(1, 8)],
    )
    copies = [
        push(totals, slots.at[d], (send, recv), d, (r, lax.rem(c + 8 + sign * d, 8))) for d in range(1, 8)
    ]
    for d in range(1, 8):

        @pl.when(d <= steps)
        def _(d=d):
            copies[d - 1].start()

    start[...] = jnp.zeros_like(start)
    for d in range(7, 0, -1):

        @pl.when(d <= behind)
        def _(d=d):
            landed(me, slots.at[d], (send, recv), d)
            start[...] = slots[d, :, 0] * start[...] + slots[d, :, 1]

    for d in range(1, 8):

        @pl.when(d <= steps)
        def _(d=d):
            copies[d - 1].wait_send()


def carry_in(totals, backward):
    seqs, _, wide = totals.shape
    return pl.pallas_call(
        partial(prefix_kernel, backward),
        name="carry_back" if backward else "carry_on",
        out_shape=jax.ShapeDtypeStruct((seqs, wide), F32),
        in_specs=[IN_VMEM],
        out_specs=IN_VMEM,
        scratch_shapes=[pltpu.VMEM((8,) + totals.shape, F32)] + sem_pair(8),
        compiler_params=comm_params(3 if backward else 2),
    )(totals)


def mixer_two_kernel(a, b, start, gate_pre, wo, state_o, mixed_o, part):
    tiles = a.shape[1] // TILE
    state = start[0]
    for t in range(tiles):
        rows = pl.ds(t * TILE, TILE)
        now = b[0, rows] + a[0, rows] * state
        state_o[0, rows] = now
        state = now[TILE - 1 : TILE]
    gate_val, _ = gelu_pair(gate_pre[0])
    mixed = (state_o[0] * gate_val).astype(LOW)
    mixed_o[0] = mixed
    part[0] = nn(mixed, wo[0]).astype(LOW)


def mixer_two(a, b, start, gate_pre, wq):
    seqs, length, wide = a.shape
    width = wq.shape[2]
    sd = jax.ShapeDtypeStruct
    block = per_seq((length, wide))
    return pl.pallas_call(
        mixer_two_kernel,
        name="mixer_forward_state",
        grid=(seqs,),
        in_specs=[block, block, per_seq((1, wide)), block,
                  pl.BlockSpec((1, wide, width), lambda s: (2, 0, 0))],
        out_specs=[block, block, per_seq((length, width))],
        out_shape=[sd(a.shape, F32), sd(a.shape, LOW), sd((seqs, length, width), LOW)],
        compiler_params=plain_params(),
    )(a, b, start.reshape(seqs, 1, wide), gate_pre, wq)


RS_CHUNKS = 4


def rows_sum_start(me, part, mate, sems):
    length = part.shape[1]
    step = length // RS_CHUNKS
    far = lax.rem(me.r_core + 2, 4)
    copies = []
    for block, owner in enumerate((far, me.r_core)):
        for k in range(RS_CHUNKS):
            rows = pl.ds(k * step, step)
            copies.append(
                push(part.at[owner, rows], mate.at[block, rows], sems, block * RS_CHUNKS + k, me.core)
            )
    for copy in copies:
        copy.start()
    return copies


def rows_sum_cross(me, part, mate, out_x, in_x, copies, sems):
    length = part.shape[1]
    step = length // RS_CHUNKS
    crossing = []
    for k in range(RS_CHUNKS):
        rows = pl.ds(k * step, step)
        copies[k].wait_recv()
        out_x[rows] = (part[me.r_x, rows].astype(F32) + mate[0, rows].astype(F32)).astype(LOW)
        copy = push(out_x.at[rows], in_x.at[rows], sems, k, me.x)
        copy.start()
        crossing.append(copy)
    return crossing


def rows_sum_chunk(me, part, mate, in_x, copies, crossing, k):
    length = part.shape[1]
    step = length // RS_CHUNKS
    rows = pl.ds(k * step, step)
    copies[RS_CHUNKS + k].wait_recv()
    crossing[k].wait_recv()
    return part[me.r, rows].astype(F32) + mate[1, rows].astype(F32) + in_x[rows].astype(F32)


def finish_sends(copies):
    for copy in copies:
        copy.wait_send()


def rows_sum_scratch(length, width):
    return [
        pltpu.VMEM((2, length, width), LOW),
        pltpu.VMEM((length, width), LOW),
        pltpu.VMEM((length, width), LOW),
    ] + sem_pair(2 * RS_CHUNKS) + sem_pair(RS_CHUNKS)


def spread_chunk(me, all_ref, k, sems_x, sems_c):
    length = all_ref.shape[1]
    step = length // RS_CHUNKS
    rows = pl.ds(k * step, step)
    mine = all_ref.at[me.r, rows]
    copies = [
        push(mine, mine, sems_x, k, me.x),
        push(mine, mine, sems_c, k, me.core),
    ]
    for copy in copies:
        copy.start()
    return copies


def spread_rest(me, all_ref, first, sems_c):
    length = all_ref.shape[1]
    step = length // RS_CHUNKS
    passed = []
    for k in range(RS_CHUNKS):
        first[k][0].wait_recv()
        theirs = all_ref.at[me.r_x, pl.ds(k * step, step)]
        copy = push(theirs, theirs, sems_c, RS_CHUNKS + k, me.core)
        copy.start()
        passed.append(copy)
    for k in range(RS_CHUNKS):
        first[k][0].wait_send()
        first[k][1].wait()
        passed[k].wait()


def resid_kernel(
    part, inputs, bias, gain, resid, nall,
    mate, out_x, in_x, ms, mr, xs, xr, ax, bx, ac, bc,
):
    me = Spot()
    greet([me.core, me.x])
    step = inputs.shape[0] // RS_CHUNKS
    copies = rows_sum_start(me, part, mate, (ms, mr))
    crossing = rows_sum_cross(me, part, mate, out_x, in_x, copies, (xs, xr))
    first = []
    for k in range(RS_CHUNKS):
        rows = pl.ds(k * step, step)
        total = rows_sum_chunk(me, part, mate, in_x, copies, crossing, k)
        res = inputs[rows].astype(F32) + total + bias[...]
        resid[rows] = res
        scale = lax.rsqrt(jnp.mean(res * res, axis=-1, keepdims=True) + EPSILON)
        nall[me.r, rows] = (res * scale * gain[...]).astype(LOW)
        first.append(spread_chunk(me, nall, k, (ax, bx), (ac, bc)))
    spread_rest(me, nall, first, (ac, bc))
    finish_sends(copies + crossing)


def resid_step(part, inputs, bias, gain):
    sd = jax.ShapeDtypeStruct
    length, width = inputs.shape
    return pl.pallas_call(
        resid_kernel,
        name="resid_sum",
        out_shape=[sd(inputs.shape, F32), sd(part.shape, LOW)],
        in_specs=[IN_VMEM] * 4,
        out_specs=[IN_VMEM] * 2,
        scratch_shapes=rows_sum_scratch(length, width)
        + sem_pair(RS_CHUNKS) + sem_pair(2 * RS_CHUNKS),
        compiler_params=comm_params(4),
    )(part, inputs, bias, gain)


def grad_resid_kernel(
    part, cot, resid, gain, gresid, ball, gains,
    mate, out_x, in_x, ms, mr, xs, xr, ax, bx, ac, bc,
):
    me = Spot()
    greet([me.core, me.x])
    step = cot.shape[0] // RS_CHUNKS
    copies = rows_sum_start(me, part, mate, (ms, mr))
    crossing = rows_sum_cross(me, part, mate, out_x, in_x, copies, (xs, xr))
    first = []
    gain_sum = 0.0
    bias_sum = 0.0
    for k in range(RS_CHUNKS):
        rows = pl.ds(k * step, step)
        grad = rows_sum_chunk(me, part, mate, in_x, copies, crossing, k)
        res = resid[rows]
        scale = lax.rsqrt(jnp.mean(res * res, axis=-1, keepdims=True) + EPSILON)
        gain_sum = gain_sum + jnp.sum(grad * res * scale, axis=0, keepdims=True)
        pulled = grad * gain[...]
        inner = jnp.mean(pulled * res, axis=-1, keepdims=True)
        total = cot[rows].astype(F32) + scale * pulled - res * (scale * scale * scale * inner)
        bias_sum = bias_sum + jnp.sum(total, axis=0, keepdims=True)
        gresid[rows] = total
        ball[me.r, rows] = total.astype(LOW)
        first.append(spread_chunk(me, ball, k, (ax, bx), (ac, bc)))
    gains[0:1] = gain_sum
    gains[1:2] = bias_sum
    spread_rest(me, ball, first, (ac, bc))
    finish_sends(copies + crossing)


def grad_resid_step(part, cot, resid, gain):
    sd = jax.ShapeDtypeStruct
    length, width = cot.shape
    return pl.pallas_call(
        grad_resid_kernel,
        name="grad_resid_sum",
        out_shape=[sd(cot.shape, F32), sd(part.shape, LOW), sd((2, width), F32)],
        in_specs=[IN_VMEM] * 4,
        out_specs=[IN_VMEM] * 3,
        scratch_shapes=rows_sum_scratch(length, width)
        + sem_pair(RS_CHUNKS) + sem_pair(2 * RS_CHUNKS),
        compiler_params=comm_params(5),
    )(part, cot, resid, gain)


def mlp_kernel(
    nall, call, wg, wu, wd, part, gpart, dg_o, du_o, dd_o,
    acc_out, acc_in, acc_g, acc_u, acc_d,
):
    block = pl.program_id(0)
    length = nall.shape[1]

    @pl.when(block == 0)
    def _():
        acc_out[...] = jnp.zeros_like(acc_out)
        acc_in[...] = jnp.zeros_like(acc_in)

    acc_g[...] = jnp.zeros_like(acc_g)
    acc_u[...] = jnp.zeros_like(acc_u)
    acc_d[...] = jnp.zeros_like(acc_d)

    @pl.loop(0, nall.shape[0])
    def _(s):
        tokens = nall[s]
        cot = call[s]
        gate = nt(tokens, wg[...])
        up = nt(tokens, wu[...])
        grad_hidden = nt(cot, wd[...])
        gate_val, slope = gelu_pair(gate)
        hidden = (gate_val * up).astype(LOW)
        grad_gate = (grad_hidden * up * slope).astype(LOW)
        grad_up = (grad_hidden * gate_val).astype(LOW)
        acc_out[s] += nn(hidden, wd[...])
        acc_in[s] += nn(grad_gate, wg[...]) + nn(grad_up, wu[...])
        acc_d[...] += tn(hidden, cot)
        acc_g[...] += tn(grad_gate, tokens)
        acc_u[...] += tn(grad_up, tokens)

    dg_o[...] = acc_g[...].astype(LOW)
    du_o[...] = acc_u[...].astype(LOW)
    dd_o[...] = acc_d[...].astype(LOW)

    @pl.when(block == pl.num_programs(0) - 1)
    def _():
        part[...] = acc_out[...].astype(LOW)
        gpart[...] = acc_in[...].astype(LOW)


def mlp(nall, call, wg, wu, wd):
    hidden, width = wg.shape
    blocks = 2
    cut = hidden // blocks
    sd = jax.ShapeDtypeStruct
    weight = pl.BlockSpec((cut, width), lambda h: (h, 0))
    return pl.pallas_call(
        mlp_kernel,
        name="mlp_both_ways",
        grid=(blocks,),
        in_specs=[whole(nall.shape), whole(call.shape), weight, weight, weight],
        out_specs=[whole(nall.shape), whole(nall.shape), weight, weight, weight],
        out_shape=[sd(nall.shape, LOW)] * 2 + [sd(wg.shape, LOW)] * 3,
        scratch_shapes=[pltpu.VMEM(nall.shape, F32)] * 2 + [pltpu.VMEM((cut, width), F32)] * 3,
        compiler_params=plain_params(),
    )(nall, call, wg, wu, wd)


def mixer_three_kernel(
    ball, wo, gate_pre, state, mixed, rec, vec, mask,
    gate_low, gs_o, a_o, b_o, tot, dwo, sums, acc_w, acc_b,
):
    seq = pl.program_id(0)
    length, wide = rec.shape[1], rec.shape[2]

    @pl.when(seq == 0)
    def _():
        acc_w[...] = jnp.zeros_like(acc_w)
        acc_b[...] = jnp.zeros_like(acc_b)

    branch = ball[0]
    grad_mixed = nt(branch, wo[0])
    gate_val, slope = gelu_pair(gate_pre[0])
    grad_gate = grad_mixed * state[0] * slope
    gate_low[0] = grad_gate.astype(LOW)
    acc_b[...] += jnp.sum(grad_gate, axis=0, keepdims=True)
    acc_w[...] += tn(mixed[0], branch)
    grad_state = grad_mixed * gate_val
    gs_o[0] = grad_state
    reset = mask[0, :, 3:4] > 0.5
    decay = jnp.where(reset, 0.0, jnp.exp(-8.0 * rec[0] * vec[5:6]))
    a = decay.reshape(length // TILE, TILE, wide)
    b = (decay * grad_state).reshape(length // TILE, TILE, wide)
    row = lax.broadcasted_iota(jnp.int32, a.shape, 1)
    for step in (1, 2, 4):
        later = row < TILE - step
        b = b + a * jnp.where(later, pltpu.roll(b, TILE - step, 1), 0.0)
        a = a * jnp.where(later, pltpu.roll(a, TILE - step, 1), 1.0)
    a_o[0] = a.reshape(length, wide)
    b_o[0] = b.reshape(length, wide)
    product = jnp.ones((1, wide), F32)
    carry = jnp.zeros((1, wide), F32)
    for t in range(length // TILE - 1, -1, -1):
        head = t * TILE
        a_head = a_o[0, head : head + 1]
        carry = b_o[0, head : head + 1] + a_head * carry
        product = product * a_head
    tot[0, 0:1] = product
    tot[0, 1:2] = carry

    @pl.when(seq == pl.num_programs(0) - 1)
    def _():
        dwo[...] = acc_w[...].astype(LOW)
        sums[...] = acc_b[...]


def mixer_three(ball, wq, gate_pre, state, mixed, rec, vec, mask):
    seqs, length, wide = rec.shape
    width = wq.shape[2]
    sd = jax.ShapeDtypeStruct
    block = per_seq((length, wide))
    full = sd(rec.shape, F32)
    return pl.pallas_call(
        mixer_three_kernel,
        name="mixer_backward_state",
        grid=(seqs,),
        in_specs=[per_seq((length, width)),
                  pl.BlockSpec((1, wide, width), lambda s: (2, 0, 0)),
                  block, block, block, block, whole(vec.shape), per_seq((length, 8))],
        out_specs=[block, block, block, block, per_seq((2, wide)),
                   whole((wide, width)), whole((1, wide))],
        out_shape=[sd(rec.shape, LOW), full, full, full, sd((seqs, 2, wide), F32),
                   sd((wide, width), LOW), sd((1, wide), F32)],
        scratch_shapes=[pltpu.VMEM((wide, width), F32), pltpu.VMEM((1, wide), F32)],
        compiler_params=plain_params(),
    )(ball, wq, gate_pre, state, mixed, rec, vec, mask)


def mixer_four_kernel(
    a, b, gs, carry_in_ref, state, start, conv_r, rec_r, open_r, vec, rgate, igate, mask,
    grad_conv, drg, dig, sums, ext, prev_ext, acc_s,
):
    seq = pl.program_id(0)
    length, wide = rec_r.shape[1], rec_r.shape[2]

    @pl.when(seq == 0)
    def _():
        drg[...] = jnp.zeros_like(drg)
        dig[...] = jnp.zeros_like(dig)
        acc_s[...] = jnp.zeros_like(acc_s)

    carry = carry_in_ref[0]
    ext[pl.ds(length, TILE)] = jnp.broadcast_to(carry, (TILE, wide))
    for t in range(length // TILE - 1, -1, -1):
        rows = pl.ds(t * TILE, TILE)
        now = b[0, rows] + a[0, rows] * carry
        ext[rows] = now
        carry = now[0:1]
    carried = gs[0] + ext[pl.ds(1, length)]
    prev_ext[0:TILE] = jnp.broadcast_to(start[0], (TILE, wide))
    prev_ext[pl.ds(TILE, length)] = state[0]
    previous = prev_ext[pl.ds(TILE - 1, length)]
    rec, opening, conv = rec_r[0], open_r[0], conv_r[0]
    reset = mask[0, :, 3:4] > 0.5
    decay, scaling = decay_terms(rec, vec[5:6], reset)
    pulled = carried * scaling
    grad_opening = pulled * conv
    direct = pulled * opening
    grad_log = carried * (previous * decay - opening * conv * (decay * decay / scaling))
    grad_log = jnp.where(reset, 0.0, grad_log)
    grad_rec = grad_log * (-8.0 * vec[5:6])
    grad_rpre = grad_rec * rec * (1.0 - rec)
    grad_opre = grad_opening * opening * (1.0 - opening)
    r_low, o_low, conv_low = grad_rpre.astype(LOW), grad_opre.astype(LOW), conv.astype(LOW)
    total = direct + nt(r_low, rgate[...]) + nt(o_low, igate[...])
    grad_conv[0] = total
    drg[...] += tn(conv_low, r_low)
    dig[...] += tn(conv_low, o_low)
    acc_s[0:1] += jnp.sum(grad_rpre, axis=0, keepdims=True)
    acc_s[1:2] += jnp.sum(grad_opre, axis=0, keepdims=True)
    acc_s[2:3] += jnp.sum(grad_log * rec, axis=0, keepdims=True) * (8.0 * vec[6:7])
    acc_s[3:4] += jnp.sum(total, axis=0, keepdims=True)
    sums[...] = acc_s[...]


def mixer_four(a, b, gs, carry, state, start, conv, rec, opening, vec, rgate, igate, mask):
    seqs, length, wide = rec.shape
    sd = jax.ShapeDtypeStruct
    block = per_seq((length, wide))
    one = per_seq((1, wide))
    square = whole((wide, wide))
    return pl.pallas_call(
        mixer_four_kernel,
        name="mixer_backward_gates",
        grid=(seqs,),
        in_specs=[block, block, block, one, block, one, block, block, block,
                  whole(vec.shape), square, square, per_seq((length, 8))],
        out_specs=[block, square, square, whole((4, wide))],
        out_shape=[sd(rec.shape, F32), sd((wide, wide), F32), sd((wide, wide), F32),
                   sd((4, wide), F32)],
        scratch_shapes=[pltpu.VMEM((length + TILE, wide), F32)] * 2 + [pltpu.VMEM((4, wide), F32)],
        compiler_params=plain_params(),
    )(a, b, gs, carry.reshape(seqs, 1, wide), state, start.reshape(seqs, 1, wide), conv, rec,
      opening, vec, rgate, igate, mask)


def mixer_five_kernel(
    grad_conv, head, lext, taps, mask, gate_low, nrm, wg, wl,
    part, dwg, dwl, sums, ext, acc_g, acc_l, acc_s,
):
    seq = pl.program_id(0)
    length, wide = grad_conv.shape[1], grad_conv.shape[2]

    @pl.when(seq == 0)
    def _():
        acc_g[...] = jnp.zeros_like(acc_g)
        acc_l[...] = jnp.zeros_like(acc_l)
        acc_s[...] = jnp.zeros_like(acc_s)

    grad = grad_conv[0]
    ext[pl.ds(0, length)] = grad
    ext[pl.ds(length, TILE)] = head[0]
    grad_lifted = taps[0:1] * grad
    acc_s[0:1] += jnp.sum(grad * lext[0, pl.ds(TILE, length)], axis=0, keepdims=True)
    for k in range(1, 4):
        grad_lifted = grad_lifted + taps[k : k + 1] * ext[pl.ds(k, length)] * mask[0, :, 3 + k : 4 + k]
        behind = lext[0, pl.ds(TILE - k, length)] * mask[0, :, k - 1 : k]
        acc_s[k : k + 1] += jnp.sum(grad * behind, axis=0, keepdims=True)
    acc_s[4:5] += jnp.sum(grad_lifted, axis=0, keepdims=True)
    lift_low = grad_lifted.astype(LOW)
    tokens = nrm[0]
    part[0] = (nn(gate_low[0], wg[0]) + nn(lift_low, wl[0])).astype(LOW)
    acc_g[...] += tn(gate_low[0], tokens)
    acc_l[...] += tn(lift_low, tokens)

    @pl.when(seq == pl.num_programs(0) - 1)
    def _():
        dwg[...] = acc_g[...].astype(LOW)
        dwl[...] = acc_l[...].astype(LOW)
        sums[...] = acc_s[...]


def mixer_five(grad_conv, head, lext, taps, mask, gate_low, nall, wq):
    seqs, length, wide = grad_conv.shape
    width = wq.shape[2]
    sd = jax.ShapeDtypeStruct
    block = per_seq((length, wide))
    return pl.pallas_call(
        mixer_five_kernel,
        name="mixer_backward_conv",
        grid=(seqs,),
        in_specs=[block, per_seq((TILE, wide)), per_seq((length + TILE, wide)), whole(taps.shape),
                  per_seq((length, 8)), block, per_seq((length, width)),
                  pl.BlockSpec((1, wide, width), lambda s: (0, 0, 0)),
                  pl.BlockSpec((1, wide, width), lambda s: (1, 0, 0))],
        out_specs=[per_seq((length, width)), whole((wide, width)), whole((wide, width)),
                   whole((8, wide))],
        out_shape=[sd((seqs, length, width), LOW), sd((wide, width), LOW), sd((wide, width), LOW),
                   sd((8, wide), F32)],
        scratch_shapes=[pltpu.VMEM((length + TILE, wide), F32), pltpu.VMEM((wide, width), F32),
                        pltpu.VMEM((wide, width), F32), pltpu.VMEM((8, wide), F32)],
        compiler_params=plain_params(),
    )(grad_conv, head, lext, taps, mask, gate_low, nall, wq, wq)


ORDER = (3, 0, 2, 1)


def final_kernel(
    gpart, opart, inputs, resid, gresid, gain, gains, even, odd,
    output, ginputs, even_all, odd_own, gains_all,
    g_mate, g_out, g_in, gs1, gr1, gs2, gr2,
    o_mate, o_out, o_in, os1, or1, os2, or2,
    y_even, z_even, s_even, y_odd, z_odd, s_odd, gain_slots, gain_sums,
    ye_s, ye_r, ze_s, ze_r, yo_s, yo_r, zo_s, zo_r,
    ra_s, ra_r, rb_s, rb_r, gg_s, gg_r, gh_s, gh_r,
):
    me = Spot()
    r, c, z, y = me.r, me.c, me.z, me.y
    diag = (me.r_x + 1 - 2 * lax.rem(me.r_x, 2), c)
    chan_peers = [(r, lax.rem(c + d, 8)) for d in range(1, 8)]
    greet([me.core, me.x, diag] + chan_peers)
    odd_y = push(odd.at[1 - y], y_odd, (yo_s, yo_r), 0, me.ymate)
    even_y = [
        push(even.at[2 * k + 1 - y], y_even.at[k], (ye_s, ye_r), k, me.ymate) for k in range(4)
    ]
    g_copies = rows_sum_start(me, gpart, g_mate, (gs1, gr1))
    even_y[ORDER[0]].start()
    even_y[ORDER[1]].start()
    g_cross = rows_sum_cross(me, gpart, g_mate, g_out, g_in, g_copies, (gs2, gr2))
    o_copies = rows_sum_start(me, opart, o_mate, (os1, or1))
    o_cross = rows_sum_cross(me, opart, o_mate, o_out, o_in, o_copies, (os2, or2))

    def z_push(k, way):
        return push(s_even.at[k], z_even.at[k, way], (ze_s, ze_r), 2 * k + way,
                    me.up if way == 0 else me.dn)

    def odd_push(way):
        return push(s_odd, z_odd.at[way], (zo_s, zo_r), way, me.up if way == 0 else me.dn)

    def add_even(k):
        even_y[k].wait_recv()
        s_even[k] = (even[2 * k + y].astype(F32) + y_even[k].astype(F32)).astype(LOW)

    def hop_even(k):
        @pl.when(z < k)
        def _():
            @pl.when(z > 0)
            def _():
                landed(me, z_even.at[k, 0], (ze_s, ze_r), 2 * k + 0)
                s_even[k] = (s_even[k].astype(F32) + z_even[k, 0].astype(F32)).astype(LOW)

            z_push(k, 0).start()

        @pl.when(z > k)
        def _():
            @pl.when(z < 3)
            def _():
                landed(me, z_even.at[k, 1], (ze_s, ze_r), 2 * k + 1)
                s_even[k] = (s_even[k].astype(F32) + z_even[k, 1].astype(F32)).astype(LOW)

            z_push(k, 1).start()

    add_even(ORDER[0])
    odd_y.start()
    hop_even(ORDER[0])
    add_even(ORDER[1])
    even_y[ORDER[2]].start()
    hop_even(ORDER[1])
    odd_y.wait_recv()
    even_y[ORDER[3]].start()
    s_odd[...] = (odd[y].astype(F32) + y_odd[...].astype(F32)).astype(LOW)

    @pl.when(z < r)
    def _():
        @pl.when(z > 0)
        def _():
            landed(me, z_odd.at[0], (zo_s, zo_r), 0)
            s_odd[...] = (s_odd[...].astype(F32) + z_odd[0].astype(F32)).astype(LOW)

        odd_push(0).start()

    @pl.when(z > r)
    def _():
        @pl.when(z < 3)
        def _():
            landed(me, z_odd.at[1], (zo_s, zo_r), 1)
            s_odd[...] = (s_odd[...].astype(F32) + z_odd[1].astype(F32)).astype(LOW)

        odd_push(1).start()

    step = inputs.shape[0] // RS_CHUNKS
    gain_sum = 0.0
    for k in range(RS_CHUNKS):
        rows = pl.ds(k * step, step)
        grad = rows_sum_chunk(me, gpart, g_mate, g_in, g_copies, g_cross, k)
        vals = inputs[rows].astype(F32)
        scale = lax.rsqrt(jnp.mean(vals * vals, axis=-1, keepdims=True) + EPSILON)
        gain_sum = gain_sum + jnp.sum(grad * vals * scale, axis=0, keepdims=True)
        pulled = grad * gain[...]
        inner = jnp.mean(pulled * vals, axis=-1, keepdims=True)
        ginputs[rows] = (
            gresid[rows] + scale * pulled - vals * (scale * scale * scale * inner)
        ).astype(LOW)
    for k in range(8):
        lanes = pl.ds(k * 128, 128)
        gain_slots[0, k, 0:1] = gain_sum[:, k * 128 : (k + 1) * 128]
        gain_slots[0, k, 1:3] = gains[:, lanes]
        gain_slots[0, k, 3:8] = jnp.zeros((5, 128), F32)
    gain_copies = [
        push(gain_slots.at[0, lax.rem(c + d, 8)], gain_slots.at[1, d], (gg_s, gg_r), d,
             chan_peers[d - 1])
        for d in range(1, 8)
    ]
    for copy in gain_copies:
        copy.start()

    add_even(ORDER[2])
    hop_even(ORDER[2])
    add_even(ORDER[3])
    hop_even(ORDER[3])

    for k in range(RS_CHUNKS):
        rows = pl.ds(k * step, step)
        total = rows_sum_chunk(me, opart, o_mate, o_in, o_copies, o_cross, k)
        output[rows] = (resid[rows] + total).astype(LOW)

    shared = gain_slots[0, c]
    for copy in gain_copies:
        copy.wait_recv()
    for d in range(1, 8):
        shared = shared + gain_slots[1, d]
    gain_sums[0] = shared
    row_copies = [
        push(gain_sums.at[0], gain_sums.at[1 + i], (gh_s, gh_r), i, device)
        for i, device in enumerate((me.core, me.x, diag))
    ]
    for copy in row_copies:
        copy.start()

    for k in range(4):

        @pl.when(z == k)
        def _(k=k):
            @pl.when(z > 0)
            def _():
                landed(me, z_even.at[k, 0], (ze_s, ze_r), 2 * k + 0)
                s_even[k] = (s_even[k].astype(F32) + z_even[k, 0].astype(F32)).astype(LOW)

            @pl.when(z < 3)
            def _():
                landed(me, z_even.at[k, 1], (ze_s, ze_r), 2 * k + 1)
                s_even[k] = (s_even[k].astype(F32) + z_even[k, 1].astype(F32)).astype(LOW)

            even_all[r] = s_even[k]

    even_x = push(even_all.at[r], even_all.at[r], (ra_s, ra_r), 0, me.x)
    even_c = push(even_all.at[r], even_all.at[r], (ra_s, ra_r), 1, me.core)
    even_f = push(even_all.at[me.r_x], even_all.at[me.r_x], (ra_s, ra_r), 2, me.core)
    even_x.start()
    even_c.start()

    odd_x = push(odd_own, odd_own, (rb_s, rb_r), 0, me.x)
    odd_c = push(odd_own, odd_own, (rb_s, rb_r), 1, me.core)

    @pl.when(z == r)
    def _():
        @pl.when(r > 0)
        def _():
            landed(me, z_odd.at[0], (zo_s, zo_r), 0)
            s_odd[...] = (s_odd[...].astype(F32) + z_odd[0].astype(F32)).astype(LOW)

        @pl.when(r < 3)
        def _():
            landed(me, z_odd.at[1], (zo_s, zo_r), 1)
            s_odd[...] = (s_odd[...].astype(F32) + z_odd[1].astype(F32)).astype(LOW)

        odd_own[...] = s_odd[...]
        odd_x.start()
        odd_c.start()

    even_x.wait_recv()
    even_f.start()

    @pl.when(me.r_x == z)
    def _():
        odd_x.wait_recv()
        odd_c.start()

    @pl.when(jnp.logical_and(z != r, me.r_x != z))
    def _():
        odd_c.wait_recv()

    for copy in row_copies:
        copy.wait()
    gains_all[...] = gain_sums[0] + gain_sums[1] + gain_sums[2] + gain_sums[3]

    @pl.when(z == r)
    def _():
        odd_x.wait_send()
        odd_c.wait_send()

    @pl.when(me.r_x == z)
    def _():
        odd_c.wait_send()

    even_x.wait_send()
    even_c.wait()
    even_f.wait()
    for k in range(4):

        @pl.when(z < k)
        def _(k=k):
            z_push(k, 0).wait_send()

        @pl.when(z > k)
        def _(k=k):
            z_push(k, 1).wait_send()

    @pl.when(z < r)
    def _():
        odd_push(0).wait_send()

    @pl.when(z > r)
    def _():
        odd_push(1).wait_send()

    finish_sends(gain_copies + even_y + [odd_y] + g_copies + g_cross + o_copies + o_cross)


def final_step(gpart, opart, inputs, resid, gresid, gain, gains, even, odd):
    sd = jax.ShapeDtypeStruct
    length, width = inputs.shape
    scr = (
        rows_sum_scratch(length, width)
        + rows_sum_scratch(length, width)
        + [
            pltpu.VMEM((4,) + even.shape[1:], LOW),
            pltpu.VMEM((4, 2) + even.shape[1:], LOW),
            pltpu.VMEM((4,) + even.shape[1:], LOW),
            pltpu.VMEM(odd.shape[1:], LOW),
            pltpu.VMEM((2,) + odd.shape[1:], LOW),
            pltpu.VMEM(odd.shape[1:], LOW),
            pltpu.VMEM((2, 8, 8, 128), F32),
            pltpu.VMEM((4, 8, 128), F32),
        ]
        + sem_pair(4) + sem_pair(8) + sem_pair(1) + sem_pair(2)
        + sem_pair(3) + sem_pair(2) + sem_pair(8) + sem_pair(3)
    )
    return pl.pallas_call(
        final_kernel,
        name="final_sums",
        out_shape=[
            sd(inputs.shape, LOW),
            sd(inputs.shape, LOW),
            sd((4,) + even.shape[1:], LOW),
            sd(odd.shape[1:], LOW),
            sd((8, 128), F32),
        ],
        in_specs=[IN_VMEM] * 9,
        out_specs=[IN_VMEM] * 5,
        scratch_shapes=scr,
        compiler_params=comm_params(6),
    )(gpart, opart, inputs, resid, gresid, gain, gains, even, odd)


def token_masks(starts, first, length, seq_length):
    where_at = first - 3 + jnp.arange(length + 6, dtype=jnp.int32)
    tally = jnp.sum((starts[:, None, :] <= where_at[None, :, None]).astype(jnp.int32), axis=2)
    inside = jnp.logical_and(where_at >= 0, where_at < seq_length)
    tally = jnp.where(inside[None, :], tally, -1)
    own = tally[:, 3 : 3 + length]
    columns = [tally[:, 3 - k : 3 - k + length] == own for k in (1, 2, 3)]
    columns.append(tally[:, 2 : 2 + length] != own)
    columns += [tally[:, 3 + k : 3 + k + length] == own for k in (1, 2, 3)]
    columns.append(jnp.zeros_like(columns[0]))
    return jnp.stack(columns, axis=2).astype(F32)


def pair_diagonal(blocks):
    side = blocks.shape[1]
    empty = jnp.zeros((side, side), blocks.dtype)
    return jnp.concatenate(
        [jnp.concatenate([blocks[0], empty], 1), jnp.concatenate([empty, blocks[1]], 1)], 0
    )


def split_body(
    inputs, mix_gain, gate_proj, gate_bias, lift_proj, lift_bias, conv_taps, conv_bias,
    recur_gate, recur_bias, input_gate, input_bias, decay_param, out_proj, out_bias, mlp_gain,
    mlp_gate, mlp_up, mlp_down, doc_starts, cotangent,
):
    r = lax.axis_index("rows")
    c = lax.axis_index("chan")
    length = inputs.shape[0]
    seq_length = length * 8
    wide = 2 * GB
    quarter = mlp_gate.shape[1] // 4
    rows_f32 = inputs.astype(F32)
    nrm = rms_scale(rows_f32, mix_gain).astype(LOW)
    wm = jnp.stack([gate_proj.T, lift_proj.T, out_proj])
    cut_columns = lambda w: lax.dynamic_slice(w, (0, r * quarter), (w.shape[0], quarter)).T
    wg, wu, wd = [
        lax.all_gather(w, "chan", axis=0, tiled=True)
        for w in (
            cut_columns(mlp_gate),
            cut_columns(mlp_up),
            lax.dynamic_slice(mlp_down, (r * quarter, 0), (quarter, mlp_down.shape[1])),
        )
    ]
    starts = jnp.pad(doc_starts, ((0, 7), (0, 120)))
    wq, nall, call, halo, starts_all = gather(wm, nrm, cotangent, starts)
    mask = token_masks(starts_all[:, 0, : doc_starts.shape[1]], c * length, length, seq_length)
    mine = lambda v: lax.dynamic_slice_in_dim(v, r * wide, wide, axis=v.ndim - 1)
    decay_own = mine(decay_param)
    vec = jnp.stack(
        [mine(gate_bias), mine(lift_bias), mine(conv_bias), mine(recur_bias), mine(input_bias),
         jax.nn.softplus(-decay_own), jax.nn.sigmoid(-decay_own), jnp.zeros_like(decay_own)]
    )
    taps = mine(conv_taps)
    rgate = pair_diagonal(lax.dynamic_slice_in_dim(recur_gate, 2 * r, 2, 0)).astype(LOW)
    igate = pair_diagonal(lax.dynamic_slice_in_dim(input_gate, 2 * r, 2, 0)).astype(LOW)
    gate_pre, lext, conv, rec, opening, a, b, tot = mixer_one(
        nall, halo, wq, vec, taps, rgate, igate, mask
    )
    start = carry_in(tot, False)
    state, mixed, part = mixer_two(a, b, start, gate_pre, wq)
    resid, n2all = resid_step(part, inputs, out_bias[None], mlp_gain[None])
    opart, gpart2, dg, du, dd = mlp(n2all, call, wg, wu, wd)
    gresid, ball, gains = grad_resid_step(gpart2, cotangent, resid, mlp_gain[None])
    gate_low, gs, a2, b2, tot2, dwo, gate_sum = mixer_three(
        ball, wq, gate_pre, state, mixed, rec, vec, mask
    )
    carry = carry_in(tot2, True)
    grad_conv, drg, dig, sums4 = mixer_four(
        a2, b2, gs, carry, state, start, conv, rec, opening, vec, rgate, igate, mask
    )
    head = from_behind(grad_conv[:, :TILE], "chan", -1)
    gpart, dwg, dwl, sums5 = mixer_five(grad_conv, head, lext, taps, mask, gate_low, nall, wq)
    vectors = jnp.concatenate([gate_sum, sums5[4:5], sums5[0:4], sums4[3:4], sums4[0:3]], axis=0)
    small_odd = jnp.pad(
        vectors.reshape(10, 2, GB).transpose(1, 0, 2).reshape(2, 10 * GB).astype(LOW),
        ((0, 0), (0, 16 * D - 10 * GB)),
    ).reshape(2, 16, D)
    odd = jnp.concatenate(
        [dwg.reshape(2, GB, D), dwl.reshape(2, GB, D), dwo.reshape(2, GB, D), small_odd], axis=1
    )
    blocks = jnp.stack(
        [jnp.stack([m[:GB, :GB], m[GB:, GB:]]) for m in (drg, dig)]
    ).reshape(2, 2, 8, GB // 8, GB)
    small_even = jnp.pad(
        blocks.transpose(2, 0, 1, 3, 4).reshape(8, 18, D).astype(LOW), ((0, 0), (0, 14), (0, 0))
    )
    even = jnp.concatenate([w.reshape(8, quarter, D) for w in (dg, du, dd)] + [small_even], axis=1)
    output, grad_inputs, even_all, odd_own, gains_all = final_step(
        gpart, opart, inputs, resid, gresid, mix_gain[None], gains, even, odd
    )
    even_all = even_all.astype(F32)
    odd_own = odd_own.astype(F32)
    piece = lambda i: even_all[:, i * quarter : (i + 1) * quarter].reshape(4 * quarter, D)
    gates = even_all[:, 3 * quarter : 3 * quarter + 18].reshape(4, 2, 2, GB // 8, GB)
    gate_out = lambda i: gates[:, i].reshape(8, GB // 8, GB)
    own = odd_own[3 * GB :].reshape(-1)[: 10 * GB].reshape(10, GB)
    return (
        output, grad_inputs, gains_all[0],
        odd_own[:GB].T, own[0], odd_own[GB : 2 * GB].T, own[1], own[2:6], own[6],
        gate_out(0), own[7], gate_out(1), own[8], own[9],
        odd_own[2 * GB : 3 * GB], gains_all[2], gains_all[1],
        piece(0).T, piece(1).T, piece(2),
    )


def solution(mesh):
    in_specs = (
        P(("rows", "chan"), None),
        P(),
        P(None, "chan"),
        P(),
        P(None, "chan"),
        P(),
        P(),
        P(),
        P(),
        P(),
        P(),
        P(),
        P(),
        P("chan", None),
        P(),
        P(),
        P(None, "chan"),
        P(None, "chan"),
        P("chan", None),
        P("rows", None),
        P(("rows", "chan"), None),
    )
    out_specs = (
        P(("rows", "chan"), None),
        P(("rows", "chan"), None),
        P("chan"),
        P(None, "chan"),
        P("chan"),
        P(None, "chan"),
        P("chan"),
        P(None, "chan"),
        P("chan"),
        P(None, "chan", None),
        P("chan"),
        P(None, "chan", None),
        P("chan"),
        P("chan"),
        P("chan", None),
        P("chan"),
        P("chan"),
        P(None, "chan"),
        P(None, "chan"),
        P("chan", None),
    )
    split = mesh.shape["rows"] == 4 and mesh.shape["chan"] == HEADS
    return jax.shard_map(split_body if split else body, mesh=mesh, in_specs=in_specs, out_specs=out_specs, check_vma=False)
```

```python
from functools import partial
import math

import jax
import jax.numpy as jnp
from jax import lax
from jax.experimental import pallas as pl
from jax.experimental.pallas import tpu as pltpu
from jax.sharding import PartitionSpec as P

D = 1024
LRU = 1536
FF = 3072
HEADS = 8
GB = 192


EPSILON = 1e-06
precise = lax.Precision.HIGHEST


def from_behind(block, axis, distance):
    devices = range(lax.axis_size(axis))
    route = [(i - distance, i) for i in devices if i - distance in devices]
    return lax.ppermute(block, axis, route)


def prefix(value, axis, join, neutral, backward):
    count, mine = (lax.axis_size(axis), lax.axis_index(axis))
    pieces = jax.tree.map(lambda part: lax.all_gather(part, axis), value)
    if backward:
        pieces = jax.tree.map(lambda part: part[::-1], pieces)
        mine = count - 1 - mine
    subtotal = jax.tree.map(
        lambda part, zero: jnp.full_like(part, 0) + jnp.asarray(zero, part.dtype), value, neutral
    )

    def hop(position, subtotal):
        longer = join(subtotal, jax.tree.map(lambda part: part[position], pieces))
        return jax.tree.map(lambda new, old: jnp.where(position < mine, new, old), longer, subtotal)

    return lax.fori_loop(0, count - 1, hop, subtotal)


def rms_scale(values, gain_vec):
    return (
        values * lax.rsqrt(jnp.mean(values * values, axis=-1, keepdims=True) + EPSILON) * gain_vec
    )


def gated_unit(gate_pre, up_vals):
    return jax.nn.gelu(gate_pre) * up_vals


def affine(earlier, later_map):
    return (earlier[0] * later_map[0], later_map[0] * earlier[1] + later_map[1])


def segment_ids(starts, start_pos, pos_count, seq_len):
    where_at = start_pos + jnp.arange(pos_count, dtype=jnp.int32)
    seq_of = jnp.floor_divide(where_at, seq_len)
    within = where_at - seq_of * seq_len
    owner = seq_of[:, None] == jnp.arange(starts.shape[0], dtype=jnp.int32)[None, :]
    passed = starts[None, :, :] <= within[:, None, None]
    doc_tally = jnp.sum(jnp.logical_and(owner[:, :, None], passed).astype(jnp.int32), axis=(1, 2))
    return seq_of * (starts.shape[1] + 1) + doc_tally


def project(normed, weights, first_bias, second_bias):
    product = jnp.einsum("td,dc->ct", normed, weights, preferred_element_type=jnp.float32)
    channels = first_bias.shape[0]
    return (product[:channels] + first_bias[:, None], product[channels:] + second_bias[:, None])


def conv_forward(lifted, tail_rows, segments, tap_vals, bias_vec):
    length = lifted.shape[1]
    extended = jnp.concatenate([tail_rows, lifted], axis=1)
    own_seg = segments[3 : 3 + length]
    result = bias_vec[:, None] + tap_vals[0][:, None] * lifted
    for offset in range(1, 4):
        same_doc = (segments[3 - offset : 3 - offset + length] == own_seg).astype(jnp.float32)
        result = (
            result
            + tap_vals[offset][:, None]
            * extended[:, 3 - offset : 3 - offset + length]
            * same_doc[None, :]
        )
    return result


def conv_backward(grad_conv, head_rows, segments, lifted, tail_rows, tap_vals):
    length = grad_conv.shape[1]
    ahead_grad = jnp.concatenate([grad_conv, head_rows], axis=1)
    behind = jnp.concatenate([tail_rows, lifted], axis=1)
    own_seg = segments[3 : 3 + length]
    grad_lifted = tap_vals[0][:, None] * grad_conv
    tap_grads = [jnp.sum(grad_conv * lifted, axis=1)]
    for offset in range(1, 4):
        later_same = (segments[3 + offset : 3 + offset + length] == own_seg).astype(jnp.float32)
        grad_lifted = (
            grad_lifted
            + tap_vals[offset][:, None]
            * ahead_grad[:, offset : offset + length]
            * later_same[None, :]
        )
        earlier = (segments[3 - offset : 3 - offset + length] == own_seg).astype(jnp.float32)
        tap_grads.append(
            jnp.sum(
                grad_conv * behind[:, 3 - offset : 3 - offset + length] * earlier[None, :], axis=1
            )
        )
    return (grad_lifted, jnp.stack(tap_grads, axis=1), jnp.sum(grad_conv, axis=1))


def coefficients(is_reset, conv_out, recur_gate, recur_bias, input_gate, input_bias, decay_param):
    channels, length = conv_out.shape
    gate_block = recur_gate.shape[1]
    grouped = conv_out.reshape(channels // gate_block, gate_block, length)
    recurrence = jax.nn.sigmoid(
        jnp.einsum("hit,hio->hot", grouped, recur_gate, precision=precise).reshape(channels, length)
        + recur_bias[:, None]
    )
    opening = jax.nn.sigmoid(
        jnp.einsum("hit,hio->hot", grouped, input_gate, precision=precise).reshape(channels, length)
        + input_bias[:, None]
    )
    log_decay = -8.0 * recurrence * jax.nn.softplus(-decay_param)[:, None]
    decay_rate = jnp.where(is_reset[None, :], 0.0, jnp.exp(log_decay))
    scaling = jnp.where(is_reset[None, :], 1.0, jnp.sqrt(-jnp.expm1(2.0 * log_decay)))
    return (decay_rate, scaling * opening * conv_out)


def reverse_local(decay_rate, grad_state):
    ones_col = jnp.ones_like(decay_rate[:, :1])
    factor = jnp.flip(jnp.concatenate([decay_rate[:, 1:], ones_col], axis=1), axis=1)
    product, carried = lax.associative_scan(affine, (factor, jnp.flip(grad_state, axis=1)), axis=1)
    return (jnp.flip(product, axis=1), jnp.flip(carried, axis=1))


def finish_state(lru_state, start_state, carried, pull_coef):
    previous = jnp.concatenate([start_state[:, None], lru_state[:, :-1]], axis=1)
    return pull_coef((carried * previous, carried))


def flatten_rows(pieces, row_count):
    return jnp.concatenate([source.reshape(row_count, -1) for source in pieces], axis=1)


def body(
    inputs,
    mix_gain,
    gate_proj,
    gate_bias,
    lift_proj,
    lift_bias,
    conv_taps,
    conv_bias,
    recur_gate,
    recur_bias,
    input_gate,
    input_bias,
    decay_param,
    out_proj,
    out_bias,
    mlp_gain,
    mlp_gate,
    mlp_up,
    mlp_down,
    doc_starts,
    cotangent,
):
    chan_count = lax.axis_size("chan")
    chan_place = lax.axis_index("chan")
    local_rows = inputs.shape[0]
    seq_length = local_rows * chan_count
    rows_f32 = inputs.astype(jnp.float32)
    cot_f32 = cotangent.astype(jnp.float32)
    normed, pull_norm = jax.vjp(rms_scale, rows_f32, mix_gain)
    normed_low = normed.astype(jnp.bfloat16)
    gate_full, lift_full, out_full, mlp_gate_full, mlp_up_full, mlp_down_full = (
        lax.all_gather(gate_proj, "chan", axis=1, tiled=True),
        lax.all_gather(lift_proj, "chan", axis=1, tiled=True),
        lax.all_gather(out_proj, "chan", axis=0, tiled=True),
        lax.all_gather(mlp_gate, "chan", axis=1, tiled=True),
        lax.all_gather(mlp_up, "chan", axis=1, tiled=True),
        lax.all_gather(mlp_down, "chan", axis=0, tiled=True),
    )
    channels = LRU
    hidden_cut = FF
    segments = segment_ids(doc_starts, chan_place * local_rows - 3, local_rows + 6, seq_length)
    mix_proj = jnp.concatenate([gate_full, lift_full], axis=1)
    gate_pre, lifted = project(normed_low, mix_proj, gate_bias, lift_bias)
    tail_rows = from_behind(lifted[:, -3:], "chan", 1)
    conv_out = conv_forward(lifted, tail_rows, segments, conv_taps, conv_bias)
    is_reset = segments[3 : 3 + local_rows] != segments[2 : 2 + local_rows]
    (decay_rate, lru_input), pull_coef = jax.vjp(
        partial(coefficients, is_reset),
        conv_out,
        recur_gate,
        recur_bias,
        input_gate,
        input_bias,
        decay_param,
    )
    running, local_state = lax.associative_scan(affine, (decay_rate, lru_input), axis=1)
    ones_vec = jnp.ones((channels,), jnp.float32)
    zeros_vec = jnp.zeros((channels,), jnp.float32)
    _, start_state = prefix(
        (running[:, -1], local_state[:, -1]), "chan", affine, (ones_vec, zeros_vec), False
    )
    lru_state = local_state + running * start_state[:, None]
    gate_val, pull_gelu = jax.vjp(jax.nn.gelu, gate_pre)
    mixed_out = (lru_state * gate_val).astype(jnp.bfloat16)
    resid = (
        rows_f32
        + jnp.einsum("ct,cd->td", mixed_out, out_full, preferred_element_type=jnp.float32)
        + out_bias
    )
    normed2, pull_norm2 = jax.vjp(rms_scale, resid, mlp_gain)
    normed2_low = normed2.astype(jnp.bfloat16)
    mlp_proj = jnp.concatenate([mlp_gate_full, mlp_up_full], axis=1)
    mlp_pre = jnp.einsum("td,df->ft", normed2_low, mlp_proj, preferred_element_type=jnp.float32)
    hidden, pull_mlp = jax.vjp(gated_unit, mlp_pre[:hidden_cut], mlp_pre[hidden_cut:])
    hidden_low = hidden.astype(jnp.bfloat16)
    output = (
        resid
        + jnp.einsum("ft,fd->td", hidden_low, mlp_down_full, preferred_element_type=jnp.float32)
    ).astype(jnp.bfloat16)
    grad_down = jnp.einsum("ft,td->fd", hidden_low, cotangent, preferred_element_type=jnp.float32)
    grad_gate_m, grad_up_m = pull_mlp(
        jnp.einsum("td,fd->ft", cotangent, mlp_down_full, preferred_element_type=jnp.float32)
    )
    grad_pre = jnp.concatenate([grad_gate_m, grad_up_m], axis=0).astype(jnp.bfloat16)
    grad_mlp_in = jnp.einsum("ft,td->fd", grad_pre, normed2_low, preferred_element_type=jnp.float32)
    grad_resid_part, grad_gain2 = pull_norm2(
        jnp.einsum("ft,df->td", grad_pre, mlp_proj, preferred_element_type=jnp.float32)
    )
    grad_resid = cot_f32 + grad_resid_part
    grad_branch = grad_resid.astype(jnp.bfloat16)
    grad_out_proj = jnp.einsum(
        "ct,td->cd", mixed_out, grad_branch, preferred_element_type=jnp.float32
    )
    grad_mixed = jnp.einsum("td,cd->ct", grad_branch, out_full, preferred_element_type=jnp.float32)
    product, carried = reverse_local(decay_rate, grad_mixed * gate_val)
    _, incoming = prefix(
        (decay_rate[:, 0] * product[:, 0], decay_rate[:, 0] * carried[:, 0]),
        "chan",
        affine,
        (ones_vec, zeros_vec),
        True,
    )
    carried = carried + product * incoming[:, None]
    coef_grads = finish_state(lru_state, start_state, carried, pull_coef)
    head_rows = from_behind(coef_grads[0][:, :3], "chan", -1)
    grad_lifted, grad_taps, grad_conv_bias = conv_backward(
        coef_grads[0], head_rows, segments, lifted, tail_rows, conv_taps
    )
    (grad_gate_pre,) = pull_gelu(grad_mixed * lru_state)
    grad_front = jnp.concatenate([grad_gate_pre, grad_lifted], axis=0).astype(jnp.bfloat16)
    grad_mix_proj = jnp.einsum(
        "ct,td->cd", grad_front, normed_low, preferred_element_type=jnp.float32
    )
    grad_normed = jnp.einsum("ct,dc->td", grad_front, mix_proj, preferred_element_type=jnp.float32)
    grad_x_part, grad_gain1 = pull_norm(grad_normed)
    grad_inputs = (grad_resid + grad_x_part).astype(jnp.bfloat16)
    grad_out_bias = jnp.sum(grad_resid, axis=0)
    pieces = [
        grad_mix_proj[:channels],
        grad_mix_proj[channels:],
        jnp.sum(grad_gate_pre, axis=1),
        jnp.sum(grad_lifted, axis=1),
        grad_taps,
        grad_conv_bias,
        jnp.transpose(coef_grads[1], (1, 0, 2)),
        coef_grads[2],
        jnp.transpose(coef_grads[3], (1, 0, 2)),
        coef_grads[4],
        coef_grads[5],
        grad_out_proj,
        grad_mlp_in[:hidden_cut],
        grad_mlp_in[hidden_cut:],
        grad_down,
        grad_gain1,
        grad_out_bias,
        grad_gain2,
    ]
    spread = flatten_rows(pieces, chan_count)
    shared = lax.psum_scatter(spread, "chan", scatter_dimension=0, tiled=True)
    summed = lax.psum(shared.reshape(-1), "rows")
    channels_dev = LRU // chan_count
    hidden_dev = FF // chan_count
    width_dev = D // chan_count
    block_dev = GB // chan_count
    shapes = [
        (channels_dev, D),
        (channels_dev, D),
        (channels_dev,),
        (channels_dev,),
        (channels_dev, 4),
        (channels_dev,),
        (block_dev, HEADS, GB),
        (channels_dev,),
        (block_dev, HEADS, GB),
        (channels_dev,),
        (channels_dev,),
        (channels_dev, D),
        (hidden_dev, D),
        (hidden_dev, D),
        (hidden_dev, D),
        (width_dev,),
        (width_dev,),
        (width_dev,),
    ]
    unpacked = []
    offset = 0
    for piece_shape in shapes:
        piece_size = math.prod(piece_shape)
        unpacked.append(summed[offset : offset + piece_size].reshape(piece_shape))
        offset = offset + piece_size
    return (
        output,
        grad_inputs,
        unpacked[15],
        unpacked[0].T,
        unpacked[2],
        unpacked[1].T,
        unpacked[3],
        unpacked[4].T,
        unpacked[5],
        jnp.transpose(unpacked[6], (1, 0, 2)),
        unpacked[7],
        jnp.transpose(unpacked[8], (1, 0, 2)),
        unpacked[9],
        unpacked[10],
        unpacked[11],
        unpacked[16],
        unpacked[17],
        unpacked[12].T,
        unpacked[13].T,
        unpacked[14],
    )


MESH = pl.DeviceIdType.MESH
LOW = jnp.bfloat16
F32 = jnp.float32
VMEM_BYTES = 60 * 2**20
TILE = 8
GELU_A = math.sqrt(2.0 / math.pi)
GELU_B = 0.044715


def nt(left, right):
    return lax.dot_general(left, right, (((1,), (1,)), ((), ())), preferred_element_type=F32)


def nn(left, right):
    return lax.dot_general(left, right, (((1,), (0,)), ((), ())), preferred_element_type=F32)


def tn(left, right):
    return lax.dot_general(left, right, (((0,), (0,)), ((), ())), preferred_element_type=F32)


def gelu_pair(values):
    squared = values * values
    bend = jnp.tanh(GELU_A * values * (1.0 + GELU_B * squared))
    half = 0.5 * (1.0 + bend)
    slope = half + 0.5 * values * (1.0 - bend * bend) * GELU_A * (1.0 + 3.0 * GELU_B * squared)
    return values * half, slope


class Spot:
    def __init__(self):
        self.r = lax.axis_index("rows")
        self.c = lax.axis_index("chan")
        self.z = lax.div(self.c, 2)
        self.y = lax.rem(self.c, 2)
        self.r_core = self.r + 1 - 2 * lax.rem(self.r, 2)
        self.r_x = lax.rem(self.r + 2, 4)
        self.core = (self.r_core, self.c)
        self.x = (self.r_x, self.c)
        self.c_y = self.c + 1 - 2 * self.y
        self.ymate = (self.r, self.c_y)
        self.up = (self.r, lax.rem(self.c + 2, 8))
        self.dn = (self.r, lax.rem(self.c + 6, 8))


def greet(always, maybe=()):
    barrier = pltpu.get_barrier_semaphore()
    count = len(always)
    for device in always:
        pl.semaphore_signal(barrier, inc=1, device_id=device, device_id_type=MESH)
    for device, there in maybe:

        @pl.when(there)
        def _(device=device):
            pl.semaphore_signal(barrier, inc=1, device_id=device, device_id_type=MESH)

        count = count + jnp.where(there, 1, 0)
    pl.semaphore_wait(barrier, count)


def push(source, target, sems, index, device):
    return pltpu.make_async_remote_copy(
        src_ref=source,
        dst_ref=target,
        send_sem=sems[0].at[index],
        recv_sem=sems[1].at[index],
        device_id=device,
        device_id_type=MESH,
    )


def landed(me, target, sems, index):
    push(target, target, sems, index, me.ymate).wait_recv()


def sem_pair(count):
    return [pltpu.SemaphoreType.DMA((count,)), pltpu.SemaphoreType.DMA((count,))]


def comm_params(collective_id):
    return pltpu.CompilerParams(
        collective_id=collective_id, has_side_effects=True, vmem_limit_bytes=VMEM_BYTES
    )


def plain_params():
    return pltpu.CompilerParams(
        dimension_semantics=("arbitrary",), vmem_limit_bytes=VMEM_BYTES
    )


ANYWHERE = pl.BlockSpec(memory_space=pl.ANY)
IN_VMEM = pl.BlockSpec(memory_space=pltpu.VMEM)


def whole(shape):
    return pl.BlockSpec(shape, lambda s: (0,) * len(shape))


def per_seq(shape):
    return pl.BlockSpec((1,) + shape, lambda s: (s,) + (0,) * len(shape))


def decay_terms(rec, softplus_row, reset):
    log_decay = -8.0 * rec * softplus_row
    decay = jnp.exp(log_decay)
    twice = 2.0 * log_decay
    series = twice * (
        1.0
        + twice * (1 / 2 + twice * (1 / 6 + twice * (1 / 24 + twice * (1 / 120 + twice * (1 / 720)))))
    )
    gap = jnp.where(twice > -0.25, -series, 1.0 - jnp.exp(twice))
    return decay, jnp.where(reset, 1.0, jnp.sqrt(gap))


def fill_tallies(tallies, starts_row, first, length, seq_length):
    position = first - 8 + lax.broadcasted_iota(jnp.int32, (length + 16, 1), 0)
    begun = jnp.sum((starts_row <= position).astype(F32), axis=1, keepdims=True)
    inside = jnp.logical_and(position >= 0, position < seq_length)
    tallies[...] = jnp.broadcast_to(jnp.where(inside, begun, -1.0), tallies.shape)


def same_document(tallies, length, shift, wide):
    own = tallies[pl.ds(8, length)]
    other = tallies[pl.ds(8 + shift, length)]
    same = (own == other).astype(F32)
    return jnp.concatenate([same] * (wide // same.shape[1]), axis=1)


def pair_diagonal(target, blocks):
    side = blocks.shape[1]
    target[...] = jnp.zeros_like(target)
    target[0:side, 0:side] = blocks[0].astype(target.dtype)
    target[side : 2 * side, side : 2 * side] = blocks[1].astype(target.dtype)


def tile_scan(a, b, backward):
    row = lax.broadcasted_iota(jnp.int32, a.shape, 1)
    for step in (1, 2, 4):
        shift = TILE - step if backward else step
        there = row < TILE - step if backward else row >= step
        b = b + a * jnp.where(there, pltpu.roll(b, shift, 1), 0.0)
        a = a * jnp.where(there, pltpu.roll(a, shift, 1), 1.0)
    return a, b


def carry_start(me, backward, totals, slots, sems):
    sign = -1 if backward else 1
    steps = me.c if backward else 7 - me.c
    copies = [
        push(totals, slots.at[d], sems, d, (me.r, lax.rem(me.c + 8 + sign * d, 8)))
        for d in range(1, 8)
    ]
    for d in range(1, 8):

        @pl.when(d <= steps)
        def _(d=d):
            copies[d - 1].start()

    return copies


def carry_join(me, backward, slots, start, sems):
    behind = 7 - me.c if backward else me.c
    start[...] = jnp.zeros_like(start)
    for d in range(7, 0, -1):

        @pl.when(d <= behind)
        def _(d=d):
            landed(me, slots.at[d], sems, d)
            start[...] = slots[d, :, 0] * start[...] + slots[d, :, 1]


def carry_sent(me, backward, copies):
    steps = me.c if backward else 7 - me.c
    for d in range(1, 8):

        @pl.when(d <= steps)
        def _(d=d):
            copies[d - 1].wait_send()


def peers_of(me):
    return [(me.r, lax.rem(me.c + d, 8)) for d in range(1, 8)]


class Spread:
    def __init__(self, me, arrays, pieces, sems):
        self.me, self.arrays, self.pieces, self.sems = me, arrays, pieces, sems
        self.go_up = jnp.logical_and(me.z >= me.r, me.z < 3)
        self.go_dn = jnp.logical_and(me.z <= me.r, me.z > 0)
        self.source = me.z == me.r
        self.hop = jnp.where(me.z < me.r, me.r - me.z, me.z - me.r)

    def slab(self, i, k, half):
        size = self.arrays[i].shape[1] // self.pieces
        return self.arrays[i].at[half, pl.ds(pl.multiple_of(k * size, 16), size)]

    def copies(self, k):
        me, found = self.me, []
        for i in range(len(self.arrays)):
            piece = self.slab(i, k, me.y)
            ys, yr, us, ds, zr = self.sems[5 * i : 5 * i + 5]
            found.append(
                (
                    push(piece, piece, (ys, yr), k, me.ymate),
                    push(piece, piece, (us, zr), k, me.up),
                    push(piece, piece, (ds, zr), k, me.dn),
                )
            )
        return found

    def send(self, k):
        found = self.copies(k)
        for copies in found:
            copies[0].start()

        @pl.when(self.go_up)
        def _():
            for copies in found:
                copies[1].start()

        @pl.when(self.go_dn)
        def _():
            for copies in found:
                copies[2].start()

    def lead(self, k):
        @pl.when(self.source)
        def _():
            self.send(k)

    def follow(self, k):
        me = self.me
        for i in range(len(self.arrays)):
            us, zr = self.sems[5 * i + 2], self.sems[5 * i + 4]
            landed(me, self.slab(i, k, me.y), (us, zr), k)
        self.send(k)

    def step(self, p):
        if p < self.pieces:
            self.lead(p)
        k = p - self.hop
        there = jnp.logical_and(k >= 0, k < self.pieces)

        @pl.when(jnp.logical_and(there, jnp.logical_not(self.source)))
        def _():
            self.follow(lax.rem(k + 2 * self.pieces, self.pieces))

    def arrived(self, k):
        for i in range(len(self.arrays)):
            ys, yr = self.sems[5 * i], self.sems[5 * i + 1]
            landed(self.me, self.slab(i, k, 1 - self.me.y), (ys, yr), k)

    def sent(self, k):
        found = self.copies(k)
        for copies in found:
            copies[0].wait_send()

        @pl.when(self.go_up)
        def _():
            for copies in found:
                copies[1].wait_send()

        @pl.when(self.go_dn)
        def _():
            for copies in found:
                copies[2].wait_send()

    def close(self):
        @pl.loop(0, self.pieces)
        def _(k):
            self.arrived(k)
            self.sent(k)


def spread_sems(arrays, pieces):
    return [pltpu.SemaphoreType.DMA((pieces,))] * (5 * arrays)


class Reduce:
    def __init__(self, me, parts, mine, from_y, from_z, own, pieces, sems):
        self.me, self.parts, self.mine = me, parts, mine
        self.from_y, self.from_z, self.own = from_y, from_z, own
        self.pieces, self.sems = pieces, sems
        self.hop = jnp.where(me.z < me.r, me.z, 3 - me.z)
        self.owner = me.z == me.r
        self.relays = me.z == me.r_x

    def rows(self, i, k):
        size = self.mine[i].shape[0] // self.pieces
        return pl.ds(pl.multiple_of(k * size, 16), size)

    def each(self, k):
        for i in range(len(self.mine)):
            yield i, self.rows(i, k), self.sems[11 * i : 11 * i + 11]

    def y_copies(self, k):
        me = self.me
        return [
            push(self.parts[i].at[1 - me.y, rows], self.from_y[i].at[rows], sems[0:2], k, me.ymate)
            for i, rows, sems in self.each(k)
        ]

    def y_send(self, k):
        for copy in self.y_copies(k):
            copy.start()

    def add(self, i, rows, other):
        total = self.mine[i][rows].astype(F32) + other[i][rows].astype(F32)
        self.mine[i][rows] = total.astype(LOW)

    def join(self, k):
        for i, rows, sems in self.each(k):
            landed(self.me, self.from_y[i].at[rows], sems[0:2], k)
            self.add(i, rows, self.from_y)

    def z_copies(self, k, way):
        found = []
        for i, rows, sems in self.each(k):
            target = self.own if way == 2 else self.from_z
            pair = ((sems[2], sems[4]), (sems[3], sems[4]), (sems[3], sems[5]))[way]
            found.append(
                push(self.mine[i].at[rows], target[i].at[rows], pair, k,
                     self.me.up if way == 0 else self.me.dn)
            )
        return found

    def z_way(self, action):
        me = self.me
        for way, there in enumerate(
            (me.z < me.r, me.z > me.r + 1, me.z == me.r + 1)
        ):

            @pl.when(there)
            def _(way=way):
                action(way)

    def chain(self, k):
        @pl.when(self.hop > 0)
        def _():
            for i, rows, sems in self.each(k):
                landed(self.me, self.from_z[i].at[rows], (sems[2], sems[4]), k)
                self.add(i, rows, self.from_z)

        def start(way):
            for copy in self.z_copies(k, way):
                copy.start()

        self.z_way(start)

    def out_copies(self, k, device, pair):
        return [
            push(self.own[i].at[rows], self.own[i].at[rows], sems[pair : pair + 2], k, device)
            for i, rows, sems in self.each(k)
        ]

    def finish(self, k):
        @pl.when(self.me.z > 0)
        def _():
            for i, rows, sems in self.each(k):
                landed(self.me, self.from_z[i].at[rows], (sems[2], sems[4]), k)
                self.add(i, rows, self.from_z)

        @pl.when(self.me.z < 3)
        def _():
            for i, rows, sems in self.each(k):
                landed(self.me, self.own[i].at[rows], (sems[3], sems[5]), k)
                self.add(i, rows, self.own)

        for i, rows, sems in self.each(k):
            self.own[i][rows] = self.mine[i][rows]
        for copy in self.out_copies(k, self.me.x, 6) + self.out_copies(k, self.me.core, 8):
            copy.start()

    def relay(self, k):
        for copy in self.out_copies(k, self.me.x, 6):
            copy.wait_recv()
        for copy in self.out_copies(k, self.me.core, 8):
            copy.start()

    def step(self, p, ahead=2):
        pieces = self.pieces
        if p < 0:
            return
        if p < pieces:
            self.join(p)
            if p + ahead < pieces:
                self.y_send(p + ahead)

        def there(k):
            return jnp.logical_and(k >= 0, k < pieces), lax.rem(k + 4 * pieces, pieces)

        if p < pieces + 3:
            inside, k = there(p - self.hop)

            @pl.when(jnp.logical_and(inside, jnp.logical_not(self.owner)))
            def _():
                self.chain(k)

        if 0 <= p - 3 < pieces:

            @pl.when(self.owner)
            def _():
                self.finish(p - 3)

        if 0 <= p - 5 < pieces:

            @pl.when(self.relays)
            def _():
                self.relay(p - 5)

    def positions(self):
        return self.pieces + 5

    def close(self):
        others = jnp.logical_not(jnp.logical_or(self.owner, self.relays))

        @pl.loop(0, self.pieces)
        def _(k):
            for copy in self.y_copies(k):
                copy.wait_send()

            def sent(way):
                for copy in self.z_copies(k, way):
                    copy.wait_send()

            self.z_way(sent)

            @pl.when(self.owner)
            def _():
                for copy in self.out_copies(k, self.me.x, 6) + self.out_copies(k, self.me.core, 8):
                    copy.wait_send()

            @pl.when(self.relays)
            def _():
                for copy in self.out_copies(k, self.me.core, 8):
                    copy.wait_send()

            @pl.when(others)
            def _():
                for copy in self.out_copies(k, self.me.core, 8):
                    copy.wait_recv()


def reduce_sems(arrays, pieces):
    return [pltpu.SemaphoreType.DMA((pieces,))] * (11 * arrays)


def front_kernel(
    inputs, cot, gain, vecs, taps_all, rgate_all, igate_all, starts, out_bias, mlp_gain,
    wm, mg, mu, md,
    wq_o, wg_o, wu_o, wd_o, nall_o, call, starts_all, gate_o, lext_o, conv_o, rec_o, open_o,
    state_o, start, mixed_o, resid, n2all,
    wq, nall, halo, gate_pre, lext, conv, rec, opening, a, b, mixed, part, tot, slots, tallies,
    rg32, ig32, rgate, igate,
    mate, out_x, in_x, ms, mr, rxs, rxr, ax, bx, ac, bc,
    loc, outs, xs, xr, cs, cr, hs, hr, ss, sr, ps, pr, *spread_refs,
):
    me = Spot()
    r, c, z, y = me.r, me.c, me.z, me.y
    length = inputs.shape[0]
    seq_length = length * 8
    wide = taps_all.shape[2]
    diag = (me.r_x + 1 - 2 * lax.rem(me.r_x, 2), c)
    barrier = pltpu.get_barrier_semaphore()
    always = [me.core, me.x, diag] + peers_of(me)
    for device in always:
        pl.semaphore_signal(barrier, inc=1, device_id=device, device_id_type=MESH)
    count = len(always)
    others = [1, 2, 3]
    for there, place in ((c < 7, lax.rem(c + 1, 8)), (c > 0, lax.rem(c + 7, 8))):
        for i in others:

            @pl.when(there)
            def _(i=i, place=place):
                pl.semaphore_signal(
                    barrier, inc=1, device_id=(lax.rem(r + i, 4), place), device_id_type=MESH
                )

        count = count + jnp.where(there, 3, 0)
    own = [
        pltpu.make_async_copy(wm, wq.at[:, y], loc.at[0]),
        pltpu.make_async_copy(mg, wg_o.at[y], loc.at[1]),
        pltpu.make_async_copy(mu, wu_o.at[y], loc.at[2]),
        pltpu.make_async_copy(md, wd_o.at[y], loc.at[3]),
    ]

    @pl.when(z == r)
    def _():
        for copy in own:
            copy.start()

    heads = [
        pltpu.make_async_copy(rgate_all.at[pl.ds(2 * r, 2)], rg32, loc.at[4]),
        pltpu.make_async_copy(igate_all.at[pl.ds(2 * r, 2)], ig32, loc.at[5]),
    ]
    for copy in heads:
        copy.start()
    here_c = pltpu.make_async_copy(cot, call.at[r], loc.at[6])
    here_c.start()
    vals = inputs[...].astype(F32)
    scale = lax.rsqrt(jnp.mean(vals * vals, axis=-1, keepdims=True) + EPSILON)
    nall[r] = (vals * scale * gain[...]).astype(LOW)
    starts_all[r] = starts[...]
    pl.semaphore_wait(barrier, count)

    x_n = push(nall.at[r], nall.at[r], (xs, xr), 0, me.x)
    c_n = push(nall.at[r], nall.at[r], (cs, cr), 0, me.core)
    c_c = push(cot, call.at[r], (cs, cr), 1, me.core)
    x_c = push(cot, call.at[r], (xs, xr), 1, me.x)
    fwd_n = push(nall.at[me.r_x], nall.at[me.r_x], (cs, cr), 2, me.core)
    fwd_c = push(call.at[me.r_x], call.at[me.r_x], (cs, cr), 3, me.core)
    s_copies = [
        push(starts_all.at[r], starts_all.at[r], (ss, sr), i, device)
        for i, device in enumerate((me.core, me.x, diag))
    ]
    tail = nall.at[r, pl.ds(length - 16, 16)]
    halo_copies = [
        push(tail, halo.at[r], (hs, hr), i, (lax.rem(r + i, 4), lax.rem(c + 1, 8))) for i in range(4)
    ]
    glo = [Spread(me, [wq.at[m]], 4, spread_refs[5 * m : 5 * m + 5]) for m in range(3)]
    pieces = 8
    mlp_w = Spread(me, [wg_o, wu_o, wd_o], pieces, spread_refs[15:])
    x_n.start()
    for copy in s_copies:
        copy.start()

    @pl.when(c < 7)
    def _():
        for copy in halo_copies:
            copy.start()

    c_n.start()
    c_c.start()

    @pl.when(c == 0)
    def _():
        halo[...] = jnp.zeros_like(halo)

    @pl.when(z == r)
    def _():
        own[0].wait()

    for k in range(12):
        glo[k // 4].lead(k % 4)

        @pl.when(z != r)
        def _(k=k):
            glo[k // 4].follow(k % 4)

        if k == 3:
            for copy in heads:
                copy.wait()
            pair_diagonal(rgate, rg32)
            pair_diagonal(igate, ig32)
        if k == 7:
            x_n.wait_recv()
            fwd_n.start()
            x_c.start()

    @pl.when(z == r)
    def _():
        for copy in own[1:]:
            copy.wait()

    mlp_w.step(0)
    for m in range(2):
        for k in range(4):
            glo[m].arrived(k)
    c_n.wait_recv()
    fwd_n.wait_recv()
    for copy in s_copies:
        copy.wait_recv()

    @pl.when(c > 0)
    def _():
        for i in range(4):
            landed(me, halo.at[i], (hs, hr), i)

    vec = vecs.at[r]
    taps = taps_all.at[r]

    def mixer_one(s):
        fill_tallies(tallies, starts_all[s, 0:1], c * length, length, seq_length)
        tokens = nall[s]
        wgate = wq[0].reshape(wide, tokens.shape[1])
        wlift = wq[1].reshape(wide, tokens.shape[1])
        gate_pre[s] = nt(tokens, wgate) + vec[0:1]
        lifted = nt(tokens, wlift) + vec[1:2]
        lext[s, 0:8] = (nt(halo[s], wlift) + vec[1:2])[8:16]
        lext[s, pl.ds(8, length)] = lifted
        out = vec[2:3] + taps[0:1] * lifted
        for k in range(1, 4):
            same = same_document(tallies, length, -k, wide)
            out = out + taps[k : k + 1] * lext[s, pl.ds(8 - k, length)] * same
        conv[s] = out
        low = out.astype(LOW)
        recur = jax.nn.sigmoid(nn(low, rgate[...]) + vec[3:4])
        opened = jax.nn.sigmoid(nn(low, igate[...]) + vec[4:5])
        rec[s] = recur
        opening[s] = opened
        reset = same_document(tallies, length, -1, wide) < 0.5
        decay, scaling = decay_terms(recur, vec[5:6], reset)
        decay = jnp.where(reset, 0.0, decay)
        tiles = (length // TILE, TILE, wide)
        a_scan, b_scan = tile_scan(
            decay.reshape(tiles), (scaling * opened * out).reshape(tiles), False
        )
        a[s] = a_scan.reshape(length, wide)
        b[s] = b_scan.reshape(length, wide)
        product = jnp.ones((1, wide), F32)
        state = jnp.zeros((1, wide), F32)
        for t in range(length // TILE):
            last = t * TILE + TILE - 1
            a_last = a[s, last : last + 1]
            state = b[s, last : last + 1] + a_last * state
            product = product * a_last
        tot[s, 0:1] = product
        tot[s, 1:2] = state

    for half in range(2):

        @pl.loop(2 * half, 2 * half + 2)
        def _(s):
            mixer_one(s)

        mlp_w.step(1 + half)

    carry_copies = carry_start(me, False, tot, slots, (ps, pr))
    saved = [
        pltpu.make_async_copy(source, target, outs.at[i])
        for i, (source, target) in enumerate(
            ((gate_pre, gate_o), (lext, lext_o), (conv, conv_o), (rec, rec_o), (opening, open_o),
             (nall, nall_o))
        )
    ]
    for copy in saved:
        copy.start()
    x_c.wait_recv()
    fwd_c.start()
    for k in range(4):
        glo[2].arrived(k)
    save_w = pltpu.make_async_copy(wq, wq_o, outs.at[6])
    save_w.start()
    mlp_w.step(3)
    carry_join(me, False, slots, start, (ps, pr))

    def mixer_two(s):
        state = start[pl.ds(s, 1)]
        for t in range(length // TILE):
            tile = pl.ds(t * TILE, TILE)
            now = b[s, tile] + a[s, tile] * state
            b[s, tile] = now
            state = now[TILE - 1 : TILE]
        gate_val, _ = gelu_pair(gate_pre[s])
        mix = (b[s] * gate_val).astype(LOW)
        mixed[s] = mix
        part[s] = nn(mix, wq[2].reshape(wide, part.shape[2])).astype(LOW)

    for half in range(2):

        @pl.loop(2 * half, 2 * half + 2)
        def _(s):
            mixer_two(s)

        mlp_w.step(4 + half)

    more = [
        pltpu.make_async_copy(b, state_o, outs.at[7]),
        pltpu.make_async_copy(mixed, mixed_o, outs.at[8]),
    ]
    for copy in more:
        copy.start()
    step = length // RS_CHUNKS
    copies = rows_sum_start(me, part, mate, (ms, mr))
    crossing = rows_sum_cross(me, part, mate, out_x, in_x, copies, (rxs, rxr))
    mlp_w.step(6)
    first = []
    for k in range(RS_CHUNKS):
        chunk = pl.ds(k * step, step)
        total = rows_sum_chunk(me, part, mate, in_x, copies, crossing, k)
        res = inputs[chunk].astype(F32) + total + out_bias[...]
        resid[chunk] = res
        scale = lax.rsqrt(jnp.mean(res * res, axis=-1, keepdims=True) + EPSILON)
        n2all[r, chunk] = (res * scale * mlp_gain[...]).astype(LOW)
        first.append(spread_chunk(me, n2all, k, (ax, bx), (ac, bc)))
        if k % 2 == 1:
            mlp_w.step(7 + k // 2)
    mlp_w.step(9)
    mlp_w.step(10)
    spread_rest(me, n2all, first, (ac, bc))
    finish_sends(copies + crossing)
    mlp_w.close()
    for m in range(3):
        for k in range(4):
            glo[m].sent(k)
    x_n.wait_send()
    x_c.wait_send()
    c_n.wait_send()
    c_c.wait()
    fwd_n.wait_send()
    fwd_c.wait()
    finish_sends(s_copies)

    @pl.when(c < 7)
    def _():
        finish_sends(halo_copies)

    carry_sent(me, False, carry_copies)
    here_c.wait()
    for copy in saved + [save_w] + more:
        copy.wait()


def front(inputs, cot, gain, vecs, taps_all, rgate_all, igate_all, starts, out_bias, mlp_gain,
          wm, mg, mu, md):
    length, width = inputs.shape
    wide = 2 * wm.shape[1]
    hidden = mg.shape[1]
    sd = jax.ShapeDtypeStruct
    tall = sd((4, length, wide), F32)
    ext = sd((4, length + 8, wide), F32)
    low = sd((4, length, wide), LOW)
    tokens = sd((4, length, width), LOW)
    vmem = lambda spec: pltpu.VMEM(spec.shape, spec.dtype)
    outs = [
        (sd((3, 2, wide // 2, width), LOW), ANYWHERE),
        (sd((2, width, hidden), LOW), ANYWHERE),
        (sd((2, width, hidden), LOW), ANYWHERE),
        (sd((2, hidden, width), LOW), ANYWHERE),
        (tokens, ANYWHERE),
        (tokens, ANYWHERE),
        (sd((4,) + starts.shape, starts.dtype), IN_VMEM),
        (tall, ANYWHERE),
        (ext, ANYWHERE),
        (tall, ANYWHERE),
        (tall, ANYWHERE),
        (tall, ANYWHERE),
        (tall, ANYWHERE),
        (sd((4, wide), F32), IN_VMEM),
        (low, ANYWHERE),
        (sd((length, width), F32), IN_VMEM),
        (tokens, IN_VMEM),
    ]
    dma = pltpu.SemaphoreType.DMA
    return pl.pallas_call(
        front_kernel,
        name="front",
        out_shape=[o[0] for o in outs],
        in_specs=[IN_VMEM, ANYWHERE] + [IN_VMEM] * 3 + [ANYWHERE] * 2 + [IN_VMEM] * 3 + [ANYWHERE] * 4,
        out_specs=[o[1] for o in outs],
        scratch_shapes=[
            pltpu.VMEM((3, 2, wide // 2, width), LOW), vmem(tokens), pltpu.VMEM((4, 16, width), LOW),
            vmem(tall), vmem(ext), vmem(tall), vmem(tall), vmem(tall), vmem(tall), vmem(tall),
            vmem(low), vmem(tokens), pltpu.VMEM((4, 2, wide), F32), pltpu.VMEM((8, 4, 2, wide), F32),
            pltpu.VMEM((length + 16, 128), F32),
            pltpu.VMEM((2, GB, GB), F32), pltpu.VMEM((2, GB, GB), F32),
            pltpu.VMEM((wide, wide), LOW), pltpu.VMEM((wide, wide), LOW),
        ]
        + rows_sum_scratch(length, width) + sem_pair(RS_CHUNKS) + sem_pair(2 * RS_CHUNKS)
        + [dma((7,)), dma((9,))] + sem_pair(2) + sem_pair(4) + sem_pair(4) + sem_pair(3)
        + sem_pair(8) + spread_sems(3, 4) + spread_sems(3, 8),
        compiler_params=comm_params(1),
    )(inputs, cot, gain, vecs, taps_all, rgate_all, igate_all, starts, out_bias, mlp_gain,
      wm, mg, mu, md)


RS_CHUNKS = 4


def rows_sum_start(me, part, mate, sems):
    length = part.shape[1]
    step = length // RS_CHUNKS
    far = lax.rem(me.r_core + 2, 4)
    copies = []
    for block, owner in enumerate((far, me.r_core)):
        for k in range(RS_CHUNKS):
            rows = pl.ds(k * step, step)
            copies.append(
                push(part.at[owner, rows], mate.at[block, rows], sems, block * RS_CHUNKS + k, me.core)
            )
    for copy in copies:
        copy.start()
    return copies


def rows_sum_cross(me, part, mate, out_x, in_x, copies, sems):
    length = part.shape[1]
    step = length // RS_CHUNKS
    crossing = []
    for k in range(RS_CHUNKS):
        rows = pl.ds(k * step, step)
        copies[k].wait_recv()
        out_x[rows] = (part[me.r_x, rows].astype(F32) + mate[0, rows].astype(F32)).astype(LOW)
        copy = push(out_x.at[rows], in_x.at[rows], sems, k, me.x)
        copy.start()
        crossing.append(copy)
    return crossing


def rows_sum_chunk(me, part, mate, in_x, copies, crossing, k):
    length = part.shape[1]
    step = length // RS_CHUNKS
    rows = pl.ds(k * step, step)
    copies[RS_CHUNKS + k].wait_recv()
    crossing[k].wait_recv()
    return part[me.r, rows].astype(F32) + mate[1, rows].astype(F32) + in_x[rows].astype(F32)


def finish_sends(copies):
    for copy in copies:
        copy.wait_send()


def rows_sum_scratch(length, width):
    return [
        pltpu.VMEM((2, length, width), LOW),
        pltpu.VMEM((length, width), LOW),
        pltpu.VMEM((length, width), LOW),
    ] + sem_pair(2 * RS_CHUNKS) + sem_pair(RS_CHUNKS)


def spread_chunk(me, all_ref, k, sems_x, sems_c):
    length = all_ref.shape[1]
    step = length // RS_CHUNKS
    rows = pl.ds(k * step, step)
    mine = all_ref.at[me.r, rows]
    copies = [
        push(mine, mine, sems_x, k, me.x),
        push(mine, mine, sems_c, k, me.core),
    ]
    for copy in copies:
        copy.start()
    return copies


def spread_rest(me, all_ref, first, sems_c):
    length = all_ref.shape[1]
    step = length // RS_CHUNKS
    passed = []
    for k in range(RS_CHUNKS):
        first[k][0].wait_recv()
        theirs = all_ref.at[me.r_x, pl.ds(k * step, step)]
        copy = push(theirs, theirs, sems_c, RS_CHUNKS + k, me.core)
        copy.start()
        passed.append(copy)
    for k in range(RS_CHUNKS):
        first[k][0].wait_send()
        first[k][1].wait()
        passed[k].wait()


def mlp_kernel(
    nall, call, wg, wu, wd, part, gpart, dg_o, du_o, dd_o,
    acc_out, acc_in, acc_g, acc_u, acc_d,
):
    block = pl.program_id(0)
    length = nall.shape[1]

    @pl.when(block == 0)
    def _():
        acc_out[...] = jnp.zeros_like(acc_out)
        acc_in[...] = jnp.zeros_like(acc_in)

    acc_g[...] = jnp.zeros_like(acc_g)
    acc_u[...] = jnp.zeros_like(acc_u)
    acc_d[...] = jnp.zeros_like(acc_d)

    @pl.loop(0, nall.shape[0])
    def _(s):
        tokens = nall[s]
        cot = call[s]
        gate = nn(tokens, wg[0])
        up = nn(tokens, wu[0])
        grad_hidden = nt(cot, wd[0])
        gate_val, slope = gelu_pair(gate)
        hidden = (gate_val * up).astype(LOW)
        grad_gate = (grad_hidden * up * slope).astype(LOW)
        grad_up = (grad_hidden * gate_val).astype(LOW)
        acc_out[s] += nn(hidden, wd[0])
        acc_in[s] += nt(grad_gate, wg[0]) + nt(grad_up, wu[0])
        acc_d[...] += tn(hidden, cot)
        acc_g[...] += tn(tokens, grad_gate)
        acc_u[...] += tn(tokens, grad_up)

    dg_o[0] = acc_g[...].astype(LOW)
    du_o[0] = acc_u[...].astype(LOW)
    dd_o[0] = acc_d[...].astype(LOW)

    @pl.when(block == pl.num_programs(0) - 1)
    def _():
        part[...] = acc_out[...].astype(LOW)
        gpart[...] = acc_in[...].astype(LOW)


def mlp(nall, call, wg, wu, wd):
    blocks, width, hidden = wg.shape
    sd = jax.ShapeDtypeStruct
    inward = pl.BlockSpec((1, width, hidden), lambda h: (h, 0, 0))
    outward = pl.BlockSpec((1, hidden, width), lambda h: (h, 0, 0))
    return pl.pallas_call(
        mlp_kernel,
        name="mlp_both_ways",
        grid=(blocks,),
        in_specs=[whole(nall.shape), whole(call.shape), inward, inward, outward],
        out_specs=[whole(nall.shape), whole(nall.shape), inward, inward, outward],
        out_shape=[sd(nall.shape, LOW)] * 2 + [sd(w.shape, LOW) for w in (wg, wu, wd)],
        scratch_shapes=[pltpu.VMEM(nall.shape, F32)] * 2
        + [pltpu.VMEM(w.shape[1:], F32) for w in (wg, wu, wd)],
        compiler_params=plain_params(),
    )(nall, call, wg, wu, wd)


def back_kernel(
    gpart2, cot, resid, inputs, mlp_gain, mix_gain, vecs, taps_all, starts_all, start,
    opart, dmg, dmu, dmd, wq_h, nall_h, gate_h, lext_h, conv_h, rec_h, open_h, state_h, mixed_h,
    rgate_all, igate_all,
    output, ginputs, own_g, own_u, own_d, own_e, own_l, gates_all, gains_all,
    wq, nall, gate_pre, lext, conv, rec, opening, state, mixed, a, b, gconv, heads_in,
    gate_low, ball, gresid, opart_v, acc_a, acc_b, acc_r, acc_i, sums, prev_ext,
    early, late, mine_g, mine_u, mine_d, y_g, y_u, y_d, y_e, y_l,
    z_g, z_u, z_d, z_e, z_l,
    tot, slots, carry, tallies, rg32, ig32, rgate, igate,
    gate_send, gate_slots, gain_slots, gain_sums,
    mate, out_x, in_x, ms, mr, rxs, rxr, o_mate, o_out, o_in, oms, omr, oxs, oxr,
    nms, nmr, nxs, nxr, ax, bx, ac, bc,
    loc, ps, pr, hs, hr, ggs, ggr, ghs, ghr, qs, qr, ts, tr, *reduce_refs,
):
    me = Spot()
    r, c, z, y = me.r, me.c, me.z, me.y
    length = inputs.shape[0]
    seq_length = length * 8
    wide = taps_all.shape[2]
    width = inputs.shape[1]
    side = wide // 2
    step = length // RS_CHUNKS
    diag = (me.r_x + 1 - 2 * lax.rem(me.r_x, 2), c)
    chan_peers = peers_of(me)
    row_peers = (me.core, me.x, diag)
    loads = [
        pltpu.make_async_copy(source, target, loc.at[i])
        for i, (source, target) in enumerate(
            (
                (dmg.at[y], mine_g), (dmu.at[y], mine_u), (dmd.at[y], mine_d),
                (gate_h, gate_pre), (state_h, state), (mixed_h, mixed), (rec_h, rec), (wq_h, wq),
                (open_h, opening), (conv_h, conv), (lext_h, lext), (nall_h, nall),
                (opart, opart_v), (rgate_all.at[pl.ds(2 * r, 2)], rg32),
                (igate_all.at[pl.ds(2 * r, 2)], ig32),
            )
        )
    ]
    for copy in loads:
        copy.start()
    greet(list(row_peers) + chan_peers)
    n_mlp = 11 * 3
    big = Reduce(me, [dmg, dmu, dmd], [mine_g, mine_u, mine_d], [y_g, y_u, y_d], [z_g, z_u, z_d],
                 [own_g, own_u, own_d], 8, reduce_refs[:n_mlp])
    mid = Reduce(me, [early], [early.at[y]], [y_e], [z_e], [own_e], 4, reduce_refs[n_mlp : n_mlp + 11])
    end = Reduce(me, [late], [late.at[y]], [y_l], [z_l], [own_l], 7, reduce_refs[n_mlp + 11 :])

    copies = rows_sum_start(me, gpart2, mate, (ms, mr))
    big.y_send(0)
    big.y_send(1)
    crossing = rows_sum_cross(me, gpart2, mate, out_x, in_x, copies, (rxs, rxr))
    for copy in loads[:3]:
        copy.wait()
    big.step(0)
    first = []
    gain2_sum = 0.0
    bias_sum = 0.0
    for k in range(RS_CHUNKS):
        rows = pl.ds(k * step, step)
        grad = rows_sum_chunk(me, gpart2, mate, in_x, copies, crossing, k)
        res = resid[rows]
        scale = lax.rsqrt(jnp.mean(res * res, axis=-1, keepdims=True) + EPSILON)
        gain2_sum = gain2_sum + jnp.sum(grad * res * scale, axis=0, keepdims=True)
        pulled = grad * mlp_gain[...]
        inner = jnp.mean(pulled * res, axis=-1, keepdims=True)
        total = cot[rows].astype(F32) + scale * pulled - res * (scale * scale * scale * inner)
        bias_sum = bias_sum + jnp.sum(total, axis=0, keepdims=True)
        gresid[rows] = total
        ball[r, rows] = total.astype(LOW)
        first.append(spread_chunk(me, ball, k, (ax, bx), (ac, bc)))
        if k % 2 == 1:
            big.step(1 + k // 2)
    for copy in loads[3:]:
        copy.wait()
    pair_diagonal(rgate, rg32)
    pair_diagonal(igate, ig32)
    big.step(3)
    spread_rest(me, ball, first, (ac, bc))
    finish_sends(copies + crossing)

    vec = vecs.at[r]
    taps = taps_all.at[r]
    acc_a[...] = jnp.zeros_like(acc_a)
    acc_b[...] = jnp.zeros_like(acc_b)
    acc_r[...] = jnp.zeros_like(acc_r)
    acc_i[...] = jnp.zeros_like(acc_i)
    sums[...] = jnp.zeros_like(sums)

    def reset_of(s):
        fill_tallies(tallies, starts_all[s, 0:1], c * length, length, seq_length)
        return same_document(tallies, length, -1, wide) < 0.5

    def mixer_three(s):
        branch = ball[s]
        grad_mixed = nt(branch, wq[2].reshape(wide, width))
        gate_val, slope = gelu_pair(gate_pre[s])
        grad_gate = grad_mixed * state[s] * slope
        low = grad_gate.astype(LOW)
        gate_low[s] = low
        sums[0:1] += jnp.sum(grad_gate, axis=0, keepdims=True)
        acc_a[...] += tn(mixed[s], branch)
        acc_b[...] += tn(low, nall[s])
        grad_state = grad_mixed * gate_val
        gate_pre[s] = grad_state
        decay = jnp.where(reset_of(s), 0.0, jnp.exp(-8.0 * rec[s] * vec[5:6]))
        tiles = (length // TILE, TILE, wide)
        a_scan, b_scan = tile_scan(
            decay.reshape(tiles), (decay * grad_state).reshape(tiles), True
        )
        a[s] = a_scan.reshape(length, wide)
        b[s] = b_scan.reshape(length, wide)
        product = jnp.ones((1, wide), F32)
        carried = jnp.zeros((1, wide), F32)
        for t in range(length // TILE - 1, -1, -1):
            head = t * TILE
            a_head = a[s, head : head + 1]
            carried = b[s, head : head + 1] + a_head * carried
            product = product * a_head
        tot[s, 0:1] = product
        tot[s, 1:2] = carried

    for half in range(2):

        @pl.loop(2 * half, 2 * half + 2)
        def _(s):
            mixer_three(s)

        if half == 0:
            big.step(4)

    carry_copies = carry_start(me, True, tot, slots, (ps, pr))
    for j in range(2):
        early[j, 0:side] = acc_a[j * side : (j + 1) * side].astype(LOW)
        early[j, side : 2 * side] = acc_b[j * side : (j + 1) * side].astype(LOW)
    acc_b[...] = jnp.zeros_like(acc_b)
    big.step(5)
    carry_join(me, True, slots, carry, (ps, pr))

    def mixer_four(s):
        now = carry[pl.ds(s, 1)]
        gconv[s, pl.ds(length, TILE)] = jnp.broadcast_to(now, (TILE, wide))
        for t in range(length // TILE - 1, -1, -1):
            rows = pl.ds(t * TILE, TILE)
            moved = b[s, rows] + a[s, rows] * now
            gconv[s, rows] = moved
            now = moved[0:1]
        carried = gate_pre[s] + gconv[s, pl.ds(1, length)]
        prev_ext[0:TILE] = jnp.broadcast_to(start[pl.ds(s, 1)], (TILE, wide))
        prev_ext[pl.ds(TILE, length)] = state[s]
        previous = prev_ext[pl.ds(TILE - 1, length)]
        recur, opened, conv_s = rec[s], opening[s], conv[s]
        reset = reset_of(s)
        decay, scaling = decay_terms(recur, vec[5:6], reset)
        pulled = carried * scaling
        grad_opening = pulled * conv_s
        grad_log = carried * (previous * decay - opened * conv_s * (decay * decay / scaling))
        grad_log = jnp.where(reset, 0.0, grad_log)
        grad_rec = grad_log * (-8.0 * vec[5:6])
        grad_rpre = grad_rec * recur * (1.0 - recur)
        grad_opre = grad_opening * opened * (1.0 - opened)
        r_low, o_low, conv_low = grad_rpre.astype(LOW), grad_opre.astype(LOW), conv_s.astype(LOW)
        total = pulled * opened + nt(r_low, rgate[...]) + nt(o_low, igate[...])
        gconv[s, 0:length] = total
        acc_r[...] += tn(conv_low, r_low)
        acc_i[...] += tn(conv_low, o_low)
        sums[7:8] += jnp.sum(grad_rpre, axis=0, keepdims=True)
        sums[8:9] += jnp.sum(grad_opre, axis=0, keepdims=True)
        sums[9:10] += jnp.sum(grad_log * recur, axis=0, keepdims=True) * (8.0 * vec[6:7])
        sums[6:7] += jnp.sum(total, axis=0, keepdims=True)

    for half in range(2):

        @pl.loop(2 * half, 2 * half + 2)
        def _(s):
            mixer_four(s)

        if half == 0:
            big.step(6)
            mid.y_send(0)
            mid.y_send(1)

    heads = [
        push(gconv.at[s, pl.ds(0, TILE)], heads_in.at[s], (hs, hr), s, (r, lax.rem(c + 7, 8)))
        for s in range(4)
    ]

    @pl.when(c > 0)
    def _():
        for copy in heads:
            copy.start()

    @pl.when(c == 7)
    def _():
        heads_in[...] = jnp.zeros_like(heads_in)

    cut = side // 8
    for k in range(8):
        at = k * cut
        gate_send[k] = jnp.concatenate(
            [m[j * side + at : j * side + at + cut, j * side : (j + 1) * side]
             for m in (acc_r, acc_i) for j in range(2)], axis=0
        ).astype(LOW)
    gate_copies = [
        push(gate_send.at[lax.rem(c + d, 8)], gate_slots.at[d], (qs, qr), d, chan_peers[d - 1])
        for d in range(1, 8)
    ]
    for copy in gate_copies:
        copy.start()
    big.step(7)

    @pl.when(c < 7)
    def _():
        for s in range(4):
            landed(me, heads_in.at[s], (hs, hr), s)

    def mixer_five(s):
        fill_tallies(tallies, starts_all[s, 0:1], c * length, length, seq_length)
        grad = gconv[s, 0:length]
        prev_ext[0:length] = grad
        prev_ext[pl.ds(length, TILE)] = heads_in[s]
        grad_lifted = taps[0:1] * grad
        sums[2:3] += jnp.sum(grad * lext[s, pl.ds(TILE, length)], axis=0, keepdims=True)
        for k in range(1, 4):
            ahead = prev_ext[pl.ds(k, length)] * same_document(tallies, length, k, wide)
            grad_lifted = grad_lifted + taps[k : k + 1] * ahead
            behind = lext[s, pl.ds(TILE - k, length)] * same_document(tallies, length, -k, wide)
            sums[2 + k : 3 + k] += jnp.sum(grad * behind, axis=0, keepdims=True)
        sums[1:2] += jnp.sum(grad_lifted, axis=0, keepdims=True)
        lift_low = grad_lifted.astype(LOW)
        acc_b[...] += tn(lift_low, nall[s])
        ball[s] = (
            nn(gate_low[s], wq[0].reshape(wide, width)) + nn(lift_low, wq[1].reshape(wide, width))
        ).astype(LOW)

    for half in range(2):

        @pl.loop(2 * half, 2 * half + 2)
        def _(s):
            mixer_five(s)

        if half == 0:
            big.step(8)
            mid.step(0)

    n_copies = rows_sum_start(me, ball, mate, (nms, nmr))
    late[...] = jnp.zeros_like(late)
    for j in range(2):
        late[j, 0:side] = acc_b[j * side : (j + 1) * side].astype(LOW)
        late[j, side : side + 16, 0:side] = sums[:, j * side : (j + 1) * side].astype(LOW)
    end.y_send(0)
    end.y_send(1)
    end.y_send(2)
    n_cross = rows_sum_cross(me, ball, mate, out_x, in_x, n_copies, (nxs, nxr))
    o_copies = rows_sum_start(me, opart_v, o_mate, (oms, omr))
    o_cross = rows_sum_cross(me, opart_v, o_mate, o_out, o_in, o_copies, (oxs, oxr))
    big.step(9)
    mid.step(1)
    big.step(10)
    mid.step(2)
    gain_sum = 0.0
    for k in range(RS_CHUNKS):
        rows = pl.ds(k * step, step)
        grad = rows_sum_chunk(me, ball, mate, in_x, n_copies, n_cross, k)
        vals = inputs[rows].astype(F32)
        scale = lax.rsqrt(jnp.mean(vals * vals, axis=-1, keepdims=True) + EPSILON)
        gain_sum = gain_sum + jnp.sum(grad * vals * scale, axis=0, keepdims=True)
        pulled = grad * mix_gain[...]
        inner = jnp.mean(pulled * vals, axis=-1, keepdims=True)
        ginputs[rows] = (
            gresid[rows] + scale * pulled - vals * (scale * scale * scale * inner)
        ).astype(LOW)
        if k == 1:
            big.step(11)
            mid.step(3)
    for k in range(8):
        lanes = slice(k * 128, (k + 1) * 128)
        gain_slots[0, k] = jnp.concatenate(
            [gain_sum[:, lanes], gain2_sum[:, lanes], bias_sum[:, lanes], jnp.zeros((5, 128), F32)], 0
        )
    gain_copies = [
        push(gain_slots.at[0, lax.rem(c + d, 8)], gain_slots.at[1, d], (ggs, ggr), d,
             chan_peers[d - 1])
        for d in range(1, 8)
    ]
    for copy in gain_copies:
        copy.start()
    big.step(12)
    for p in range(3):
        end.step(p, 3)
    mid.step(4)
    for k in range(RS_CHUNKS):
        rows = pl.ds(k * step, step)
        total = rows_sum_chunk(me, opart_v, o_mate, o_in, o_copies, o_cross, k)
        output[rows] = (resid[rows] + total).astype(LOW)
    for p in range(3, 6):
        end.step(p, 3)
    mid.step(5)
    gate_total = gate_send[c].astype(F32)
    for d in range(1, 8):
        gate_copies[d - 1].wait_recv()
        gate_total = gate_total + gate_slots[d].astype(F32)
    gates_all[r] = gate_total.astype(LOW)
    gate_rows = [
        push(gates_all.at[r], gates_all.at[r], (ts, tr), i, device)
        for i, device in enumerate(row_peers)
    ]
    for copy in gate_rows:
        copy.start()
    shared = gain_slots[0, c]
    for d in range(1, 8):
        gain_copies[d - 1].wait_recv()
        shared = shared + gain_slots[1, d]
    gain_sums[0] = shared
    row_copies = [
        push(gain_sums.at[0], gain_sums.at[1 + i], (ghs, ghr), i, device)
        for i, device in enumerate(row_peers)
    ]
    for copy in row_copies:
        copy.start()
    end.step(6, 3)
    mid.step(6)
    for p in range(7, end.positions()):
        end.step(p, 3)
        mid.step(p)
    for copy in row_copies + gate_rows:
        copy.wait()
    gains_all[...] = gain_sums[0] + gain_sums[1] + gain_sums[2] + gain_sums[3]

    @pl.when(c > 0)
    def _():
        finish_sends(heads)

    finish_sends(gain_copies + gate_copies + n_copies + n_cross + o_copies + o_cross)
    carry_sent(me, True, carry_copies)
    big.close()
    mid.close()
    end.close()


def back(gpart2, cot, resid, inputs, mlp_gain, mix_gain, vecs, taps_all, starts_all, start,
         opart, dmg, dmu, dmd, wq, nall, gate_pre, lext, conv, rec, opening, state, mixed,
         rgate_all, igate_all):
    length, width = inputs.shape
    wide = taps_all.shape[2]
    side = wide // 2
    sd = jax.ShapeDtypeStruct
    vmem = pltpu.VMEM
    dma = pltpu.SemaphoreType.DMA
    like = lambda v: vmem(v.shape, v.dtype)
    shard = lambda v: vmem(v.shape[1:], LOW)
    tall = vmem((4, length, wide), F32)
    early, late = (2, 2 * side, width), (2, side + 32, width)
    odd = lambda: [shard(dmg), shard(dmu), shard(dmd), vmem(early[1:], LOW), vmem(late[1:], LOW)]
    outs = [
        sd(inputs.shape, LOW), sd(inputs.shape, LOW),
        sd(dmg.shape[1:], LOW), sd(dmu.shape[1:], LOW), sd(dmd.shape[1:], LOW),
        sd(early[1:], LOW), sd(late[1:], LOW), sd((4, side // 2, side), LOW), sd((8, 128), F32),
    ]
    return pl.pallas_call(
        back_kernel,
        name="back",
        out_shape=outs,
        in_specs=[IN_VMEM] * 10 + [ANYWHERE] * 15,
        out_specs=[IN_VMEM] * len(outs),
        scratch_shapes=[
            like(wq), like(nall), tall, like(lext), tall, tall, tall, tall, like(mixed),
            tall, tall, vmem((4, length + TILE, wide), F32), vmem((4, TILE, wide), F32),
            vmem((4, length, wide), LOW), like(gpart2), vmem((length, width), F32), like(opart),
            vmem((wide, width), F32), vmem((wide, width), F32),
            vmem((wide, wide), F32), vmem((wide, wide), F32), vmem((16, wide), F32),
            vmem((length + TILE, wide), F32),
            vmem(early, LOW), vmem(late, LOW),
        ]
        + odd()[:3] + odd() + odd()
        + [
            vmem((4, 2, wide), F32), vmem((8, 4, 2, wide), F32), vmem((4, wide), F32),
            vmem((length + 16, 128), F32), vmem((2, GB, GB), F32), vmem((2, GB, GB), F32),
            vmem((wide, wide), LOW), vmem((wide, wide), LOW),
            vmem((8, side // 2, side), LOW), vmem((8, side // 2, side), LOW),
            vmem((2, 8, 8, 128), F32), vmem((4, 8, 128), F32),
        ]
        + rows_sum_scratch(length, width) + rows_sum_scratch(length, width)
        + sem_pair(2 * RS_CHUNKS) + sem_pair(RS_CHUNKS)
        + sem_pair(RS_CHUNKS) + sem_pair(2 * RS_CHUNKS)
        + [dma((15,))] + sem_pair(8) + sem_pair(4) + sem_pair(8) + sem_pair(3)
        + sem_pair(8) + sem_pair(3)
        + reduce_sems(3, 8) + reduce_sems(1, 4) + reduce_sems(1, 7),
        compiler_params=comm_params(2),
    )(gpart2, cot, resid, inputs, mlp_gain, mix_gain, vecs, taps_all, starts_all, start,
      opart, dmg, dmu, dmd, wq, nall, gate_pre, lext, conv, rec, opening, state, mixed,
      rgate_all, igate_all)


def split_body(
    inputs, mix_gain, gate_proj, gate_bias, lift_proj, lift_bias, conv_taps, conv_bias,
    recur_gate, recur_bias, input_gate, input_bias, decay_param, out_proj, out_bias, mlp_gain,
    mlp_gate, mlp_up, mlp_down, doc_starts, cotangent,
):
    wide = 2 * GB
    wm = jnp.stack([gate_proj.T, lift_proj.T, out_proj])
    vecs = jnp.stack(
        [gate_bias, lift_bias, conv_bias, recur_bias, input_bias, jax.nn.softplus(-decay_param),
         jax.nn.sigmoid(-decay_param), jnp.zeros_like(decay_param)]
    ).reshape(8, 4, wide).transpose(1, 0, 2)
    taps = conv_taps.reshape(4, 4, wide).transpose(1, 0, 2)
    starts = jnp.pad(
        doc_starts, ((0, 7), (0, 128 - doc_starts.shape[1])),
        constant_values=jnp.iinfo(jnp.int32).max,
    )
    (wq, wg, wu, wd, nall, call, starts_all, gate_pre, lext, conv, rec, opening, state, start,
     mixed, resid, n2all) = front(
        inputs, cotangent, mix_gain[None], vecs, taps, recur_gate, input_gate, starts,
        out_bias[None], mlp_gain[None], wm, mlp_gate, mlp_up, mlp_down,
    )
    opart, gpart2, dmg, dmu, dmd = mlp(n2all, call, wg, wu, wd)
    output, grad_inputs, own_g, own_u, own_d, own_e, own_l, gates, gains = back(
        gpart2, cotangent, resid, inputs, mlp_gain[None], mix_gain[None], vecs, taps, starts_all,
        start, opart, dmg, dmu, dmd, wq, nall, gate_pre, lext, conv, rec, opening, state, mixed,
        recur_gate, input_gate,
    )
    wide_out = lambda v: v.astype(F32)
    gates = wide_out(gates).reshape(4, 2, 2, GB // 8, GB)
    gate_out = lambda i: gates[:, i].reshape(8, GB // 8, GB)
    own = wide_out(own_l[GB : GB + 16, :GB])
    return (
        output, grad_inputs, gains[0],
        wide_out(own_e[GB:].T), own[0], wide_out(own_l[:GB].T), own[1], own[2:6], own[6],
        gate_out(0), own[7], gate_out(1), own[8], own[9],
        wide_out(own_e[:GB]), gains[2], gains[1],
        wide_out(own_g), wide_out(own_u), wide_out(own_d),
    )


def solution(mesh):
    in_specs = (
        P(("rows", "chan"), None),
        P(),
        P(None, "chan"),
        P(),
        P(None, "chan"),
        P(),
        P(),
        P(),
        P(),
        P(),
        P(),
        P(),
        P(),
        P("chan", None),
        P(),
        P(),
        P(None, "chan"),
        P(None, "chan"),
        P("chan", None),
        P("rows", None),
        P(("rows", "chan"), None),
    )
    out_specs = (
        P(("rows", "chan"), None),
        P(("rows", "chan"), None),
        P("chan"),
        P(None, "chan"),
        P("chan"),
        P(None, "chan"),
        P("chan"),
        P(None, "chan"),
        P("chan"),
        P(None, "chan", None),
        P("chan"),
        P(None, "chan", None),
        P("chan"),
        P("chan"),
        P("chan", None),
        P("chan"),
        P("chan"),
        P(None, "chan"),
        P(None, "chan"),
        P("chan", None),
    )
    split = mesh.shape["rows"] == 4 and mesh.shape["chan"] == HEADS
    return jax.shard_map(split_body if split else body, mesh=mesh, in_specs=in_specs, out_specs=out_specs, check_vma=False)
```

```python
from functools import partial
import math

import jax
import jax.numpy as jnp
from jax import lax
from jax.experimental import pallas as pl
from jax.experimental.pallas import tpu as pltpu
from jax.sharding import PartitionSpec as P

D = 1024
LRU = 1536
FF = 3072
HEADS = 8
GB = 192


EPSILON = 1e-06
precise = lax.Precision.HIGHEST


def from_behind(block, axis, distance):
    devices = range(lax.axis_size(axis))
    route = [(i - distance, i) for i in devices if i - distance in devices]
    return lax.ppermute(block, axis, route)


def prefix(value, axis, join, neutral, backward):
    count, mine = (lax.axis_size(axis), lax.axis_index(axis))
    pieces = jax.tree.map(lambda part: lax.all_gather(part, axis), value)
    if backward:
        pieces = jax.tree.map(lambda part: part[::-1], pieces)
        mine = count - 1 - mine
    subtotal = jax.tree.map(
        lambda part, zero: jnp.full_like(part, 0) + jnp.asarray(zero, part.dtype), value, neutral
    )

    def hop(position, subtotal):
        longer = join(subtotal, jax.tree.map(lambda part: part[position], pieces))
        return jax.tree.map(lambda new, old: jnp.where(position < mine, new, old), longer, subtotal)

    return lax.fori_loop(0, count - 1, hop, subtotal)


def rms_scale(values, gain_vec):
    return (
        values * lax.rsqrt(jnp.mean(values * values, axis=-1, keepdims=True) + EPSILON) * gain_vec
    )


def gated_unit(gate_pre, up_vals):
    return jax.nn.gelu(gate_pre) * up_vals


def affine(earlier, later_map):
    return (earlier[0] * later_map[0], later_map[0] * earlier[1] + later_map[1])


def segment_ids(starts, start_pos, pos_count, seq_len):
    where_at = start_pos + jnp.arange(pos_count, dtype=jnp.int32)
    seq_of = jnp.floor_divide(where_at, seq_len)
    within = where_at - seq_of * seq_len
    owner = seq_of[:, None] == jnp.arange(starts.shape[0], dtype=jnp.int32)[None, :]
    passed = starts[None, :, :] <= within[:, None, None]
    doc_tally = jnp.sum(jnp.logical_and(owner[:, :, None], passed).astype(jnp.int32), axis=(1, 2))
    return seq_of * (starts.shape[1] + 1) + doc_tally


def project(normed, weights, first_bias, second_bias):
    product = jnp.einsum("td,dc->ct", normed, weights, preferred_element_type=jnp.float32)
    channels = first_bias.shape[0]
    return (product[:channels] + first_bias[:, None], product[channels:] + second_bias[:, None])


def conv_forward(lifted, tail_rows, segments, tap_vals, bias_vec):
    length = lifted.shape[1]
    extended = jnp.concatenate([tail_rows, lifted], axis=1)
    own_seg = segments[3 : 3 + length]
    result = bias_vec[:, None] + tap_vals[0][:, None] * lifted
    for offset in range(1, 4):
        same_doc = (segments[3 - offset : 3 - offset + length] == own_seg).astype(jnp.float32)
        result = (
            result
            + tap_vals[offset][:, None]
            * extended[:, 3 - offset : 3 - offset + length]
            * same_doc[None, :]
        )
    return result


def conv_backward(grad_conv, head_rows, segments, lifted, tail_rows, tap_vals):
    length = grad_conv.shape[1]
    ahead_grad = jnp.concatenate([grad_conv, head_rows], axis=1)
    behind = jnp.concatenate([tail_rows, lifted], axis=1)
    own_seg = segments[3 : 3 + length]
    grad_lifted = tap_vals[0][:, None] * grad_conv
    tap_grads = [jnp.sum(grad_conv * lifted, axis=1)]
    for offset in range(1, 4):
        later_same = (segments[3 + offset : 3 + offset + length] == own_seg).astype(jnp.float32)
        grad_lifted = (
            grad_lifted
            + tap_vals[offset][:, None]
            * ahead_grad[:, offset : offset + length]
            * later_same[None, :]
        )
        earlier = (segments[3 - offset : 3 - offset + length] == own_seg).astype(jnp.float32)
        tap_grads.append(
            jnp.sum(
                grad_conv * behind[:, 3 - offset : 3 - offset + length] * earlier[None, :], axis=1
            )
        )
    return (grad_lifted, jnp.stack(tap_grads, axis=1), jnp.sum(grad_conv, axis=1))


def coefficients(is_reset, conv_out, recur_gate, recur_bias, input_gate, input_bias, decay_param):
    channels, length = conv_out.shape
    gate_block = recur_gate.shape[1]
    grouped = conv_out.reshape(channels // gate_block, gate_block, length)
    recurrence = jax.nn.sigmoid(
        jnp.einsum("hit,hio->hot", grouped, recur_gate, precision=precise).reshape(channels, length)
        + recur_bias[:, None]
    )
    opening = jax.nn.sigmoid(
        jnp.einsum("hit,hio->hot", grouped, input_gate, precision=precise).reshape(channels, length)
        + input_bias[:, None]
    )
    log_decay = -8.0 * recurrence * jax.nn.softplus(-decay_param)[:, None]
    decay_rate = jnp.where(is_reset[None, :], 0.0, jnp.exp(log_decay))
    scaling = jnp.where(is_reset[None, :], 1.0, jnp.sqrt(-jnp.expm1(2.0 * log_decay)))
    return (decay_rate, scaling * opening * conv_out)


def reverse_local(decay_rate, grad_state):
    ones_col = jnp.ones_like(decay_rate[:, :1])
    factor = jnp.flip(jnp.concatenate([decay_rate[:, 1:], ones_col], axis=1), axis=1)
    product, carried = lax.associative_scan(affine, (factor, jnp.flip(grad_state, axis=1)), axis=1)
    return (jnp.flip(product, axis=1), jnp.flip(carried, axis=1))


def finish_state(lru_state, start_state, carried, pull_coef):
    previous = jnp.concatenate([start_state[:, None], lru_state[:, :-1]], axis=1)
    return pull_coef((carried * previous, carried))


def flatten_rows(pieces, row_count):
    return jnp.concatenate([source.reshape(row_count, -1) for source in pieces], axis=1)


def body(
    inputs,
    mix_gain,
    gate_proj,
    gate_bias,
    lift_proj,
    lift_bias,
    conv_taps,
    conv_bias,
    recur_gate,
    recur_bias,
    input_gate,
    input_bias,
    decay_param,
    out_proj,
    out_bias,
    mlp_gain,
    mlp_gate,
    mlp_up,
    mlp_down,
    doc_starts,
    cotangent,
):
    chan_count = lax.axis_size("chan")
    chan_place = lax.axis_index("chan")
    local_rows = inputs.shape[0]
    seq_length = local_rows * chan_count
    rows_f32 = inputs.astype(jnp.float32)
    cot_f32 = cotangent.astype(jnp.float32)
    normed, pull_norm = jax.vjp(rms_scale, rows_f32, mix_gain)
    normed_low = normed.astype(jnp.bfloat16)
    gate_full, lift_full, out_full, mlp_gate_full, mlp_up_full, mlp_down_full = (
        lax.all_gather(gate_proj, "chan", axis=1, tiled=True),
        lax.all_gather(lift_proj, "chan", axis=1, tiled=True),
        lax.all_gather(out_proj, "chan", axis=0, tiled=True),
        lax.all_gather(mlp_gate, "chan", axis=1, tiled=True),
        lax.all_gather(mlp_up, "chan", axis=1, tiled=True),
        lax.all_gather(mlp_down, "chan", axis=0, tiled=True),
    )
    channels = LRU
    hidden_cut = FF
    segments = segment_ids(doc_starts, chan_place * local_rows - 3, local_rows + 6, seq_length)
    mix_proj = jnp.concatenate([gate_full, lift_full], axis=1)
    gate_pre, lifted = project(normed_low, mix_proj, gate_bias, lift_bias)
    tail_rows = from_behind(lifted[:, -3:], "chan", 1)
    conv_out = conv_forward(lifted, tail_rows, segments, conv_taps, conv_bias)
    is_reset = segments[3 : 3 + local_rows] != segments[2 : 2 + local_rows]
    (decay_rate, lru_input), pull_coef = jax.vjp(
        partial(coefficients, is_reset),
        conv_out,
        recur_gate,
        recur_bias,
        input_gate,
        input_bias,
        decay_param,
    )
    running, local_state = lax.associative_scan(affine, (decay_rate, lru_input), axis=1)
    ones_vec = jnp.ones((channels,), jnp.float32)
    zeros_vec = jnp.zeros((channels,), jnp.float32)
    _, start_state = prefix(
        (running[:, -1], local_state[:, -1]), "chan", affine, (ones_vec, zeros_vec), False
    )
    lru_state = local_state + running * start_state[:, None]
    gate_val, pull_gelu = jax.vjp(jax.nn.gelu, gate_pre)
    mixed_out = (lru_state * gate_val).astype(jnp.bfloat16)
    resid = (
        rows_f32
        + jnp.einsum("ct,cd->td", mixed_out, out_full, preferred_element_type=jnp.float32)
        + out_bias
    )
    normed2, pull_norm2 = jax.vjp(rms_scale, resid, mlp_gain)
    normed2_low = normed2.astype(jnp.bfloat16)
    mlp_proj = jnp.concatenate([mlp_gate_full, mlp_up_full], axis=1)
    mlp_pre = jnp.einsum("td,df->ft", normed2_low, mlp_proj, preferred_element_type=jnp.float32)
    hidden, pull_mlp = jax.vjp(gated_unit, mlp_pre[:hidden_cut], mlp_pre[hidden_cut:])
    hidden_low = hidden.astype(jnp.bfloat16)
    output = (
        resid
        + jnp.einsum("ft,fd->td", hidden_low, mlp_down_full, preferred_element_type=jnp.float32)
    ).astype(jnp.bfloat16)
    grad_down = jnp.einsum("ft,td->fd", hidden_low, cotangent, preferred_element_type=jnp.float32)
    grad_gate_m, grad_up_m = pull_mlp(
        jnp.einsum("td,fd->ft", cotangent, mlp_down_full, preferred_element_type=jnp.float32)
    )
    grad_pre = jnp.concatenate([grad_gate_m, grad_up_m], axis=0).astype(jnp.bfloat16)
    grad_mlp_in = jnp.einsum("ft,td->fd", grad_pre, normed2_low, preferred_element_type=jnp.float32)
    grad_resid_part, grad_gain2 = pull_norm2(
        jnp.einsum("ft,df->td", grad_pre, mlp_proj, preferred_element_type=jnp.float32)
    )
    grad_resid = cot_f32 + grad_resid_part
    grad_branch = grad_resid.astype(jnp.bfloat16)
    grad_out_proj = jnp.einsum(
        "ct,td->cd", mixed_out, grad_branch, preferred_element_type=jnp.float32
    )
    grad_mixed = jnp.einsum("td,cd->ct", grad_branch, out_full, preferred_element_type=jnp.float32)
    product, carried = reverse_local(decay_rate, grad_mixed * gate_val)
    _, incoming = prefix(
        (decay_rate[:, 0] * product[:, 0], decay_rate[:, 0] * carried[:, 0]),
        "chan",
        affine,
        (ones_vec, zeros_vec),
        True,
    )
    carried = carried + product * incoming[:, None]
    coef_grads = finish_state(lru_state, start_state, carried, pull_coef)
    head_rows = from_behind(coef_grads[0][:, :3], "chan", -1)
    grad_lifted, grad_taps, grad_conv_bias = conv_backward(
        coef_grads[0], head_rows, segments, lifted, tail_rows, conv_taps
    )
    (grad_gate_pre,) = pull_gelu(grad_mixed * lru_state)
    grad_front = jnp.concatenate([grad_gate_pre, grad_lifted], axis=0).astype(jnp.bfloat16)
    grad_mix_proj = jnp.einsum(
        "ct,td->cd", grad_front, normed_low, preferred_element_type=jnp.float32
    )
    grad_normed = jnp.einsum("ct,dc->td", grad_front, mix_proj, preferred_element_type=jnp.float32)
    grad_x_part, grad_gain1 = pull_norm(grad_normed)
    grad_inputs = (grad_resid + grad_x_part).astype(jnp.bfloat16)
    grad_out_bias = jnp.sum(grad_resid, axis=0)
    pieces = [
        grad_mix_proj[:channels],
        grad_mix_proj[channels:],
        jnp.sum(grad_gate_pre, axis=1),
        jnp.sum(grad_lifted, axis=1),
        grad_taps,
        grad_conv_bias,
        jnp.transpose(coef_grads[1], (1, 0, 2)),
        coef_grads[2],
        jnp.transpose(coef_grads[3], (1, 0, 2)),
        coef_grads[4],
        coef_grads[5],
        grad_out_proj,
        grad_mlp_in[:hidden_cut],
        grad_mlp_in[hidden_cut:],
        grad_down,
        grad_gain1,
        grad_out_bias,
        grad_gain2,
    ]
    spread = flatten_rows(pieces, chan_count)
    shared = lax.psum_scatter(spread, "chan", scatter_dimension=0, tiled=True)
    summed = lax.psum(shared.reshape(-1), "rows")
    channels_dev = LRU // chan_count
    hidden_dev = FF // chan_count
    width_dev = D // chan_count
    block_dev = GB // chan_count
    shapes = [
        (channels_dev, D),
        (channels_dev, D),
        (channels_dev,),
        (channels_dev,),
        (channels_dev, 4),
        (channels_dev,),
        (block_dev, HEADS, GB),
        (channels_dev,),
        (block_dev, HEADS, GB),
        (channels_dev,),
        (channels_dev,),
        (channels_dev, D),
        (hidden_dev, D),
        (hidden_dev, D),
        (hidden_dev, D),
        (width_dev,),
        (width_dev,),
        (width_dev,),
    ]
    unpacked = []
    offset = 0
    for piece_shape in shapes:
        piece_size = math.prod(piece_shape)
        unpacked.append(summed[offset : offset + piece_size].reshape(piece_shape))
        offset = offset + piece_size
    return (
        output,
        grad_inputs,
        unpacked[15],
        unpacked[0].T,
        unpacked[2],
        unpacked[1].T,
        unpacked[3],
        unpacked[4].T,
        unpacked[5],
        jnp.transpose(unpacked[6], (1, 0, 2)),
        unpacked[7],
        jnp.transpose(unpacked[8], (1, 0, 2)),
        unpacked[9],
        unpacked[10],
        unpacked[11],
        unpacked[16],
        unpacked[17],
        unpacked[12].T,
        unpacked[13].T,
        unpacked[14],
    )


MESH = pl.DeviceIdType.MESH
LOW = jnp.bfloat16
F32 = jnp.float32
VMEM_BYTES = 60 * 2**20
TILE = 8
GELU_A = math.sqrt(2.0 / math.pi)
GELU_B = 0.044715


def nt(left, right):
    return lax.dot_general(left, right, (((1,), (1,)), ((), ())), preferred_element_type=F32)


def nn(left, right):
    return lax.dot_general(left, right, (((1,), (0,)), ((), ())), preferred_element_type=F32)


def tn(left, right):
    return lax.dot_general(left, right, (((0,), (0,)), ((), ())), preferred_element_type=F32)


def gelu_pair(values):
    squared = values * values
    bend = jnp.tanh(GELU_A * values * (1.0 + GELU_B * squared))
    half = 0.5 * (1.0 + bend)
    slope = half + 0.5 * values * (1.0 - bend * bend) * GELU_A * (1.0 + 3.0 * GELU_B * squared)
    return values * half, slope


class Spot:
    def __init__(self):
        self.r = lax.axis_index("rows")
        self.c = lax.axis_index("chan")
        self.z = lax.div(self.c, 2)
        self.y = lax.rem(self.c, 2)
        self.r_core = self.r + 1 - 2 * lax.rem(self.r, 2)
        self.r_x = lax.rem(self.r + 2, 4)
        self.core = (self.r_core, self.c)
        self.x = (self.r_x, self.c)
        self.c_y = self.c + 1 - 2 * self.y
        self.ymate = (self.r, self.c_y)
        self.up = (self.r, lax.rem(self.c + 2, 8))
        self.dn = (self.r, lax.rem(self.c + 6, 8))


def greet(always, maybe=()):
    barrier = pltpu.get_barrier_semaphore()
    count = len(always)
    for device in always:
        pl.semaphore_signal(barrier, inc=1, device_id=device, device_id_type=MESH)
    for device, there in maybe:

        @pl.when(there)
        def _(device=device):
            pl.semaphore_signal(barrier, inc=1, device_id=device, device_id_type=MESH)

        count = count + jnp.where(there, 1, 0)
    pl.semaphore_wait(barrier, count)


def push(source, target, sems, index, device):
    return pltpu.make_async_remote_copy(
        src_ref=source,
        dst_ref=target,
        send_sem=sems[0].at[index],
        recv_sem=sems[1].at[index],
        device_id=device,
        device_id_type=MESH,
    )


def landed(me, target, sems, index):
    push(target, target, sems, index, me.ymate).wait_recv()


def sem_pair(count):
    return [pltpu.SemaphoreType.DMA((count,)), pltpu.SemaphoreType.DMA((count,))]


def comm_params(collective_id):
    return pltpu.CompilerParams(
        collective_id=collective_id, has_side_effects=True, vmem_limit_bytes=VMEM_BYTES
    )


def plain_params():
    return pltpu.CompilerParams(
        dimension_semantics=("arbitrary",), vmem_limit_bytes=VMEM_BYTES
    )


ANYWHERE = pl.BlockSpec(memory_space=pl.ANY)
IN_VMEM = pl.BlockSpec(memory_space=pltpu.VMEM)


def whole(shape):
    return pl.BlockSpec(shape, lambda s: (0,) * len(shape))


def per_seq(shape):
    return pl.BlockSpec((1,) + shape, lambda s: (s,) + (0,) * len(shape))


def decay_terms(rec, softplus_row, reset):
    log_decay = -8.0 * rec * softplus_row
    decay = jnp.exp(log_decay)
    twice = 2.0 * log_decay
    series = twice * (
        1.0
        + twice * (1 / 2 + twice * (1 / 6 + twice * (1 / 24 + twice * (1 / 120 + twice * (1 / 720)))))
    )
    gap = jnp.where(twice > -0.25, -series, 1.0 - jnp.exp(twice))
    return decay, jnp.where(reset, 1.0, jnp.sqrt(gap))


def fill_tallies(tallies, starts_row, first, length, seq_length):
    position = first - 8 + lax.broadcasted_iota(jnp.int32, (length + 16, 1), 0)
    begun = jnp.sum((starts_row <= position).astype(F32), axis=1, keepdims=True)
    inside = jnp.logical_and(position >= 0, position < seq_length)
    tallies[...] = jnp.broadcast_to(jnp.where(inside, begun, -1.0), tallies.shape)


def same_document(tallies, length, shift, wide):
    own = tallies[pl.ds(8, length)]
    other = tallies[pl.ds(8 + shift, length)]
    same = (own == other).astype(F32)
    return jnp.concatenate([same] * (wide // same.shape[1]), axis=1)


def pair_diagonal(target, blocks):
    side = blocks.shape[1]
    target[...] = jnp.zeros_like(target)
    target[0:side, 0:side] = blocks[0].astype(target.dtype)
    target[side : 2 * side, side : 2 * side] = blocks[1].astype(target.dtype)


def tile_scan(a, b, backward):
    row = lax.broadcasted_iota(jnp.int32, a.shape, 1)
    for step in (1, 2, 4):
        shift = TILE - step if backward else step
        there = row < TILE - step if backward else row >= step
        b = b + a * jnp.where(there, pltpu.roll(b, shift, 1), 0.0)
        a = a * jnp.where(there, pltpu.roll(a, shift, 1), 1.0)
    return a, b


def carry_start(me, backward, totals, slots, sems):
    sign = -1 if backward else 1
    steps = me.c if backward else 7 - me.c
    copies = [
        push(totals, slots.at[d], sems, d, (me.r, lax.rem(me.c + 8 + sign * d, 8)))
        for d in range(1, 8)
    ]
    for d in range(1, 8):

        @pl.when(d <= steps)
        def _(d=d):
            copies[d - 1].start()

    return copies


def carry_join(me, backward, slots, start, sems):
    behind = 7 - me.c if backward else me.c
    start[...] = jnp.zeros_like(start)
    for d in range(7, 0, -1):

        @pl.when(d <= behind)
        def _(d=d):
            landed(me, slots.at[d], sems, d)
            start[...] = slots[d, :, 0] * start[...] + slots[d, :, 1]


def carry_sent(me, backward, copies):
    steps = me.c if backward else 7 - me.c
    for d in range(1, 8):

        @pl.when(d <= steps)
        def _(d=d):
            copies[d - 1].wait_send()


def peers_of(me):
    return [(me.r, lax.rem(me.c + d, 8)) for d in range(1, 8)]


class Spread:
    def __init__(self, me, arrays, pieces, sems):
        self.me, self.arrays, self.pieces, self.sems = me, arrays, pieces, sems
        self.go_up = jnp.logical_and(me.z >= me.r, me.z < 3)
        self.go_dn = jnp.logical_and(me.z <= me.r, me.z > 0)
        self.source = me.z == me.r
        self.hop = jnp.where(me.z < me.r, me.r - me.z, me.z - me.r)

    def slab(self, i, k, half):
        size = self.arrays[i].shape[1] // self.pieces
        return self.arrays[i].at[half, pl.ds(pl.multiple_of(k * size, 16), size)]

    def copies(self, k):
        me, found = self.me, []
        for i in range(len(self.arrays)):
            piece = self.slab(i, k, me.y)
            ys, yr, us, ds, zr = self.sems[5 * i : 5 * i + 5]
            found.append(
                (
                    push(piece, piece, (ys, yr), k, me.ymate),
                    push(piece, piece, (us, zr), k, me.up),
                    push(piece, piece, (ds, zr), k, me.dn),
                )
            )
        return found

    def send(self, k):
        found = self.copies(k)
        for copies in found:
            copies[0].start()

        @pl.when(self.go_up)
        def _():
            for copies in found:
                copies[1].start()

        @pl.when(self.go_dn)
        def _():
            for copies in found:
                copies[2].start()

    def lead(self, k):
        @pl.when(self.source)
        def _():
            self.send(k)

    def follow(self, k):
        me = self.me
        for i in range(len(self.arrays)):
            us, zr = self.sems[5 * i + 2], self.sems[5 * i + 4]
            landed(me, self.slab(i, k, me.y), (us, zr), k)
        self.send(k)

    def step(self, p):
        if p < self.pieces:
            self.lead(p)
        k = p - self.hop
        there = jnp.logical_and(k >= 0, k < self.pieces)

        @pl.when(jnp.logical_and(there, jnp.logical_not(self.source)))
        def _():
            self.follow(lax.rem(k + 2 * self.pieces, self.pieces))

    def arrived(self, k):
        for i in range(len(self.arrays)):
            ys, yr = self.sems[5 * i], self.sems[5 * i + 1]
            landed(self.me, self.slab(i, k, 1 - self.me.y), (ys, yr), k)

    def sent(self, k):
        found = self.copies(k)
        for copies in found:
            copies[0].wait_send()

        @pl.when(self.go_up)
        def _():
            for copies in found:
                copies[1].wait_send()

        @pl.when(self.go_dn)
        def _():
            for copies in found:
                copies[2].wait_send()

    def close(self):
        @pl.loop(0, self.pieces)
        def _(k):
            self.arrived(k)
            self.sent(k)


def spread_sems(arrays, pieces):
    return [pltpu.SemaphoreType.DMA((pieces,))] * (5 * arrays)


AHEAD = 4
HOP_LAG = 3
END_LAG = 10
RELAY_LAG = 13


class Reduce:
    def __init__(self, me, parts, mine, from_y, from_z, own, pieces, sems):
        self.me, self.parts, self.mine = me, parts, mine
        self.from_y, self.from_z, self.own = from_y, from_z, own
        self.pieces, self.sems = pieces, sems
        self.hop = jnp.where(me.z < me.r, me.z, 3 - me.z)
        self.owner = me.z == me.r
        self.relays = me.z == me.r_x

    def rows(self, i, k):
        size = self.mine[i].shape[0] // self.pieces
        return pl.ds(pl.multiple_of(k * size, 16), size)

    def each(self, k):
        for i in range(len(self.mine)):
            yield i, self.rows(i, k), self.sems[11 * i : 11 * i + 11]

    def y_copies(self, k):
        me = self.me
        return [
            push(self.parts[i].at[1 - me.y, rows], self.from_y[i].at[rows], sems[0:2], k, me.ymate)
            for i, rows, sems in self.each(k)
        ]

    def y_send(self, k):
        for copy in self.y_copies(k):
            copy.start()

    def add(self, i, rows, other):
        total = self.mine[i][rows].astype(F32) + other[i][rows].astype(F32)
        self.mine[i][rows] = total.astype(LOW)

    def join(self, k):
        for i, rows, sems in self.each(k):
            landed(self.me, self.from_y[i].at[rows], sems[0:2], k)
            self.add(i, rows, self.from_y)

    def z_copies(self, k, way):
        found = []
        for i, rows, sems in self.each(k):
            target = self.own if way == 2 else self.from_z
            pair = ((sems[2], sems[4]), (sems[3], sems[4]), (sems[3], sems[5]))[way]
            found.append(
                push(self.mine[i].at[rows], target[i].at[rows], pair, k,
                     self.me.up if way == 0 else self.me.dn)
            )
        return found

    def z_way(self, action):
        me = self.me
        for way, there in enumerate(
            (me.z < me.r, me.z > me.r + 1, me.z == me.r + 1)
        ):

            @pl.when(there)
            def _(way=way):
                action(way)

    def chain(self, k):
        @pl.when(self.hop > 0)
        def _():
            for i, rows, sems in self.each(k):
                landed(self.me, self.from_z[i].at[rows], (sems[2], sems[4]), k)
                self.add(i, rows, self.from_z)

        def start(way):
            for copy in self.z_copies(k, way):
                copy.start()

        self.z_way(start)

    def out_copies(self, k, device, pair):
        return [
            push(self.own[i].at[rows], self.own[i].at[rows], sems[pair : pair + 2], k, device)
            for i, rows, sems in self.each(k)
        ]

    def finish(self, k):
        @pl.when(self.me.z > 0)
        def _():
            for i, rows, sems in self.each(k):
                landed(self.me, self.from_z[i].at[rows], (sems[2], sems[4]), k)
                self.add(i, rows, self.from_z)

        @pl.when(self.me.z < 3)
        def _():
            for i, rows, sems in self.each(k):
                landed(self.me, self.own[i].at[rows], (sems[3], sems[5]), k)
                self.add(i, rows, self.own)

        for i, rows, sems in self.each(k):
            self.own[i][rows] = self.mine[i][rows]
        for copy in self.out_copies(k, self.me.x, 6) + self.out_copies(k, self.me.core, 8):
            copy.start()

    def relay(self, k):
        for copy in self.out_copies(k, self.me.x, 6):
            copy.wait_recv()
        for copy in self.out_copies(k, self.me.core, 8):
            copy.start()

    def step(self, q):
        n = self.pieces

        def at(k, also, action):
            there = jnp.logical_and(k >= 0, k < n)

            @pl.when(there if also is None else jnp.logical_and(there, also))
            def _():
                action(lax.rem(k + 8 * n, n))

        at(q + AHEAD, None, self.y_send)
        at(q, None, self.join)
        at(q - HOP_LAG * self.hop, jnp.logical_not(self.owner), self.chain)
        at(q - END_LAG, self.owner, self.finish)
        at(q - RELAY_LAG, self.relays, self.relay)

    def close(self):
        others = jnp.logical_not(jnp.logical_or(self.owner, self.relays))

        @pl.loop(0, self.pieces)
        def _(k):
            for copy in self.y_copies(k):
                copy.wait_send()

            def sent(way):
                for copy in self.z_copies(k, way):
                    copy.wait_send()

            self.z_way(sent)

            @pl.when(self.owner)
            def _():
                for copy in self.out_copies(k, self.me.x, 6) + self.out_copies(k, self.me.core, 8):
                    copy.wait_send()

            @pl.when(self.relays)
            def _():
                for copy in self.out_copies(k, self.me.core, 8):
                    copy.wait_send()

            @pl.when(others)
            def _():
                for copy in self.out_copies(k, self.me.core, 8):
                    copy.wait_recv()


class Line:
    def __init__(self, reduces, offsets):
        self.reduces, self.offsets, self.done = reduces, offsets, -AHEAD

    def position(self, p, low, high):
        for one, offset in zip(self.reduces, self.offsets):
            if offset - AHEAD < high and low < offset + one.pieces + RELAY_LAG:
                one.step(p - offset)

    def advance(self, high):
        low, self.done = self.done, high
        if high > low + 1:

            @pl.loop(low, high)
            def _(p):
                self.position(p, low, high)

        elif high > low:
            self.position(low, low, high)

    def during(self, begin, end, action):
        low, self.done = self.done, self.done + end - begin

        @pl.loop(begin, end)
        def _(s):
            action(s)
            self.position(low - begin + s, low, low + end - begin)

    def last(self):
        return self.offsets[-1] + self.reduces[-1].pieces + RELAY_LAG

    def close(self):
        for one in self.reduces:
            one.close()


def reduce_sems(arrays, pieces):
    return [pltpu.SemaphoreType.DMA((pieces,))] * (11 * arrays)


def front_kernel(
    inputs, cot, gain, vecs, taps_all, rgate_all, igate_all, starts, out_bias, mlp_gain,
    wm, mg, mu, md,
    wq_o, wg_o, wu_o, wd_o, nall_o, call, starts_all, gate_o, lext_o, conv_o, rec_o, open_o,
    state_o, start, mixed_o, resid, n2all,
    wq, nall, halo, gate_pre, lext, conv, rec, opening, a, b, mixed, part, tot, slots, tallies,
    rg32, ig32, rgate, igate,
    mate, out_x, in_x, ms, mr, rxs, rxr, ax, bx, ac, bc,
    loc, outs, xs, xr, cs, cr, hs, hr, ss, sr, ps, pr, *spread_refs,
):
    me = Spot()
    r, c, z, y = me.r, me.c, me.z, me.y
    length = inputs.shape[0]
    seq_length = length * 8
    wide = taps_all.shape[2]
    diag = (me.r_x + 1 - 2 * lax.rem(me.r_x, 2), c)
    barrier = pltpu.get_barrier_semaphore()
    always = [me.core, me.x, diag] + peers_of(me)
    for device in always:
        pl.semaphore_signal(barrier, inc=1, device_id=device, device_id_type=MESH)
    count = len(always)
    others = [1, 2, 3]
    for there, place in ((c < 7, lax.rem(c + 1, 8)), (c > 0, lax.rem(c + 7, 8))):
        for i in others:

            @pl.when(there)
            def _(i=i, place=place):
                pl.semaphore_signal(
                    barrier, inc=1, device_id=(lax.rem(r + i, 4), place), device_id_type=MESH
                )

        count = count + jnp.where(there, 3, 0)
    own = [
        pltpu.make_async_copy(wm, wq.at[:, y], loc.at[0]),
        pltpu.make_async_copy(mg, wg_o.at[y], loc.at[1]),
        pltpu.make_async_copy(mu, wu_o.at[y], loc.at[2]),
        pltpu.make_async_copy(md, wd_o.at[y], loc.at[3]),
    ]

    @pl.when(z == r)
    def _():
        for copy in own:
            copy.start()

    heads = [
        pltpu.make_async_copy(rgate_all.at[pl.ds(2 * r, 2)], rg32, loc.at[4]),
        pltpu.make_async_copy(igate_all.at[pl.ds(2 * r, 2)], ig32, loc.at[5]),
    ]
    for copy in heads:
        copy.start()
    call[r] = cot[...]
    vals = inputs[...].astype(F32)
    scale = lax.rsqrt(jnp.mean(vals * vals, axis=-1, keepdims=True) + EPSILON)
    nall[r] = (vals * scale * gain[...]).astype(LOW)
    starts_all[r] = starts[...]
    pl.semaphore_wait(barrier, count)

    x_n = push(nall.at[r], nall.at[r], (xs, xr), 0, me.x)
    c_n = push(nall.at[r], nall.at[r], (cs, cr), 0, me.core)
    c_c = push(call.at[r], call.at[r], (cs, cr), 1, me.core)
    x_c = push(call.at[r], call.at[r], (xs, xr), 1, me.x)
    fwd_n = push(nall.at[me.r_x], nall.at[me.r_x], (cs, cr), 2, me.core)
    fwd_c = push(call.at[me.r_x], call.at[me.r_x], (cs, cr), 3, me.core)
    s_copies = [
        push(starts_all.at[r], starts_all.at[r], (ss, sr), i, device)
        for i, device in enumerate((me.core, me.x, diag))
    ]
    tail = nall.at[r, pl.ds(length - 16, 16)]
    halo_copies = [
        push(tail, halo.at[r], (hs, hr), i, (lax.rem(r + i, 4), lax.rem(c + 1, 8))) for i in range(4)
    ]
    glo = [Spread(me, [wq.at[m]], 4, spread_refs[5 * m : 5 * m + 5]) for m in range(3)]
    pieces = 8
    mlp_w = Spread(me, [wg_o, wu_o, wd_o], pieces, spread_refs[15:])
    x_n.start()
    for copy in s_copies:
        copy.start()

    @pl.when(c < 7)
    def _():
        for copy in halo_copies:
            copy.start()

    c_n.start()
    c_c.start()

    @pl.when(c == 0)
    def _():
        halo[...] = jnp.zeros_like(halo)

    @pl.when(z == r)
    def _():
        own[0].wait()

    for k in range(12):
        glo[k // 4].lead(k % 4)

        @pl.when(z != r)
        def _(k=k):
            glo[k // 4].follow(k % 4)

        if k == 3:
            for copy in heads:
                copy.wait()
            pair_diagonal(rgate, rg32)
            pair_diagonal(igate, ig32)
        if k == 7:
            x_n.wait_recv()
            fwd_n.start()
            x_c.start()

    @pl.when(z == r)
    def _():
        for copy in own[1:]:
            copy.wait()

    mlp_w.step(0)
    for m in range(2):
        for k in range(4):
            glo[m].arrived(k)
    c_n.wait_recv()
    fwd_n.wait_recv()
    for copy in s_copies:
        copy.wait_recv()

    @pl.when(c > 0)
    def _():
        for i in range(4):
            landed(me, halo.at[i], (hs, hr), i)

    vec = vecs.at[r]
    taps = taps_all.at[r]

    def mixer_one(s):
        fill_tallies(tallies, starts_all[s, 0:1], c * length, length, seq_length)
        tokens = nall[s]
        wgate = wq[0].reshape(wide, tokens.shape[1])
        wlift = wq[1].reshape(wide, tokens.shape[1])
        gate_pre[s] = nt(tokens, wgate) + vec[0:1]
        lifted = nt(tokens, wlift) + vec[1:2]
        lext[s, 0:8] = (nt(halo[s], wlift) + vec[1:2])[8:16]
        lext[s, pl.ds(8, length)] = lifted
        out = vec[2:3] + taps[0:1] * lifted
        for k in range(1, 4):
            same = same_document(tallies, length, -k, wide)
            out = out + taps[k : k + 1] * lext[s, pl.ds(8 - k, length)] * same
        conv[s] = out
        low = out.astype(LOW)
        recur = jax.nn.sigmoid(nn(low, rgate[...]) + vec[3:4])
        opened = jax.nn.sigmoid(nn(low, igate[...]) + vec[4:5])
        rec[s] = recur
        opening[s] = opened
        reset = same_document(tallies, length, -1, wide) < 0.5
        decay, scaling = decay_terms(recur, vec[5:6], reset)
        decay = jnp.where(reset, 0.0, decay)
        tiles = (length // TILE, TILE, wide)
        a_scan, b_scan = tile_scan(
            decay.reshape(tiles), (scaling * opened * out).reshape(tiles), False
        )
        a[s] = a_scan.reshape(length, wide)
        b[s] = b_scan.reshape(length, wide)
        product = jnp.ones((1, wide), F32)
        state = jnp.zeros((1, wide), F32)
        for t in range(length // TILE):
            last = t * TILE + TILE - 1
            a_last = a[s, last : last + 1]
            state = b[s, last : last + 1] + a_last * state
            product = product * a_last
        tot[s, 0:1] = product
        tot[s, 1:2] = state

    for half in range(2):

        @pl.loop(2 * half, 2 * half + 2)
        def _(s):
            mixer_one(s)

        mlp_w.step(1 + half)

    carry_copies = carry_start(me, False, tot, slots, (ps, pr))
    saved = [
        pltpu.make_async_copy(source, target, outs.at[i])
        for i, (source, target) in enumerate(
            ((gate_pre, gate_o), (lext, lext_o), (conv, conv_o), (rec, rec_o), (opening, open_o),
             (nall, nall_o))
        )
    ]
    for copy in saved:
        copy.start()
    x_c.wait_recv()
    fwd_c.start()
    for k in range(4):
        glo[2].arrived(k)
    save_w = pltpu.make_async_copy(wq, wq_o, outs.at[6])
    save_w.start()
    mlp_w.step(3)
    carry_join(me, False, slots, start, (ps, pr))

    def mixer_two(s):
        state = start[pl.ds(s, 1)]
        for t in range(length // TILE):
            tile = pl.ds(t * TILE, TILE)
            now = b[s, tile] + a[s, tile] * state
            b[s, tile] = now
            state = now[TILE - 1 : TILE]
        gate_val, _ = gelu_pair(gate_pre[s])
        mix = (b[s] * gate_val).astype(LOW)
        mixed[s] = mix
        part[s] = nn(mix, wq[2].reshape(wide, part.shape[2])).astype(LOW)

    for half in range(2):

        @pl.loop(2 * half, 2 * half + 2)
        def _(s):
            mixer_two(s)

        mlp_w.step(4 + half)

    more = [
        pltpu.make_async_copy(b, state_o, outs.at[7]),
        pltpu.make_async_copy(mixed, mixed_o, outs.at[8]),
    ]
    for copy in more:
        copy.start()
    step = length // RS_CHUNKS
    copies = rows_sum_start(me, part, mate, (ms, mr))
    crossing = rows_sum_cross(me, part, mate, out_x, in_x, copies, (rxs, rxr))
    mlp_w.step(6)
    first = []
    for k in range(RS_CHUNKS):
        chunk = pl.ds(k * step, step)
        total = rows_sum_chunk(me, part, mate, in_x, copies, crossing, k)
        res = inputs[chunk].astype(F32) + total + out_bias[...]
        resid[chunk] = res
        scale = lax.rsqrt(jnp.mean(res * res, axis=-1, keepdims=True) + EPSILON)
        n2all[r, chunk] = (res * scale * mlp_gain[...]).astype(LOW)
        first.append(spread_chunk(me, n2all, k, (ax, bx), (ac, bc)))
        if k % 2 == 1:
            mlp_w.step(7 + k // 2)
    mlp_w.step(9)
    mlp_w.step(10)
    spread_rest(me, n2all, first, (ac, bc))
    finish_sends(copies + crossing)
    mlp_w.close()
    for m in range(3):
        for k in range(4):
            glo[m].sent(k)
    x_n.wait_send()
    x_c.wait_send()
    c_n.wait_send()
    c_c.wait()
    fwd_n.wait_send()
    fwd_c.wait()
    finish_sends(s_copies)

    @pl.when(c < 7)
    def _():
        finish_sends(halo_copies)

    carry_sent(me, False, carry_copies)
    for copy in saved + [save_w] + more:
        copy.wait()


def front(inputs, cot, gain, vecs, taps_all, rgate_all, igate_all, starts, out_bias, mlp_gain,
          wm, mg, mu, md):
    length, width = inputs.shape
    wide = 2 * wm.shape[1]
    hidden = mg.shape[1]
    sd = jax.ShapeDtypeStruct
    tall = sd((4, length, wide), F32)
    ext = sd((4, length + 8, wide), F32)
    low = sd((4, length, wide), LOW)
    tokens = sd((4, length, width), LOW)
    vmem = lambda spec: pltpu.VMEM(spec.shape, spec.dtype)
    outs = [
        (sd((3, 2, wide // 2, width), LOW), ANYWHERE),
        (sd((2, width, hidden), LOW), IN_VMEM),
        (sd((2, width, hidden), LOW), IN_VMEM),
        (sd((2, hidden, width), LOW), IN_VMEM),
        (tokens, ANYWHERE),
        (tokens, IN_VMEM),
        (sd((4,) + starts.shape, starts.dtype), IN_VMEM),
        (tall, ANYWHERE),
        (ext, ANYWHERE),
        (tall, ANYWHERE),
        (tall, ANYWHERE),
        (tall, ANYWHERE),
        (tall, ANYWHERE),
        (sd((4, wide), F32), IN_VMEM),
        (low, ANYWHERE),
        (sd((length, width), F32), IN_VMEM),
        (tokens, IN_VMEM),
    ]
    dma = pltpu.SemaphoreType.DMA
    return pl.pallas_call(
        front_kernel,
        name="front",
        out_shape=[o[0] for o in outs],
        in_specs=[IN_VMEM] * 5 + [ANYWHERE] * 2 + [IN_VMEM] * 3 + [ANYWHERE] * 4,
        out_specs=[o[1] for o in outs],
        scratch_shapes=[
            pltpu.VMEM((3, 2, wide // 2, width), LOW), vmem(tokens), pltpu.VMEM((4, 16, width), LOW),
            vmem(tall), vmem(ext), vmem(tall), vmem(tall), vmem(tall), vmem(tall), vmem(tall),
            vmem(low), vmem(tokens), pltpu.VMEM((4, 2, wide), F32), pltpu.VMEM((8, 4, 2, wide), F32),
            pltpu.VMEM((length + 16, 128), F32),
            pltpu.VMEM((2, GB, GB), F32), pltpu.VMEM((2, GB, GB), F32),
            pltpu.VMEM((wide, wide), LOW), pltpu.VMEM((wide, wide), LOW),
        ]
        + rows_sum_scratch(length, width) + sem_pair(RS_CHUNKS) + sem_pair(2 * RS_CHUNKS)
        + [dma((7,)), dma((9,))] + sem_pair(2) + sem_pair(4) + sem_pair(4) + sem_pair(3)
        + sem_pair(8) + spread_sems(3, 4) + spread_sems(3, 8),
        compiler_params=comm_params(1),
    )(inputs, cot, gain, vecs, taps_all, rgate_all, igate_all, starts, out_bias, mlp_gain,
      wm, mg, mu, md)


RS_CHUNKS = 4


def rows_sum_start(me, part, mate, sems):
    length = part.shape[1]
    step = length // RS_CHUNKS
    far = lax.rem(me.r_core + 2, 4)
    copies = []
    for block, owner in enumerate((far, me.r_core)):
        for k in range(RS_CHUNKS):
            rows = pl.ds(k * step, step)
            copies.append(
                push(part.at[owner, rows], mate.at[block, rows], sems, block * RS_CHUNKS + k, me.core)
            )
    for copy in copies:
        copy.start()
    return copies


def rows_sum_cross(me, part, mate, out_x, in_x, copies, sems):
    length = part.shape[1]
    step = length // RS_CHUNKS
    crossing = []
    for k in range(RS_CHUNKS):
        rows = pl.ds(k * step, step)
        copies[k].wait_recv()
        out_x[rows] = (part[me.r_x, rows].astype(F32) + mate[0, rows].astype(F32)).astype(LOW)
        copy = push(out_x.at[rows], in_x.at[rows], sems, k, me.x)
        copy.start()
        crossing.append(copy)
    return crossing


def rows_sum_chunk(me, part, mate, in_x, copies, crossing, k):
    length = part.shape[1]
    step = length // RS_CHUNKS
    rows = pl.ds(k * step, step)
    copies[RS_CHUNKS + k].wait_recv()
    crossing[k].wait_recv()
    return part[me.r, rows].astype(F32) + mate[1, rows].astype(F32) + in_x[rows].astype(F32)


def finish_sends(copies):
    for copy in copies:
        copy.wait_send()


def rows_sum_scratch(length, width):
    return [
        pltpu.VMEM((2, length, width), LOW),
        pltpu.VMEM((length, width), LOW),
        pltpu.VMEM((length, width), LOW),
    ] + sem_pair(2 * RS_CHUNKS) + sem_pair(RS_CHUNKS)


def spread_chunk(me, all_ref, k, sems_x, sems_c):
    length = all_ref.shape[1]
    step = length // RS_CHUNKS
    rows = pl.ds(k * step, step)
    mine = all_ref.at[me.r, rows]
    copies = [
        push(mine, mine, sems_x, k, me.x),
        push(mine, mine, sems_c, k, me.core),
    ]
    for copy in copies:
        copy.start()
    return copies


def spread_rest(me, all_ref, first, sems_c, beside=None):
    length = all_ref.shape[1]
    step = length // RS_CHUNKS
    passed = []
    for k in range(RS_CHUNKS):
        first[k][0].wait_recv()
        theirs = all_ref.at[me.r_x, pl.ds(k * step, step)]
        copy = push(theirs, theirs, sems_c, RS_CHUNKS + k, me.core)
        copy.start()
        passed.append(copy)
        if beside is not None:
            beside(k)
    for k in range(RS_CHUNKS):
        first[k][0].wait_send()
        first[k][1].wait()
        passed[k].wait()


def mlp_kernel(
    nall, call, wg, wu, wd, part, gpart, dg_o, du_o, dd_o,
    acc_out, acc_in, acc_g, acc_u, acc_d,
):
    block = pl.program_id(0)
    length = nall.shape[1]

    @pl.when(block == 0)
    def _():
        acc_out[...] = jnp.zeros_like(acc_out)
        acc_in[...] = jnp.zeros_like(acc_in)

    acc_g[...] = jnp.zeros_like(acc_g)
    acc_u[...] = jnp.zeros_like(acc_u)
    acc_d[...] = jnp.zeros_like(acc_d)

    @pl.loop(0, nall.shape[0])
    def _(s):
        tokens = nall[s]
        cot = call[s]
        gate = nn(tokens, wg[0])
        up = nn(tokens, wu[0])
        grad_hidden = nt(cot, wd[0])
        gate_val, slope = gelu_pair(gate)
        hidden = (gate_val * up).astype(LOW)
        grad_gate = (grad_hidden * up * slope).astype(LOW)
        grad_up = (grad_hidden * gate_val).astype(LOW)
        acc_out[s] += nn(hidden, wd[0])
        acc_in[s] += nt(grad_gate, wg[0]) + nt(grad_up, wu[0])
        acc_d[...] += tn(hidden, cot)
        acc_g[...] += tn(tokens, grad_gate)
        acc_u[...] += tn(tokens, grad_up)

    dg_o[0] = acc_g[...].astype(LOW)
    du_o[0] = acc_u[...].astype(LOW)
    dd_o[0] = acc_d[...].astype(LOW)

    @pl.when(block == pl.num_programs(0) - 1)
    def _():
        part[...] = acc_out[...].astype(LOW)
        gpart[...] = acc_in[...].astype(LOW)


def mlp(nall, call, wg, wu, wd):
    blocks, width, hidden = wg.shape
    sd = jax.ShapeDtypeStruct
    inward = pl.BlockSpec((1, width, hidden), lambda h: (h, 0, 0))
    outward = pl.BlockSpec((1, hidden, width), lambda h: (h, 0, 0))
    return pl.pallas_call(
        mlp_kernel,
        name="mlp_both_ways",
        grid=(blocks,),
        in_specs=[whole(nall.shape), whole(call.shape), inward, inward, outward],
        out_specs=[whole(nall.shape), whole(nall.shape), inward, inward, outward],
        out_shape=[sd(nall.shape, LOW)] * 2 + [sd(w.shape, LOW) for w in (wg, wu, wd)],
        scratch_shapes=[pltpu.VMEM(nall.shape, F32)] * 2
        + [pltpu.VMEM(w.shape[1:], F32) for w in (wg, wu, wd)],
        compiler_params=plain_params(),
    )(nall, call, wg, wu, wd)


def back_kernel(
    gpart2, cot, resid, inputs, mlp_gain, mix_gain, vecs, taps_all, starts_all, start,
    opart, dmg, dmu, dmd, wq_h, nall_h, gate_h, lext_h, conv_h, rec_h, open_h, state_h, mixed_h,
    rgate_all, igate_all,
    output, ginputs, own_g, own_u, own_d, own_e, own_l, gates_all, gains_all,
    wq, nall, gate_pre, lext, conv, rec, opening, state, mixed, a, b, gconv, heads_in,
    gate_low, ball, gresid, opart_v, acc_a, acc_b, acc_r, acc_i, sums, prev_ext,
    early, late, mine_g, mine_u, mine_d, y_g, y_u, y_d, y_e, y_l,
    z_g, z_u, z_d, z_e, z_l,
    tot, slots, carry, tallies, rg32, ig32, rgate, igate,
    gate_send, gate_slots, gain_slots, gain_sums,
    mate, out_x, in_x, ms, mr, rxs, rxr, o_mate, o_out, o_in, oms, omr, oxs, oxr,
    nms, nmr, nxs, nxr, ax, bx, ac, bc,
    loc, ps, pr, hs, hr, ggs, ggr, ghs, ghr, qs, qr, ts, tr, *reduce_refs,
):
    me = Spot()
    r, c, z, y = me.r, me.c, me.z, me.y
    length = inputs.shape[0]
    seq_length = length * 8
    wide = taps_all.shape[2]
    width = inputs.shape[1]
    side = wide // 2
    step = length // RS_CHUNKS
    diag = (me.r_x + 1 - 2 * lax.rem(me.r_x, 2), c)
    chan_peers = peers_of(me)
    row_peers = (me.core, me.x, diag)
    loads = [
        pltpu.make_async_copy(source, target, loc.at[i])
        for i, (source, target) in enumerate(
            (
                (dmg.at[y], mine_g), (dmu.at[y], mine_u), (dmd.at[y], mine_d),
                (gate_h, gate_pre), (state_h, state), (mixed_h, mixed), (rec_h, rec), (wq_h, wq),
                (open_h, opening), (conv_h, conv), (lext_h, lext), (nall_h, nall),
                (opart, opart_v), (rgate_all.at[pl.ds(2 * r, 2)], rg32),
                (igate_all.at[pl.ds(2 * r, 2)], ig32),
            )
        )
    ]
    for copy in loads:
        copy.start()
    greet(list(row_peers) + chan_peers)
    groups = [reduce_refs[11 * i : 11 * i + 11] for i in range(5)]
    line = Line(
        [
            Reduce(me, [dmg], [mine_g], [y_g], [z_g], [own_g], 8, groups[0]),
            Reduce(me, [dmu], [mine_u], [y_u], [z_u], [own_u], 8, groups[1]),
            Reduce(me, [dmd], [mine_d], [y_d], [z_d], [own_d], 8, groups[2]),
            Reduce(me, [early], [early.at[y]], [y_e], [z_e], [own_e], 8, groups[3]),
            Reduce(me, [late], [late.at[y]], [y_l], [z_l], [own_l], 7, groups[4]),
        ],
        (0, 8, 16, 24, 33),
    )

    copies = rows_sum_start(me, gpart2, mate, (ms, mr))
    line.advance(0)
    crossing = rows_sum_cross(me, gpart2, mate, out_x, in_x, copies, (rxs, rxr))
    for copy in loads[:3]:
        copy.wait()
    line.advance(1)
    first = []
    gain2_sum = 0.0
    bias_sum = 0.0
    for k in range(RS_CHUNKS):
        rows = pl.ds(k * step, step)
        grad = rows_sum_chunk(me, gpart2, mate, in_x, copies, crossing, k)
        res = resid[rows]
        scale = lax.rsqrt(jnp.mean(res * res, axis=-1, keepdims=True) + EPSILON)
        gain2_sum = gain2_sum + jnp.sum(grad * res * scale, axis=0, keepdims=True)
        pulled = grad * mlp_gain[...]
        inner = jnp.mean(pulled * res, axis=-1, keepdims=True)
        total = cot[rows].astype(F32) + scale * pulled - res * (scale * scale * scale * inner)
        bias_sum = bias_sum + jnp.sum(total, axis=0, keepdims=True)
        gresid[rows] = total
        ball[r, rows] = total.astype(LOW)
        first.append(spread_chunk(me, ball, k, (ax, bx), (ac, bc)))
        line.advance((2, 3, 5, 6)[k])
    for copy in loads[3:]:
        copy.wait()
    pair_diagonal(rgate, rg32)
    pair_diagonal(igate, ig32)
    line.advance(7)
    spread_rest(me, ball, first, (ac, bc), lambda k: line.advance(9 + k))
    o_copies = rows_sum_start(me, opart_v, o_mate, (oms, omr))
    finish_sends(copies + crossing)

    vec = vecs.at[r]
    taps = taps_all.at[r]
    acc_a[...] = jnp.zeros_like(acc_a)
    acc_b[...] = jnp.zeros_like(acc_b)
    acc_r[...] = jnp.zeros_like(acc_r)
    acc_i[...] = jnp.zeros_like(acc_i)
    sums[...] = jnp.zeros_like(sums)

    def reset_of(s):
        fill_tallies(tallies, starts_all[s, 0:1], c * length, length, seq_length)
        return same_document(tallies, length, -1, wide) < 0.5

    def mixer_three(s):
        branch = ball[s]
        grad_mixed = nt(branch, wq[2].reshape(wide, width))
        gate_val, slope = gelu_pair(gate_pre[s])
        grad_gate = grad_mixed * state[s] * slope
        low = grad_gate.astype(LOW)
        gate_low[s] = low
        sums[0:1] += jnp.sum(grad_gate, axis=0, keepdims=True)
        acc_a[...] += tn(mixed[s], branch)
        acc_b[...] += tn(low, nall[s])
        grad_state = grad_mixed * gate_val
        gate_pre[s] = grad_state
        decay = jnp.where(reset_of(s), 0.0, jnp.exp(-8.0 * rec[s] * vec[5:6]))
        tiles = (length // TILE, TILE, wide)
        a_scan, b_scan = tile_scan(
            decay.reshape(tiles), (decay * grad_state).reshape(tiles), True
        )
        a[s] = a_scan.reshape(length, wide)
        b[s] = b_scan.reshape(length, wide)
        product = jnp.ones((1, wide), F32)
        carried = jnp.zeros((1, wide), F32)
        for t in range(length // TILE - 1, -1, -1):
            head = t * TILE
            a_head = a[s, head : head + 1]
            carried = b[s, head : head + 1] + a_head * carried
            product = product * a_head
        tot[s, 0:1] = product
        tot[s, 1:2] = carried

    line.during(0, 4, mixer_three)
    o_cross = rows_sum_cross(me, opart_v, o_mate, o_out, o_in, o_copies, (oxs, oxr))

    carry_copies = carry_start(me, True, tot, slots, (ps, pr))
    for j in range(2):
        early[j, 0:side] = acc_a[j * side : (j + 1) * side].astype(LOW)
        early[j, side : 2 * side] = acc_b[j * side : (j + 1) * side].astype(LOW)
    acc_b[...] = jnp.zeros_like(acc_b)
    line.advance(18)
    carry_join(me, True, slots, carry, (ps, pr))

    def mixer_four(s):
        now = carry[pl.ds(s, 1)]
        gconv[s, pl.ds(length, TILE)] = jnp.broadcast_to(now, (TILE, wide))
        for t in range(length // TILE - 1, -1, -1):
            rows = pl.ds(t * TILE, TILE)
            moved = b[s, rows] + a[s, rows] * now
            gconv[s, rows] = moved
            now = moved[0:1]
        carried = gate_pre[s] + gconv[s, pl.ds(1, length)]
        prev_ext[0:TILE] = jnp.broadcast_to(start[pl.ds(s, 1)], (TILE, wide))
        prev_ext[pl.ds(TILE, length)] = state[s]
        previous = prev_ext[pl.ds(TILE - 1, length)]
        recur, opened, conv_s = rec[s], opening[s], conv[s]
        reset = reset_of(s)
        decay, scaling = decay_terms(recur, vec[5:6], reset)
        pulled = carried * scaling
        grad_opening = pulled * conv_s
        grad_log = carried * (previous * decay - opened * conv_s * (decay * decay / scaling))
        grad_log = jnp.where(reset, 0.0, grad_log)
        grad_rec = grad_log * (-8.0 * vec[5:6])
        grad_rpre = grad_rec * recur * (1.0 - recur)
        grad_opre = grad_opening * opened * (1.0 - opened)
        r_low, o_low, conv_low = grad_rpre.astype(LOW), grad_opre.astype(LOW), conv_s.astype(LOW)
        total = pulled * opened + nt(r_low, rgate[...]) + nt(o_low, igate[...])
        gconv[s, 0:length] = total
        acc_r[...] += tn(conv_low, r_low)
        acc_i[...] += tn(conv_low, o_low)
        sums[7:8] += jnp.sum(grad_rpre, axis=0, keepdims=True)
        sums[8:9] += jnp.sum(grad_opre, axis=0, keepdims=True)
        sums[9:10] += jnp.sum(grad_log * recur, axis=0, keepdims=True) * (8.0 * vec[6:7])
        sums[6:7] += jnp.sum(total, axis=0, keepdims=True)

    line.during(0, 4, mixer_four)

    heads = [
        push(gconv.at[s, pl.ds(0, TILE)], heads_in.at[s], (hs, hr), s, (r, lax.rem(c + 7, 8)))
        for s in range(4)
    ]

    @pl.when(c > 0)
    def _():
        for copy in heads:
            copy.start()

    @pl.when(c == 7)
    def _():
        heads_in[...] = jnp.zeros_like(heads_in)

    cut = side // 8
    for k in range(8):
        at = k * cut
        gate_send[k] = jnp.concatenate(
            [m[j * side + at : j * side + at + cut, j * side : (j + 1) * side]
             for m in (acc_r, acc_i) for j in range(2)], axis=0
        ).astype(LOW)
    gate_copies = [
        push(gate_send.at[lax.rem(c + d, 8)], gate_slots.at[d], (qs, qr), d, chan_peers[d - 1])
        for d in range(1, 8)
    ]
    for copy in gate_copies:
        copy.start()
    line.advance(24)

    @pl.when(c < 7)
    def _():
        for s in range(4):
            landed(me, heads_in.at[s], (hs, hr), s)

    def mixer_five(s):
        fill_tallies(tallies, starts_all[s, 0:1], c * length, length, seq_length)
        grad = gconv[s, 0:length]
        prev_ext[0:length] = grad
        prev_ext[pl.ds(length, TILE)] = heads_in[s]
        grad_lifted = taps[0:1] * grad
        sums[2:3] += jnp.sum(grad * lext[s, pl.ds(TILE, length)], axis=0, keepdims=True)
        for k in range(1, 4):
            ahead = prev_ext[pl.ds(k, length)] * same_document(tallies, length, k, wide)
            grad_lifted = grad_lifted + taps[k : k + 1] * ahead
            behind = lext[s, pl.ds(TILE - k, length)] * same_document(tallies, length, -k, wide)
            sums[2 + k : 3 + k] += jnp.sum(grad * behind, axis=0, keepdims=True)
        sums[1:2] += jnp.sum(grad_lifted, axis=0, keepdims=True)
        lift_low = grad_lifted.astype(LOW)
        acc_b[...] += tn(lift_low, nall[s])
        ball[s] = (
            nn(gate_low[s], wq[0].reshape(wide, width)) + nn(lift_low, wq[1].reshape(wide, width))
        ).astype(LOW)

    for k in range(RS_CHUNKS):
        rows = pl.ds(k * step, step)
        total = rows_sum_chunk(me, opart_v, o_mate, o_in, o_copies, o_cross, k)
        output[rows] = (resid[rows] + total).astype(LOW)
    line.during(0, 4, mixer_five)

    n_copies = rows_sum_start(me, ball, mate, (nms, nmr))
    late[...] = jnp.zeros_like(late)
    for j in range(2):
        late[j, 0:side] = acc_b[j * side : (j + 1) * side].astype(LOW)
        late[j, side : side + 16, 0:side] = sums[:, j * side : (j + 1) * side].astype(LOW)
    line.advance(30)
    n_cross = rows_sum_cross(me, ball, mate, out_x, in_x, n_copies, (nxs, nxr))
    line.advance(32)
    gain_sum = 0.0
    for k in range(RS_CHUNKS):
        rows = pl.ds(k * step, step)
        grad = rows_sum_chunk(me, ball, mate, in_x, n_copies, n_cross, k)
        vals = inputs[rows].astype(F32)
        scale = lax.rsqrt(jnp.mean(vals * vals, axis=-1, keepdims=True) + EPSILON)
        gain_sum = gain_sum + jnp.sum(grad * vals * scale, axis=0, keepdims=True)
        pulled = grad * mix_gain[...]
        inner = jnp.mean(pulled * vals, axis=-1, keepdims=True)
        ginputs[rows] = (
            gresid[rows] + scale * pulled - vals * (scale * scale * scale * inner)
        ).astype(LOW)
        line.advance(33 + k)
    for k in range(8):
        lanes = slice(k * 128, (k + 1) * 128)
        gain_slots[0, k] = jnp.concatenate(
            [gain_sum[:, lanes], gain2_sum[:, lanes], bias_sum[:, lanes], jnp.zeros((5, 128), F32)], 0
        )
    gain_copies = [
        push(gain_slots.at[0, lax.rem(c + d, 8)], gain_slots.at[1, d], (ggs, ggr), d,
             chan_peers[d - 1])
        for d in range(1, 8)
    ]
    for copy in gain_copies:
        copy.start()
    line.advance(38)
    gate_total = gate_send[c].astype(F32)
    for d in range(1, 8):
        gate_copies[d - 1].wait_recv()
        gate_total = gate_total + gate_slots[d].astype(F32)
    gates_all[r] = gate_total.astype(LOW)
    gate_rows = [
        push(gates_all.at[r], gates_all.at[r], (ts, tr), i, device)
        for i, device in enumerate(row_peers)
    ]
    for copy in gate_rows:
        copy.start()
    shared = gain_slots[0, c]
    for d in range(1, 8):
        gain_copies[d - 1].wait_recv()
        shared = shared + gain_slots[1, d]
    gain_sums[0] = shared
    row_copies = [
        push(gain_sums.at[0], gain_sums.at[1 + i], (ghs, ghr), i, device)
        for i, device in enumerate(row_peers)
    ]
    for copy in row_copies:
        copy.start()
    line.advance(line.last())
    for copy in row_copies + gate_rows:
        copy.wait()
    gains_all[...] = gain_sums[0] + gain_sums[1] + gain_sums[2] + gain_sums[3]

    @pl.when(c > 0)
    def _():
        finish_sends(heads)

    finish_sends(gain_copies + gate_copies + n_copies + n_cross + o_copies + o_cross)
    carry_sent(me, True, carry_copies)
    line.close()


def back(gpart2, cot, resid, inputs, mlp_gain, mix_gain, vecs, taps_all, starts_all, start,
         opart, dmg, dmu, dmd, wq, nall, gate_pre, lext, conv, rec, opening, state, mixed,
         rgate_all, igate_all):
    length, width = inputs.shape
    wide = taps_all.shape[2]
    side = wide // 2
    sd = jax.ShapeDtypeStruct
    vmem = pltpu.VMEM
    dma = pltpu.SemaphoreType.DMA
    like = lambda v: vmem(v.shape, v.dtype)
    shard = lambda v: vmem(v.shape[1:], LOW)
    tall = vmem((4, length, wide), F32)
    early, late = (2, 2 * side, width), (2, side + 32, width)
    odd = lambda: [shard(dmg), shard(dmu), shard(dmd), vmem(early[1:], LOW), vmem(late[1:], LOW)]
    outs = [
        sd(inputs.shape, LOW), sd(inputs.shape, LOW),
        sd(dmg.shape[1:], LOW), sd(dmu.shape[1:], LOW), sd(dmd.shape[1:], LOW),
        sd(early[1:], LOW), sd(late[1:], LOW), sd((4, side // 2, side), LOW), sd((8, 128), F32),
    ]
    return pl.pallas_call(
        back_kernel,
        name="back",
        out_shape=outs,
        in_specs=[IN_VMEM] * 10 + [ANYWHERE] * 15,
        out_specs=[IN_VMEM] * len(outs),
        scratch_shapes=[
            like(wq), like(nall), tall, like(lext), tall, tall, tall, tall, like(mixed),
            tall, tall, vmem((4, length + TILE, wide), F32), vmem((4, TILE, wide), F32),
            vmem((4, length, wide), LOW), like(gpart2), vmem((length, width), F32), like(opart),
            vmem((wide, width), F32), vmem((wide, width), F32),
            vmem((wide, wide), F32), vmem((wide, wide), F32), vmem((16, wide), F32),
            vmem((length + TILE, wide), F32),
            vmem(early, LOW), vmem(late, LOW),
        ]
        + odd()[:3] + odd() + odd()
        + [
            vmem((4, 2, wide), F32), vmem((8, 4, 2, wide), F32), vmem((4, wide), F32),
            vmem((length + 16, 128), F32), vmem((2, GB, GB), F32), vmem((2, GB, GB), F32),
            vmem((wide, wide), LOW), vmem((wide, wide), LOW),
            vmem((8, side // 2, side), LOW), vmem((8, side // 2, side), LOW),
            vmem((2, 8, 8, 128), F32), vmem((4, 8, 128), F32),
        ]
        + rows_sum_scratch(length, width) + rows_sum_scratch(length, width)
        + sem_pair(2 * RS_CHUNKS) + sem_pair(RS_CHUNKS)
        + sem_pair(RS_CHUNKS) + sem_pair(2 * RS_CHUNKS)
        + [dma((15,))] + sem_pair(8) + sem_pair(4) + sem_pair(8) + sem_pair(3)
        + sem_pair(8) + sem_pair(3)
        + reduce_sems(4, 8) + reduce_sems(1, 7),
        compiler_params=comm_params(2),
    )(gpart2, cot, resid, inputs, mlp_gain, mix_gain, vecs, taps_all, starts_all, start,
      opart, dmg, dmu, dmd, wq, nall, gate_pre, lext, conv, rec, opening, state, mixed,
      rgate_all, igate_all)


def split_body(
    inputs, mix_gain, gate_proj, gate_bias, lift_proj, lift_bias, conv_taps, conv_bias,
    recur_gate, recur_bias, input_gate, input_bias, decay_param, out_proj, out_bias, mlp_gain,
    mlp_gate, mlp_up, mlp_down, doc_starts, cotangent,
):
    wide = 2 * GB
    wm = jnp.stack([gate_proj.T, lift_proj.T, out_proj])
    vecs = jnp.stack(
        [gate_bias, lift_bias, conv_bias, recur_bias, input_bias, jax.nn.softplus(-decay_param),
         jax.nn.sigmoid(-decay_param), jnp.zeros_like(decay_param)]
    ).reshape(8, 4, wide).transpose(1, 0, 2)
    taps = conv_taps.reshape(4, 4, wide).transpose(1, 0, 2)
    starts = jnp.pad(
        doc_starts, ((0, 7), (0, 128 - doc_starts.shape[1])),
        constant_values=jnp.iinfo(jnp.int32).max,
    )
    (wq, wg, wu, wd, nall, call, starts_all, gate_pre, lext, conv, rec, opening, state, start,
     mixed, resid, n2all) = front(
        inputs, cotangent, mix_gain[None], vecs, taps, recur_gate, input_gate, starts,
        out_bias[None], mlp_gain[None], wm, mlp_gate, mlp_up, mlp_down,
    )
    opart, gpart2, dmg, dmu, dmd = mlp(n2all, call, wg, wu, wd)
    output, grad_inputs, own_g, own_u, own_d, own_e, own_l, gates, gains = back(
        gpart2, cotangent, resid, inputs, mlp_gain[None], mix_gain[None], vecs, taps, starts_all,
        start, opart, dmg, dmu, dmd, wq, nall, gate_pre, lext, conv, rec, opening, state, mixed,
        recur_gate, input_gate,
    )
    wide_out = lambda v: v.astype(F32)
    gates = wide_out(gates).reshape(4, 2, 2, GB // 8, GB)
    gate_out = lambda i: gates[:, i].reshape(8, GB // 8, GB)
    own = wide_out(own_l[GB : GB + 16, :GB])
    return (
        output, grad_inputs, gains[0],
        wide_out(own_e[GB:].T), own[0], wide_out(own_l[:GB].T), own[1], own[2:6], own[6],
        gate_out(0), own[7], gate_out(1), own[8], own[9],
        wide_out(own_e[:GB]), gains[2], gains[1],
        wide_out(own_g), wide_out(own_u), wide_out(own_d),
    )


def solution(mesh):
    in_specs = (
        P(("rows", "chan"), None),
        P(),
        P(None, "chan"),
        P(),
        P(None, "chan"),
        P(),
        P(),
        P(),
        P(),
        P(),
        P(),
        P(),
        P(),
        P("chan", None),
        P(),
        P(),
        P(None, "chan"),
        P(None, "chan"),
        P("chan", None),
        P("rows", None),
        P(("rows", "chan"), None),
    )
    out_specs = (
        P(("rows", "chan"), None),
        P(("rows", "chan"), None),
        P("chan"),
        P(None, "chan"),
        P("chan"),
        P(None, "chan"),
        P("chan"),
        P(None, "chan"),
        P("chan"),
        P(None, "chan", None),
        P("chan"),
        P(None, "chan", None),
        P("chan"),
        P("chan"),
        P("chan", None),
        P("chan"),
        P("chan"),
        P(None, "chan"),
        P(None, "chan"),
        P("chan", None),
    )
    split = mesh.shape["rows"] == 4 and mesh.shape["chan"] == HEADS
    return jax.shard_map(split_body if split else body, mesh=mesh, in_specs=in_specs, out_specs=out_specs, check_vma=False)
```

```python
from functools import partial
import math

import jax
import jax.numpy as jnp
from jax import lax
from jax.experimental import pallas as pl
from jax.experimental.pallas import tpu as pltpu
from jax.sharding import PartitionSpec as P

D = 1024
LRU = 1536
FF = 3072
HEADS = 8
GB = 192


EPSILON = 1e-06
precise = lax.Precision.HIGHEST


def from_behind(block, axis, distance):
    devices = range(lax.axis_size(axis))
    route = [(i - distance, i) for i in devices if i - distance in devices]
    return lax.ppermute(block, axis, route)


def prefix(value, axis, join, neutral, backward):
    count, mine = (lax.axis_size(axis), lax.axis_index(axis))
    pieces = jax.tree.map(lambda part: lax.all_gather(part, axis), value)
    if backward:
        pieces = jax.tree.map(lambda part: part[::-1], pieces)
        mine = count - 1 - mine
    subtotal = jax.tree.map(
        lambda part, zero: jnp.full_like(part, 0) + jnp.asarray(zero, part.dtype), value, neutral
    )

    def hop(position, subtotal):
        longer = join(subtotal, jax.tree.map(lambda part: part[position], pieces))
        return jax.tree.map(lambda new, old: jnp.where(position < mine, new, old), longer, subtotal)

    return lax.fori_loop(0, count - 1, hop, subtotal)


def rms_scale(values, gain_vec):
    return (
        values * lax.rsqrt(jnp.mean(values * values, axis=-1, keepdims=True) + EPSILON) * gain_vec
    )


def gated_unit(gate_pre, up_vals):
    return jax.nn.gelu(gate_pre) * up_vals


def affine(earlier, later_map):
    return (earlier[0] * later_map[0], later_map[0] * earlier[1] + later_map[1])


def segment_ids(starts, start_pos, pos_count, seq_len):
    where_at = start_pos + jnp.arange(pos_count, dtype=jnp.int32)
    seq_of = jnp.floor_divide(where_at, seq_len)
    within = where_at - seq_of * seq_len
    owner = seq_of[:, None] == jnp.arange(starts.shape[0], dtype=jnp.int32)[None, :]
    passed = starts[None, :, :] <= within[:, None, None]
    doc_tally = jnp.sum(jnp.logical_and(owner[:, :, None], passed).astype(jnp.int32), axis=(1, 2))
    return seq_of * (starts.shape[1] + 1) + doc_tally


def project(normed, weights, first_bias, second_bias):
    product = jnp.einsum("td,dc->ct", normed, weights, preferred_element_type=jnp.float32)
    channels = first_bias.shape[0]
    return (product[:channels] + first_bias[:, None], product[channels:] + second_bias[:, None])


def conv_forward(lifted, tail_rows, segments, tap_vals, bias_vec):
    length = lifted.shape[1]
    extended = jnp.concatenate([tail_rows, lifted], axis=1)
    own_seg = segments[3 : 3 + length]
    result = bias_vec[:, None] + tap_vals[0][:, None] * lifted
    for offset in range(1, 4):
        same_doc = (segments[3 - offset : 3 - offset + length] == own_seg).astype(jnp.float32)
        result = (
            result
            + tap_vals[offset][:, None]
            * extended[:, 3 - offset : 3 - offset + length]
            * same_doc[None, :]
        )
    return result


def conv_backward(grad_conv, head_rows, segments, lifted, tail_rows, tap_vals):
    length = grad_conv.shape[1]
    ahead_grad = jnp.concatenate([grad_conv, head_rows], axis=1)
    behind = jnp.concatenate([tail_rows, lifted], axis=1)
    own_seg = segments[3 : 3 + length]
    grad_lifted = tap_vals[0][:, None] * grad_conv
    tap_grads = [jnp.sum(grad_conv * lifted, axis=1)]
    for offset in range(1, 4):
        later_same = (segments[3 + offset : 3 + offset + length] == own_seg).astype(jnp.float32)
        grad_lifted = (
            grad_lifted
            + tap_vals[offset][:, None]
            * ahead_grad[:, offset : offset + length]
            * later_same[None, :]
        )
        earlier = (segments[3 - offset : 3 - offset + length] == own_seg).astype(jnp.float32)
        tap_grads.append(
            jnp.sum(
                grad_conv * behind[:, 3 - offset : 3 - offset + length] * earlier[None, :], axis=1
            )
        )
    return (grad_lifted, jnp.stack(tap_grads, axis=1), jnp.sum(grad_conv, axis=1))


def coefficients(is_reset, conv_out, recur_gate, recur_bias, input_gate, input_bias, decay_param):
    channels, length = conv_out.shape
    gate_block = recur_gate.shape[1]
    grouped = conv_out.reshape(channels // gate_block, gate_block, length)
    recurrence = jax.nn.sigmoid(
        jnp.einsum("hit,hio->hot", grouped, recur_gate, precision=precise).reshape(channels, length)
        + recur_bias[:, None]
    )
    opening = jax.nn.sigmoid(
        jnp.einsum("hit,hio->hot", grouped, input_gate, precision=precise).reshape(channels, length)
        + input_bias[:, None]
    )
    log_decay = -8.0 * recurrence * jax.nn.softplus(-decay_param)[:, None]
    decay_rate = jnp.where(is_reset[None, :], 0.0, jnp.exp(log_decay))
    scaling = jnp.where(is_reset[None, :], 1.0, jnp.sqrt(-jnp.expm1(2.0 * log_decay)))
    return (decay_rate, scaling * opening * conv_out)


def reverse_local(decay_rate, grad_state):
    ones_col = jnp.ones_like(decay_rate[:, :1])
    factor = jnp.flip(jnp.concatenate([decay_rate[:, 1:], ones_col], axis=1), axis=1)
    product, carried = lax.associative_scan(affine, (factor, jnp.flip(grad_state, axis=1)), axis=1)
    return (jnp.flip(product, axis=1), jnp.flip(carried, axis=1))


def finish_state(lru_state, start_state, carried, pull_coef):
    previous = jnp.concatenate([start_state[:, None], lru_state[:, :-1]], axis=1)
    return pull_coef((carried * previous, carried))


def flatten_rows(pieces, row_count):
    return jnp.concatenate([source.reshape(row_count, -1) for source in pieces], axis=1)


def body(
    inputs,
    mix_gain,
    gate_proj,
    gate_bias,
    lift_proj,
    lift_bias,
    conv_taps,
    conv_bias,
    recur_gate,
    recur_bias,
    input_gate,
    input_bias,
    decay_param,
    out_proj,
    out_bias,
    mlp_gain,
    mlp_gate,
    mlp_up,
    mlp_down,
    doc_starts,
    cotangent,
):
    chan_count = lax.axis_size("chan")
    chan_place = lax.axis_index("chan")
    local_rows = inputs.shape[0]
    seq_length = local_rows * chan_count
    rows_f32 = inputs.astype(jnp.float32)
    cot_f32 = cotangent.astype(jnp.float32)
    normed, pull_norm = jax.vjp(rms_scale, rows_f32, mix_gain)
    normed_low = normed.astype(jnp.bfloat16)
    gate_full, lift_full, out_full, mlp_gate_full, mlp_up_full, mlp_down_full = (
        lax.all_gather(gate_proj, "chan", axis=1, tiled=True),
        lax.all_gather(lift_proj, "chan", axis=1, tiled=True),
        lax.all_gather(out_proj, "chan", axis=0, tiled=True),
        lax.all_gather(mlp_gate, "chan", axis=1, tiled=True),
        lax.all_gather(mlp_up, "chan", axis=1, tiled=True),
        lax.all_gather(mlp_down, "chan", axis=0, tiled=True),
    )
    channels = LRU
    hidden_cut = FF
    segments = segment_ids(doc_starts, chan_place * local_rows - 3, local_rows + 6, seq_length)
    mix_proj = jnp.concatenate([gate_full, lift_full], axis=1)
    gate_pre, lifted = project(normed_low, mix_proj, gate_bias, lift_bias)
    tail_rows = from_behind(lifted[:, -3:], "chan", 1)
    conv_out = conv_forward(lifted, tail_rows, segments, conv_taps, conv_bias)
    is_reset = segments[3 : 3 + local_rows] != segments[2 : 2 + local_rows]
    (decay_rate, lru_input), pull_coef = jax.vjp(
        partial(coefficients, is_reset),
        conv_out,
        recur_gate,
        recur_bias,
        input_gate,
        input_bias,
        decay_param,
    )
    running, local_state = lax.associative_scan(affine, (decay_rate, lru_input), axis=1)
    ones_vec = jnp.ones((channels,), jnp.float32)
    zeros_vec = jnp.zeros((channels,), jnp.float32)
    _, start_state = prefix(
        (running[:, -1], local_state[:, -1]), "chan", affine, (ones_vec, zeros_vec), False
    )
    lru_state = local_state + running * start_state[:, None]
    gate_val, pull_gelu = jax.vjp(jax.nn.gelu, gate_pre)
    mixed_out = (lru_state * gate_val).astype(jnp.bfloat16)
    resid = (
        rows_f32
        + jnp.einsum("ct,cd->td", mixed_out, out_full, preferred_element_type=jnp.float32)
        + out_bias
    )
    normed2, pull_norm2 = jax.vjp(rms_scale, resid, mlp_gain)
    normed2_low = normed2.astype(jnp.bfloat16)
    mlp_proj = jnp.concatenate([mlp_gate_full, mlp_up_full], axis=1)
    mlp_pre = jnp.einsum("td,df->ft", normed2_low, mlp_proj, preferred_element_type=jnp.float32)
    hidden, pull_mlp = jax.vjp(gated_unit, mlp_pre[:hidden_cut], mlp_pre[hidden_cut:])
    hidden_low = hidden.astype(jnp.bfloat16)
    output = (
        resid
        + jnp.einsum("ft,fd->td", hidden_low, mlp_down_full, preferred_element_type=jnp.float32)
    ).astype(jnp.bfloat16)
    grad_down = jnp.einsum("ft,td->fd", hidden_low, cotangent, preferred_element_type=jnp.float32)
    grad_gate_m, grad_up_m = pull_mlp(
        jnp.einsum("td,fd->ft", cotangent, mlp_down_full, preferred_element_type=jnp.float32)
    )
    grad_pre = jnp.concatenate([grad_gate_m, grad_up_m], axis=0).astype(jnp.bfloat16)
    grad_mlp_in = jnp.einsum("ft,td->fd", grad_pre, normed2_low, preferred_element_type=jnp.float32)
    grad_resid_part, grad_gain2 = pull_norm2(
        jnp.einsum("ft,df->td", grad_pre, mlp_proj, preferred_element_type=jnp.float32)
    )
    grad_resid = cot_f32 + grad_resid_part
    grad_branch = grad_resid.astype(jnp.bfloat16)
    grad_out_proj = jnp.einsum(
        "ct,td->cd", mixed_out, grad_branch, preferred_element_type=jnp.float32
    )
    grad_mixed = jnp.einsum("td,cd->ct", grad_branch, out_full, preferred_element_type=jnp.float32)
    product, carried = reverse_local(decay_rate, grad_mixed * gate_val)
    _, incoming = prefix(
        (decay_rate[:, 0] * product[:, 0], decay_rate[:, 0] * carried[:, 0]),
        "chan",
        affine,
        (ones_vec, zeros_vec),
        True,
    )
    carried = carried + product * incoming[:, None]
    coef_grads = finish_state(lru_state, start_state, carried, pull_coef)
    head_rows = from_behind(coef_grads[0][:, :3], "chan", -1)
    grad_lifted, grad_taps, grad_conv_bias = conv_backward(
        coef_grads[0], head_rows, segments, lifted, tail_rows, conv_taps
    )
    (grad_gate_pre,) = pull_gelu(grad_mixed * lru_state)
    grad_front = jnp.concatenate([grad_gate_pre, grad_lifted], axis=0).astype(jnp.bfloat16)
    grad_mix_proj = jnp.einsum(
        "ct,td->cd", grad_front, normed_low, preferred_element_type=jnp.float32
    )
    grad_normed = jnp.einsum("ct,dc->td", grad_front, mix_proj, preferred_element_type=jnp.float32)
    grad_x_part, grad_gain1 = pull_norm(grad_normed)
    grad_inputs = (grad_resid + grad_x_part).astype(jnp.bfloat16)
    grad_out_bias = jnp.sum(grad_resid, axis=0)
    pieces = [
        grad_mix_proj[:channels],
        grad_mix_proj[channels:],
        jnp.sum(grad_gate_pre, axis=1),
        jnp.sum(grad_lifted, axis=1),
        grad_taps,
        grad_conv_bias,
        jnp.transpose(coef_grads[1], (1, 0, 2)),
        coef_grads[2],
        jnp.transpose(coef_grads[3], (1, 0, 2)),
        coef_grads[4],
        coef_grads[5],
        grad_out_proj,
        grad_mlp_in[:hidden_cut],
        grad_mlp_in[hidden_cut:],
        grad_down,
        grad_gain1,
        grad_out_bias,
        grad_gain2,
    ]
    spread = flatten_rows(pieces, chan_count)
    shared = lax.psum_scatter(spread, "chan", scatter_dimension=0, tiled=True)
    summed = lax.psum(shared.reshape(-1), "rows")
    channels_dev = LRU // chan_count
    hidden_dev = FF // chan_count
    width_dev = D // chan_count
    block_dev = GB // chan_count
    shapes = [
        (channels_dev, D),
        (channels_dev, D),
        (channels_dev,),
        (channels_dev,),
        (channels_dev, 4),
        (channels_dev,),
        (block_dev, HEADS, GB),
        (channels_dev,),
        (block_dev, HEADS, GB),
        (channels_dev,),
        (channels_dev,),
        (channels_dev, D),
        (hidden_dev, D),
        (hidden_dev, D),
        (hidden_dev, D),
        (width_dev,),
        (width_dev,),
        (width_dev,),
    ]
    unpacked = []
    offset = 0
    for piece_shape in shapes:
        piece_size = math.prod(piece_shape)
        unpacked.append(summed[offset : offset + piece_size].reshape(piece_shape))
        offset = offset + piece_size
    return (
        output,
        grad_inputs,
        unpacked[15],
        unpacked[0].T,
        unpacked[2],
        unpacked[1].T,
        unpacked[3],
        unpacked[4].T,
        unpacked[5],
        jnp.transpose(unpacked[6], (1, 0, 2)),
        unpacked[7],
        jnp.transpose(unpacked[8], (1, 0, 2)),
        unpacked[9],
        unpacked[10],
        unpacked[11],
        unpacked[16],
        unpacked[17],
        unpacked[12].T,
        unpacked[13].T,
        unpacked[14],
    )


MESH = pl.DeviceIdType.MESH
LOW = jnp.bfloat16
F32 = jnp.float32
VMEM_BYTES = 63 * 2**20
TILE = 8
GELU_A = math.sqrt(2.0 / math.pi)
GELU_B = 0.044715


def nt(left, right):
    return lax.dot_general(left, right, (((1,), (1,)), ((), ())), preferred_element_type=F32)


def nn(left, right):
    return lax.dot_general(left, right, (((1,), (0,)), ((), ())), preferred_element_type=F32)


def tn(left, right):
    return lax.dot_general(left, right, (((0,), (0,)), ((), ())), preferred_element_type=F32)


def gelu_pair(values):
    squared = values * values
    bend = jnp.tanh(GELU_A * values * (1.0 + GELU_B * squared))
    half = 0.5 * (1.0 + bend)
    slope = half + 0.5 * values * (1.0 - bend * bend) * GELU_A * (1.0 + 3.0 * GELU_B * squared)
    return values * half, slope


class Spot:
    def __init__(self):
        self.r = lax.axis_index("rows")
        self.c = lax.axis_index("chan")
        self.z = lax.div(self.c, 2)
        self.y = lax.rem(self.c, 2)
        self.r_core = self.r + 1 - 2 * lax.rem(self.r, 2)
        self.r_x = lax.rem(self.r + 2, 4)
        self.core = (self.r_core, self.c)
        self.x = (self.r_x, self.c)
        self.c_y = self.c + 1 - 2 * self.y
        self.ymate = (self.r, self.c_y)
        self.up = (self.r, lax.rem(self.c + 2, 8))
        self.dn = (self.r, lax.rem(self.c + 6, 8))


def greet(always, maybe=()):
    barrier = pltpu.get_barrier_semaphore()
    count = len(always)
    for device in always:
        pl.semaphore_signal(barrier, inc=1, device_id=device, device_id_type=MESH)
    for device, there in maybe:

        @pl.when(there)
        def _(device=device):
            pl.semaphore_signal(barrier, inc=1, device_id=device, device_id_type=MESH)

        count = count + jnp.where(there, 1, 0)
    pl.semaphore_wait(barrier, count)


def push(source, target, sems, index, device):
    return pltpu.make_async_remote_copy(
        src_ref=source,
        dst_ref=target,
        send_sem=sems[0].at[index],
        recv_sem=sems[1].at[index],
        device_id=device,
        device_id_type=MESH,
    )


def landed(me, target, sems, index):
    push(target, target, sems, index, me.ymate).wait_recv()


def sem_pair(count):
    return [pltpu.SemaphoreType.DMA((count,)), pltpu.SemaphoreType.DMA((count,))]


def comm_params(collective_id):
    return pltpu.CompilerParams(
        collective_id=collective_id, has_side_effects=True, vmem_limit_bytes=VMEM_BYTES
    )


ANYWHERE = pl.BlockSpec(memory_space=pl.ANY)
IN_VMEM = pl.BlockSpec(memory_space=pltpu.VMEM)


def decay_terms(rec, softplus_row, reset):
    log_decay = -8.0 * rec * softplus_row
    decay = jnp.exp(log_decay)
    twice = 2.0 * log_decay
    series = twice * (
        1.0
        + twice * (1 / 2 + twice * (1 / 6 + twice * (1 / 24 + twice * (1 / 120 + twice * (1 / 720)))))
    )
    gap = jnp.where(twice > -0.25, -series, 1.0 - jnp.exp(twice))
    return decay, jnp.where(reset, 1.0, jnp.sqrt(gap))


def fill_tallies(tallies, starts_row, first, length, seq_length):
    position = first - 8 + lax.broadcasted_iota(jnp.int32, (length + 16, 1), 0)
    begun = jnp.sum((starts_row <= position).astype(F32), axis=1, keepdims=True)
    inside = jnp.logical_and(position >= 0, position < seq_length)
    tallies[...] = jnp.broadcast_to(jnp.where(inside, begun, -1.0), tallies.shape)


def same_document(tallies, length, shift, wide):
    own = tallies[pl.ds(8, length)]
    other = tallies[pl.ds(8 + shift, length)]
    same = (own == other).astype(F32)
    return jnp.concatenate([same] * (wide // same.shape[1]), axis=1)


def pair_diagonal(target, blocks):
    side = blocks.shape[1]
    target[...] = jnp.zeros_like(target)
    target[0:side, 0:side] = blocks[0].astype(target.dtype)
    target[side : 2 * side, side : 2 * side] = blocks[1].astype(target.dtype)


def tile_scan(a, b, backward):
    row = lax.broadcasted_iota(jnp.int32, a.shape, 1)
    for step in (1, 2, 4):
        shift = TILE - step if backward else step
        there = row < TILE - step if backward else row >= step
        b = b + a * jnp.where(there, pltpu.roll(b, shift, 1), 0.0)
        a = a * jnp.where(there, pltpu.roll(a, shift, 1), 1.0)
    return a, b


def carry_start(me, backward, totals, slots, sems):
    sign = -1 if backward else 1
    steps = me.c if backward else 7 - me.c
    copies = [
        push(totals, slots.at[d], sems, d, (me.r, lax.rem(me.c + 8 + sign * d, 8)))
        for d in range(1, 8)
    ]
    for d in range(1, 8):

        @pl.when(d <= steps)
        def _(d=d):
            copies[d - 1].start()

    return copies


def carry_join(me, backward, slots, start, sems):
    behind = 7 - me.c if backward else me.c
    start[...] = jnp.zeros_like(start)
    for d in range(7, 0, -1):

        @pl.when(d <= behind)
        def _(d=d):
            landed(me, slots.at[d], sems, d)
            start[...] = slots[d, :, 0] * start[...] + slots[d, :, 1]


def carry_sent(me, backward, copies):
    steps = me.c if backward else 7 - me.c
    for d in range(1, 8):

        @pl.when(d <= steps)
        def _(d=d):
            copies[d - 1].wait_send()


def peers_of(me):
    return [(me.r, lax.rem(me.c + d, 8)) for d in range(1, 8)]


class Spread:
    def __init__(self, me, slabs, pieces, sems):
        self.me, self.slabs, self.pieces, self.sems = me, slabs, pieces, sems
        self.go_up = jnp.logical_and(me.z >= me.r, me.z < 3)
        self.go_dn = jnp.logical_and(me.z <= me.r, me.z > 0)
        self.source = me.z == me.r
        self.hop = jnp.where(me.z < me.r, me.r - me.z, me.z - me.r)

    def copies(self, k):
        me, found = self.me, []
        for i, slab in enumerate(self.slabs):
            piece = slab(k, me.y)
            ys, yr, us, ds, zr = self.sems[5 * i : 5 * i + 5]
            found.append(
                (
                    push(piece, piece, (ys, yr), k, me.ymate),
                    push(piece, piece, (us, zr), k, me.up),
                    push(piece, piece, (ds, zr), k, me.dn),
                )
            )
        return found

    def send(self, k):
        found = self.copies(k)
        for copies in found:
            copies[0].start()

        @pl.when(self.go_up)
        def _():
            for copies in found:
                copies[1].start()

        @pl.when(self.go_dn)
        def _():
            for copies in found:
                copies[2].start()

    def follow(self, k):
        for i, slab in enumerate(self.slabs):
            us, zr = self.sems[5 * i + 2], self.sems[5 * i + 4]
            landed(self.me, slab(k, self.me.y), (us, zr), k)
        self.send(k)

    def step(self, q):
        n = self.pieces

        def at(k, also, action):
            there = jnp.logical_and(k >= 0, k < n)

            @pl.when(jnp.logical_and(there, also))
            def _():
                action(lax.rem(k + 8 * n, n))

        at(q + SPREAD_AHEAD, self.source, self.send)
        at(q - SPREAD_LAG * (self.hop - 1), jnp.logical_not(self.source), self.follow)

    def reach(self):
        return -SPREAD_AHEAD, self.pieces + 2 * SPREAD_LAG

    def arrived(self):
        @pl.loop(0, self.pieces)
        def _(k):
            for i, slab in enumerate(self.slabs):
                ys, yr = self.sems[5 * i], self.sems[5 * i + 1]
                landed(self.me, slab(k, 1 - self.me.y), (ys, yr), k)

    def close(self):
        @pl.loop(0, self.pieces)
        def _(k):
            found = self.copies(k)
            for copies in found:
                copies[0].wait_send()

            @pl.when(self.go_up)
            def _():
                for copies in found:
                    copies[1].wait_send()

            @pl.when(self.go_dn)
            def _():
                for copies in found:
                    copies[2].wait_send()


SPREAD_AHEAD = 4
SPREAD_LAG = 3


def spread_sems(arrays, pieces):
    return [pltpu.SemaphoreType.DMA((pieces,))] * (5 * arrays)


AHEAD = 4
HOP_LAG = 3
END_LAG = 10
RELAY_LAG = 13


class Reduce:
    def __init__(self, me, parts, mine, from_y, from_z, own, pieces, sems):
        self.me, self.parts, self.mine = me, parts, mine
        self.from_y, self.from_z, self.own = from_y, from_z, own
        self.pieces, self.sems = pieces, sems
        self.hop = jnp.where(me.z < me.r, me.z, 3 - me.z)
        self.owner = me.z == me.r
        self.relays = me.z == me.r_x

    def rows(self, i, k):
        size = self.mine[i].shape[0] // self.pieces
        return pl.ds(pl.multiple_of(k * size, 16), size)

    def each(self, k):
        for i in range(len(self.mine)):
            yield i, self.rows(i, k), self.sems[11 * i : 11 * i + 11]

    def y_copies(self, k):
        me = self.me
        return [
            push(self.parts[i].at[1 - me.y, rows], self.from_y[i].at[rows], sems[0:2], k, me.ymate)
            for i, rows, sems in self.each(k)
        ]

    def y_send(self, k):
        for copy in self.y_copies(k):
            copy.start()

    def add(self, i, rows, other):
        total = self.mine[i][rows].astype(F32) + other[i][rows].astype(F32)
        self.mine[i][rows] = total.astype(LOW)

    def join(self, k):
        for i, rows, sems in self.each(k):
            landed(self.me, self.from_y[i].at[rows], sems[0:2], k)
            self.add(i, rows, self.from_y)

    def z_copies(self, k, way):
        found = []
        for i, rows, sems in self.each(k):
            target = self.own if way == 2 else self.from_z
            pair = ((sems[2], sems[4]), (sems[3], sems[4]), (sems[3], sems[5]))[way]
            found.append(
                push(self.mine[i].at[rows], target[i].at[rows], pair, k,
                     self.me.up if way == 0 else self.me.dn)
            )
        return found

    def z_way(self, action):
        me = self.me
        for way, there in enumerate(
            (me.z < me.r, me.z > me.r + 1, me.z == me.r + 1)
        ):

            @pl.when(there)
            def _(way=way):
                action(way)

    def chain(self, k):
        @pl.when(self.hop > 0)
        def _():
            for i, rows, sems in self.each(k):
                landed(self.me, self.from_z[i].at[rows], (sems[2], sems[4]), k)
                self.add(i, rows, self.from_z)

        def start(way):
            for copy in self.z_copies(k, way):
                copy.start()

        self.z_way(start)

    def out_copies(self, k, device, pair):
        return [
            push(self.own[i].at[rows], self.own[i].at[rows], sems[pair : pair + 2], k, device)
            for i, rows, sems in self.each(k)
        ]

    def finish(self, k):
        @pl.when(self.me.z > 0)
        def _():
            for i, rows, sems in self.each(k):
                landed(self.me, self.from_z[i].at[rows], (sems[2], sems[4]), k)
                self.add(i, rows, self.from_z)

        @pl.when(self.me.z < 3)
        def _():
            for i, rows, sems in self.each(k):
                landed(self.me, self.own[i].at[rows], (sems[3], sems[5]), k)
                self.add(i, rows, self.own)

        for i, rows, sems in self.each(k):
            self.own[i][rows] = self.mine[i][rows]
        for copy in self.out_copies(k, self.me.x, 6) + self.out_copies(k, self.me.core, 8):
            copy.start()

    def relay(self, k):
        for copy in self.out_copies(k, self.me.x, 6):
            copy.wait_recv()
        for copy in self.out_copies(k, self.me.core, 8):
            copy.start()

    def step(self, q):
        n = self.pieces

        def at(k, also, action):
            there = jnp.logical_and(k >= 0, k < n)

            @pl.when(there if also is None else jnp.logical_and(there, also))
            def _():
                action(lax.rem(k + 8 * n, n))

        at(q + AHEAD, None, self.y_send)
        at(q, None, self.join)
        at(q - HOP_LAG * self.hop, jnp.logical_not(self.owner), self.chain)
        at(q - END_LAG, self.owner, self.finish)
        at(q - RELAY_LAG, self.relays, self.relay)

    def reach(self):
        return -AHEAD, self.pieces + RELAY_LAG

    def close(self):
        others = jnp.logical_not(jnp.logical_or(self.owner, self.relays))

        @pl.loop(0, self.pieces)
        def _(k):
            for copy in self.y_copies(k):
                copy.wait_send()

            def sent(way):
                for copy in self.z_copies(k, way):
                    copy.wait_send()

            self.z_way(sent)

            @pl.when(self.owner)
            def _():
                for copy in self.out_copies(k, self.me.x, 6) + self.out_copies(k, self.me.core, 8):
                    copy.wait_send()

            @pl.when(self.relays)
            def _():
                for copy in self.out_copies(k, self.me.core, 8):
                    copy.wait_send()

            @pl.when(others)
            def _():
                for copy in self.out_copies(k, self.me.core, 8):
                    copy.wait_recv()


class Line:
    def __init__(self, reduces, offsets):
        self.reduces, self.offsets = reduces, offsets
        self.done = reduces[0].reach()[0]

    def position(self, p, low, high):
        for one, offset in zip(self.reduces, self.offsets):
            first, last = one.reach()
            if offset + first < high and low < offset + last:
                one.step(p - offset)

    def advance(self, high):
        low, self.done = self.done, high
        if high > low + 1:

            @pl.loop(low, high)
            def _(p):
                self.position(p, low, high)

        elif high > low:
            self.position(low, low, high)

    def ready(self, i):
        assert self.done <= self.offsets[i] + self.reduces[i].reach()[0]

    def during(self, begin, end, action):
        low, self.done = self.done, self.done + end - begin

        @pl.loop(begin, end)
        def _(s):
            action(s)
            self.position(low - begin + s, low, low + end - begin)

    def last(self):
        return self.offsets[-1] + self.reduces[-1].reach()[1]

    def close(self):
        for one in self.reduces:
            one.close()


def reduce_sems(arrays, pieces):
    return [pltpu.SemaphoreType.DMA((pieces,))] * (11 * arrays)


RS_CHUNKS = 4


def rows_sum_start(me, part, mate, sems, only=None):
    length = part.shape[1]
    step = length // RS_CHUNKS
    far = lax.rem(me.r_core + 2, 4)
    copies = []
    for block, owner in enumerate((far, me.r_core)):
        if only not in (None, block):
            continue
        for k in range(RS_CHUNKS):
            rows = pl.ds(k * step, step)
            copies.append(
                push(part.at[owner, rows], mate.at[block, rows], sems, block * RS_CHUNKS + k, me.core)
            )
    for copy in copies:
        copy.start()
    return copies


def rows_sum_cross(me, part, mate, out_x, in_x, copies, sems):
    length = part.shape[1]
    step = length // RS_CHUNKS
    crossing = []
    for k in range(RS_CHUNKS):
        rows = pl.ds(k * step, step)
        copies[k].wait_recv()
        out_x[rows] = (part[me.r_x, rows].astype(F32) + mate[0, rows].astype(F32)).astype(LOW)
        copy = push(out_x.at[rows], in_x.at[rows], sems, k, me.x)
        copy.start()
        crossing.append(copy)
    return crossing


def rows_sum_chunk(me, part, mate, in_x, copies, crossing, k):
    length = part.shape[1]
    step = length // RS_CHUNKS
    rows = pl.ds(k * step, step)
    copies[RS_CHUNKS + k].wait_recv()
    crossing[k].wait_recv()
    return part[me.r, rows].astype(F32) + mate[1, rows].astype(F32) + in_x[rows].astype(F32)


def finish_sends(copies):
    for copy in copies:
        copy.wait_send()


def rows_sum_scratch(length, width):
    return [
        pltpu.VMEM((2, length, width), LOW),
        pltpu.VMEM((length, width), LOW),
        pltpu.VMEM((length, width), LOW),
    ] + sem_pair(2 * RS_CHUNKS) + sem_pair(RS_CHUNKS)


def spread_chunk(me, all_ref, k, sems_x, sems_c):
    length = all_ref.shape[1]
    step = length // RS_CHUNKS
    rows = pl.ds(k * step, step)
    mine = all_ref.at[me.r, rows]
    copies = [
        push(mine, mine, sems_x, k, me.x),
        push(mine, mine, sems_c, k, me.core),
    ]
    for copy in copies:
        copy.start()
    return copies


def spread_rest(me, all_ref, first, sems_c, beside=None):
    length = all_ref.shape[1]
    step = length // RS_CHUNKS
    passed = []
    for k in range(RS_CHUNKS):
        first[k][0].wait_recv()
        theirs = all_ref.at[me.r_x, pl.ds(k * step, step)]
        copy = push(theirs, theirs, sems_c, RS_CHUNKS + k, me.core)
        copy.start()
        passed.append(copy)
        if beside is not None:
            beside(k)
    for k in range(RS_CHUNKS):
        first[k][0].wait_send()
        first[k][1].wait()
        passed[k].wait()


class Bag:
    def __init__(self, names, refs):
        self.__dict__.update(zip(names, refs))


MLP_BLOCKS = 3
LANES = 128


def block_kernel(names, *refs):
    R = Bag(names, refs)
    me = Spot()
    r, c, z, y = me.r, me.c, me.z, me.y
    length, width = R.inputs.shape
    seq_length = length * 8
    wide = R.taps_all.shape[2]
    side = wide // 2
    step = length // RS_CHUNKS
    tokens_all = 4 * length
    tiles = (length // TILE, TILE, wide)
    diag = (me.r_x + 1 - 2 * lax.rem(me.r_x, 2), c)
    row_peers = (me.core, me.x, diag)
    chan_peers = peers_of(me)
    x_place, core_place = lax.div(r, 2), lax.rem(r, 2)

    def far_first(i):
        return 2 * lax.rem(x_place + 1 + lax.div(i, 2), 2) + lax.rem(core_place + 1 + lax.rem(i, 2), 2)

    vec = R.vecs.at[r]
    taps = R.taps_all.at[r]
    keep = dict(gate_pre=R.gate_h, lext=R.lext_h, conv=R.conv_h, rec=R.rec_h, opening=R.open_h,
                state=R.state_h, mixed_t=R.mixed_h)

    def tallies_of(s):
        fill_tallies(R.tallies, R.starts_all[s, 0:1], c * length, length, seq_length)

    def same(shift):
        return same_document(R.tallies, length, shift, wide)


    glo = [
        Spread(me, [lambda k, half, m=m: R.wq.at[m, half, pl.ds(pl.multiple_of(k * 48, 16), 48)]], 4,
               R.spread[5 * m : 5 * m + 5])
        for m in range(3)
    ]

    def mlp_slabs(b):
        column = lambda half: pl.ds(pl.multiple_of(half * LANES, LANES), LANES)
        rows = lambda k, size: pl.ds(pl.multiple_of(k * size, 16), size)
        size = width // 8
        return [
            lambda k, half: R.wg.at[b, rows(k, size), column(half)],
            lambda k, half: R.wu.at[b, rows(k, size), column(half)],
            lambda k, half: R.wd.at[b, pl.ds(pl.multiple_of(half * LANES + k * 16, 16), 16)],
        ]

    mlp_w = [
        Spread(me, mlp_slabs(b), 8, R.spread[15 + 15 * b : 30 + 15 * b]) for b in range(MLP_BLOCKS)
    ]
    sline = Line([glo[2]] + mlp_w, (0, 4, 12, 20))

    def forward(gate_pre, lext, conv, rec, opening, a, b, mixed_t, part, rg32, ig32):
        barrier = pltpu.get_barrier_semaphore()
        always = list(row_peers) + chan_peers
        for device in always:
            pl.semaphore_signal(barrier, inc=1, device_id=device, device_id_type=MESH)
        count = len(always)
        for there, place in ((c < 7, lax.rem(c + 1, 8)), (c > 0, lax.rem(c + 7, 8))):
            for i in (1, 2, 3):

                @pl.when(there)
                def _(i=i, place=place):
                    pl.semaphore_signal(
                        barrier, inc=1, device_id=(lax.rem(r + i, 4), place), device_id_type=MESH
                    )

            count = count + jnp.where(there, 3, 0)
        own = [pltpu.make_async_copy(R.wm, R.wq.at[:, y], R.loc.at[0])]
        for blk in range(MLP_BLOCKS):
            lanes = pl.ds(blk * LANES, LANES)
            column = pl.ds(pl.multiple_of(y * LANES, LANES), LANES)
            own += [
                pltpu.make_async_copy(R.mg.at[:, lanes], R.wg.at[blk, :, column], R.loc.at[1 + blk]),
                pltpu.make_async_copy(R.mu.at[:, lanes], R.wu.at[blk, :, column], R.loc.at[4 + blk]),
                pltpu.make_async_copy(R.md.at[lanes], R.wd.at[blk, column], R.loc.at[7 + blk]),
            ]

        @pl.when(z == r)
        def _():
            for copy in own:
                copy.start()

        heads = [
            pltpu.make_async_copy(R.rgate_all.at[pl.ds(2 * r, 2)], rg32, R.loc.at[10]),
            pltpu.make_async_copy(R.igate_all.at[pl.ds(2 * r, 2)], ig32, R.loc.at[11]),
        ]
        for copy in heads:
            copy.start()
        R.call[r] = R.cot[...]
        vals = R.inputs[...].astype(F32)
        scale = lax.rsqrt(jnp.mean(vals * vals, axis=-1, keepdims=True) + EPSILON)
        R.nall[r] = (vals * scale * R.mix_gain[...]).astype(LOW)
        R.starts_all[r] = R.starts[...]
        pl.semaphore_wait(barrier, count)

        mine_n, mine_c = R.nall.at[r], R.call.at[r]
        theirs_n, theirs_c = R.nall.at[me.r_x], R.call.at[me.r_x]
        x_n = push(mine_n, mine_n, (R.xs, R.xr), 0, me.x)
        c_n = push(mine_n, mine_n, (R.cs, R.cr), 0, me.core)
        c_c = push(mine_c, mine_c, (R.cs, R.cr), 1, me.core)
        x_c = push(mine_c, mine_c, (R.xs, R.xr), 1, me.x)
        fwd_n = push(theirs_n, theirs_n, (R.cs, R.cr), 2, me.core)
        fwd_c = push(theirs_c, theirs_c, (R.cs, R.cr), 3, me.core)
        s_copies = [
            push(R.starts_all.at[r], R.starts_all.at[r], (R.ss, R.sr), i, device)
            for i, device in enumerate(row_peers)
        ]
        tail = R.nall.at[r, pl.ds(length - 16, 16)]
        halo_copies = [
            push(tail, R.halo.at[r], (R.hs, R.hr), i, (lax.rem(r + i, 4), lax.rem(c + 1, 8)))
            for i in range(4)
        ]
        x_n.start()
        for copy in s_copies:
            copy.start()

        @pl.when(c < 7)
        def _():
            for copy in halo_copies:
                copy.start()

        c_n.start()
        c_c.start()

        @pl.when(c == 0)
        def _():
            R.halo[...] = jnp.zeros_like(R.halo)

        @pl.when(z == r)
        def _():
            own[0].wait()

        for m in range(2):
            for k in range(4):

                @pl.when(z == r)
                def _(m=m, k=k):
                    glo[m].send(k)

                @pl.when(z != r)
                def _(m=m, k=k):
                    glo[m].follow(k)

            if m == 0:
                for copy in heads:
                    copy.wait()
                pair_diagonal(R.rgate, rg32)
                pair_diagonal(R.igate, ig32)
        x_n.wait_recv()
        fwd_n.start()
        x_c.start()

        @pl.when(z == r)
        def _():
            for copy in own[1:]:
                copy.wait()

        sline.advance(0)
        glo[0].arrived()
        glo[1].arrived()
        c_n.wait_recv()
        fwd_n.wait_recv()
        for copy in s_copies:
            copy.wait_recv()

        @pl.when(c > 0)
        def _():
            for i in range(4):
                landed(me, R.halo.at[i], (R.hs, R.hr), i)

        def mixer_one(s):
            tallies_of(s)
            tokens = R.nall[s]
            wgate = R.wq[0].reshape(wide, width)
            wlift = R.wq[1].reshape(wide, width)
            gate_pre[s] = nt(tokens, wgate) + vec[0:1]
            lifted = nt(tokens, wlift) + vec[1:2]
            lext[s, 0:8] = (nt(R.halo[s], wlift) + vec[1:2])[8:16]
            lext[s, pl.ds(8, length)] = lifted
            out = vec[2:3] + taps[0:1] * lifted
            for k in range(1, 4):
                out = out + taps[k : k + 1] * lext[s, pl.ds(8 - k, length)] * same(-k)
            conv[s] = out
            low = out.astype(LOW)
            recur = jax.nn.sigmoid(nn(low, R.rgate[...]) + vec[3:4])
            opened = jax.nn.sigmoid(nn(low, R.igate[...]) + vec[4:5])
            rec[s] = recur
            opening[s] = opened
            reset = same(-1) < 0.5
            decay, scaling = decay_terms(recur, vec[5:6], reset)
            decay = jnp.where(reset, 0.0, decay)
            a_scan, b_scan = tile_scan(
                decay.reshape(tiles), (scaling * opened * out).reshape(tiles), False
            )
            a[s] = a_scan.reshape(length, wide)
            b[s] = b_scan.reshape(length, wide)
            product = jnp.ones((1, wide), F32)
            state = jnp.zeros((1, wide), F32)
            for t in range(length // TILE):
                last = t * TILE + TILE - 1
                a_last = a[s, last : last + 1]
                state = b[s, last : last + 1] + a_last * state
                product = product * a_last
            R.tot[s, 0:1] = product
            R.tot[s, 1:2] = state

        sline.during(0, 4, mixer_one)
        carry_copies = carry_start(me, False, R.tot, R.slots, (R.ps, R.pr))
        local = dict(gate_pre=gate_pre, lext=lext, conv=conv, rec=rec, opening=opening, state=b,
                     mixed_t=mixed_t)
        saved = {
            name: pltpu.make_async_copy(local[name], keep[name], R.outs.at[i])
            for i, name in enumerate(keep)
        }
        for name in ("gate_pre", "lext", "conv", "rec", "opening"):
            saved[name].start()
        sline.advance(6)
        x_c.wait_recv()
        fwd_c.start()
        sline.advance(8)
        carry_join(me, False, R.slots, R.start, (R.ps, R.pr))
        sline.advance(4 + 2 * SPREAD_LAG)
        glo[2].arrived()

        def mixer_two(i):
            s = far_first(i)
            state = R.start[pl.ds(s, 1)]
            for t in range(length // TILE):
                tile = pl.ds(t * TILE, TILE)
                now = b[s, tile] + a[s, tile] * state
                b[s, tile] = now
                state = now[TILE - 1 : TILE]
            gate_val, _ = gelu_pair(gate_pre[s])
            mix = (b[s] * gate_val).astype(LOW)
            mixed_t[:, pl.ds(pl.multiple_of(s * length, LANES), length)] = mix.T
            part[s] = nn(mix, R.wq[2].reshape(wide, width)).astype(LOW)

        sline.during(0, 2, mixer_two)
        copies = rows_sum_start(me, part, R.mate, (R.ms, R.mr), 0)
        sline.during(2, 3, mixer_two)
        copies += rows_sum_start(me, part, R.mate, (R.ms, R.mr), 1)
        crossing = rows_sum_cross(me, part, R.mate, R.out_x, R.in_x, copies, (R.rxs, R.rxr))
        sline.during(3, 4, mixer_two)
        for name in ("state", "mixed_t"):
            saved[name].start()
        first = []
        for k in range(RS_CHUNKS):
            chunk = pl.ds(k * step, step)
            total = rows_sum_chunk(me, part, R.mate, R.in_x, copies, crossing, k)
            res = R.inputs[chunk].astype(F32) + total + R.out_bias[...]
            R.resid[chunk] = res
            scale = lax.rsqrt(jnp.mean(res * res, axis=-1, keepdims=True) + EPSILON)
            R.n2all[r, chunk] = (res * scale * R.mlp_gain[...]).astype(LOW)
            first.append(spread_chunk(me, R.n2all, k, (R.ax, R.bx), (R.ac, R.bc)))
            sline.advance(sline.done + 2)
        spread_rest(me, R.n2all, first, (R.ac, R.bc), lambda k: sline.advance(sline.done + 1))
        finish_sends(copies + crossing)
        for m in range(3):
            glo[m].close()
        for copy in (x_n, x_c, c_n, fwd_n):
            copy.wait_send()
        c_c.wait()
        fwd_c.wait()
        finish_sends(s_copies)

        @pl.when(c < 7)
        def _():
            finish_sends(halo_copies)

        carry_sent(me, False, carry_copies)
        for copy in saved.values():
            copy.wait()

    tall = pltpu.VMEM((4, length, wide), F32)
    ext = pltpu.VMEM((4, length + TILE, wide), F32)
    low_t = pltpu.VMEM((wide, tokens_all), LOW)
    pl.run_scoped(
        forward, gate_pre=tall, lext=ext, conv=tall, rec=tall, opening=tall, a=tall, b=tall,
        mixed_t=low_t, part=pltpu.VMEM((4, length, width), LOW),
        rg32=pltpu.VMEM((2, GB, GB), F32), ig32=pltpu.VMEM((2, GB, GB), F32),
    )


    groups = [R.reduce[33 * i : 33 * i + 33] for i in range(MLP_BLOCKS)]
    rest = R.reduce[33 * MLP_BLOCKS :]
    own_view = lambda ref, blk: ref.at[:, pl.ds(blk * LANES, LANES)]
    line = Line(
        [
            Reduce(
                me,
                [R.grad_g.at[blk], R.grad_u.at[blk], R.grad_d.at[blk]],
                [R.grad_g.at[blk, y], R.grad_u.at[blk, y], R.grad_d.at[blk, y]],
                [R.y_g.at[blk], R.y_u.at[blk], R.y_d.at[blk]],
                [R.z_g.at[blk], R.z_u.at[blk], R.z_d.at[blk]],
                [own_view(R.own_g, blk), own_view(R.own_u, blk), R.own_d.at[pl.ds(blk * LANES, LANES)]],
                8,
                groups[blk],
            )
            for blk in range(MLP_BLOCKS)
        ]
        + [
            Reduce(me, [R.early], [R.early.at[y]], [R.y_e], [R.z_e], [R.own_e], 8, rest[:11]),
            Reduce(me, [R.late], [R.late.at[y]], [R.y_l], [R.z_l], [R.own_l], 7, rest[11:]),
        ],
        (0, 8, 16, 26, 36),
    )
    gpart = R.call

    def mlp(acc_out, acc_in, n2_t, hid, low_g, low_u):
        def turn(s):
            n2_t[:, pl.ds(pl.multiple_of(s * length, LANES), length)] = R.n2all[s].T

        def mlp_tokens(blk, s):
            tokens, cot = R.n2all[s], R.call[s]
            gate = nn(tokens, R.wg[blk])
            up = nn(tokens, R.wu[blk])
            grad_hidden = nt(cot, R.wd[blk])
            gate_val, slope = gelu_pair(gate)
            hidden = (gate_val * up).astype(LOW)
            grad_gate = (grad_hidden * up * slope).astype(LOW)
            grad_up = (grad_hidden * gate_val).astype(LOW)
            hid[s], low_g[s], low_u[s] = hidden, grad_gate, grad_up
            out = nn(hidden, R.wd[blk])
            back = nt(grad_gate, R.wg[blk]) + nt(grad_up, R.wu[blk])
            if blk == 0:
                acc_out[s] = out
                acc_in[s] = back
            elif blk < MLP_BLOCKS - 1:
                acc_out[s] += out
                acc_in[s] += back
            else:
                R.opart[s] = (acc_out[s] + out).astype(LOW)
                acc_in[s] += back

        def mlp_weights(blk, ahead):
            columns = lambda i: pl.ds(pl.multiple_of(i * 256, 256), 256)
            hid_t = hid[...].reshape(tokens_all, 2 * LANES).T

            @pl.loop(0, width // 256)
            def _(i):
                down = nn(hid_t, R.call[:, :, columns(i)].reshape(tokens_all, 256)).astype(LOW)
                gate = nn(n2_t[columns(i)], low_g[...].reshape(tokens_all, 2 * LANES)).astype(LOW)
                up = nn(n2_t[columns(i)], low_u[...].reshape(tokens_all, 2 * LANES)).astype(LOW)
                for j in range(2):
                    part = slice(j * LANES, (j + 1) * LANES)
                    R.grad_d[blk, j, :, columns(i)] = down[part]
                    R.grad_g[blk, j, columns(i)] = gate[:, part]
                    R.grad_u[blk, j, columns(i)] = up[:, part]

        for blk in range(MLP_BLOCKS):
            sline.advance(max(sline.done, sline.offsets[1 + blk] + 8 + 2 * SPREAD_LAG))
            mlp_w[blk].arrived()
            if blk == 0:

                @pl.loop(0, 4)
                def _(s):
                    turn(s)

            if blk == 0:
                sline.during(0, 4, lambda s: mlp_tokens(0, s))
            else:
                line.during(0, 4, lambda s: mlp_tokens(blk, far_first(s)))
            if blk == MLP_BLOCKS - 1:
                mlp_weights(blk, None)
                gpart[...] = acc_in[...].astype(LOW)
            else:
                mlp_weights(blk, None)
            line.ready(blk)
            line.advance((-2, 3, 7)[blk])

    pl.run_scoped(
        mlp, acc_out=pltpu.VMEM((4, length, width), F32), acc_in=pltpu.VMEM((4, length, width), F32),
        n2_t=pltpu.VMEM((width, tokens_all), LOW), hid=pltpu.VMEM((4, length, 2 * LANES), LOW),
        low_g=pltpu.VMEM((4, length, 2 * LANES), LOW), low_u=pltpu.VMEM((4, length, 2 * LANES), LOW),
    )
    for one in mlp_w:
        one.close()


    def backward(gate_pre, conv, rec, opening, state, a, b, gconv, gate_low, gate_t, mixed_t, acc_r,
                 acc_i, prev_ext):
        local = dict(gate_pre=gate_pre, conv=conv, rec=rec, opening=opening, state=state,
                     mixed_t=mixed_t)
        loads = [
            pltpu.make_async_copy(keep[name], ref, R.outs.at[i])
            for i, (name, ref) in enumerate(local.items())
        ]
        for copy in loads:
            copy.start()
        ball = R.n2all
        copies = rows_sum_start(me, gpart, R.mate, (R.m2s, R.m2r))
        line.advance(8)
        crossing = rows_sum_cross(me, gpart, R.mate, R.out_x, R.in_x, copies, (R.rx2s, R.rx2r))
        first = []
        gain2_sum = 0.0
        bias_sum = 0.0
        for k in range(RS_CHUNKS):
            rows = pl.ds(k * step, step)
            grad = rows_sum_chunk(me, gpart, R.mate, R.in_x, copies, crossing, k)
            res = R.resid[rows]
            scale = lax.rsqrt(jnp.mean(res * res, axis=-1, keepdims=True) + EPSILON)
            gain2_sum = gain2_sum + jnp.sum(grad * res * scale, axis=0, keepdims=True)
            pulled = grad * R.mlp_gain[...]
            inner = jnp.mean(pulled * res, axis=-1, keepdims=True)
            total = R.cot[rows].astype(F32) + scale * pulled - res * (scale * scale * scale * inner)
            bias_sum = bias_sum + jnp.sum(total, axis=0, keepdims=True)
            R.gresid[rows] = total
            ball[r, rows] = total.astype(LOW)
            first.append(spread_chunk(me, ball, k, (R.a2x, R.b2x), (R.a2c, R.b2c)))
            line.advance((9, 11, 12, 13)[k])
        for copy in loads:
            copy.wait()
        line.advance(14)
        spread_rest(me, ball, first, (R.a2c, R.b2c), lambda k: line.advance(15 + k))
        o_copies = rows_sum_start(me, R.opart, R.o_mate, (R.oms, R.omr))
        finish_sends(copies + crossing)
        acc_r[...] = jnp.zeros_like(acc_r)
        acc_i[...] = jnp.zeros_like(acc_i)
        R.sums[...] = jnp.zeros_like(R.sums)

        def reset_of(s):
            tallies_of(s)
            return same(-1) < 0.5

        def mixer_three(s):
            grad_mixed = nt(ball[s], R.wq[2].reshape(wide, width))
            gate_val, slope = gelu_pair(gate_pre[s])
            grad_gate = grad_mixed * state[s] * slope
            low = grad_gate.astype(LOW)
            gate_low[s] = low
            gate_t[:, pl.ds(pl.multiple_of(s * length, LANES), length)] = low.T
            R.sums[0:1] += jnp.sum(grad_gate, axis=0, keepdims=True)
            grad_state = grad_mixed * gate_val
            gate_pre[s] = grad_state
            decay = jnp.where(reset_of(s), 0.0, jnp.exp(-8.0 * rec[s] * vec[5:6]))
            a_scan, b_scan = tile_scan(
                decay.reshape(tiles), (decay * grad_state).reshape(tiles), True
            )
            a[s, 0:length] = a_scan.reshape(length, wide)
            b[s] = b_scan.reshape(length, wide)
            product = jnp.ones((1, wide), F32)
            carried = jnp.zeros((1, wide), F32)
            for t in range(length // TILE - 1, -1, -1):
                head = t * TILE
                a_head = a[s, head : head + 1]
                carried = b[s, head : head + 1] + a_head * carried
                product = product * a_head
            R.tot[s, 0:1] = product
            R.tot[s, 1:2] = carried

        line.during(0, 4, mixer_three)
        carry_copies = carry_start(me, True, R.tot, R.slots2, (R.p2s, R.p2r))
        columns = lambda i: pl.ds(pl.multiple_of(i * 256, 256), 256)

        def weight_grad(target, at, left_t, right):
            @pl.loop(0, width // 256)
            def _(i):
                product = nn(left_t[...], right[:, :, columns(i)].reshape(tokens_all, 256)).astype(LOW)
                for j in range(2):
                    target[j, at : at + side, columns(i)] = product[j * side : (j + 1) * side]

        weight_grad(R.early, 0, mixed_t, ball)
        weight_grad(R.early, side, gate_t, R.nall)
        line.ready(3)
        o_cross = rows_sum_cross(me, R.opart, R.o_mate, R.o_out, R.o_in, o_copies, (R.oxs, R.oxr))
        line.advance(24)
        carry_join(me, True, R.slots2, R.carry, (R.p2s, R.p2r))

        def mixer_four(s):
            now = R.carry[pl.ds(s, 1)]
            gconv[s, pl.ds(length, TILE)] = jnp.broadcast_to(now, (TILE, wide))
            for t in range(length // TILE - 1, -1, -1):
                rows = pl.ds(t * TILE, TILE)
                moved = b[s, rows] + a[s, rows] * now
                gconv[s, rows] = moved
                now = moved[0:1]
            carried = gate_pre[s] + gconv[s, pl.ds(1, length)]
            prev_ext[0:TILE] = jnp.broadcast_to(R.start[pl.ds(s, 1)], (TILE, wide))
            prev_ext[pl.ds(TILE, length)] = state[s]
            previous = prev_ext[pl.ds(TILE - 1, length)]
            recur, opened, conv_s = rec[s], opening[s], conv[s]
            reset = reset_of(s)
            decay, scaling = decay_terms(recur, vec[5:6], reset)
            pulled = carried * scaling
            grad_opening = pulled * conv_s
            grad_log = carried * (previous * decay - opened * conv_s * (decay * decay / scaling))
            grad_log = jnp.where(reset, 0.0, grad_log)
            grad_rec = grad_log * (-8.0 * vec[5:6])
            grad_rpre = grad_rec * recur * (1.0 - recur)
            grad_opre = grad_opening * opened * (1.0 - opened)
            r_low, o_low, conv_low = grad_rpre.astype(LOW), grad_opre.astype(LOW), conv_s.astype(LOW)
            total = pulled * opened + nt(r_low, R.rgate[...]) + nt(o_low, R.igate[...])
            gconv[s, 0:length] = total
            acc_r[...] += tn(conv_low, r_low)
            acc_i[...] += tn(conv_low, o_low)
            R.sums[7:8] += jnp.sum(grad_rpre, axis=0, keepdims=True)
            R.sums[8:9] += jnp.sum(grad_opre, axis=0, keepdims=True)
            R.sums[9:10] += jnp.sum(grad_log * recur, axis=0, keepdims=True) * (8.0 * vec[6:7])
            R.sums[6:7] += jnp.sum(total, axis=0, keepdims=True)

        line.during(0, 4, mixer_four)
        lext = a
        load_lext = pltpu.make_async_copy(keep["lext"], lext, R.outs.at[6])
        load_lext.start()
        heads = [
            push(gconv.at[s, pl.ds(0, TILE)], R.heads_in.at[s], (R.h2s, R.h2r), s,
                 (r, lax.rem(c + 7, 8)))
            for s in range(4)
        ]

        @pl.when(c > 0)
        def _():
            for copy in heads:
                copy.start()

        @pl.when(c == 7)
        def _():
            R.heads_in[...] = jnp.zeros_like(R.heads_in)

        cut = side // 8
        for k in range(8):
            at = k * cut
            R.gate_send[k] = jnp.concatenate(
                [m[j * side + at : j * side + at + cut, j * side : (j + 1) * side]
                 for m in (acc_r, acc_i) for j in range(2)], axis=0
            ).astype(LOW)
        gate_copies = [
            push(R.gate_send.at[lax.rem(c + d, 8)], R.gate_slots.at[d], (R.qs, R.qr), d,
                 chan_peers[d - 1])
            for d in range(1, 8)
        ]
        for copy in gate_copies:
            copy.start()
        for k in range(RS_CHUNKS):
            rows = pl.ds(k * step, step)
            total = rows_sum_chunk(me, R.opart, R.o_mate, R.o_in, o_copies, o_cross, k)
            R.output[rows] = (R.resid[rows] + total).astype(LOW)
        load_lext.wait()

        @pl.when(c < 7)
        def _():
            for s in range(4):
                landed(me, R.heads_in.at[s], (R.h2s, R.h2r), s)

        lift_t = mixed_t
        gpart1 = R.call

        def mixer_five(i):
            s = far_first(i)
            tallies_of(s)
            grad = gconv[s, 0:length]
            prev_ext[0:length] = grad
            prev_ext[pl.ds(length, TILE)] = R.heads_in[s]
            grad_lifted = taps[0:1] * grad
            R.sums[2:3] += jnp.sum(grad * lext[s, pl.ds(TILE, length)], axis=0, keepdims=True)
            for k in range(1, 4):
                ahead = prev_ext[pl.ds(k, length)] * same(k)
                grad_lifted = grad_lifted + taps[k : k + 1] * ahead
                behind = lext[s, pl.ds(TILE - k, length)] * same(-k)
                R.sums[2 + k : 3 + k] += jnp.sum(grad * behind, axis=0, keepdims=True)
            R.sums[1:2] += jnp.sum(grad_lifted, axis=0, keepdims=True)
            lift_low = grad_lifted.astype(LOW)
            lift_t[:, pl.ds(pl.multiple_of(s * length, LANES), length)] = lift_low.T
            gpart1[s] = (
                nn(gate_low[s], R.wq[0].reshape(wide, width))
                + nn(lift_low, R.wq[1].reshape(wide, width))
            ).astype(LOW)

        line.during(0, 2, mixer_five)
        n_copies = rows_sum_start(me, gpart1, R.mate, (R.m3s, R.m3r), 0)
        line.during(2, 3, mixer_five)
        n_copies += rows_sum_start(me, gpart1, R.mate, (R.m3s, R.m3r), 1)
        n_cross = rows_sum_cross(me, gpart1, R.mate, R.out_x, R.in_x, n_copies, (R.rx3s, R.rx3r))
        line.during(3, 4, mixer_five)
        R.late[...] = jnp.zeros_like(R.late)
        weight_grad(R.late, 0, lift_t, R.nall)
        for j in range(2):
            R.late[j, side : side + 16, 0:side] = R.sums[:, j * side : (j + 1) * side].astype(LOW)
        line.ready(4)
        line.advance(34)
        gain_sum = 0.0
        for k in range(RS_CHUNKS):
            rows = pl.ds(k * step, step)
            grad = rows_sum_chunk(me, gpart1, R.mate, R.in_x, n_copies, n_cross, k)
            vals = R.inputs[rows].astype(F32)
            scale = lax.rsqrt(jnp.mean(vals * vals, axis=-1, keepdims=True) + EPSILON)
            gain_sum = gain_sum + jnp.sum(grad * vals * scale, axis=0, keepdims=True)
            pulled = grad * R.mix_gain[...]
            inner = jnp.mean(pulled * vals, axis=-1, keepdims=True)
            R.ginputs[rows] = (
                R.gresid[rows] + scale * pulled - vals * (scale * scale * scale * inner)
            ).astype(LOW)
            line.advance(35 + k)
        for k in range(8):
            lanes = slice(k * LANES, (k + 1) * LANES)
            R.gain_slots[0, k] = jnp.concatenate(
                [gain_sum[:, lanes], gain2_sum[:, lanes], bias_sum[:, lanes],
                 jnp.zeros((5, LANES), F32)], 0
            )
        gain_copies = [
            push(R.gain_slots.at[0, lax.rem(c + d, 8)], R.gain_slots.at[1, d], (R.ggs, R.ggr), d,
                 chan_peers[d - 1])
            for d in range(1, 8)
        ]
        for copy in gain_copies:
            copy.start()
        line.advance(40)
        gate_total = R.gate_send[c].astype(F32)
        for d in range(1, 8):
            gate_copies[d - 1].wait_recv()
            gate_total = gate_total + R.gate_slots[d].astype(F32)
        R.gates_all[r] = gate_total.astype(LOW)
        gate_rows = [
            push(R.gates_all.at[r], R.gates_all.at[r], (R.ts, R.tr), i, device)
            for i, device in enumerate(row_peers)
        ]
        for copy in gate_rows:
            copy.start()
        shared = R.gain_slots[0, c]
        for d in range(1, 8):
            gain_copies[d - 1].wait_recv()
            shared = shared + R.gain_slots[1, d]
        R.gain_sums[0] = shared
        row_copies = [
            push(R.gain_sums.at[0], R.gain_sums.at[1 + i], (R.ghs, R.ghr), i, device)
            for i, device in enumerate(row_peers)
        ]
        for copy in row_copies:
            copy.start()
        line.advance(line.last())
        for copy in row_copies + gate_rows:
            copy.wait()
        R.gains_all[...] = R.gain_sums[0] + R.gain_sums[1] + R.gain_sums[2] + R.gain_sums[3]

        @pl.when(c > 0)
        def _():
            finish_sends(heads)

        finish_sends(gain_copies + gate_copies + n_copies + n_cross + o_copies + o_cross)
        carry_sent(me, True, carry_copies)
        line.close()

    square = pltpu.VMEM((wide, wide), F32)
    pl.run_scoped(
        backward, gate_pre=tall, conv=tall, rec=tall, opening=tall, state=tall, a=ext, b=tall,
        gconv=ext, gate_low=pltpu.VMEM((4, length, wide), LOW), gate_t=low_t, mixed_t=low_t,
        acc_r=square, acc_i=square, prev_ext=pltpu.VMEM((length + TILE, wide), F32),
    )


def block(inputs, cot, mix_gain, vecs, taps_all, starts, out_bias, mlp_gain, rgate_all, igate_all,
          wm, mg, mu, md):
    length, width = inputs.shape
    wide = taps_all.shape[2]
    side = wide // 2
    hidden = mg.shape[1]
    sd, vmem = jax.ShapeDtypeStruct, pltpu.VMEM
    blocks = hidden // LANES
    tall = sd((4, length, wide), F32)
    tokens = (4, length, width)
    ins = dict(inputs=inputs, cot=cot, mix_gain=mix_gain, vecs=vecs, taps_all=taps_all, starts=starts,
               out_bias=out_bias, mlp_gain=mlp_gain, rgate_all=rgate_all, igate_all=igate_all,
               wm=wm, mg=mg, mu=mu, md=md)
    far = ("rgate_all", "igate_all", "wm", "mg", "mu", "md")
    outs = dict(
        output=sd(inputs.shape, LOW), ginputs=sd(inputs.shape, LOW),
        own_g=sd((width, hidden), LOW), own_u=sd((width, hidden), LOW), own_d=sd((hidden, width), LOW),
        own_e=sd((2 * side, width), LOW), own_l=sd((side + 32, width), LOW),
        gates_all=sd((4, side // 2, side), LOW), gains_all=sd((8, LANES), F32),
    )
    saved = dict(
        gate_h=tall, lext_h=sd((4, length + TILE, wide), F32), conv_h=tall, rec_h=tall, open_h=tall,
        state_h=tall, mixed_h=sd((wide, 4 * length), LOW),
    )
    inward, outward = (blocks, 2, width, LANES), (blocks, 2, LANES, width)
    scratch = dict(
        wq=vmem((3, 2, side, width), LOW), nall=vmem(tokens, LOW), halo=vmem((4, 16, width), LOW),
        starts_all=vmem((4,) + starts.shape, starts.dtype),
        wg=vmem((blocks, width, 2 * LANES), LOW), wu=vmem((blocks, width, 2 * LANES), LOW),
        wd=vmem((blocks, 2 * LANES, width), LOW),
        call=vmem(tokens, LOW), n2all=vmem(tokens, LOW), opart=vmem(tokens, LOW),
        rgate=vmem((wide, wide), LOW), igate=vmem((wide, wide), LOW),
        tallies=vmem((length + 16, LANES), F32), start=vmem((4, wide), F32), carry=vmem((4, wide), F32),
        tot=vmem((4, 2, wide), F32), slots=vmem((8, 4, 2, wide), F32), slots2=vmem((8, 4, 2, wide), F32),
        resid=vmem((length, width), F32), gresid=vmem((length, width), F32),
        mate=vmem((2, length, width), LOW), out_x=vmem((length, width), LOW),
        in_x=vmem((length, width), LOW),
        o_mate=vmem((2, length, width), LOW), o_out=vmem((length, width), LOW),
        o_in=vmem((length, width), LOW),
        grad_g=vmem(inward, LOW), grad_u=vmem(inward, LOW), grad_d=vmem(outward, LOW),
        early=vmem((2, 2 * side, width), LOW), late=vmem((2, side + 32, width), LOW),
        heads_in=vmem((4, TILE, wide), F32), sums=vmem((16, wide), F32),
        gate_send=vmem((8, side // 2, side), LOW), gate_slots=vmem((8, side // 2, side), LOW),
        gain_slots=vmem((2, 8, 8, LANES), F32), gain_sums=vmem((4, 8, LANES), F32),
    )
    for way in "yz":
        scratch.update(
            {
                way + "_g": vmem(inward[:1] + inward[2:], LOW),
                way + "_u": vmem(inward[:1] + inward[2:], LOW),
                way + "_d": vmem(outward[:1] + outward[2:], LOW),
                way + "_e": vmem((2 * side, width), LOW),
                way + "_l": vmem((side + 32, width), LOW),
            }
        )
    dma = pltpu.SemaphoreType.DMA
    counts = dict(
        loc=12, outs=7, xs=2, xr=2, cs=4, cr=4, hs=4, hr=4, ss=3, sr=3, ps=8, pr=8, p2s=8, p2r=8,
        h2s=4, h2r=4, qs=8, qr=8, ts=3, tr=3, ggs=8, ggr=8, ghs=3, ghr=3,
    )
    for name in ("m", "m2", "m3", "om"):
        counts.update({name + "s": 2 * RS_CHUNKS, name + "r": 2 * RS_CHUNKS})
    for name in ("rx", "rx2", "rx3", "ox"):
        counts.update({name + "s": RS_CHUNKS, name + "r": RS_CHUNKS})
    for name in ("", "2"):
        counts.update({f"a{name}x": RS_CHUNKS, f"b{name}x": RS_CHUNKS})
        counts.update({f"a{name}c": 2 * RS_CHUNKS, f"b{name}c": 2 * RS_CHUNKS})
    scratch.update({name: dma((count,)) for name, count in counts.items()})
    names = list(ins) + list(outs) + list(saved) + list(scratch)
    spread = spread_sems(1, 4) * 3 + spread_sems(3, 8) * blocks
    reduce = reduce_sems(3, 8) * blocks + reduce_sems(1, 8) + reduce_sems(1, 7)

    def kernel(*refs):
        n, m = len(names), len(spread)
        block_kernel(names + ["spread", "reduce"], *refs[:n], refs[n : n + m], refs[n + m :])

    results = pl.pallas_call(
        kernel,
        name="block",
        out_shape=list(outs.values()) + list(saved.values()),
        in_specs=[ANYWHERE if name in far else IN_VMEM for name in ins],
        out_specs=[IN_VMEM] * len(outs) + [ANYWHERE] * len(saved),
        scratch_shapes=list(scratch.values()) + spread + reduce,
        compiler_params=comm_params(1),
    )(*ins.values())
    return results[: len(outs)]


def split_body(
    inputs, mix_gain, gate_proj, gate_bias, lift_proj, lift_bias, conv_taps, conv_bias,
    recur_gate, recur_bias, input_gate, input_bias, decay_param, out_proj, out_bias, mlp_gain,
    mlp_gate, mlp_up, mlp_down, doc_starts, cotangent,
):
    wide = 2 * GB
    wm = jnp.stack([gate_proj.T, lift_proj.T, out_proj])
    vecs = jnp.stack(
        [gate_bias, lift_bias, conv_bias, recur_bias, input_bias, jax.nn.softplus(-decay_param),
         jax.nn.sigmoid(-decay_param), jnp.zeros_like(decay_param)]
    ).reshape(8, 4, wide).transpose(1, 0, 2)
    taps = conv_taps.reshape(4, 4, wide).transpose(1, 0, 2)
    starts = jnp.pad(
        doc_starts, ((0, 7), (0, 128 - doc_starts.shape[1])),
        constant_values=jnp.iinfo(jnp.int32).max,
    )
    output, grad_inputs, own_g, own_u, own_d, own_e, own_l, gates, gains = block(
        inputs, cotangent, mix_gain[None], vecs, taps, starts, out_bias[None], mlp_gain[None],
        recur_gate, input_gate, wm, mlp_gate, mlp_up, mlp_down,
    )
    wide_out = lambda v: v.astype(F32)
    gates = wide_out(gates).reshape(4, 2, 2, GB // 8, GB)
    gate_out = lambda i: gates[:, i].reshape(8, GB // 8, GB)
    own = wide_out(own_l[GB : GB + 16, :GB])
    return (
        output, grad_inputs, gains[0],
        wide_out(own_e[GB:].T), own[0], wide_out(own_l[:GB].T), own[1], own[2:6], own[6],
        gate_out(0), own[7], gate_out(1), own[8], own[9],
        wide_out(own_e[:GB]), gains[2], gains[1],
        wide_out(own_g), wide_out(own_u), wide_out(own_d),
    )


def solution(mesh):
    in_specs = (
        P(("rows", "chan"), None),
        P(),
        P(None, "chan"),
        P(),
        P(None, "chan"),
        P(),
        P(),
        P(),
        P(),
        P(),
        P(),
        P(),
        P(),
        P("chan", None),
        P(),
        P(),
        P(None, "chan"),
        P(None, "chan"),
        P("chan", None),
        P("rows", None),
        P(("rows", "chan"), None),
    )
    out_specs = (
        P(("rows", "chan"), None),
        P(("rows", "chan"), None),
        P("chan"),
        P(None, "chan"),
        P("chan"),
        P(None, "chan"),
        P("chan"),
        P(None, "chan"),
        P("chan"),
        P(None, "chan", None),
        P("chan"),
        P(None, "chan", None),
        P("chan"),
        P("chan"),
        P("chan", None),
        P("chan"),
        P("chan"),
        P(None, "chan"),
        P(None, "chan"),
        P("chan", None),
    )
    split = mesh.shape["rows"] == 4 and mesh.shape["chan"] == HEADS
    return jax.shard_map(split_body if split else body, mesh=mesh, in_specs=in_specs, out_specs=out_specs, check_vma=False)
```

```python
from functools import partial
import math

import jax
import jax.numpy as jnp
from jax import lax
from jax.experimental import pallas as pl
from jax.experimental.pallas import tpu as pltpu
from jax.sharding import PartitionSpec as P

D = 1024
LRU = 1536
FF = 3072
HEADS = 8
GB = 192


EPSILON = 1e-06
precise = lax.Precision.HIGHEST


def from_behind(block, axis, distance):
    devices = range(lax.axis_size(axis))
    route = [(i - distance, i) for i in devices if i - distance in devices]
    return lax.ppermute(block, axis, route)


def prefix(value, axis, join, neutral, backward):
    count, mine = (lax.axis_size(axis), lax.axis_index(axis))
    pieces = jax.tree.map(lambda part: lax.all_gather(part, axis), value)
    if backward:
        pieces = jax.tree.map(lambda part: part[::-1], pieces)
        mine = count - 1 - mine
    subtotal = jax.tree.map(
        lambda part, zero: jnp.full_like(part, 0) + jnp.asarray(zero, part.dtype), value, neutral
    )

    def hop(position, subtotal):
        longer = join(subtotal, jax.tree.map(lambda part: part[position], pieces))
        return jax.tree.map(lambda new, old: jnp.where(position < mine, new, old), longer, subtotal)

    return lax.fori_loop(0, count - 1, hop, subtotal)


def rms_scale(values, gain_vec):
    return (
        values * lax.rsqrt(jnp.mean(values * values, axis=-1, keepdims=True) + EPSILON) * gain_vec
    )


def gated_unit(gate_pre, up_vals):
    return jax.nn.gelu(gate_pre) * up_vals


def affine(earlier, later_map):
    return (earlier[0] * later_map[0], later_map[0] * earlier[1] + later_map[1])


def segment_ids(starts, start_pos, pos_count, seq_len):
    where_at = start_pos + jnp.arange(pos_count, dtype=jnp.int32)
    seq_of = jnp.floor_divide(where_at, seq_len)
    within = where_at - seq_of * seq_len
    owner = seq_of[:, None] == jnp.arange(starts.shape[0], dtype=jnp.int32)[None, :]
    passed = starts[None, :, :] <= within[:, None, None]
    doc_tally = jnp.sum(jnp.logical_and(owner[:, :, None], passed).astype(jnp.int32), axis=(1, 2))
    return seq_of * (starts.shape[1] + 1) + doc_tally


def project(normed, weights, first_bias, second_bias):
    product = jnp.einsum("td,dc->ct", normed, weights, preferred_element_type=jnp.float32)
    channels = first_bias.shape[0]
    return (product[:channels] + first_bias[:, None], product[channels:] + second_bias[:, None])


def conv_forward(lifted, tail_rows, segments, tap_vals, bias_vec):
    length = lifted.shape[1]
    extended = jnp.concatenate([tail_rows, lifted], axis=1)
    own_seg = segments[3 : 3 + length]
    result = bias_vec[:, None] + tap_vals[0][:, None] * lifted
    for offset in range(1, 4):
        same_doc = (segments[3 - offset : 3 - offset + length] == own_seg).astype(jnp.float32)
        result = (
            result
            + tap_vals[offset][:, None]
            * extended[:, 3 - offset : 3 - offset + length]
            * same_doc[None, :]
        )
    return result


def conv_backward(grad_conv, head_rows, segments, lifted, tail_rows, tap_vals):
    length = grad_conv.shape[1]
    ahead_grad = jnp.concatenate([grad_conv, head_rows], axis=1)
    behind = jnp.concatenate([tail_rows, lifted], axis=1)
    own_seg = segments[3 : 3 + length]
    grad_lifted = tap_vals[0][:, None] * grad_conv
    tap_grads = [jnp.sum(grad_conv * lifted, axis=1)]
    for offset in range(1, 4):
        later_same = (segments[3 + offset : 3 + offset + length] == own_seg).astype(jnp.float32)
        grad_lifted = (
            grad_lifted
            + tap_vals[offset][:, None]
            * ahead_grad[:, offset : offset + length]
            * later_same[None, :]
        )
        earlier = (segments[3 - offset : 3 - offset + length] == own_seg).astype(jnp.float32)
        tap_grads.append(
            jnp.sum(
                grad_conv * behind[:, 3 - offset : 3 - offset + length] * earlier[None, :], axis=1
            )
        )
    return (grad_lifted, jnp.stack(tap_grads, axis=1), jnp.sum(grad_conv, axis=1))


def coefficients(is_reset, conv_out, recur_gate, recur_bias, input_gate, input_bias, decay_param):
    channels, length = conv_out.shape
    gate_block = recur_gate.shape[1]
    grouped = conv_out.reshape(channels // gate_block, gate_block, length)
    recurrence = jax.nn.sigmoid(
        jnp.einsum("hit,hio->hot", grouped, recur_gate, precision=precise).reshape(channels, length)
        + recur_bias[:, None]
    )
    opening = jax.nn.sigmoid(
        jnp.einsum("hit,hio->hot", grouped, input_gate, precision=precise).reshape(channels, length)
        + input_bias[:, None]
    )
    log_decay = -8.0 * recurrence * jax.nn.softplus(-decay_param)[:, None]
    decay_rate = jnp.where(is_reset[None, :], 0.0, jnp.exp(log_decay))
    scaling = jnp.where(is_reset[None, :], 1.0, jnp.sqrt(-jnp.expm1(2.0 * log_decay)))
    return (decay_rate, scaling * opening * conv_out)


def reverse_local(decay_rate, grad_state):
    ones_col = jnp.ones_like(decay_rate[:, :1])
    factor = jnp.flip(jnp.concatenate([decay_rate[:, 1:], ones_col], axis=1), axis=1)
    product, carried = lax.associative_scan(affine, (factor, jnp.flip(grad_state, axis=1)), axis=1)
    return (jnp.flip(product, axis=1), jnp.flip(carried, axis=1))


def finish_state(lru_state, start_state, carried, pull_coef):
    previous = jnp.concatenate([start_state[:, None], lru_state[:, :-1]], axis=1)
    return pull_coef((carried * previous, carried))


def flatten_rows(pieces, row_count):
    return jnp.concatenate([source.reshape(row_count, -1) for source in pieces], axis=1)


def body(
    inputs,
    mix_gain,
    gate_proj,
    gate_bias,
    lift_proj,
    lift_bias,
    conv_taps,
    conv_bias,
    recur_gate,
    recur_bias,
    input_gate,
    input_bias,
    decay_param,
    out_proj,
    out_bias,
    mlp_gain,
    mlp_gate,
    mlp_up,
    mlp_down,
    doc_starts,
    cotangent,
):
    chan_count = lax.axis_size("chan")
    chan_place = lax.axis_index("chan")
    local_rows = inputs.shape[0]
    seq_length = local_rows * chan_count
    rows_f32 = inputs.astype(jnp.float32)
    cot_f32 = cotangent.astype(jnp.float32)
    normed, pull_norm = jax.vjp(rms_scale, rows_f32, mix_gain)
    normed_low = normed.astype(jnp.bfloat16)
    gate_full, lift_full, out_full, mlp_gate_full, mlp_up_full, mlp_down_full = (
        lax.all_gather(gate_proj, "chan", axis=1, tiled=True),
        lax.all_gather(lift_proj, "chan", axis=1, tiled=True),
        lax.all_gather(out_proj, "chan", axis=0, tiled=True),
        lax.all_gather(mlp_gate, "chan", axis=1, tiled=True),
        lax.all_gather(mlp_up, "chan", axis=1, tiled=True),
        lax.all_gather(mlp_down, "chan", axis=0, tiled=True),
    )
    channels = LRU
    hidden_cut = FF
    segments = segment_ids(doc_starts, chan_place * local_rows - 3, local_rows + 6, seq_length)
    mix_proj = jnp.concatenate([gate_full, lift_full], axis=1)
    gate_pre, lifted = project(normed_low, mix_proj, gate_bias, lift_bias)
    tail_rows = from_behind(lifted[:, -3:], "chan", 1)
    conv_out = conv_forward(lifted, tail_rows, segments, conv_taps, conv_bias)
    is_reset = segments[3 : 3 + local_rows] != segments[2 : 2 + local_rows]
    (decay_rate, lru_input), pull_coef = jax.vjp(
        partial(coefficients, is_reset),
        conv_out,
        recur_gate,
        recur_bias,
        input_gate,
        input_bias,
        decay_param,
    )
    running, local_state = lax.associative_scan(affine, (decay_rate, lru_input), axis=1)
    ones_vec = jnp.ones((channels,), jnp.float32)
    zeros_vec = jnp.zeros((channels,), jnp.float32)
    _, start_state = prefix(
        (running[:, -1], local_state[:, -1]), "chan", affine, (ones_vec, zeros_vec), False
    )
    lru_state = local_state + running * start_state[:, None]
    gate_val, pull_gelu = jax.vjp(jax.nn.gelu, gate_pre)
    mixed_out = (lru_state * gate_val).astype(jnp.bfloat16)
    resid = (
        rows_f32
        + jnp.einsum("ct,cd->td", mixed_out, out_full, preferred_element_type=jnp.float32)
        + out_bias
    )
    normed2, pull_norm2 = jax.vjp(rms_scale, resid, mlp_gain)
    normed2_low = normed2.astype(jnp.bfloat16)
    mlp_proj = jnp.concatenate([mlp_gate_full, mlp_up_full], axis=1)
    mlp_pre = jnp.einsum("td,df->ft", normed2_low, mlp_proj, preferred_element_type=jnp.float32)
    hidden, pull_mlp = jax.vjp(gated_unit, mlp_pre[:hidden_cut], mlp_pre[hidden_cut:])
    hidden_low = hidden.astype(jnp.bfloat16)
    output = (
        resid
        + jnp.einsum("ft,fd->td", hidden_low, mlp_down_full, preferred_element_type=jnp.float32)
    ).astype(jnp.bfloat16)
    grad_down = jnp.einsum("ft,td->fd", hidden_low, cotangent, preferred_element_type=jnp.float32)
    grad_gate_m, grad_up_m = pull_mlp(
        jnp.einsum("td,fd->ft", cotangent, mlp_down_full, preferred_element_type=jnp.float32)
    )
    grad_pre = jnp.concatenate([grad_gate_m, grad_up_m], axis=0).astype(jnp.bfloat16)
    grad_mlp_in = jnp.einsum("ft,td->fd", grad_pre, normed2_low, preferred_element_type=jnp.float32)
    grad_resid_part, grad_gain2 = pull_norm2(
        jnp.einsum("ft,df->td", grad_pre, mlp_proj, preferred_element_type=jnp.float32)
    )
    grad_resid = cot_f32 + grad_resid_part
    grad_branch = grad_resid.astype(jnp.bfloat16)
    grad_out_proj = jnp.einsum(
        "ct,td->cd", mixed_out, grad_branch, preferred_element_type=jnp.float32
    )
    grad_mixed = jnp.einsum("td,cd->ct", grad_branch, out_full, preferred_element_type=jnp.float32)
    product, carried = reverse_local(decay_rate, grad_mixed * gate_val)
    _, incoming = prefix(
        (decay_rate[:, 0] * product[:, 0], decay_rate[:, 0] * carried[:, 0]),
        "chan",
        affine,
        (ones_vec, zeros_vec),
        True,
    )
    carried = carried + product * incoming[:, None]
    coef_grads = finish_state(lru_state, start_state, carried, pull_coef)
    head_rows = from_behind(coef_grads[0][:, :3], "chan", -1)
    grad_lifted, grad_taps, grad_conv_bias = conv_backward(
        coef_grads[0], head_rows, segments, lifted, tail_rows, conv_taps
    )
    (grad_gate_pre,) = pull_gelu(grad_mixed * lru_state)
    grad_front = jnp.concatenate([grad_gate_pre, grad_lifted], axis=0).astype(jnp.bfloat16)
    grad_mix_proj = jnp.einsum(
        "ct,td->cd", grad_front, normed_low, preferred_element_type=jnp.float32
    )
    grad_normed = jnp.einsum("ct,dc->td", grad_front, mix_proj, preferred_element_type=jnp.float32)
    grad_x_part, grad_gain1 = pull_norm(grad_normed)
    grad_inputs = (grad_resid + grad_x_part).astype(jnp.bfloat16)
    grad_out_bias = jnp.sum(grad_resid, axis=0)
    pieces = [
        grad_mix_proj[:channels],
        grad_mix_proj[channels:],
        jnp.sum(grad_gate_pre, axis=1),
        jnp.sum(grad_lifted, axis=1),
        grad_taps,
        grad_conv_bias,
        jnp.transpose(coef_grads[1], (1, 0, 2)),
        coef_grads[2],
        jnp.transpose(coef_grads[3], (1, 0, 2)),
        coef_grads[4],
        coef_grads[5],
        grad_out_proj,
        grad_mlp_in[:hidden_cut],
        grad_mlp_in[hidden_cut:],
        grad_down,
        grad_gain1,
        grad_out_bias,
        grad_gain2,
    ]
    spread = flatten_rows(pieces, chan_count)
    shared = lax.psum_scatter(spread, "chan", scatter_dimension=0, tiled=True)
    summed = lax.psum(shared.reshape(-1), "rows")
    channels_dev = LRU // chan_count
    hidden_dev = FF // chan_count
    width_dev = D // chan_count
    block_dev = GB // chan_count
    shapes = [
        (channels_dev, D),
        (channels_dev, D),
        (channels_dev,),
        (channels_dev,),
        (channels_dev, 4),
        (channels_dev,),
        (block_dev, HEADS, GB),
        (channels_dev,),
        (block_dev, HEADS, GB),
        (channels_dev,),
        (channels_dev,),
        (channels_dev, D),
        (hidden_dev, D),
        (hidden_dev, D),
        (hidden_dev, D),
        (width_dev,),
        (width_dev,),
        (width_dev,),
    ]
    unpacked = []
    offset = 0
    for piece_shape in shapes:
        piece_size = math.prod(piece_shape)
        unpacked.append(summed[offset : offset + piece_size].reshape(piece_shape))
        offset = offset + piece_size
    return (
        output,
        grad_inputs,
        unpacked[15],
        unpacked[0].T,
        unpacked[2],
        unpacked[1].T,
        unpacked[3],
        unpacked[4].T,
        unpacked[5],
        jnp.transpose(unpacked[6], (1, 0, 2)),
        unpacked[7],
        jnp.transpose(unpacked[8], (1, 0, 2)),
        unpacked[9],
        unpacked[10],
        unpacked[11],
        unpacked[16],
        unpacked[17],
        unpacked[12].T,
        unpacked[13].T,
        unpacked[14],
    )


MESH = pl.DeviceIdType.MESH
LOW = jnp.bfloat16
F32 = jnp.float32
VMEM_BYTES = 63 * 2**20
TILE = 8
GELU_A = math.sqrt(2.0 / math.pi)
GELU_B = 0.044715


def nt(left, right):
    return lax.dot_general(left, right, (((1,), (1,)), ((), ())), preferred_element_type=F32)


def nn(left, right):
    return lax.dot_general(left, right, (((1,), (0,)), ((), ())), preferred_element_type=F32)


def tn(left, right):
    return lax.dot_general(left, right, (((0,), (0,)), ((), ())), preferred_element_type=F32)


def gelu_pair(values):
    squared = values * values
    bend = jnp.tanh(GELU_A * values * (1.0 + GELU_B * squared))
    half = 0.5 * (1.0 + bend)
    slope = half + 0.5 * values * (1.0 - bend * bend) * GELU_A * (1.0 + 3.0 * GELU_B * squared)
    return values * half, slope


class Spot:
    def __init__(self):
        self.r = lax.axis_index("rows")
        self.c = lax.axis_index("chan")
        self.z = lax.div(self.c, 2)
        self.y = lax.rem(self.c, 2)
        self.r_core = self.r + 1 - 2 * lax.rem(self.r, 2)
        self.r_x = lax.rem(self.r + 2, 4)
        self.core = (self.r_core, self.c)
        self.x = (self.r_x, self.c)
        self.c_y = self.c + 1 - 2 * self.y
        self.ymate = (self.r, self.c_y)
        self.up = (self.r, lax.rem(self.c + 2, 8))
        self.dn = (self.r, lax.rem(self.c + 6, 8))


def greet(always, maybe=()):
    barrier = pltpu.get_barrier_semaphore()
    count = len(always)
    for device in always:
        pl.semaphore_signal(barrier, inc=1, device_id=device, device_id_type=MESH)
    for device, there in maybe:

        @pl.when(there)
        def _(device=device):
            pl.semaphore_signal(barrier, inc=1, device_id=device, device_id_type=MESH)

        count = count + jnp.where(there, 1, 0)
    pl.semaphore_wait(barrier, count)


def push(source, target, sems, index, device):
    return pltpu.make_async_remote_copy(
        src_ref=source,
        dst_ref=target,
        send_sem=sems[0].at[index],
        recv_sem=sems[1].at[index],
        device_id=device,
        device_id_type=MESH,
    )


def landed(me, target, sems, index):
    push(target, target, sems, index, me.ymate).wait_recv()


def sem_pair(count):
    return [pltpu.SemaphoreType.DMA((count,)), pltpu.SemaphoreType.DMA((count,))]


def comm_params(collective_id):
    return pltpu.CompilerParams(
        collective_id=collective_id, has_side_effects=True, vmem_limit_bytes=VMEM_BYTES
    )


ANYWHERE = pl.BlockSpec(memory_space=pl.ANY)
IN_VMEM = pl.BlockSpec(memory_space=pltpu.VMEM)


def decay_terms(rec, softplus_row, reset):
    log_decay = -8.0 * rec * softplus_row
    decay = jnp.exp(log_decay)
    twice = 2.0 * log_decay
    series = twice * (
        1.0
        + twice * (1 / 2 + twice * (1 / 6 + twice * (1 / 24 + twice * (1 / 120 + twice * (1 / 720)))))
    )
    gap = jnp.where(twice > -0.25, -series, 1.0 - jnp.exp(twice))
    return decay, jnp.where(reset, 1.0, jnp.sqrt(gap))


def fill_tallies(tallies, starts_row, first, length, seq_length):
    position = first - 8 + lax.broadcasted_iota(jnp.int32, (length + 16, 1), 0)
    begun = jnp.sum((starts_row <= position).astype(F32), axis=1, keepdims=True)
    inside = jnp.logical_and(position >= 0, position < seq_length)
    tallies[...] = jnp.broadcast_to(jnp.where(inside, begun, -1.0), tallies.shape)


def same_document(tallies, length, shift, wide):
    own = tallies[pl.ds(8, length)]
    other = tallies[pl.ds(8 + shift, length)]
    same = (own == other).astype(F32)
    return jnp.concatenate([same] * (wide // same.shape[1]), axis=1)


def pair_diagonal(target, blocks):
    side = blocks.shape[1]
    target[...] = jnp.zeros_like(target)
    target[0:side, 0:side] = blocks[0].astype(target.dtype)
    target[side : 2 * side, side : 2 * side] = blocks[1].astype(target.dtype)


def tile_scan(a, b, backward):
    row = lax.broadcasted_iota(jnp.int32, a.shape, 1)
    for step in (1, 2, 4):
        shift = TILE - step if backward else step
        there = row < TILE - step if backward else row >= step
        b = b + a * jnp.where(there, pltpu.roll(b, shift, 1), 0.0)
        a = a * jnp.where(there, pltpu.roll(a, shift, 1), 1.0)
    return a, b


def carry_start(me, backward, totals, slots, sems):
    sign = -1 if backward else 1
    steps = me.c if backward else 7 - me.c
    copies = [
        push(totals, slots.at[d], sems, d, (me.r, lax.rem(me.c + 8 + sign * d, 8)))
        for d in range(1, 8)
    ]
    for d in range(1, 8):

        @pl.when(d <= steps)
        def _(d=d):
            copies[d - 1].start()

    return copies


def carry_join(me, backward, slots, start, sems):
    behind = 7 - me.c if backward else me.c
    start[...] = jnp.zeros_like(start)
    for d in range(7, 0, -1):

        @pl.when(d <= behind)
        def _(d=d):
            landed(me, slots.at[d], sems, d)
            start[...] = slots[d, :, 0] * start[...] + slots[d, :, 1]


def carry_sent(me, backward, copies):
    steps = me.c if backward else 7 - me.c
    for d in range(1, 8):

        @pl.when(d <= steps)
        def _(d=d):
            copies[d - 1].wait_send()


def peers_of(me):
    return [(me.r, lax.rem(me.c + d, 8)) for d in range(1, 8)]


class Spread:
    def __init__(self, me, slabs, pieces, sems):
        self.me, self.slabs, self.pieces, self.sems = me, slabs, pieces, sems
        self.go_up = jnp.logical_and(me.z >= me.r, me.z < 3)
        self.go_dn = jnp.logical_and(me.z <= me.r, me.z > 0)
        self.source = me.z == me.r
        self.hop = jnp.where(me.z < me.r, me.r - me.z, me.z - me.r)

    def copies(self, k):
        me, found = self.me, []
        for i, slab in enumerate(self.slabs):
            piece = slab(k, me.y)
            ys, yr, us, ds, zr = self.sems[5 * i : 5 * i + 5]
            found.append(
                (
                    push(piece, piece, (ys, yr), k, me.ymate),
                    push(piece, piece, (us, zr), k, me.up),
                    push(piece, piece, (ds, zr), k, me.dn),
                )
            )
        return found

    def send(self, k):
        found = self.copies(k)
        for copies in found:
            copies[0].start()

        @pl.when(self.go_up)
        def _():
            for copies in found:
                copies[1].start()

        @pl.when(self.go_dn)
        def _():
            for copies in found:
                copies[2].start()

    def follow(self, k):
        for i, slab in enumerate(self.slabs):
            us, zr = self.sems[5 * i + 2], self.sems[5 * i + 4]
            landed(self.me, slab(k, self.me.y), (us, zr), k)
        self.send(k)

    def step(self, q):
        n = self.pieces

        def at(k, also, action):
            there = jnp.logical_and(k >= 0, k < n)

            @pl.when(jnp.logical_and(there, also))
            def _():
                action(lax.rem(k + 8 * n, n))

        at(q + SPREAD_AHEAD, self.source, self.send)
        at(q - SPREAD_LAG * (self.hop - 1), jnp.logical_not(self.source), self.follow)

    def reach(self):
        return -SPREAD_AHEAD, self.pieces + 2 * SPREAD_LAG

    def arrived(self):
        @pl.loop(0, self.pieces)
        def _(k):
            for i, slab in enumerate(self.slabs):
                ys, yr = self.sems[5 * i], self.sems[5 * i + 1]
                landed(self.me, slab(k, 1 - self.me.y), (ys, yr), k)

    def close(self):
        @pl.loop(0, self.pieces)
        def _(k):
            found = self.copies(k)
            for copies in found:
                copies[0].wait_send()

            @pl.when(self.go_up)
            def _():
                for copies in found:
                    copies[1].wait_send()

            @pl.when(self.go_dn)
            def _():
                for copies in found:
                    copies[2].wait_send()


SPREAD_AHEAD = 4
SPREAD_LAG = 1


def spread_sems(arrays, pieces):
    return [pltpu.SemaphoreType.DMA((pieces,))] * (5 * arrays)


AHEAD = 3
HOP_LAG = 3
END_LAG = 10
RELAY_LAG = 13


class Reduce:
    def __init__(self, me, parts, mine, from_y, from_z, own, pieces, sems):
        self.me, self.parts, self.mine = me, parts, mine
        self.from_y, self.from_z, self.own = from_y, from_z, own
        self.pieces, self.sems = pieces, sems
        self.hop = jnp.where(me.z < me.r, me.z, 3 - me.z)
        self.owner = me.z == me.r
        self.relays = me.z == me.r_x

    def rows(self, i, k):
        size = self.mine[i].shape[0] // self.pieces
        return pl.ds(pl.multiple_of(k * size, 16), size)

    def each(self, k):
        for i in range(len(self.mine)):
            yield i, self.rows(i, k), self.sems[11 * i : 11 * i + 11]

    def y_copies(self, k):
        me = self.me
        return [
            push(self.parts[i].at[1 - me.y, rows], self.from_y[i].at[rows], sems[0:2], k, me.ymate)
            for i, rows, sems in self.each(k)
        ]

    def y_send(self, k):
        for copy in self.y_copies(k):
            copy.start()

    def add(self, i, rows, other):
        total = self.mine[i][rows].astype(F32) + other[i][rows].astype(F32)
        self.mine[i][rows] = total.astype(LOW)

    def join(self, k):
        for i, rows, sems in self.each(k):
            landed(self.me, self.from_y[i].at[rows], sems[0:2], k)
            self.add(i, rows, self.from_y)

    def z_copies(self, k, way):
        found = []
        for i, rows, sems in self.each(k):
            target = self.own if way == 2 else self.from_z
            pair = ((sems[2], sems[4]), (sems[3], sems[4]), (sems[3], sems[5]))[way]
            found.append(
                push(self.mine[i].at[rows], target[i].at[rows], pair, k,
                     self.me.up if way == 0 else self.me.dn)
            )
        return found

    def z_way(self, action):
        me = self.me
        for way, there in enumerate(
            (me.z < me.r, me.z > me.r + 1, me.z == me.r + 1)
        ):

            @pl.when(there)
            def _(way=way):
                action(way)

    def chain(self, k):
        @pl.when(self.hop > 0)
        def _():
            for i, rows, sems in self.each(k):
                landed(self.me, self.from_z[i].at[rows], (sems[2], sems[4]), k)
                self.add(i, rows, self.from_z)

        def start(way):
            for copy in self.z_copies(k, way):
                copy.start()

        self.z_way(start)

    def out_copies(self, k, device, pair):
        return [
            push(self.own[i].at[rows], self.own[i].at[rows], sems[pair : pair + 2], k, device)
            for i, rows, sems in self.each(k)
        ]

    def finish(self, k):
        @pl.when(self.me.z > 0)
        def _():
            for i, rows, sems in self.each(k):
                landed(self.me, self.from_z[i].at[rows], (sems[2], sems[4]), k)
                self.add(i, rows, self.from_z)

        @pl.when(self.me.z < 3)
        def _():
            for i, rows, sems in self.each(k):
                landed(self.me, self.own[i].at[rows], (sems[3], sems[5]), k)
                self.add(i, rows, self.own)

        for i, rows, sems in self.each(k):
            self.own[i][rows] = self.mine[i][rows]
        for copy in self.out_copies(k, self.me.x, 6) + self.out_copies(k, self.me.core, 8):
            copy.start()

    def relay(self, k):
        for copy in self.out_copies(k, self.me.x, 6):
            copy.wait_recv()
        for copy in self.out_copies(k, self.me.core, 8):
            copy.start()

    def step(self, q):
        n = self.pieces

        def at(k, also, action):
            there = jnp.logical_and(k >= 0, k < n)

            @pl.when(there if also is None else jnp.logical_and(there, also))
            def _():
                action(lax.rem(k + 8 * n, n))

        at(q + AHEAD, None, self.y_send)
        at(q, None, self.join)
        at(q - HOP_LAG * self.hop, jnp.logical_not(self.owner), self.chain)
        at(q - END_LAG, self.owner, self.finish)
        at(q - RELAY_LAG, self.relays, self.relay)

    def reach(self):
        return -AHEAD, self.pieces + RELAY_LAG

    def close(self):
        others = jnp.logical_not(jnp.logical_or(self.owner, self.relays))

        @pl.loop(0, self.pieces)
        def _(k):
            for copy in self.y_copies(k):
                copy.wait_send()

            def sent(way):
                for copy in self.z_copies(k, way):
                    copy.wait_send()

            self.z_way(sent)

            @pl.when(self.owner)
            def _():
                for copy in self.out_copies(k, self.me.x, 6) + self.out_copies(k, self.me.core, 8):
                    copy.wait_send()

            @pl.when(self.relays)
            def _():
                for copy in self.out_copies(k, self.me.core, 8):
                    copy.wait_send()

            @pl.when(others)
            def _():
                for copy in self.out_copies(k, self.me.core, 8):
                    copy.wait_recv()


class Line:
    def __init__(self, reduces, offsets):
        self.reduces, self.offsets = reduces, offsets
        self.done = reduces[0].reach()[0]

    def position(self, p, low, high):
        for one, offset in zip(self.reduces, self.offsets):
            first, last = one.reach()
            if offset + first < high and low < offset + last:
                one.step(p - offset)

    def advance(self, high):
        low, self.done = self.done, max(self.done, high)
        if high > low + 1:

            @pl.loop(low, high)
            def _(p):
                self.position(p, low, high)

        elif high > low:
            self.position(low, low, high)

    def ready(self, i):
        assert self.done <= self.offsets[i] + self.reduces[i].reach()[0]

    def during(self, begin, end, action):
        low, self.done = self.done, self.done + end - begin

        @pl.loop(begin, end)
        def _(s):
            action(s)
            self.position(low - begin + s, low, low + end - begin)

    def last(self):
        return self.offsets[-1] + self.reduces[-1].reach()[1]

    def close(self):
        for one in self.reduces:
            one.close()


def reduce_sems(arrays, pieces):
    return [pltpu.SemaphoreType.DMA((pieces,))] * (11 * arrays)


RS_CHUNKS = 4


class RowsSum:
    def __init__(self, me, part, mate, out_x, in_x, core_sems, x_sems):
        self.me, self.part, self.mate, self.out_x, self.in_x = me, part, mate, out_x, in_x
        self.size = part.shape[1] // RS_CHUNKS
        far = lax.rem(me.r_core + 2, 4)
        self.to_core = [
            [
                push(part.at[owner, self.rows(k)], mate.at[block, self.rows(k)], core_sems,
                     block * RS_CHUNKS + k, me.core)
                for k in range(RS_CHUNKS)
            ]
            for block, owner in enumerate((far, me.r_core))
        ]
        self.to_x = [
            push(out_x.at[self.rows(k)], in_x.at[self.rows(k)], x_sems, k, me.x)
            for k in range(RS_CHUNKS)
        ]

    def rows(self, k):
        return pl.ds(k * self.size, self.size)

    def start(self, block, chunks=range(RS_CHUNKS)):
        for k in chunks:
            self.to_core[block][k].start()

    def cross(self, chunks=range(RS_CHUNKS)):
        for k in chunks:
            rows = self.rows(k)
            self.to_core[0][k].wait_recv()
            total = self.part[self.me.r_x, rows].astype(F32) + self.mate[0, rows].astype(F32)
            self.out_x[rows] = total.astype(LOW)
            self.to_x[k].start()

    def total(self, k):
        rows = self.rows(k)
        self.to_core[1][k].wait_recv()
        self.to_x[k].wait_recv()
        return (
            self.part[self.me.r, rows].astype(F32) + self.mate[1, rows].astype(F32)
            + self.in_x[rows].astype(F32)
        )

    def close(self):
        for copy in self.to_core[0] + self.to_core[1] + self.to_x:
            copy.wait_send()


class Share:
    def __init__(self, me, array, x_sems, core_sems):
        size = array.shape[1] // RS_CHUNKS

        def piece(row, k):
            return array.at[row, pl.ds(k * size, size)]

        self.to_x = [
            push(piece(me.r, k), piece(me.r, k), x_sems, k, me.x) for k in range(RS_CHUNKS)
        ]
        self.to_core = [
            push(piece(me.r, k), piece(me.r, k), core_sems, k, me.core) for k in range(RS_CHUNKS)
        ]
        self.passed = [
            push(piece(me.r_x, k), piece(me.r_x, k), core_sems, RS_CHUNKS + k, me.core)
            for k in range(RS_CHUNKS)
        ]

    def send(self, k):
        self.to_x[k].start()
        self.to_core[k].start()

    def relay(self, k):
        self.to_x[k].wait_recv()
        self.passed[k].start()

    def arrived(self, k):
        self.to_core[k].wait_recv()
        self.passed[k].wait_recv()

    def close(self):
        for copy in self.to_x + self.to_core + self.passed:
            copy.wait_send()


def finish_sends(copies):
    for copy in copies:
        copy.wait_send()


class Bag:
    def __init__(self, names, refs):
        self.__dict__.update(zip(names, refs))


MLP_BLOCKS = 3
VECTORS = ("gate_bias", "lift_bias", "conv_bias", "recur_bias", "input_bias", "decay_param")
LANES = 128


def block_kernel(names, *refs):
    R = Bag(names, refs)
    me = Spot()
    r, c, z, y = me.r, me.c, me.z, me.y
    length, width = R.inputs.shape
    seq_length = length * 8
    wide = 2 * R.gp.shape[0]
    side = wide // 2
    step = length // RS_CHUNKS
    tokens_all = 4 * length
    tiles = (length // TILE, TILE, wide)
    diag = (me.r_x + 1 - 2 * lax.rem(me.r_x, 2), c)
    row_peers = (me.core, me.x, diag)
    chan_peers = peers_of(me)
    x_place, core_place = lax.div(r, 2), lax.rem(r, 2)

    def far_first(i):
        return 2 * lax.rem(x_place + 1 + lax.div(i, 2), 2) + lax.rem(core_place + 1 + lax.rem(i, 2), 2)

    vec, taps = R.vec, R.taps
    keep = dict(gate_pre=R.gate_h, lext=R.lext_h, conv=R.conv_h, rec=R.rec_h, opening=R.open_h,
                state=R.state_h, mixed_t=R.mixed_h)

    def tallies_of(s):
        fill_tallies(R.tallies, R.starts_all[s, 0:1], c * length, length, seq_length)

    def same(shift):
        return same_document(R.tallies, length, shift, wide)


    glo = [
        Spread(me, [lambda k, half, m=m: R.wq.at[m, half, pl.ds(pl.multiple_of(k * 48, 16), 48)]], 4,
               R.spread[5 * m : 5 * m + 5])
        for m in range(3)
    ]

    def mlp_slab(b):
        size = width // 8

        def slab(k, half):
            rows = pl.ds(pl.multiple_of(k * size, 16), size)
            return R.w.at[b, rows, pl.ds(pl.multiple_of(half * 3 * LANES, LANES), 3 * LANES)]

        return slab

    mlp_w = [
        Spread(me, [mlp_slab(b)], 8, R.spread[15 + 5 * b : 20 + 5 * b]) for b in range(MLP_BLOCKS)
    ]
    sline = Line([glo[2]] + mlp_w, (0, 4, 12, 20))

    part = R.opart
    sum1 = RowsSum(me, part, R.mate, R.out_x, R.in_x, (R.ms, R.mr), (R.rxs, R.rxr))

    def forward(gate_pre, lext, conv, rec, opening, a, b, mixed_t, rg32, ig32, md_v):
        barrier = pltpu.get_barrier_semaphore()
        always = list(row_peers) + chan_peers
        for device in always:
            pl.semaphore_signal(barrier, inc=1, device_id=device, device_id_type=MESH)
        count = len(always)
        for there, place in ((c < 7, lax.rem(c + 1, 8)), (c > 0, lax.rem(c + 7, 8))):
            for i in (1, 2, 3):

                @pl.when(there)
                def _(i=i, place=place):
                    pl.semaphore_signal(
                        barrier, inc=1, device_id=(lax.rem(r + i, 4), place), device_id_type=MESH
                    )

            count = count + jnp.where(there, 3, 0)
        own = [
            pltpu.make_async_copy(R.gp, R.wq.at[0, y], R.loc.at[12]),
            pltpu.make_async_copy(R.lp, R.wq.at[1, y], R.loc.at[13]),
            pltpu.make_async_copy(R.op, R.wq.at[2, y], R.loc.at[0]),
            pltpu.make_async_copy(R.md, md_v, R.loc.at[14]),
        ]
        for blk in range(MLP_BLOCKS):
            lanes = pl.ds(blk * LANES, LANES)
            for i, (source, at) in enumerate(
                ((R.mg, 4 * y), (R.mu, 4 * y + 1))
            ):
                column = pl.ds(pl.multiple_of(at * LANES, LANES), LANES)
                own.append(
                    pltpu.make_async_copy(
                        source.at[:, lanes], R.w.at[blk, :, column], R.loc.at[1 + 2 * blk + i]
                    )
                )

        @pl.when(z == r)
        def _():
            for copy in own:
                copy.start()

        heads = [
            pltpu.make_async_copy(R.rgate_all.at[pl.ds(2 * r, 2)], rg32, R.loc.at[10]),
            pltpu.make_async_copy(R.igate_all.at[pl.ds(2 * r, 2)], ig32, R.loc.at[11]),
        ]
        for copy in heads:
            copy.start()
        R.call[r] = R.cot[...]
        vals = R.inputs[...].astype(F32)
        scale = lax.rsqrt(jnp.mean(vals * vals, axis=-1, keepdims=True) + EPSILON)
        R.nall[r] = (vals * scale * R.mix_gain[...]).astype(LOW)
        R.starts_all[r] = jnp.full(R.starts_all.shape[1:], jnp.iinfo(jnp.int32).max, jnp.int32)
        R.starts_all[r, 0:1, 0 : R.starts.shape[1]] = R.starts[...]
        mine = pl.ds(pl.multiple_of(r * wide, LANES), wide)
        count_rows = wide // LANES
        for i, name in enumerate(VECTORS):
            for k in range(count_rows):
                place = pl.ds(r * count_rows + k, 1)
                vec[i : i + 1, k * LANES : (k + 1) * LANES] = getattr(R, name)[place]
        decay = vec[5:6]
        vec[5:6] = jnp.log1p(jnp.exp(-decay))
        vec[6:7] = jax.nn.sigmoid(-decay)
        taps[...] = R.conv_taps[:, mine]

        @pl.when(z == r)
        def _():
            for copy in own[:2]:
                copy.wait()

        pl.semaphore_wait(barrier, count)

        mine_n, mine_c = R.nall.at[r], R.call.at[r]
        theirs_n, theirs_c = R.nall.at[me.r_x], R.call.at[me.r_x]
        x_n = push(mine_n, mine_n, (R.xs, R.xr), 0, me.x)
        c_n = push(mine_n, mine_n, (R.cs, R.cr), 0, me.core)
        c_c = push(mine_c, mine_c, (R.cs, R.cr), 1, me.core)
        x_c = push(mine_c, mine_c, (R.xs, R.xr), 1, me.x)
        fwd_n = push(theirs_n, theirs_n, (R.cs, R.cr), 2, me.core)
        fwd_c = push(theirs_c, theirs_c, (R.cs, R.cr), 3, me.core)
        s_copies = [
            push(R.starts_all.at[r], R.starts_all.at[r], (R.ss, R.sr), i, device)
            for i, device in enumerate(row_peers)
        ]
        tail = R.nall.at[r, pl.ds(length - 16, 16)]
        halo_copies = [
            push(tail, R.halo.at[r], (R.hs, R.hr), i, (lax.rem(r + i, 4), lax.rem(c + 1, 8)))
            for i in range(4)
        ]
        x_n.start()
        x_c.start()
        for copy in s_copies:
            copy.start()

        @pl.when(c < 7)
        def _():
            for copy in halo_copies:
                copy.start()

        c_n.start()
        c_c.start()

        @pl.when(c == 0)
        def _():
            R.halo[...] = jnp.zeros_like(R.halo)

        for m in range(2):
            for k in range(4):

                @pl.when(z == r)
                def _(m=m, k=k):
                    glo[m].send(k)

                @pl.when(z != r)
                def _(m=m, k=k):
                    glo[m].follow(k)

            if m == 0:
                for copy in heads:
                    copy.wait()
                pair_diagonal(R.rgate, rg32)
                pair_diagonal(R.igate, ig32)
        x_n.wait_recv()
        fwd_n.start()

        @pl.when(z == r)
        def _():
            for copy in own[2:]:
                copy.wait()
            column = pl.ds(pl.multiple_of((2 + y) * LANES, LANES), LANES)
            for blk in range(MLP_BLOCKS):
                R.w[blk, :, column] = md_v[blk * LANES : (blk + 1) * LANES].T

        sline.advance(0)
        glo[0].arrived()
        glo[1].arrived()
        c_n.wait_recv()
        fwd_n.wait_recv()
        for copy in s_copies:
            copy.wait_recv()

        @pl.when(c > 0)
        def _():
            for i in range(4):
                landed(me, R.halo.at[i], (R.hs, R.hr), i)

        def mixer_one(s):
            tallies_of(s)
            tokens = R.nall[s]
            wgate = R.wq[0].reshape(wide, width)
            wlift = R.wq[1].reshape(wide, width)
            gate_pre[s] = nt(tokens, wgate) + vec[0:1]
            lifted = nt(tokens, wlift) + vec[1:2]
            lext[s, 0:8] = (nt(R.halo[s], wlift) + vec[1:2])[8:16]
            lext[s, pl.ds(8, length)] = lifted
            out = vec[2:3] + taps[0:1] * lifted
            for k in range(1, 4):
                out = out + taps[k : k + 1] * lext[s, pl.ds(8 - k, length)] * same(-k)
            conv[s] = out
            low = out.astype(LOW)
            recur = jax.nn.sigmoid(nn(low, R.rgate[...]) + vec[3:4])
            opened = jax.nn.sigmoid(nn(low, R.igate[...]) + vec[4:5])
            rec[s] = recur
            opening[s] = opened
            reset = same(-1) < 0.5
            decay, scaling = decay_terms(recur, vec[5:6], reset)
            decay = jnp.where(reset, 0.0, decay)
            a_scan, b_scan = tile_scan(
                decay.reshape(tiles), (scaling * opened * out).reshape(tiles), False
            )
            a[s] = a_scan.reshape(length, wide)
            b[s] = b_scan.reshape(length, wide)
            product = jnp.ones((1, wide), F32)
            state = jnp.zeros((1, wide), F32)
            for t in range(length // TILE):
                last = t * TILE + TILE - 1
                a_last = a[s, last : last + 1]
                state = b[s, last : last + 1] + a_last * state
                product = product * a_last
            R.tot[s, 0:1] = product
            R.tot[s, 1:2] = state

        sline.during(0, 4, mixer_one)
        carry_copies = carry_start(me, False, R.tot, R.slots, (R.ps, R.pr))
        local = dict(gate_pre=gate_pre, lext=lext, conv=conv, rec=rec, opening=opening, state=b,
                     mixed_t=mixed_t)
        saved = {
            name: pltpu.make_async_copy(local[name], keep[name], R.outs.at[i])
            for i, name in enumerate(keep)
        }
        for name in ("gate_pre", "lext", "conv", "rec", "opening"):
            saved[name].start()
        sline.advance(6)
        x_c.wait_recv()
        fwd_c.start()
        sline.advance(8)
        carry_join(me, False, R.slots, R.start, (R.ps, R.pr))
        sline.advance(4 + 2 * SPREAD_LAG)
        glo[2].arrived()

        def mixer_two(i):
            s = far_first(i)
            state = R.start[pl.ds(s, 1)]
            for t in range(length // TILE):
                tile = pl.ds(t * TILE, TILE)
                now = b[s, tile] + a[s, tile] * state
                b[s, tile] = now
                state = now[TILE - 1 : TILE]
            gate_val, _ = gelu_pair(gate_pre[s])
            mix = (b[s] * gate_val).astype(LOW)
            mixed_t[:, pl.ds(pl.multiple_of(s * length, LANES), length)] = mix.T
            part[s] = nn(mix, R.wq[2].reshape(wide, width)).astype(LOW)

        sline.during(0, 2, mixer_two)
        sum1.start(0)
        sline.during(2, 3, mixer_two)
        sum1.start(1)
        sum1.cross((0, 1, 2))
        sline.during(3, 4, mixer_two)
        for name in ("state", "mixed_t"):
            saved[name].start()
        for m in range(3):
            glo[m].close()
        for copy in (x_n, x_c, c_n, fwd_n):
            copy.wait_send()
        c_c.wait()
        fwd_c.wait()
        finish_sends(s_copies)

        @pl.when(c < 7)
        def _():
            finish_sends(halo_copies)

        carry_sent(me, False, carry_copies)
        for copy in saved.values():
            copy.wait()

    tall = pltpu.VMEM((4, length, wide), F32)
    ext = pltpu.VMEM((4, length + TILE, wide), F32)
    low_t = pltpu.VMEM((wide, tokens_all), LOW)
    pl.run_scoped(
        forward, gate_pre=tall, lext=ext, conv=tall, rec=tall, opening=tall, a=tall, b=tall,
        mixed_t=low_t, rg32=pltpu.VMEM((2, GB, GB), F32),
        ig32=pltpu.VMEM((2, GB, GB), F32), md_v=pltpu.VMEM(R.md.shape, LOW),
    )


    groups = [R.reduce[11 * i : 11 * i + 11] for i in range(MLP_BLOCKS)]
    rest = R.reduce[11 * MLP_BLOCKS :]
    line = Line(
        [
            Reduce(
                me, [R.grad.at[blk]], [R.grad.at[blk, y]], [R.y_w.at[blk]], [R.z_w.at[blk]],
                [R.own_w.at[:, pl.ds(blk * 3 * LANES, 3 * LANES)]], 8, groups[blk],
            )
            for blk in range(MLP_BLOCKS)
        ]
        + [
            Reduce(me, [R.early], [R.early.at[y]], [R.y_e], [R.z_e], [R.own_e], 8, rest[:11]),
            Reduce(me, [R.late], [R.late.at[y]], [R.y_l], [R.z_l], [R.own_l], 7, rest[11:]),
        ],
        (0, 8, 16, 24, 33),
    )
    half = length // 2

    def mlp(acc_out, acc_in, n2_t, hid, low_a, low_b, gpart):
        share1 = Share(me, R.n2all, (R.ax, R.bx), (R.ac, R.bc))

        def norm_chunk(k):
            rows = pl.ds(k * step, step)
            res = R.inputs[rows].astype(F32) + sum1.total(k) + R.out_bias[...]
            R.resid[rows] = res
            scale = lax.rsqrt(jnp.mean(res * res, axis=-1, keepdims=True) + EPSILON)
            R.n2all[r, rows] = (res * scale * R.mlp_gain[...]).astype(LOW)
            share1.send(k)

        def turn(h):
            @pl.loop(0, 4)
            def _(s):
                at = pl.ds(pl.multiple_of(s * length + h * half, LANES), half)
                n2_t[:, at] = R.n2all[s, pl.ds(h * half, half)].T

        def mlp_tokens(blk, h, i):
            pair = pl.ds(2 * lax.rem(x_place + 1 + i, 2), 2)
            rows = pl.ds(h * half, half)
            fold = lambda v: v.reshape(2, half, v.shape[1])
            flat = lambda v: v.reshape(2 * half, v.shape[2])
            tokens, cot = flat(R.n2all[pair, rows]), flat(R.call[pair, rows])
            sides = (slice(0, 2 * LANES), slice(4 * LANES, 6 * LANES))
            across = slice(2 * LANES, 4 * LANES)
            first, second = [nn(tokens, R.w[blk, :, side_of]) for side_of in sides]
            gate = jnp.concatenate([first[:, :LANES], second[:, :LANES]], axis=1)
            up = jnp.concatenate([first[:, LANES:], second[:, LANES:]], axis=1)
            grad_hidden = nn(cot, R.w[blk, :, across])
            gate_val, slope = gelu_pair(gate)
            hidden = (gate_val * up).astype(LOW)
            grad_gate = (grad_hidden * up * slope).astype(LOW)
            grad_up = (grad_hidden * gate_val).astype(LOW)
            kept = blk % 2
            hid[kept, pair, rows] = fold(hidden)
            lows = [
                jnp.concatenate([grad_gate[:, at], grad_up[:, at]], axis=1)
                for at in (slice(0, LANES), slice(LANES, 2 * LANES))
            ]
            low_a[kept, pair, rows] = fold(lows[0])
            low_b[kept, pair, rows] = fold(lows[1])
            out = fold(nt(hidden, R.w[blk, :, across]))
            back = fold(nt(lows[0], R.w[blk, :, sides[0]]) + nt(lows[1], R.w[blk, :, sides[1]]))
            if blk == 0:
                acc_out[pair, rows] = out
                acc_in[pair, rows] = back
            elif blk < MLP_BLOCKS - 1:
                acc_out[pair, rows] += out
                acc_in[pair, rows] += back
            else:
                R.opart[pair, rows] = (acc_out[pair, rows] + out).astype(LOW)
                gpart[pair, rows] = (acc_in[pair, rows] + back).astype(LOW)

        def mlp_weights(blk):
            kept = blk % 2
            columns = lambda i: pl.ds(pl.multiple_of(i * 256, 256), 256)
            flat = lambda v: v.reshape(tokens_all, v.shape[2])
            hid_t = flat(hid[kept]).T

            @pl.loop(0, width // 256)
            def _(i):
                at = columns(i)
                down = nn(hid_t, flat(R.call[:, :, at])).astype(LOW).T
                for j, low in enumerate((low_a, low_b)):
                    R.grad[blk, j, at, 0 : 2 * LANES] = nn(n2_t[at], flat(low[kept])).astype(LOW)
                    R.grad[blk, j, at, 2 * LANES :] = down[:, j * LANES : (j + 1) * LANES]

        def weights_here(blk):
            sline.advance(max(sline.done, sline.offsets[1 + blk] + 8 + 2 * SPREAD_LAG))
            mlp_w[blk].arrived()

        norm_chunk(0)
        sline.advance(17)
        norm_chunk(1)
        sum1.cross((3,))
        sline.advance(19)
        norm_chunk(2)
        for k in range(2):
            share1.relay(k)
            sline.advance(20 + k)
        for k in range(2):
            share1.arrived(k)
        weights_here(0)
        turn(0)
        sline.during(0, 2, lambda i: mlp_tokens(0, 0, i))
        norm_chunk(3)
        share1.relay(2)
        weights_here(1)
        sline.during(0, 2, lambda i: mlp_tokens(1, 0, i))
        share1.relay(3)
        for k in range(2, RS_CHUNKS):
            share1.arrived(k)
        turn(1)
        sline.during(0, 2, lambda i: mlp_tokens(0, 1, i))
        sline.during(0, 2, lambda i: mlp_tokens(1, 1, i))
        mlp_weights(0)
        sline.advance(max(sline.done, sline.offsets[3] + 8 + 2 * SPREAD_LAG))
        mlp_weights(1)
        weights_here(2)
        line.ready(1)
        line.advance(0)
        sum1.close()
        share1.close()
        sum2 = RowsSum(me, gpart, R.mate, R.out_x, R.in_x, (R.m2s, R.m2r), (R.rx2s, R.rx2r))
        line.during(0, 2, lambda i: mlp_tokens(2, 0, i))
        for block in range(2):
            sum2.start(block, (0, 1))
        line.during(0, 1, lambda i: mlp_tokens(2, 1, i))
        sum2.cross((0, 1))
        line.during(1, 2, lambda i: mlp_tokens(2, 1, i))
        for block in range(2):
            sum2.start(block, (2, 3))
        mlp_weights(2)
        line.ready(2)
        line.advance(5)
        sum2.cross((2, 3))
        ball = R.n2all
        share2 = Share(me, ball, (R.a2x, R.b2x), (R.a2c, R.b2c))
        gain_sum = 0.0
        bias_sum = 0.0
        for k in range(RS_CHUNKS):
            rows = pl.ds(k * step, step)
            grad = sum2.total(k)
            res = R.resid[rows]
            scale = lax.rsqrt(jnp.mean(res * res, axis=-1, keepdims=True) + EPSILON)
            gain_sum = gain_sum + jnp.sum(grad * res * scale, axis=0, keepdims=True)
            pulled = grad * R.mlp_gain[...]
            inner = jnp.mean(pulled * res, axis=-1, keepdims=True)
            total = R.cot[rows].astype(F32) + scale * pulled - res * (scale * scale * scale * inner)
            bias_sum = bias_sum + jnp.sum(total, axis=0, keepdims=True)
            R.gresid[rows] = total
            ball[r, rows] = total.astype(LOW)
            share2.send(k)
            line.advance(6 + k)
        R.gain_keep[0:1] = gain_sum
        R.gain_keep[1:2] = bias_sum
        for k in range(RS_CHUNKS):
            share2.relay(k)
            line.advance(10 + k)
        for k in range(RS_CHUNKS):
            share2.arrived(k)
        share2.close()
        sum2.close()

    kept = pltpu.VMEM((2, 4, length, 2 * LANES), LOW)
    pl.run_scoped(
        mlp, acc_out=pltpu.VMEM((4, length, width), F32), acc_in=pltpu.VMEM((4, length, width), F32),
        n2_t=pltpu.VMEM((width, tokens_all), LOW), hid=kept, low_a=kept, low_b=kept,
        gpart=pltpu.VMEM((4, length, width), LOW),
    )
    for one in mlp_w:
        one.close()


    def backward(gate_pre, conv, rec, opening, state, a, b, gconv, gate_low, gate_t, mixed_t, acc_r,
                 acc_i, prev_ext):
        local = dict(gate_pre=gate_pre, conv=conv, rec=rec, opening=opening, state=state,
                     mixed_t=mixed_t)
        loads = [
            pltpu.make_async_copy(keep[name], ref, R.outs.at[i])
            for i, (name, ref) in enumerate(local.items())
        ]
        for copy in loads:
            copy.start()
        ball = R.n2all
        sum3 = RowsSum(me, R.opart, R.o_mate, R.o_out, R.o_in, (R.oms, R.omr), (R.oxs, R.oxr))
        for block in range(2):
            sum3.start(block)
        for copy in loads:
            copy.wait()
        acc_r[...] = jnp.zeros_like(acc_r)
        acc_i[...] = jnp.zeros_like(acc_i)
        R.sums[...] = jnp.zeros_like(R.sums)

        def reset_of(s):
            tallies_of(s)
            return same(-1) < 0.5

        def mixer_three(s):
            grad_mixed = nt(ball[s], R.wq[2].reshape(wide, width))
            gate_val, slope = gelu_pair(gate_pre[s])
            grad_gate = grad_mixed * state[s] * slope
            low = grad_gate.astype(LOW)
            gate_low[s] = low
            gate_t[:, pl.ds(pl.multiple_of(s * length, LANES), length)] = low.T
            R.sums[0:1] += jnp.sum(grad_gate, axis=0, keepdims=True)
            grad_state = grad_mixed * gate_val
            gate_pre[s] = grad_state
            decay = jnp.where(reset_of(s), 0.0, jnp.exp(-8.0 * rec[s] * vec[5:6]))
            a_scan, b_scan = tile_scan(
                decay.reshape(tiles), (decay * grad_state).reshape(tiles), True
            )
            a[s, 0:length] = a_scan.reshape(length, wide)
            b[s] = b_scan.reshape(length, wide)
            product = jnp.ones((1, wide), F32)
            carried = jnp.zeros((1, wide), F32)
            for t in range(length // TILE - 1, -1, -1):
                head = t * TILE
                a_head = a[s, head : head + 1]
                carried = b[s, head : head + 1] + a_head * carried
                product = product * a_head
            R.tot[s, 0:1] = product
            R.tot[s, 1:2] = carried

        line.during(0, 4, mixer_three)
        carry_copies = carry_start(me, True, R.tot, R.slots2, (R.p2s, R.p2r))
        columns = lambda i: pl.ds(pl.multiple_of(i * 256, 256), 256)

        def weight_grad(target, at, left_t, right):
            @pl.loop(0, width // 256)
            def _(i):
                product = nn(left_t[...], right[:, :, columns(i)].reshape(tokens_all, 256)).astype(LOW)
                for j in range(2):
                    target[j, at : at + side, columns(i)] = product[j * side : (j + 1) * side]

        weight_grad(R.early, 0, mixed_t, ball)
        weight_grad(R.early, side, gate_t, R.nall)
        line.ready(3)
        sum3.cross()
        line.advance(20)
        carry_join(me, True, R.slots2, R.carry, (R.p2s, R.p2r))

        def mixer_four(s):
            now = R.carry[pl.ds(s, 1)]
            gconv[s, pl.ds(length, TILE)] = jnp.broadcast_to(now, (TILE, wide))
            for t in range(length // TILE - 1, -1, -1):
                rows = pl.ds(t * TILE, TILE)
                moved = b[s, rows] + a[s, rows] * now
                gconv[s, rows] = moved
                now = moved[0:1]
            carried = gate_pre[s] + gconv[s, pl.ds(1, length)]
            prev_ext[0:TILE] = jnp.broadcast_to(R.start[pl.ds(s, 1)], (TILE, wide))
            prev_ext[pl.ds(TILE, length)] = state[s]
            previous = prev_ext[pl.ds(TILE - 1, length)]
            recur, opened, conv_s = rec[s], opening[s], conv[s]
            reset = reset_of(s)
            decay, scaling = decay_terms(recur, vec[5:6], reset)
            pulled = carried * scaling
            grad_opening = pulled * conv_s
            grad_log = carried * (previous * decay - opened * conv_s * (decay * decay / scaling))
            grad_log = jnp.where(reset, 0.0, grad_log)
            grad_rec = grad_log * (-8.0 * vec[5:6])
            grad_rpre = grad_rec * recur * (1.0 - recur)
            grad_opre = grad_opening * opened * (1.0 - opened)
            r_low, o_low, conv_low = grad_rpre.astype(LOW), grad_opre.astype(LOW), conv_s.astype(LOW)
            total = pulled * opened + nt(r_low, R.rgate[...]) + nt(o_low, R.igate[...])
            gconv[s, 0:length] = total
            acc_r[...] += tn(conv_low, r_low)
            acc_i[...] += tn(conv_low, o_low)
            R.sums[7:8] += jnp.sum(grad_rpre, axis=0, keepdims=True)
            R.sums[8:9] += jnp.sum(grad_opre, axis=0, keepdims=True)
            R.sums[9:10] += jnp.sum(grad_log * recur, axis=0, keepdims=True) * (8.0 * vec[6:7])
            R.sums[6:7] += jnp.sum(total, axis=0, keepdims=True)

        line.during(0, 4, mixer_four)
        lext = a
        load_lext = pltpu.make_async_copy(keep["lext"], lext, R.outs.at[6])
        load_lext.start()
        heads = [
            push(gconv.at[s, pl.ds(0, TILE)], R.heads_in.at[s], (R.h2s, R.h2r), s,
                 (r, lax.rem(c + 7, 8)))
            for s in range(4)
        ]

        @pl.when(c > 0)
        def _():
            for copy in heads:
                copy.start()

        @pl.when(c == 7)
        def _():
            R.heads_in[...] = jnp.zeros_like(R.heads_in)

        cut = side // 8
        for k in range(8):
            at = k * cut
            R.gate_send[k] = jnp.concatenate(
                [m[j * side + at : j * side + at + cut, j * side : (j + 1) * side]
                 for m in (acc_r, acc_i) for j in range(2)], axis=0
            ).astype(LOW)
        gate_copies = [
            push(R.gate_send.at[lax.rem(c + d, 8)], R.gate_slots.at[d], (R.qs, R.qr), d,
                 chan_peers[d - 1])
            for d in range(1, 8)
        ]
        for copy in gate_copies:
            copy.start()
        for k in range(RS_CHUNKS):
            rows = pl.ds(k * step, step)
            R.output[rows] = (R.resid[rows] + sum3.total(k)).astype(LOW)
        line.advance(26)
        load_lext.wait()

        @pl.when(c < 7)
        def _():
            for s in range(4):
                landed(me, R.heads_in.at[s], (R.h2s, R.h2r), s)

        lift_t = mixed_t
        gpart1 = R.call

        def mixer_five(i):
            s = far_first(i)
            tallies_of(s)
            grad = gconv[s, 0:length]
            prev_ext[0:length] = grad
            prev_ext[pl.ds(length, TILE)] = R.heads_in[s]
            grad_lifted = taps[0:1] * grad
            R.sums[2:3] += jnp.sum(grad * lext[s, pl.ds(TILE, length)], axis=0, keepdims=True)
            for k in range(1, 4):
                ahead = prev_ext[pl.ds(k, length)] * same(k)
                grad_lifted = grad_lifted + taps[k : k + 1] * ahead
                behind = lext[s, pl.ds(TILE - k, length)] * same(-k)
                R.sums[2 + k : 3 + k] += jnp.sum(grad * behind, axis=0, keepdims=True)
            R.sums[1:2] += jnp.sum(grad_lifted, axis=0, keepdims=True)
            lift_low = grad_lifted.astype(LOW)
            lift_t[:, pl.ds(pl.multiple_of(s * length, LANES), length)] = lift_low.T
            gpart1[s] = (
                nn(gate_low[s], R.wq[0].reshape(wide, width))
                + nn(lift_low, R.wq[1].reshape(wide, width))
            ).astype(LOW)

        sum4 = RowsSum(me, gpart1, R.mate, R.out_x, R.in_x, (R.m3s, R.m3r), (R.rx3s, R.rx3r))
        line.during(0, 2, mixer_five)
        sum4.start(0)
        line.during(2, 3, mixer_five)
        sum4.start(1)
        sum4.cross()
        line.during(3, 4, mixer_five)
        R.late[...] = jnp.zeros_like(R.late)
        weight_grad(R.late, 0, lift_t, R.nall)
        for j in range(2):
            R.late[j, side : side + 16, 0:side] = R.sums[:, j * side : (j + 1) * side].astype(LOW)
        line.ready(4)
        line.advance(32)
        gain_sum = 0.0
        for k in range(RS_CHUNKS):
            rows = pl.ds(k * step, step)
            grad = sum4.total(k)
            vals = R.inputs[rows].astype(F32)
            scale = lax.rsqrt(jnp.mean(vals * vals, axis=-1, keepdims=True) + EPSILON)
            gain_sum = gain_sum + jnp.sum(grad * vals * scale, axis=0, keepdims=True)
            pulled = grad * R.mix_gain[...]
            inner = jnp.mean(pulled * vals, axis=-1, keepdims=True)
            R.ginputs[rows] = (
                R.gresid[rows] + scale * pulled - vals * (scale * scale * scale * inner)
            ).astype(LOW)
            line.advance(33 + k)
        for k in range(8):
            lanes = slice(k * LANES, (k + 1) * LANES)
            R.gain_slots[0, k] = jnp.concatenate(
                [gain_sum[:, lanes], R.gain_keep[0:1, lanes], R.gain_keep[1:2, lanes],
                 jnp.zeros((5, LANES), F32)], 0
            )
        gain_copies = [
            push(R.gain_slots.at[0, lax.rem(c + d, 8)], R.gain_slots.at[1, d], (R.ggs, R.ggr), d,
                 chan_peers[d - 1])
            for d in range(1, 8)
        ]
        for copy in gain_copies:
            copy.start()
        line.advance(38)
        gate_total = R.gate_send[c].astype(F32)
        for d in range(1, 8):
            gate_copies[d - 1].wait_recv()
            gate_total = gate_total + R.gate_slots[d].astype(F32)
        R.gates_all[r] = gate_total.astype(LOW)
        gate_rows = [
            push(R.gates_all.at[r], R.gates_all.at[r], (R.ts, R.tr), i, device)
            for i, device in enumerate(row_peers)
        ]
        for copy in gate_rows:
            copy.start()
        shared = R.gain_slots[0, c]
        for d in range(1, 8):
            gain_copies[d - 1].wait_recv()
            shared = shared + R.gain_slots[1, d]
        R.gain_sums[0] = shared
        row_copies = [
            push(R.gain_sums.at[0], R.gain_sums.at[1 + i], (R.ghs, R.ghr), i, device)
            for i, device in enumerate(row_peers)
        ]
        for copy in row_copies:
            copy.start()
        line.advance(line.last())
        for copy in row_copies + gate_rows:
            copy.wait()
        for row in range(4):
            found = R.gates_all[row].astype(F32)
            for head in range(2):
                R.rgate_o[2 * row + head] = found[head * cut : (head + 1) * cut]
                R.igate_o[2 * row + head] = found[(2 + head) * cut : (3 + head) * cut]
        R.gains_all[...] = R.gain_sums[0] + R.gain_sums[1] + R.gain_sums[2] + R.gain_sums[3]

        @pl.when(c > 0)
        def _():
            finish_sends(heads)

        finish_sends(gain_copies + gate_copies)
        sum3.close()
        sum4.close()
        carry_sent(me, True, carry_copies)
        line.close()

    square = pltpu.VMEM((wide, wide), F32)
    pl.run_scoped(
        backward, gate_pre=tall, conv=tall, rec=tall, opening=tall, state=tall, a=ext, b=tall,
        gconv=ext, gate_low=pltpu.VMEM((4, length, wide), LOW), gate_t=low_t, mixed_t=low_t,
        acc_r=square, acc_i=square, prev_ext=pltpu.VMEM((length + TILE, wide), F32),
    )


def block(ins):
    far = ("rgate_all", "igate_all", "gp", "lp", "op", "mg", "mu", "md")
    inputs, starts, mg = ins["inputs"], ins["starts"], ins["mg"]
    length, width = inputs.shape
    side = ins["gp"].shape[0]
    wide = 2 * side
    hidden = mg.shape[1]
    sd, vmem = jax.ShapeDtypeStruct, pltpu.VMEM
    blocks = hidden // LANES
    tall = sd((4, length, wide), F32)
    tokens = (4, length, width)
    outs = dict(
        output=sd(inputs.shape, LOW), ginputs=sd(inputs.shape, LOW),
        own_w=sd((width, 3 * hidden), LOW),
        own_e=sd((2 * side, width), LOW), own_l=sd((side + 32, width), LOW),
        rgate_o=sd((8, side // 8, side), F32), igate_o=sd((8, side // 8, side), F32),
        gains_all=sd((8, LANES), F32),
    )
    saved = dict(
        gate_h=tall, lext_h=sd((4, length + TILE, wide), F32), conv_h=tall, rec_h=tall, open_h=tall,
        state_h=tall, mixed_h=sd((wide, 4 * length), LOW),
    )
    scratch = dict(
        wq=vmem((3, 2, side, width), LOW), nall=vmem(tokens, LOW), halo=vmem((4, 16, width), LOW),
        starts_all=vmem((4, 8, LANES), starts.dtype), vec=vmem((8, wide), F32), taps=vmem((4, wide), F32),
        gates_all=vmem((4, side // 2, side), LOW),
        w=vmem((blocks, width, 6 * LANES), LOW),
        call=vmem(tokens, LOW), n2all=vmem(tokens, LOW), opart=vmem(tokens, LOW),
        rgate=vmem((wide, wide), LOW), igate=vmem((wide, wide), LOW),
        tallies=vmem((length + 16, LANES), F32), start=vmem((4, wide), F32), carry=vmem((4, wide), F32),
        tot=vmem((4, 2, wide), F32), slots=vmem((8, 4, 2, wide), F32), slots2=vmem((8, 4, 2, wide), F32),
        resid=vmem((length, width), F32), gresid=vmem((length, width), F32),
        mate=vmem((2, length, width), LOW), out_x=vmem((length, width), LOW),
        in_x=vmem((length, width), LOW),
        o_mate=vmem((2, length, width), LOW), o_out=vmem((length, width), LOW),
        o_in=vmem((length, width), LOW),
        grad=vmem((blocks, 2, width, 3 * LANES), LOW),
        early=vmem((2, 2 * side, width), LOW), late=vmem((2, side + 32, width), LOW),
        heads_in=vmem((4, TILE, wide), F32), sums=vmem((16, wide), F32),
        gate_send=vmem((8, side // 2, side), LOW), gate_slots=vmem((8, side // 2, side), LOW),
        gain_keep=vmem((8, width), F32), gain_slots=vmem((2, 8, 8, LANES), F32), gain_sums=vmem((4, 8, LANES), F32),
    )
    for way in "yz":
        scratch.update(
            {
                way + "_w": vmem((blocks, width, 3 * LANES), LOW),
                way + "_e": vmem((2 * side, width), LOW),
                way + "_l": vmem((side + 32, width), LOW),
            }
        )
    dma = pltpu.SemaphoreType.DMA
    counts = dict(
        loc=15, outs=7, xs=2, xr=2, cs=4, cr=4, hs=4, hr=4, ss=3, sr=3, ps=8, pr=8, p2s=8, p2r=8,
        h2s=4, h2r=4, qs=8, qr=8, ts=3, tr=3, ggs=8, ggr=8, ghs=3, ghr=3,
    )
    for name in ("m", "m2", "m3", "om"):
        counts.update({name + "s": 2 * RS_CHUNKS, name + "r": 2 * RS_CHUNKS})
    for name in ("rx", "rx2", "rx3", "ox"):
        counts.update({name + "s": RS_CHUNKS, name + "r": RS_CHUNKS})
    for name in ("", "2"):
        counts.update({f"a{name}x": RS_CHUNKS, f"b{name}x": RS_CHUNKS})
        counts.update({f"a{name}c": 2 * RS_CHUNKS, f"b{name}c": 2 * RS_CHUNKS})
    scratch.update({name: dma((count,)) for name, count in counts.items()})
    names = list(ins) + list(outs) + list(saved) + list(scratch)
    spread = spread_sems(1, 4) * 3 + spread_sems(1, 8) * blocks
    reduce = reduce_sems(1, 8) * blocks + reduce_sems(1, 8) + reduce_sems(1, 7)

    def kernel(*refs):
        n, m = len(names), len(spread)
        block_kernel(names + ["spread", "reduce"], *refs[:n], refs[n : n + m], refs[n + m :])

    results = pl.pallas_call(
        kernel,
        name="block",
        out_shape=list(outs.values()) + list(saved.values()),
        in_specs=[ANYWHERE if name in far else IN_VMEM for name in ins],
        out_specs=[IN_VMEM] * len(outs) + [ANYWHERE] * len(saved),
        scratch_shapes=list(scratch.values()) + spread + reduce,
        compiler_params=comm_params(1),
    )(*ins.values())
    return results[: len(outs)]


def split_body(
    inputs, mix_gain, gate_proj, gate_bias, lift_proj, lift_bias, conv_taps, conv_bias,
    recur_gate, recur_bias, input_gate, input_bias, decay_param, out_proj, out_bias, mlp_gain,
    mlp_gate, mlp_up, mlp_down, doc_starts, cotangent,
):
    row = lambda v: v[None]
    vectors = (gate_bias, lift_bias, conv_bias, recur_bias, input_bias, decay_param)
    output, grad_inputs, own_w, own_e, own_l, rgate_o, igate_o, gains = block(
        dict(
            inputs=inputs, cot=cotangent, mix_gain=row(mix_gain), out_bias=row(out_bias),
            mlp_gain=row(mlp_gain), **{name: v.reshape(-1, LANES) for name, v in zip(VECTORS, vectors)}, conv_taps=conv_taps, starts=doc_starts,
            rgate_all=recur_gate, igate_all=input_gate, gp=gate_proj.T, lp=lift_proj.T, op=out_proj,
            mg=mlp_gate, mu=mlp_up, md=mlp_down,
        )
    )
    wide_out = lambda v: v.astype(F32)
    own = wide_out(own_l[GB : GB + 16, :GB])
    mlp_out = lambda i: jnp.concatenate(
        [wide_out(own_w[:, at * LANES : (at + 1) * LANES]) for at in range(i, 3 * MLP_BLOCKS, 3)], axis=1
    )
    return (
        output, grad_inputs, gains[0],
        wide_out(own_e[GB:].T), own[0], wide_out(own_l[:GB].T), own[1], own[2:6], own[6],
        rgate_o, own[7], igate_o, own[8], own[9],
        wide_out(own_e[:GB]), gains[2], gains[1],
        mlp_out(0), mlp_out(1), mlp_out(2).T,
    )


def solution(mesh):
    in_specs = (
        P(("rows", "chan"), None),
        P(),
        P(None, "chan"),
        P(),
        P(None, "chan"),
        P(),
        P(),
        P(),
        P(),
        P(),
        P(),
        P(),
        P(),
        P("chan", None),
        P(),
        P(),
        P(None, "chan"),
        P(None, "chan"),
        P("chan", None),
        P("rows", None),
        P(("rows", "chan"), None),
    )
    out_specs = (
        P(("rows", "chan"), None),
        P(("rows", "chan"), None),
        P("chan"),
        P(None, "chan"),
        P("chan"),
        P(None, "chan"),
        P("chan"),
        P(None, "chan"),
        P("chan"),
        P(None, "chan", None),
        P("chan"),
        P(None, "chan", None),
        P("chan"),
        P("chan"),
        P("chan", None),
        P("chan"),
        P("chan"),
        P(None, "chan"),
        P(None, "chan"),
        P("chan", None),
    )
    split = mesh.shape["rows"] == 4 and mesh.shape["chan"] == HEADS
    return jax.shard_map(split_body if split else body, mesh=mesh, in_specs=in_specs, out_specs=out_specs, check_vma=False)
```

```python
from functools import partial
import math

import jax
import jax.numpy as jnp
from jax import lax
from jax.experimental import pallas as pl
from jax.experimental.pallas import tpu as pltpu
from jax.sharding import PartitionSpec as P

D = 1024
LRU = 1536
FF = 3072
HEADS = 8
GB = 192


EPSILON = 1e-06
precise = lax.Precision.HIGHEST


def from_behind(block, axis, distance):
    devices = range(lax.axis_size(axis))
    route = [(i - distance, i) for i in devices if i - distance in devices]
    return lax.ppermute(block, axis, route)


def prefix(value, axis, join, neutral, backward):
    count, mine = (lax.axis_size(axis), lax.axis_index(axis))
    pieces = jax.tree.map(lambda part: lax.all_gather(part, axis), value)
    if backward:
        pieces = jax.tree.map(lambda part: part[::-1], pieces)
        mine = count - 1 - mine
    subtotal = jax.tree.map(
        lambda part, zero: jnp.full_like(part, 0) + jnp.asarray(zero, part.dtype), value, neutral
    )

    def hop(position, subtotal):
        longer = join(subtotal, jax.tree.map(lambda part: part[position], pieces))
        return jax.tree.map(lambda new, old: jnp.where(position < mine, new, old), longer, subtotal)

    return lax.fori_loop(0, count - 1, hop, subtotal)


def rms_scale(values, gain_vec):
    return (
        values * lax.rsqrt(jnp.mean(values * values, axis=-1, keepdims=True) + EPSILON) * gain_vec
    )


def gated_unit(gate_pre, up_vals):
    return jax.nn.gelu(gate_pre) * up_vals


def affine(earlier, later_map):
    return (earlier[0] * later_map[0], later_map[0] * earlier[1] + later_map[1])


def segment_ids(starts, start_pos, pos_count, seq_len):
    where_at = start_pos + jnp.arange(pos_count, dtype=jnp.int32)
    seq_of = jnp.floor_divide(where_at, seq_len)
    within = where_at - seq_of * seq_len
    owner = seq_of[:, None] == jnp.arange(starts.shape[0], dtype=jnp.int32)[None, :]
    passed = starts[None, :, :] <= within[:, None, None]
    doc_tally = jnp.sum(jnp.logical_and(owner[:, :, None], passed).astype(jnp.int32), axis=(1, 2))
    return seq_of * (starts.shape[1] + 1) + doc_tally


def project(normed, weights, first_bias, second_bias):
    product = jnp.einsum("td,dc->ct", normed, weights, preferred_element_type=jnp.float32)
    channels = first_bias.shape[0]
    return (product[:channels] + first_bias[:, None], product[channels:] + second_bias[:, None])


def conv_forward(lifted, tail_rows, segments, tap_vals, bias_vec):
    length = lifted.shape[1]
    extended = jnp.concatenate([tail_rows, lifted], axis=1)
    own_seg = segments[3 : 3 + length]
    result = bias_vec[:, None] + tap_vals[0][:, None] * lifted
    for offset in range(1, 4):
        same_doc = (segments[3 - offset : 3 - offset + length] == own_seg).astype(jnp.float32)
        result = (
            result
            + tap_vals[offset][:, None]
            * extended[:, 3 - offset : 3 - offset + length]
            * same_doc[None, :]
        )
    return result


def conv_backward(grad_conv, head_rows, segments, lifted, tail_rows, tap_vals):
    length = grad_conv.shape[1]
    ahead_grad = jnp.concatenate([grad_conv, head_rows], axis=1)
    behind = jnp.concatenate([tail_rows, lifted], axis=1)
    own_seg = segments[3 : 3 + length]
    grad_lifted = tap_vals[0][:, None] * grad_conv
    tap_grads = [jnp.sum(grad_conv * lifted, axis=1)]
    for offset in range(1, 4):
        later_same = (segments[3 + offset : 3 + offset + length] == own_seg).astype(jnp.float32)
        grad_lifted = (
            grad_lifted
            + tap_vals[offset][:, None]
            * ahead_grad[:, offset : offset + length]
            * later_same[None, :]
        )
        earlier = (segments[3 - offset : 3 - offset + length] == own_seg).astype(jnp.float32)
        tap_grads.append(
            jnp.sum(
                grad_conv * behind[:, 3 - offset : 3 - offset + length] * earlier[None, :], axis=1
            )
        )
    return (grad_lifted, jnp.stack(tap_grads, axis=1), jnp.sum(grad_conv, axis=1))


def coefficients(is_reset, conv_out, recur_gate, recur_bias, input_gate, input_bias, decay_param):
    channels, length = conv_out.shape
    gate_block = recur_gate.shape[1]
    grouped = conv_out.reshape(channels // gate_block, gate_block, length)
    recurrence = jax.nn.sigmoid(
        jnp.einsum("hit,hio->hot", grouped, recur_gate, precision=precise).reshape(channels, length)
        + recur_bias[:, None]
    )
    opening = jax.nn.sigmoid(
        jnp.einsum("hit,hio->hot", grouped, input_gate, precision=precise).reshape(channels, length)
        + input_bias[:, None]
    )
    log_decay = -8.0 * recurrence * jax.nn.softplus(-decay_param)[:, None]
    decay_rate = jnp.where(is_reset[None, :], 0.0, jnp.exp(log_decay))
    scaling = jnp.where(is_reset[None, :], 1.0, jnp.sqrt(-jnp.expm1(2.0 * log_decay)))
    return (decay_rate, scaling * opening * conv_out)


def reverse_local(decay_rate, grad_state):
    ones_col = jnp.ones_like(decay_rate[:, :1])
    factor = jnp.flip(jnp.concatenate([decay_rate[:, 1:], ones_col], axis=1), axis=1)
    product, carried = lax.associative_scan(affine, (factor, jnp.flip(grad_state, axis=1)), axis=1)
    return (jnp.flip(product, axis=1), jnp.flip(carried, axis=1))


def finish_state(lru_state, start_state, carried, pull_coef):
    previous = jnp.concatenate([start_state[:, None], lru_state[:, :-1]], axis=1)
    return pull_coef((carried * previous, carried))


def flatten_rows(pieces, row_count):
    return jnp.concatenate([source.reshape(row_count, -1) for source in pieces], axis=1)


def body(
    inputs,
    mix_gain,
    gate_proj,
    gate_bias,
    lift_proj,
    lift_bias,
    conv_taps,
    conv_bias,
    recur_gate,
    recur_bias,
    input_gate,
    input_bias,
    decay_param,
    out_proj,
    out_bias,
    mlp_gain,
    mlp_gate,
    mlp_up,
    mlp_down,
    doc_starts,
    cotangent,
):
    chan_count = lax.axis_size("chan")
    chan_place = lax.axis_index("chan")
    local_rows = inputs.shape[0]
    seq_length = local_rows * chan_count
    rows_f32 = inputs.astype(jnp.float32)
    cot_f32 = cotangent.astype(jnp.float32)
    normed, pull_norm = jax.vjp(rms_scale, rows_f32, mix_gain)
    normed_low = normed.astype(jnp.bfloat16)
    gate_full, lift_full, out_full, mlp_gate_full, mlp_up_full, mlp_down_full = (
        lax.all_gather(gate_proj, "chan", axis=1, tiled=True),
        lax.all_gather(lift_proj, "chan", axis=1, tiled=True),
        lax.all_gather(out_proj, "chan", axis=0, tiled=True),
        lax.all_gather(mlp_gate, "chan", axis=1, tiled=True),
        lax.all_gather(mlp_up, "chan", axis=1, tiled=True),
        lax.all_gather(mlp_down, "chan", axis=0, tiled=True),
    )
    channels = LRU
    hidden_cut = FF
    segments = segment_ids(doc_starts, chan_place * local_rows - 3, local_rows + 6, seq_length)
    mix_proj = jnp.concatenate([gate_full, lift_full], axis=1)
    gate_pre, lifted = project(normed_low, mix_proj, gate_bias, lift_bias)
    tail_rows = from_behind(lifted[:, -3:], "chan", 1)
    conv_out = conv_forward(lifted, tail_rows, segments, conv_taps, conv_bias)
    is_reset = segments[3 : 3 + local_rows] != segments[2 : 2 + local_rows]
    (decay_rate, lru_input), pull_coef = jax.vjp(
        partial(coefficients, is_reset),
        conv_out,
        recur_gate,
        recur_bias,
        input_gate,
        input_bias,
        decay_param,
    )
    running, local_state = lax.associative_scan(affine, (decay_rate, lru_input), axis=1)
    ones_vec = jnp.ones((channels,), jnp.float32)
    zeros_vec = jnp.zeros((channels,), jnp.float32)
    _, start_state = prefix(
        (running[:, -1], local_state[:, -1]), "chan", affine, (ones_vec, zeros_vec), False
    )
    lru_state = local_state + running * start_state[:, None]
    gate_val, pull_gelu = jax.vjp(jax.nn.gelu, gate_pre)
    mixed_out = (lru_state * gate_val).astype(jnp.bfloat16)
    resid = (
        rows_f32
        + jnp.einsum("ct,cd->td", mixed_out, out_full, preferred_element_type=jnp.float32)
        + out_bias
    )
    normed2, pull_norm2 = jax.vjp(rms_scale, resid, mlp_gain)
    normed2_low = normed2.astype(jnp.bfloat16)
    mlp_proj = jnp.concatenate([mlp_gate_full, mlp_up_full], axis=1)
    mlp_pre = jnp.einsum("td,df->ft", normed2_low, mlp_proj, preferred_element_type=jnp.float32)
    hidden, pull_mlp = jax.vjp(gated_unit, mlp_pre[:hidden_cut], mlp_pre[hidden_cut:])
    hidden_low = hidden.astype(jnp.bfloat16)
    output = (
        resid
        + jnp.einsum("ft,fd->td", hidden_low, mlp_down_full, preferred_element_type=jnp.float32)
    ).astype(jnp.bfloat16)
    grad_down = jnp.einsum("ft,td->fd", hidden_low, cotangent, preferred_element_type=jnp.float32)
    grad_gate_m, grad_up_m = pull_mlp(
        jnp.einsum("td,fd->ft", cotangent, mlp_down_full, preferred_element_type=jnp.float32)
    )
    grad_pre = jnp.concatenate([grad_gate_m, grad_up_m], axis=0).astype(jnp.bfloat16)
    grad_mlp_in = jnp.einsum("ft,td->fd", grad_pre, normed2_low, preferred_element_type=jnp.float32)
    grad_resid_part, grad_gain2 = pull_norm2(
        jnp.einsum("ft,df->td", grad_pre, mlp_proj, preferred_element_type=jnp.float32)
    )
    grad_resid = cot_f32 + grad_resid_part
    grad_branch = grad_resid.astype(jnp.bfloat16)
    grad_out_proj = jnp.einsum(
        "ct,td->cd", mixed_out, grad_branch, preferred_element_type=jnp.float32
    )
    grad_mixed = jnp.einsum("td,cd->ct", grad_branch, out_full, preferred_element_type=jnp.float32)
    product, carried = reverse_local(decay_rate, grad_mixed * gate_val)
    _, incoming = prefix(
        (decay_rate[:, 0] * product[:, 0], decay_rate[:, 0] * carried[:, 0]),
        "chan",
        affine,
        (ones_vec, zeros_vec),
        True,
    )
    carried = carried + product * incoming[:, None]
    coef_grads = finish_state(lru_state, start_state, carried, pull_coef)
    head_rows = from_behind(coef_grads[0][:, :3], "chan", -1)
    grad_lifted, grad_taps, grad_conv_bias = conv_backward(
        coef_grads[0], head_rows, segments, lifted, tail_rows, conv_taps
    )
    (grad_gate_pre,) = pull_gelu(grad_mixed * lru_state)
    grad_front = jnp.concatenate([grad_gate_pre, grad_lifted], axis=0).astype(jnp.bfloat16)
    grad_mix_proj = jnp.einsum(
        "ct,td->cd", grad_front, normed_low, preferred_element_type=jnp.float32
    )
    grad_normed = jnp.einsum("ct,dc->td", grad_front, mix_proj, preferred_element_type=jnp.float32)
    grad_x_part, grad_gain1 = pull_norm(grad_normed)
    grad_inputs = (grad_resid + grad_x_part).astype(jnp.bfloat16)
    grad_out_bias = jnp.sum(grad_resid, axis=0)
    pieces = [
        grad_mix_proj[:channels],
        grad_mix_proj[channels:],
        jnp.sum(grad_gate_pre, axis=1),
        jnp.sum(grad_lifted, axis=1),
        grad_taps,
        grad_conv_bias,
        jnp.transpose(coef_grads[1], (1, 0, 2)),
        coef_grads[2],
        jnp.transpose(coef_grads[3], (1, 0, 2)),
        coef_grads[4],
        coef_grads[5],
        grad_out_proj,
        grad_mlp_in[:hidden_cut],
        grad_mlp_in[hidden_cut:],
        grad_down,
        grad_gain1,
        grad_out_bias,
        grad_gain2,
    ]
    spread = flatten_rows(pieces, chan_count)
    shared = lax.psum_scatter(spread, "chan", scatter_dimension=0, tiled=True)
    summed = lax.psum(shared.reshape(-1), "rows")
    channels_dev = LRU // chan_count
    hidden_dev = FF // chan_count
    width_dev = D // chan_count
    block_dev = GB // chan_count
    shapes = [
        (channels_dev, D),
        (channels_dev, D),
        (channels_dev,),
        (channels_dev,),
        (channels_dev, 4),
        (channels_dev,),
        (block_dev, HEADS, GB),
        (channels_dev,),
        (block_dev, HEADS, GB),
        (channels_dev,),
        (channels_dev,),
        (channels_dev, D),
        (hidden_dev, D),
        (hidden_dev, D),
        (hidden_dev, D),
        (width_dev,),
        (width_dev,),
        (width_dev,),
    ]
    unpacked = []
    offset = 0
    for piece_shape in shapes:
        piece_size = math.prod(piece_shape)
        unpacked.append(summed[offset : offset + piece_size].reshape(piece_shape))
        offset = offset + piece_size
    return (
        output,
        grad_inputs,
        unpacked[15],
        unpacked[0].T,
        unpacked[2],
        unpacked[1].T,
        unpacked[3],
        unpacked[4].T,
        unpacked[5],
        jnp.transpose(unpacked[6], (1, 0, 2)),
        unpacked[7],
        jnp.transpose(unpacked[8], (1, 0, 2)),
        unpacked[9],
        unpacked[10],
        unpacked[11],
        unpacked[16],
        unpacked[17],
        unpacked[12].T,
        unpacked[13].T,
        unpacked[14],
    )


MESH = pl.DeviceIdType.MESH
LOW = jnp.bfloat16
F32 = jnp.float32
VMEM_BYTES = 63 * 2**20
TILE = 8
GELU_A = math.sqrt(2.0 / math.pi)
GELU_B = 0.044715


def nt(left, right):
    return lax.dot_general(left, right, (((1,), (1,)), ((), ())), preferred_element_type=F32)


def nn(left, right):
    return lax.dot_general(left, right, (((1,), (0,)), ((), ())), preferred_element_type=F32)


def tn(left, right):
    return lax.dot_general(left, right, (((0,), (0,)), ((), ())), preferred_element_type=F32)


def gelu_pair(values):
    squared = values * values
    bend = jnp.tanh(GELU_A * values * (1.0 + GELU_B * squared))
    half = 0.5 * (1.0 + bend)
    slope = half + 0.5 * values * (1.0 - bend * bend) * GELU_A * (1.0 + 3.0 * GELU_B * squared)
    return values * half, slope


class Spot:
    def __init__(self):
        self.r = lax.axis_index("rows")
        self.c = lax.axis_index("chan")
        self.z = lax.div(self.c, 2)
        self.y = lax.rem(self.c, 2)
        self.r_core = self.r + 1 - 2 * lax.rem(self.r, 2)
        self.r_x = lax.rem(self.r + 2, 4)
        self.core = (self.r_core, self.c)
        self.x = (self.r_x, self.c)
        self.c_y = self.c + 1 - 2 * self.y
        self.ymate = (self.r, self.c_y)
        self.up = (self.r, lax.rem(self.c + 2, 8))
        self.dn = (self.r, lax.rem(self.c + 6, 8))


def greet(always, maybe=()):
    barrier = pltpu.get_barrier_semaphore()
    count = len(always)
    for device in always:
        pl.semaphore_signal(barrier, inc=1, device_id=device, device_id_type=MESH)
    for device, there in maybe:

        @pl.when(there)
        def _(device=device):
            pl.semaphore_signal(barrier, inc=1, device_id=device, device_id_type=MESH)

        count = count + jnp.where(there, 1, 0)
    pl.semaphore_wait(barrier, count)


def push(source, target, sems, index, device):
    return pltpu.make_async_remote_copy(
        src_ref=source,
        dst_ref=target,
        send_sem=sems[0].at[index],
        recv_sem=sems[1].at[index],
        device_id=device,
        device_id_type=MESH,
    )


def landed(me, target, sems, index):
    push(target, target, sems, index, me.ymate).wait_recv()


def sem_pair(count):
    return [pltpu.SemaphoreType.DMA((count,)), pltpu.SemaphoreType.DMA((count,))]


def comm_params(collective_id):
    return pltpu.CompilerParams(
        collective_id=collective_id, has_side_effects=True, vmem_limit_bytes=VMEM_BYTES
    )


ANYWHERE = pl.BlockSpec(memory_space=pl.ANY)
IN_VMEM = pl.BlockSpec(memory_space=pltpu.VMEM)


def decay_terms(rec, softplus_row, reset):
    log_decay = -8.0 * rec * softplus_row
    decay = jnp.exp(log_decay)
    twice = 2.0 * log_decay
    series = twice * (
        1.0
        + twice * (1 / 2 + twice * (1 / 6 + twice * (1 / 24 + twice * (1 / 120 + twice * (1 / 720)))))
    )
    gap = jnp.where(twice > -0.25, -series, 1.0 - jnp.exp(twice))
    return decay, jnp.where(reset, 1.0, jnp.sqrt(gap))


def fill_tallies(tallies, starts_row, first, length, seq_length):
    position = first - 8 + lax.broadcasted_iota(jnp.int32, (length + 16, 1), 0)
    begun = jnp.sum((starts_row <= position).astype(F32), axis=1, keepdims=True)
    inside = jnp.logical_and(position >= 0, position < seq_length)
    tallies[...] = jnp.broadcast_to(jnp.where(inside, begun, -1.0), tallies.shape)


def same_document(tallies, length, shift, wide):
    own = tallies[pl.ds(8, length)]
    other = tallies[pl.ds(8 + shift, length)]
    same = (own == other).astype(F32)
    return jnp.concatenate([same] * (wide // same.shape[1]), axis=1)


def pair_diagonal(target, blocks):
    side = blocks.shape[1]
    target[...] = jnp.zeros_like(target)
    target[0:side, 0:side] = blocks[0].astype(target.dtype)
    target[side : 2 * side, side : 2 * side] = blocks[1].astype(target.dtype)


def tile_scan(a, b, backward):
    row = lax.broadcasted_iota(jnp.int32, a.shape, 1)
    for step in (1, 2, 4):
        shift = TILE - step if backward else step
        there = row < TILE - step if backward else row >= step
        b = b + a * jnp.where(there, pltpu.roll(b, shift, 1), 0.0)
        a = a * jnp.where(there, pltpu.roll(a, shift, 1), 1.0)
    return a, b


def carry_start(me, backward, totals, slots, sems):
    sign = -1 if backward else 1
    steps = me.c if backward else 7 - me.c
    copies = [
        push(totals, slots.at[d], sems, d, (me.r, lax.rem(me.c + 8 + sign * d, 8)))
        for d in range(1, 8)
    ]
    for d in range(1, 8):

        @pl.when(d <= steps)
        def _(d=d):
            copies[d - 1].start()

    return copies


def carry_join(me, backward, slots, start, sems):
    behind = 7 - me.c if backward else me.c
    start[...] = jnp.zeros_like(start)
    for d in range(7, 0, -1):

        @pl.when(d <= behind)
        def _(d=d):
            landed(me, slots.at[d], sems, d)
            start[...] = slots[d, :, 0] * start[...] + slots[d, :, 1]


def carry_sent(me, backward, copies):
    steps = me.c if backward else 7 - me.c
    for d in range(1, 8):

        @pl.when(d <= steps)
        def _(d=d):
            copies[d - 1].wait_send()


def peers_of(me):
    return [(me.r, lax.rem(me.c + d, 8)) for d in range(1, 8)]


class Spread:
    def __init__(self, me, slabs, pieces, sems):
        self.me, self.slabs, self.pieces, self.sems = me, slabs, pieces, sems
        self.go_up = jnp.logical_and(me.z >= me.r, me.z < 3)
        self.go_dn = jnp.logical_and(me.z <= me.r, me.z > 0)
        self.source = me.z == me.r
        self.hop = jnp.where(me.z < me.r, me.r - me.z, me.z - me.r)

    def copies(self, k):
        me, found = self.me, []
        for i, slab in enumerate(self.slabs):
            piece = slab(k, me.y)
            ys, yr, us, ds, zr = self.sems[5 * i : 5 * i + 5]
            found.append(
                (
                    push(piece, piece, (ys, yr), k, me.ymate),
                    push(piece, piece, (us, zr), k, me.up),
                    push(piece, piece, (ds, zr), k, me.dn),
                )
            )
        return found

    def send(self, k):
        found = self.copies(k)
        for copies in found:
            copies[0].start()

        @pl.when(self.go_up)
        def _():
            for copies in found:
                copies[1].start()

        @pl.when(self.go_dn)
        def _():
            for copies in found:
                copies[2].start()

    def follow(self, k):
        for i, slab in enumerate(self.slabs):
            us, zr = self.sems[5 * i + 2], self.sems[5 * i + 4]
            landed(self.me, slab(k, self.me.y), (us, zr), k)
        self.send(k)

    def step(self, q):
        n = self.pieces

        def at(k, also, action):
            there = jnp.logical_and(k >= 0, k < n)

            @pl.when(jnp.logical_and(there, also))
            def _():
                action(lax.rem(k + 8 * n, n))

        at(q + SPREAD_AHEAD, self.source, self.send)
        at(q - SPREAD_LAG * (self.hop - 1), jnp.logical_not(self.source), self.follow)

    def reach(self):
        return -SPREAD_AHEAD, self.pieces + 2 * SPREAD_LAG

    def arrived(self):
        @pl.loop(0, self.pieces)
        def _(k):
            for i, slab in enumerate(self.slabs):
                ys, yr = self.sems[5 * i], self.sems[5 * i + 1]
                landed(self.me, slab(k, 1 - self.me.y), (ys, yr), k)

    def close(self):
        @pl.loop(0, self.pieces)
        def _(k):
            found = self.copies(k)
            for copies in found:
                copies[0].wait_send()

            @pl.when(self.go_up)
            def _():
                for copies in found:
                    copies[1].wait_send()

            @pl.when(self.go_dn)
            def _():
                for copies in found:
                    copies[2].wait_send()


SPREAD_AHEAD = 4
SPREAD_LAG = 1


def spread_sems(arrays, pieces):
    return [pltpu.SemaphoreType.DMA((pieces,))] * (5 * arrays)


AHEAD = 3
LAGS = (3, 10, 16)
LATE_LAGS = (2, 7, 9)


class Reduce:
    def __init__(self, me, parts, mine, from_y, from_z, own, pieces, sems, ahead=AHEAD, lags=LAGS):
        self.me, self.parts, self.mine = me, parts, mine
        self.from_y, self.from_z, self.own = from_y, from_z, own
        self.pieces, self.sems, self.ahead, self.lags = pieces, sems, ahead, lags
        self.hop = jnp.where(me.z < me.r, me.z, 3 - me.z)
        self.owner = me.z == me.r
        self.relays = me.z == me.r_x

    def rows(self, i, k):
        size = self.mine[i].shape[0] // self.pieces
        return pl.ds(pl.multiple_of(k * size, 16), size)

    def each(self, k):
        for i in range(len(self.mine)):
            yield i, self.rows(i, k), self.sems[11 * i : 11 * i + 11]

    def y_copies(self, k):
        me = self.me
        return [
            push(self.parts[i].at[1 - me.y, rows], self.from_y[i].at[rows], sems[0:2], k, me.ymate)
            for i, rows, sems in self.each(k)
        ]

    def y_send(self, k):
        for copy in self.y_copies(k):
            copy.start()

    def add(self, i, rows, other):
        total = self.mine[i][rows].astype(F32) + other[i][rows].astype(F32)
        self.mine[i][rows] = total.astype(LOW)

    def join(self, k):
        for i, rows, sems in self.each(k):
            landed(self.me, self.from_y[i].at[rows], sems[0:2], k)
            self.add(i, rows, self.from_y)

    def z_copies(self, k, way):
        found = []
        for i, rows, sems in self.each(k):
            target = self.own if way == 2 else self.from_z
            pair = ((sems[2], sems[4]), (sems[3], sems[4]), (sems[3], sems[5]))[way]
            found.append(
                push(self.mine[i].at[rows], target[i].at[rows], pair, k,
                     self.me.up if way == 0 else self.me.dn)
            )
        return found

    def z_way(self, action):
        me = self.me
        for way, there in enumerate(
            (me.z < me.r, me.z > me.r + 1, me.z == me.r + 1)
        ):

            @pl.when(there)
            def _(way=way):
                action(way)

    def chain(self, k):
        @pl.when(self.hop > 0)
        def _():
            for i, rows, sems in self.each(k):
                landed(self.me, self.from_z[i].at[rows], (sems[2], sems[4]), k)
                self.add(i, rows, self.from_z)

        def start(way):
            for copy in self.z_copies(k, way):
                copy.start()

        self.z_way(start)

    def out_copies(self, k, device, pair):
        return [
            push(self.own[i].at[rows], self.own[i].at[rows], sems[pair : pair + 2], k, device)
            for i, rows, sems in self.each(k)
        ]

    def finish(self, k):
        @pl.when(self.me.z > 0)
        def _():
            for i, rows, sems in self.each(k):
                landed(self.me, self.from_z[i].at[rows], (sems[2], sems[4]), k)
                self.add(i, rows, self.from_z)

        @pl.when(self.me.z < 3)
        def _():
            for i, rows, sems in self.each(k):
                landed(self.me, self.own[i].at[rows], (sems[3], sems[5]), k)
                self.add(i, rows, self.own)

        for i, rows, sems in self.each(k):
            self.own[i][rows] = self.mine[i][rows]
        for copy in self.out_copies(k, self.me.x, 6) + self.out_copies(k, self.me.core, 8):
            copy.start()

    def relay(self, k):
        for copy in self.out_copies(k, self.me.x, 6):
            copy.wait_recv()
        for copy in self.out_copies(k, self.me.core, 8):
            copy.start()

    def step(self, q):
        n = self.pieces

        def at(k, also, action):
            there = jnp.logical_and(k >= 0, k < n)

            @pl.when(there if also is None else jnp.logical_and(there, also))
            def _():
                action(lax.rem(k + 8 * n, n))

        hop_lag, end_lag, relay_lag = self.lags
        if self.ahead:
            at(q + self.ahead, None, self.y_send)
        at(q, None, self.join)
        at(q - hop_lag * self.hop, jnp.logical_not(self.owner), self.chain)
        at(q - end_lag, self.owner, self.finish)
        at(q - relay_lag, self.relays, self.relay)

    def reach(self):
        return -self.ahead, self.pieces + self.lags[2]

    def close(self):
        others = jnp.logical_not(jnp.logical_or(self.owner, self.relays))

        @pl.loop(0, self.pieces)
        def _(k):
            for copy in self.y_copies(k):
                copy.wait_send()

            def sent(way):
                for copy in self.z_copies(k, way):
                    copy.wait_send()

            self.z_way(sent)

            @pl.when(self.owner)
            def _():
                for copy in self.out_copies(k, self.me.x, 6) + self.out_copies(k, self.me.core, 8):
                    copy.wait_send()

            @pl.when(self.relays)
            def _():
                for copy in self.out_copies(k, self.me.core, 8):
                    copy.wait_send()

            @pl.when(others)
            def _():
                for copy in self.out_copies(k, self.me.core, 8):
                    copy.wait_recv()


class Line:
    def __init__(self, reduces, offsets):
        self.reduces, self.offsets = reduces, offsets
        self.done = reduces[0].reach()[0]

    def position(self, p, low, high):
        for one, offset in zip(self.reduces, self.offsets):
            first, last = one.reach()
            if offset + first < high and low < offset + last:
                one.step(p - offset)

    def advance(self, high):
        low, self.done = self.done, max(self.done, high)
        if high > low + 1:

            @pl.loop(low, high)
            def _(p):
                self.position(p, low, high)

        elif high > low:
            self.position(low, low, high)

    def ready(self, i):
        assert self.done <= self.offsets[i] + self.reduces[i].reach()[0]

    def during(self, begin, end, action):
        low, self.done = self.done, self.done + end - begin

        @pl.loop(begin, end)
        def _(s):
            action(s)
            self.position(low - begin + s, low, low + end - begin)

    def last(self):
        return max(offset + one.reach()[1] for offset, one in zip(self.offsets, self.reduces))

    def close(self):
        for one in self.reduces:
            one.close()


def reduce_sems(arrays, pieces):
    return [pltpu.SemaphoreType.DMA((pieces,))] * (11 * arrays)


RS_CHUNKS = 4


class RowsSum:
    def __init__(self, me, part, mate, out_x, in_x, core_sems, x_sems):
        self.me, self.part, self.mate, self.out_x, self.in_x = me, part, mate, out_x, in_x
        self.size = part.shape[1] // RS_CHUNKS
        far = lax.rem(me.r_core + 2, 4)
        self.to_core = [
            [
                push(part.at[owner, self.rows(k)], mate.at[block, self.rows(k)], core_sems,
                     block * RS_CHUNKS + k, me.core)
                for k in range(RS_CHUNKS)
            ]
            for block, owner in enumerate((far, me.r_core))
        ]
        self.to_x = [
            push(out_x.at[self.rows(k)], in_x.at[self.rows(k)], x_sems, k, me.x)
            for k in range(RS_CHUNKS)
        ]

    def rows(self, k):
        return pl.ds(k * self.size, self.size)

    def start(self, block, chunks=range(RS_CHUNKS)):
        for k in chunks:
            self.to_core[block][k].start()

    def cross(self, chunks=range(RS_CHUNKS)):
        for k in chunks:
            rows = self.rows(k)
            self.to_core[0][k].wait_recv()
            total = self.part[self.me.r_x, rows].astype(F32) + self.mate[0, rows].astype(F32)
            self.out_x[rows] = total.astype(LOW)
            self.to_x[k].start()

    def total(self, k):
        rows = self.rows(k)
        self.to_core[1][k].wait_recv()
        self.to_x[k].wait_recv()
        return (
            self.part[self.me.r, rows].astype(F32) + self.mate[1, rows].astype(F32)
            + self.in_x[rows].astype(F32)
        )

    def close(self):
        for copy in self.to_core[0] + self.to_core[1] + self.to_x:
            copy.wait_send()


class Share:
    def __init__(self, me, array, x_sems, core_sems):
        size = array.shape[1] // RS_CHUNKS

        def piece(row, k):
            return array.at[row, pl.ds(k * size, size)]

        self.to_x = [
            push(piece(me.r, k), piece(me.r, k), x_sems, k, me.x) for k in range(RS_CHUNKS)
        ]
        self.to_core = [
            push(piece(me.r, k), piece(me.r, k), core_sems, k, me.core) for k in range(RS_CHUNKS)
        ]
        self.passed = [
            push(piece(me.r_x, k), piece(me.r_x, k), core_sems, RS_CHUNKS + k, me.core)
            for k in range(RS_CHUNKS)
        ]

    def send(self, k):
        self.to_x[k].start()
        self.to_core[k].start()

    def relay(self, k):
        self.to_x[k].wait_recv()
        self.passed[k].start()

    def arrived(self, k):
        self.to_core[k].wait_recv()
        self.passed[k].wait_recv()

    def close(self):
        for copy in self.to_x + self.to_core + self.passed:
            copy.wait_send()


def finish_sends(copies):
    for copy in copies:
        copy.wait_send()


class Bag:
    def __init__(self, names, refs):
        self.__dict__.update(zip(names, refs))


MLP_BLOCKS = 3
VECTORS = ("gate_bias", "lift_bias", "conv_bias", "recur_bias", "input_bias", "decay_param")
LANES = 128


def block_kernel(names, *refs):
    R = Bag(names, refs)
    me = Spot()
    r, c, z, y = me.r, me.c, me.z, me.y
    length, width = R.inputs.shape
    seq_length = length * 8
    wide = 2 * R.gp.shape[0]
    side = wide // 2
    step = length // RS_CHUNKS
    tokens_all = 4 * length
    tiles = (length // TILE, TILE, wide)
    diag = (me.r_x + 1 - 2 * lax.rem(me.r_x, 2), c)
    row_peers = (me.core, me.x, diag)
    chan_peers = peers_of(me)
    x_place, core_place = lax.div(r, 2), lax.rem(r, 2)

    def far_first(i):
        return 2 * lax.rem(x_place + 1 + lax.div(i, 2), 2) + lax.rem(core_place + 1 + lax.rem(i, 2), 2)

    vec, taps = R.vec, R.taps
    keep = dict(gate_pre=R.gate_h, lext=R.lext_h, conv=R.conv_h, rec=R.rec_h, opening=R.open_h,
                state=R.state_h, mixed_t=R.mixed_h)

    def tallies_of(s):
        fill_tallies(R.tallies, R.starts_all[s, 0:1], c * length, length, seq_length)

    def same(shift):
        return same_document(R.tallies, length, shift, wide)


    glo = [
        Spread(me, [lambda k, half, m=m: R.wq.at[m, half, pl.ds(pl.multiple_of(k * 48, 16), 48)]], 4,
               R.spread[5 * m : 5 * m + 5])
        for m in range(3)
    ]

    def mlp_slab(b):
        size = width // 8

        def slab(k, half):
            rows = pl.ds(pl.multiple_of(k * size, 16), size)
            return R.w.at[b, rows, pl.ds(pl.multiple_of(half * 3 * LANES, LANES), 3 * LANES)]

        return slab

    mlp_w = [
        Spread(me, [mlp_slab(b)], 8, R.spread[15 + 5 * b : 20 + 5 * b]) for b in range(MLP_BLOCKS)
    ]
    sline = Line([glo[0], glo[2]] + mlp_w, (0, 4, 8, 16, 24))

    part = R.opart
    sum1 = RowsSum(me, part, R.mate, R.out_x, R.in_x, (R.ms, R.mr), (R.rxs, R.rxr))

    def forward(gate_pre, lext, conv, rec, opening, a, b, mixed_t, rg32, ig32, md_v):
        barrier = pltpu.get_barrier_semaphore()
        always = list(row_peers) + chan_peers
        for device in always:
            pl.semaphore_signal(barrier, inc=1, device_id=device, device_id_type=MESH)
        count = len(always)
        for there, place in ((c < 7, lax.rem(c + 1, 8)), (c > 0, lax.rem(c + 7, 8))):
            for i in (1, 2, 3):

                @pl.when(there)
                def _(i=i, place=place):
                    pl.semaphore_signal(
                        barrier, inc=1, device_id=(lax.rem(r + i, 4), place), device_id_type=MESH
                    )

            count = count + jnp.where(there, 3, 0)
        own = [
            pltpu.make_async_copy(R.gp, R.wq.at[0, y], R.loc.at[12]),
            pltpu.make_async_copy(R.lp, R.wq.at[1, y], R.loc.at[13]),
            pltpu.make_async_copy(R.op, R.wq.at[2, y], R.loc.at[0]),
            pltpu.make_async_copy(R.md, md_v, R.loc.at[14]),
        ]
        for blk in range(MLP_BLOCKS):
            lanes = pl.ds(blk * LANES, LANES)
            for i, (source, at) in enumerate(
                ((R.mg, 4 * y), (R.mu, 4 * y + 1))
            ):
                column = pl.ds(pl.multiple_of(at * LANES, LANES), LANES)
                own.append(
                    pltpu.make_async_copy(
                        source.at[:, lanes], R.w.at[blk, :, column], R.loc.at[1 + 2 * blk + i]
                    )
                )

        @pl.when(z == r)
        def _():
            for copy in own:
                copy.start()

        heads = [
            pltpu.make_async_copy(R.rgate_all.at[pl.ds(2 * r, 2)], rg32, R.loc.at[10]),
            pltpu.make_async_copy(R.igate_all.at[pl.ds(2 * r, 2)], ig32, R.loc.at[11]),
        ]
        for copy in heads:
            copy.start()
        R.call[r] = R.cot[...]
        vals = R.inputs[...].astype(F32)
        scale = lax.rsqrt(jnp.mean(vals * vals, axis=-1, keepdims=True) + EPSILON)
        R.nall[r] = (vals * scale * R.mix_gain[...]).astype(LOW)
        R.starts_all[r] = jnp.full(R.starts_all.shape[1:], jnp.iinfo(jnp.int32).max, jnp.int32)
        R.starts_all[r, 0:1, 0 : R.starts.shape[1]] = R.starts[...]
        mine = pl.ds(pl.multiple_of(r * wide, LANES), wide)
        count_rows = wide // LANES
        for i, name in enumerate(VECTORS):
            for k in range(count_rows):
                place = pl.ds(r * count_rows + k, 1)
                vec[i : i + 1, k * LANES : (k + 1) * LANES] = getattr(R, name)[place]
        decay = vec[5:6]
        vec[5:6] = jnp.log1p(jnp.exp(-decay))
        vec[6:7] = jax.nn.sigmoid(-decay)
        taps[...] = R.conv_taps[:, mine]

        @pl.when(z == r)
        def _():
            for copy in own[:2]:
                copy.wait()

        pl.semaphore_wait(barrier, count)

        mine_n, mine_c = R.nall.at[r], R.call.at[r]
        theirs_n, theirs_c = R.nall.at[me.r_x], R.call.at[me.r_x]
        x_n = push(mine_n, mine_n, (R.xs, R.xr), 0, me.x)
        c_n = push(mine_n, mine_n, (R.cs, R.cr), 0, me.core)
        c_c = push(mine_c, mine_c, (R.cs, R.cr), 1, me.core)
        x_c = push(mine_c, mine_c, (R.xs, R.xr), 1, me.x)
        fwd_n = push(theirs_n, theirs_n, (R.cs, R.cr), 2, me.core)
        fwd_c = push(theirs_c, theirs_c, (R.cs, R.cr), 3, me.core)
        s_copies = [
            push(R.starts_all.at[r], R.starts_all.at[r], (R.ss, R.sr), i, device)
            for i, device in enumerate(row_peers)
        ]
        tail = R.nall.at[r, pl.ds(length - 16, 16)]
        halo_copies = [
            push(tail, R.halo.at[r], (R.hs, R.hr), i, (lax.rem(r + i, 4), lax.rem(c + 1, 8)))
            for i in range(4)
        ]
        x_n.start()
        for copy in s_copies:
            copy.start()

        @pl.when(c < 7)
        def _():
            for copy in halo_copies:
                copy.start()

        c_n.start()
        c_c.start()

        @pl.when(c == 0)
        def _():
            R.halo[...] = jnp.zeros_like(R.halo)

        for k in range(4):

            @pl.when(z == r)
            def _(k=k):
                glo[1].send(k)

            @pl.when(z != r)
            def _(k=k):
                glo[1].follow(k)

            if k == 1:
                for copy in heads:
                    copy.wait()
                pair_diagonal(R.rgate, rg32)
                pair_diagonal(R.igate, ig32)
        x_n.wait_recv()
        fwd_n.start()
        x_c.start()

        @pl.when(z == r)
        def _():
            for copy in own[2:]:
                copy.wait()
            column = pl.ds(pl.multiple_of((2 + y) * LANES, LANES), LANES)
            for blk in range(MLP_BLOCKS):
                R.w[blk, :, column] = md_v[blk * LANES : (blk + 1) * LANES].T

        sline.advance(0)
        glo[1].arrived()
        c_n.wait_recv()
        fwd_n.wait_recv()
        for copy in s_copies:
            copy.wait_recv()

        @pl.when(c > 0)
        def _():
            for i in range(4):
                landed(me, R.halo.at[i], (R.hs, R.hr), i)

        def mixer_one(s):
            tallies_of(s)
            tokens = R.nall[s]
            wlift = R.wq[1].reshape(wide, width)
            lifted = nt(tokens, wlift) + vec[1:2]
            lext[s, 0:8] = (nt(R.halo[s], wlift) + vec[1:2])[8:16]
            lext[s, pl.ds(8, length)] = lifted
            out = vec[2:3] + taps[0:1] * lifted
            for k in range(1, 4):
                out = out + taps[k : k + 1] * lext[s, pl.ds(8 - k, length)] * same(-k)
            conv[s] = out
            low = out.astype(LOW)
            recur = jax.nn.sigmoid(nn(low, R.rgate[...]) + vec[3:4])
            opened = jax.nn.sigmoid(nn(low, R.igate[...]) + vec[4:5])
            rec[s] = recur
            opening[s] = opened
            reset = same(-1) < 0.5
            decay, scaling = decay_terms(recur, vec[5:6], reset)
            decay = jnp.where(reset, 0.0, decay)
            a_scan, b_scan = tile_scan(
                decay.reshape(tiles), (scaling * opened * out).reshape(tiles), False
            )
            a[s] = a_scan.reshape(length, wide)
            b[s] = b_scan.reshape(length, wide)
            product = jnp.ones((1, wide), F32)
            state = jnp.zeros((1, wide), F32)
            for t in range(length // TILE):
                last = t * TILE + TILE - 1
                a_last = a[s, last : last + 1]
                state = b[s, last : last + 1] + a_last * state
                product = product * a_last
            R.tot[s, 0:1] = product
            R.tot[s, 1:2] = state

        sline.during(0, 4, mixer_one)
        carry_copies = carry_start(me, False, R.tot, R.slots, (R.ps, R.pr))
        local = dict(gate_pre=gate_pre, lext=lext, conv=conv, rec=rec, opening=opening, state=b,
                     mixed_t=mixed_t)
        saved = {
            name: pltpu.make_async_copy(local[name], keep[name], R.outs.at[i])
            for i, name in enumerate(keep)
        }
        for name in ("lext", "conv", "rec", "opening"):
            saved[name].start()
        sline.advance(4 + 2 * SPREAD_LAG)
        glo[0].arrived()

        def gate_part(s):
            gate_pre[s] = nt(R.nall[s], R.wq[0].reshape(wide, width)) + vec[0:1]

        sline.during(0, 4, gate_part)
        saved["gate_pre"].start()
        carry_join(me, False, R.slots, R.start, (R.ps, R.pr))
        sline.advance(8 + 2 * SPREAD_LAG)
        glo[2].arrived()

        def mixer_two(i):
            s = far_first(i)
            state = R.start[pl.ds(s, 1)]
            for t in range(length // TILE):
                tile = pl.ds(t * TILE, TILE)
                now = b[s, tile] + a[s, tile] * state
                b[s, tile] = now
                state = now[TILE - 1 : TILE]
            gate_val, _ = gelu_pair(gate_pre[s])
            mix = (b[s] * gate_val).astype(LOW)
            mixed_t[:, pl.ds(pl.multiple_of(s * length, LANES), length)] = mix.T
            part[s] = nn(mix, R.wq[2].reshape(wide, width)).astype(LOW)

        sline.during(0, 2, mixer_two)
        sum1.start(0)
        sline.during(2, 3, mixer_two)
        sum1.start(1)
        sum1.cross((0, 1, 2))
        sline.during(3, 4, mixer_two)
        x_c.wait_recv()
        fwd_c.start()
        for name in ("state", "mixed_t"):
            saved[name].start()
        for m in range(3):
            glo[m].close()
        for copy in (x_n, x_c, c_n, fwd_n):
            copy.wait_send()
        c_c.wait()
        fwd_c.wait()
        finish_sends(s_copies)

        @pl.when(c < 7)
        def _():
            finish_sends(halo_copies)

        carry_sent(me, False, carry_copies)
        for copy in saved.values():
            copy.wait()

    tall = pltpu.VMEM((4, length, wide), F32)
    ext = pltpu.VMEM((4, length + TILE, wide), F32)
    low_t = pltpu.VMEM((wide, tokens_all), LOW)
    pl.run_scoped(
        forward, gate_pre=tall, lext=ext, conv=tall, rec=tall, opening=tall, a=tall, b=tall,
        mixed_t=low_t, rg32=pltpu.VMEM((2, GB, GB), F32),
        ig32=pltpu.VMEM((2, GB, GB), F32), md_v=pltpu.VMEM(R.md.shape, LOW),
    )


    groups = [R.reduce[11 * i : 11 * i + 11] for i in range(MLP_BLOCKS)]
    rest = R.reduce[11 * MLP_BLOCKS :]
    line = Line(
        [
            Reduce(
                me, [R.grad.at[blk]], [R.grad.at[blk, y]], [R.y_w.at[blk]], [R.z_w.at[blk]],
                [R.own_w.at[:, pl.ds(blk * 3 * LANES, 3 * LANES)]], 8, groups[blk],
            )
            for blk in range(MLP_BLOCKS)
        ]
        + [
            Reduce(me, [R.early], [R.early.at[y]], [R.y_e], [R.z_e], [R.own_e], 8, rest[:11]),
            Reduce(me, [R.late], [R.late.at[y]], [R.y_l], [R.z_l], [R.own_l], 7, rest[11:], 0,
                   LATE_LAGS),
        ],
        (0, 8, 16, 24, 33),
    )
    half = length // 2

    def mlp(acc_out, acc_in, n2_t, hid, low_a, low_b, gpart):
        share1 = Share(me, R.n2all, (R.ax, R.bx), (R.ac, R.bc))

        def norm_chunk(k):
            rows = pl.ds(k * step, step)
            res = R.inputs[rows].astype(F32) + sum1.total(k) + R.out_bias[...]
            R.resid[rows] = res
            scale = lax.rsqrt(jnp.mean(res * res, axis=-1, keepdims=True) + EPSILON)
            R.n2all[r, rows] = (res * scale * R.mlp_gain[...]).astype(LOW)
            share1.send(k)

        def turn(h):
            @pl.loop(0, 4)
            def _(s):
                at = pl.ds(pl.multiple_of(s * length + h * half, LANES), half)
                n2_t[:, at] = R.n2all[s, pl.ds(h * half, half)].T

        def mlp_tokens(blk, h, i):
            pair = pl.ds(2 * lax.rem(x_place + 1 + i, 2), 2)
            rows = pl.ds(h * half, half)
            fold = lambda v: v.reshape(2, half, v.shape[1])
            flat = lambda v: v.reshape(2 * half, v.shape[2])
            tokens, cot = flat(R.n2all[pair, rows]), flat(R.call[pair, rows])
            sides = (slice(0, 2 * LANES), slice(4 * LANES, 6 * LANES))
            across = slice(2 * LANES, 4 * LANES)
            first, second = [nn(tokens, R.w[blk, :, side_of]) for side_of in sides]
            gate = jnp.concatenate([first[:, :LANES], second[:, :LANES]], axis=1)
            up = jnp.concatenate([first[:, LANES:], second[:, LANES:]], axis=1)
            grad_hidden = nn(cot, R.w[blk, :, across])
            gate_val, slope = gelu_pair(gate)
            hidden = (gate_val * up).astype(LOW)
            grad_gate = (grad_hidden * up * slope).astype(LOW)
            grad_up = (grad_hidden * gate_val).astype(LOW)
            kept = blk % 2
            hid[kept, pair, rows] = fold(hidden)
            lows = [
                jnp.concatenate([grad_gate[:, at], grad_up[:, at]], axis=1)
                for at in (slice(0, LANES), slice(LANES, 2 * LANES))
            ]
            low_a[kept, pair, rows] = fold(lows[0])
            low_b[kept, pair, rows] = fold(lows[1])
            out = fold(nt(hidden, R.w[blk, :, across]))
            back = fold(nt(lows[0], R.w[blk, :, sides[0]]) + nt(lows[1], R.w[blk, :, sides[1]]))
            if blk == 0:
                acc_out[pair, rows] = out
                acc_in[pair, rows] = back
            elif blk < MLP_BLOCKS - 1:
                acc_out[pair, rows] += out
                acc_in[pair, rows] += back
            else:
                R.opart[pair, rows] = (acc_out[pair, rows] + out).astype(LOW)
                gpart[pair, rows] = (acc_in[pair, rows] + back).astype(LOW)

        def mlp_weights(blk):
            kept = blk % 2
            columns = lambda i: pl.ds(pl.multiple_of(i * 256, 256), 256)
            flat = lambda v: v.reshape(tokens_all, v.shape[2])
            hid_t = flat(hid[kept]).T

            @pl.loop(0, width // 256)
            def _(i):
                at = columns(i)
                down = nn(hid_t, flat(R.call[:, :, at])).astype(LOW).T
                for j, low in enumerate((low_a, low_b)):
                    R.grad[blk, j, at, 0 : 2 * LANES] = nn(n2_t[at], flat(low[kept])).astype(LOW)
                    R.grad[blk, j, at, 2 * LANES :] = down[:, j * LANES : (j + 1) * LANES]

        def weights_here(blk):
            sline.advance(max(sline.done, sline.offsets[2 + blk] + 8 + 2 * SPREAD_LAG))
            mlp_w[blk].arrived()

        norm_chunk(0)
        sline.advance(17)
        norm_chunk(1)
        sum1.cross((3,))
        sline.advance(19)
        norm_chunk(2)
        for k in range(2):
            share1.relay(k)
            sline.advance(20 + k)
        for k in range(2):
            share1.arrived(k)
        weights_here(0)
        turn(0)
        sline.during(0, 2, lambda i: mlp_tokens(0, 0, i))
        norm_chunk(3)
        share1.relay(2)
        weights_here(1)
        sline.during(0, 2, lambda i: mlp_tokens(1, 0, i))
        share1.relay(3)
        for k in range(2, RS_CHUNKS):
            share1.arrived(k)
        turn(1)
        sline.during(0, 2, lambda i: mlp_tokens(0, 1, i))
        sline.during(0, 2, lambda i: mlp_tokens(1, 1, i))
        mlp_weights(0)
        sline.advance(max(sline.done, sline.offsets[4] + 8 + 2 * SPREAD_LAG))
        mlp_weights(1)
        weights_here(2)
        line.ready(1)
        line.advance(0)
        sum1.close()
        share1.close()
        sum2 = RowsSum(me, gpart, R.mate, R.out_x, R.in_x, (R.m2s, R.m2r), (R.rx2s, R.rx2r))
        line.during(0, 2, lambda i: mlp_tokens(2, 0, i))
        for block in range(2):
            sum2.start(block, (0, 1))
        line.during(0, 1, lambda i: mlp_tokens(2, 1, i))
        sum2.cross((0, 1))
        line.during(1, 2, lambda i: mlp_tokens(2, 1, i))
        for block in range(2):
            sum2.start(block, (2, 3))
        mlp_weights(2)
        line.ready(2)
        line.advance(5)
        sum2.cross((2, 3))
        ball = R.n2all
        share2 = Share(me, ball, (R.a2x, R.b2x), (R.a2c, R.b2c))
        gain_sum = 0.0
        bias_sum = 0.0
        for k in range(RS_CHUNKS):
            rows = pl.ds(k * step, step)
            grad = sum2.total(k)
            res = R.resid[rows]
            scale = lax.rsqrt(jnp.mean(res * res, axis=-1, keepdims=True) + EPSILON)
            gain_sum = gain_sum + jnp.sum(grad * res * scale, axis=0, keepdims=True)
            pulled = grad * R.mlp_gain[...]
            inner = jnp.mean(pulled * res, axis=-1, keepdims=True)
            total = R.cot[rows].astype(F32) + scale * pulled - res * (scale * scale * scale * inner)
            bias_sum = bias_sum + jnp.sum(total, axis=0, keepdims=True)
            R.gresid[rows] = total
            ball[r, rows] = total.astype(LOW)
            share2.send(k)
            line.advance(6 + k)
        R.gain_keep[0:1] = gain_sum
        R.gain_keep[1:2] = bias_sum
        for k in range(RS_CHUNKS):
            share2.relay(k)
            line.advance(10 + k)
        for k in range(RS_CHUNKS):
            share2.arrived(k)
        share2.close()
        sum2.close()

    kept = pltpu.VMEM((2, 4, length, 2 * LANES), LOW)
    pl.run_scoped(
        mlp, acc_out=pltpu.VMEM((4, length, width), F32), acc_in=pltpu.VMEM((4, length, width), F32),
        n2_t=pltpu.VMEM((width, tokens_all), LOW), hid=kept, low_a=kept, low_b=kept,
        gpart=pltpu.VMEM((4, length, width), LOW),
    )
    for one in mlp_w:
        one.close()


    def backward(gate_pre, conv, rec, opening, state, a, b, gconv, gate_low, gate_t, mixed_t, acc_r,
                 acc_i, prev_ext):
        local = dict(gate_pre=gate_pre, conv=conv, rec=rec, opening=opening, state=state,
                     mixed_t=mixed_t)
        loads = [
            pltpu.make_async_copy(keep[name], ref, R.outs.at[i])
            for i, (name, ref) in enumerate(local.items())
        ]
        for copy in loads:
            copy.start()
        ball = R.n2all
        sum3 = RowsSum(me, R.opart, R.o_mate, R.o_out, R.o_in, (R.oms, R.omr), (R.oxs, R.oxr))
        for block in range(2):
            sum3.start(block)
        for copy in loads:
            copy.wait()
        acc_r[...] = jnp.zeros_like(acc_r)
        acc_i[...] = jnp.zeros_like(acc_i)
        R.sums[...] = jnp.zeros_like(R.sums)

        def reset_of(s):
            tallies_of(s)
            return same(-1) < 0.5

        def mixer_three(s):
            grad_mixed = nt(ball[s], R.wq[2].reshape(wide, width))
            gate_val, slope = gelu_pair(gate_pre[s])
            grad_gate = grad_mixed * state[s] * slope
            low = grad_gate.astype(LOW)
            gate_low[s] = low
            gate_t[:, pl.ds(pl.multiple_of(s * length, LANES), length)] = low.T
            R.sums[0:1] += jnp.sum(grad_gate, axis=0, keepdims=True)
            grad_state = grad_mixed * gate_val
            gate_pre[s] = grad_state
            decay = jnp.where(reset_of(s), 0.0, jnp.exp(-8.0 * rec[s] * vec[5:6]))
            a_scan, b_scan = tile_scan(
                decay.reshape(tiles), (decay * grad_state).reshape(tiles), True
            )
            a[s, 0:length] = a_scan.reshape(length, wide)
            b[s] = b_scan.reshape(length, wide)
            product = jnp.ones((1, wide), F32)
            carried = jnp.zeros((1, wide), F32)
            for t in range(length // TILE - 1, -1, -1):
                head = t * TILE
                a_head = a[s, head : head + 1]
                carried = b[s, head : head + 1] + a_head * carried
                product = product * a_head
            R.tot[s, 0:1] = product
            R.tot[s, 1:2] = carried

        line.during(0, 4, mixer_three)
        carry_copies = carry_start(me, True, R.tot, R.slots2, (R.p2s, R.p2r))
        columns = lambda i: pl.ds(pl.multiple_of(i * 256, 256), 256)

        def weight_grad(target, at, left_t, right):
            @pl.loop(0, width // 256)
            def _(i):
                product = nn(left_t[...], right[:, :, columns(i)].reshape(tokens_all, 256)).astype(LOW)
                for j in range(2):
                    target[j, at : at + side, columns(i)] = product[j * side : (j + 1) * side]

        weight_grad(R.early, 0, mixed_t, ball)
        weight_grad(R.early, side, gate_t, R.nall)
        line.ready(3)
        sum3.cross()
        line.advance(20)
        carry_join(me, True, R.slots2, R.carry, (R.p2s, R.p2r))

        def mixer_four(s):
            now = R.carry[pl.ds(s, 1)]
            gconv[s, pl.ds(length, TILE)] = jnp.broadcast_to(now, (TILE, wide))
            for t in range(length // TILE - 1, -1, -1):
                rows = pl.ds(t * TILE, TILE)
                moved = b[s, rows] + a[s, rows] * now
                gconv[s, rows] = moved
                now = moved[0:1]
            carried = gate_pre[s] + gconv[s, pl.ds(1, length)]
            prev_ext[0:TILE] = jnp.broadcast_to(R.start[pl.ds(s, 1)], (TILE, wide))
            prev_ext[pl.ds(TILE, length)] = state[s]
            previous = prev_ext[pl.ds(TILE - 1, length)]
            recur, opened, conv_s = rec[s], opening[s], conv[s]
            reset = reset_of(s)
            decay, scaling = decay_terms(recur, vec[5:6], reset)
            pulled = carried * scaling
            grad_opening = pulled * conv_s
            grad_log = carried * (previous * decay - opened * conv_s * (decay * decay / scaling))
            grad_log = jnp.where(reset, 0.0, grad_log)
            grad_rec = grad_log * (-8.0 * vec[5:6])
            grad_rpre = grad_rec * recur * (1.0 - recur)
            grad_opre = grad_opening * opened * (1.0 - opened)
            r_low, o_low, conv_low = grad_rpre.astype(LOW), grad_opre.astype(LOW), conv_s.astype(LOW)
            total = pulled * opened + nt(r_low, R.rgate[...]) + nt(o_low, R.igate[...])
            gconv[s, 0:length] = total
            acc_r[...] += tn(conv_low, r_low)
            acc_i[...] += tn(conv_low, o_low)
            R.sums[7:8] += jnp.sum(grad_rpre, axis=0, keepdims=True)
            R.sums[8:9] += jnp.sum(grad_opre, axis=0, keepdims=True)
            R.sums[9:10] += jnp.sum(grad_log * recur, axis=0, keepdims=True) * (8.0 * vec[6:7])
            R.sums[6:7] += jnp.sum(total, axis=0, keepdims=True)

        line.during(0, 4, mixer_four)
        lext = a
        load_lext = pltpu.make_async_copy(keep["lext"], lext, R.outs.at[6])
        load_lext.start()
        heads = [
            push(gconv.at[s, pl.ds(0, TILE)], R.heads_in.at[s], (R.h2s, R.h2r), s,
                 (r, lax.rem(c + 7, 8)))
            for s in range(4)
        ]

        @pl.when(c > 0)
        def _():
            for copy in heads:
                copy.start()

        @pl.when(c == 7)
        def _():
            R.heads_in[...] = jnp.zeros_like(R.heads_in)

        cut = side // 8
        for k in range(8):
            at = k * cut
            R.gate_send[k] = jnp.concatenate(
                [m[j * side + at : j * side + at + cut, j * side : (j + 1) * side]
                 for m in (acc_r, acc_i) for j in range(2)], axis=0
            ).astype(LOW)
        gate_copies = [
            push(R.gate_send.at[lax.rem(c + d, 8)], R.gate_slots.at[d], (R.qs, R.qr), d,
                 chan_peers[d - 1])
            for d in range(1, 8)
        ]
        for copy in gate_copies:
            copy.start()
        for k in range(RS_CHUNKS):
            rows = pl.ds(k * step, step)
            R.output[rows] = (R.resid[rows] + sum3.total(k)).astype(LOW)
        line.advance(26)
        load_lext.wait()

        @pl.when(c < 7)
        def _():
            for s in range(4):
                landed(me, R.heads_in.at[s], (R.h2s, R.h2r), s)

        lift_t = mixed_t
        gpart1 = R.call

        def mixer_five(i):
            s = far_first(i)
            tallies_of(s)
            grad = gconv[s, 0:length]
            prev_ext[0:length] = grad
            prev_ext[pl.ds(length, TILE)] = R.heads_in[s]
            grad_lifted = taps[0:1] * grad
            R.sums[2:3] += jnp.sum(grad * lext[s, pl.ds(TILE, length)], axis=0, keepdims=True)
            for k in range(1, 4):
                ahead = prev_ext[pl.ds(k, length)] * same(k)
                grad_lifted = grad_lifted + taps[k : k + 1] * ahead
                behind = lext[s, pl.ds(TILE - k, length)] * same(-k)
                R.sums[2 + k : 3 + k] += jnp.sum(grad * behind, axis=0, keepdims=True)
            R.sums[1:2] += jnp.sum(grad_lifted, axis=0, keepdims=True)
            lift_low = grad_lifted.astype(LOW)
            lift_t[:, pl.ds(pl.multiple_of(s * length, LANES), length)] = lift_low.T
            gpart1[s] = (
                nn(gate_low[s], R.wq[0].reshape(wide, width))
                + nn(lift_low, R.wq[1].reshape(wide, width))
            ).astype(LOW)

        sum4 = RowsSum(me, gpart1, R.mate, R.out_x, R.in_x, (R.m3s, R.m3r), (R.rx3s, R.rx3r))
        line.during(0, 2, mixer_five)
        sum4.start(0)
        line.during(2, 3, mixer_five)
        sum4.start(1)
        sum4.cross()
        line.during(3, 4, mixer_five)
        R.late[...] = jnp.zeros_like(R.late)
        weight_grad(R.late, 0, lift_t, R.nall)
        for j in range(2):
            R.late[j, side : side + 16, 0:side] = R.sums[:, j * side : (j + 1) * side].astype(LOW)
        line.ready(4)
        for k in range(7):
            line.reduces[4].y_send(k)
        line.advance(32)
        gain_sum = 0.0
        for k in range(RS_CHUNKS):
            rows = pl.ds(k * step, step)
            grad = sum4.total(k)
            vals = R.inputs[rows].astype(F32)
            scale = lax.rsqrt(jnp.mean(vals * vals, axis=-1, keepdims=True) + EPSILON)
            gain_sum = gain_sum + jnp.sum(grad * vals * scale, axis=0, keepdims=True)
            pulled = grad * R.mix_gain[...]
            inner = jnp.mean(pulled * vals, axis=-1, keepdims=True)
            R.ginputs[rows] = (
                R.gresid[rows] + scale * pulled - vals * (scale * scale * scale * inner)
            ).astype(LOW)
            line.advance(34 + 2 * k)
        for k in range(8):
            lanes = slice(k * LANES, (k + 1) * LANES)
            R.gain_slots[0, k] = jnp.concatenate(
                [gain_sum[:, lanes], R.gain_keep[0:1, lanes], R.gain_keep[1:2, lanes],
                 jnp.zeros((5, LANES), F32)], 0
            )
        gain_copies = [
            push(R.gain_slots.at[0, lax.rem(c + d, 8)], R.gain_slots.at[1, d], (R.ggs, R.ggr), d,
                 chan_peers[d - 1])
            for d in range(1, 8)
        ]
        for copy in gain_copies:
            copy.start()
        line.advance(42)
        gate_total = R.gate_send[c].astype(F32)
        for d in range(1, 8):
            gate_copies[d - 1].wait_recv()
            gate_total = gate_total + R.gate_slots[d].astype(F32)
        R.gates_all[r] = gate_total.astype(LOW)
        gate_rows = [
            push(R.gates_all.at[r], R.gates_all.at[r], (R.ts, R.tr), i, device)
            for i, device in enumerate(row_peers)
        ]
        for copy in gate_rows:
            copy.start()
        shared = R.gain_slots[0, c]
        for d in range(1, 8):
            gain_copies[d - 1].wait_recv()
            shared = shared + R.gain_slots[1, d]
        R.gain_sums[0] = shared
        row_copies = [
            push(R.gain_sums.at[0], R.gain_sums.at[1 + i], (R.ghs, R.ghr), i, device)
            for i, device in enumerate(row_peers)
        ]
        for copy in row_copies:
            copy.start()
        line.advance(line.last())
        for copy in row_copies + gate_rows:
            copy.wait()
        for row in range(4):
            found = R.gates_all[row].astype(F32)
            for head in range(2):
                R.rgate_o[2 * row + head] = found[head * cut : (head + 1) * cut]
                R.igate_o[2 * row + head] = found[(2 + head) * cut : (3 + head) * cut]
        R.gains_all[...] = R.gain_sums[0] + R.gain_sums[1] + R.gain_sums[2] + R.gain_sums[3]

        @pl.when(c > 0)
        def _():
            finish_sends(heads)

        finish_sends(gain_copies + gate_copies)
        sum3.close()
        sum4.close()
        carry_sent(me, True, carry_copies)
        line.close()

    square = pltpu.VMEM((wide, wide), F32)
    pl.run_scoped(
        backward, gate_pre=tall, conv=tall, rec=tall, opening=tall, state=tall, a=ext, b=tall,
        gconv=ext, gate_low=pltpu.VMEM((4, length, wide), LOW), gate_t=low_t, mixed_t=low_t,
        acc_r=square, acc_i=square, prev_ext=pltpu.VMEM((length + TILE, wide), F32),
    )


def block(ins):
    far = ("rgate_all", "igate_all", "gp", "lp", "op", "mg", "mu", "md")
    inputs, starts, mg = ins["inputs"], ins["starts"], ins["mg"]
    length, width = inputs.shape
    side = ins["gp"].shape[0]
    wide = 2 * side
    hidden = mg.shape[1]
    sd, vmem = jax.ShapeDtypeStruct, pltpu.VMEM
    blocks = hidden // LANES
    tall = sd((4, length, wide), F32)
    tokens = (4, length, width)
    outs = dict(
        output=sd(inputs.shape, LOW), ginputs=sd(inputs.shape, LOW),
        own_w=sd((width, 3 * hidden), LOW),
        own_e=sd((2 * side, width), LOW), own_l=sd((side + 32, width), LOW),
        rgate_o=sd((8, side // 8, side), F32), igate_o=sd((8, side // 8, side), F32),
        gains_all=sd((8, LANES), F32),
    )
    saved = dict(
        gate_h=tall, lext_h=sd((4, length + TILE, wide), F32), conv_h=tall, rec_h=tall, open_h=tall,
        state_h=tall, mixed_h=sd((wide, 4 * length), LOW),
    )
    scratch = dict(
        wq=vmem((3, 2, side, width), LOW), nall=vmem(tokens, LOW), halo=vmem((4, 16, width), LOW),
        starts_all=vmem((4, 8, LANES), starts.dtype), vec=vmem((8, wide), F32), taps=vmem((4, wide), F32),
        gates_all=vmem((4, side // 2, side), LOW),
        w=vmem((blocks, width, 6 * LANES), LOW),
        call=vmem(tokens, LOW), n2all=vmem(tokens, LOW), opart=vmem(tokens, LOW),
        rgate=vmem((wide, wide), LOW), igate=vmem((wide, wide), LOW),
        tallies=vmem((length + 16, LANES), F32), start=vmem((4, wide), F32), carry=vmem((4, wide), F32),
        tot=vmem((4, 2, wide), F32), slots=vmem((8, 4, 2, wide), F32), slots2=vmem((8, 4, 2, wide), F32),
        resid=vmem((length, width), F32), gresid=vmem((length, width), F32),
        mate=vmem((2, length, width), LOW), out_x=vmem((length, width), LOW),
        in_x=vmem((length, width), LOW),
        o_mate=vmem((2, length, width), LOW), o_out=vmem((length, width), LOW),
        o_in=vmem((length, width), LOW),
        grad=vmem((blocks, 2, width, 3 * LANES), LOW),
        early=vmem((2, 2 * side, width), LOW), late=vmem((2, side + 32, width), LOW),
        heads_in=vmem((4, TILE, wide), F32), sums=vmem((16, wide), F32),
        gate_send=vmem((8, side // 2, side), LOW), gate_slots=vmem((8, side // 2, side), LOW),
        gain_keep=vmem((8, width), F32), gain_slots=vmem((2, 8, 8, LANES), F32), gain_sums=vmem((4, 8, LANES), F32),
    )
    for way in "yz":
        scratch.update(
            {
                way + "_w": vmem((blocks, width, 3 * LANES), LOW),
                way + "_e": vmem((2 * side, width), LOW),
                way + "_l": vmem((side + 32, width), LOW),
            }
        )
    dma = pltpu.SemaphoreType.DMA
    counts = dict(
        loc=15, outs=7, xs=2, xr=2, cs=4, cr=4, hs=4, hr=4, ss=3, sr=3, ps=8, pr=8, p2s=8, p2r=8,
        h2s=4, h2r=4, qs=8, qr=8, ts=3, tr=3, ggs=8, ggr=8, ghs=3, ghr=3,
    )
    for name in ("m", "m2", "m3", "om"):
        counts.update({name + "s": 2 * RS_CHUNKS, name + "r": 2 * RS_CHUNKS})
    for name in ("rx", "rx2", "rx3", "ox"):
        counts.update({name + "s": RS_CHUNKS, name + "r": RS_CHUNKS})
    for name in ("", "2"):
        counts.update({f"a{name}x": RS_CHUNKS, f"b{name}x": RS_CHUNKS})
        counts.update({f"a{name}c": 2 * RS_CHUNKS, f"b{name}c": 2 * RS_CHUNKS})
    scratch.update({name: dma((count,)) for name, count in counts.items()})
    names = list(ins) + list(outs) + list(saved) + list(scratch)
    spread = spread_sems(1, 4) * 3 + spread_sems(1, 8) * blocks
    reduce = reduce_sems(1, 8) * blocks + reduce_sems(1, 8) + reduce_sems(1, 7)

    def kernel(*refs):
        n, m = len(names), len(spread)
        block_kernel(names + ["spread", "reduce"], *refs[:n], refs[n : n + m], refs[n + m :])

    results = pl.pallas_call(
        kernel,
        name="block",
        out_shape=list(outs.values()) + list(saved.values()),
        in_specs=[ANYWHERE if name in far else IN_VMEM for name in ins],
        out_specs=[IN_VMEM] * len(outs) + [ANYWHERE] * len(saved),
        scratch_shapes=list(scratch.values()) + spread + reduce,
        compiler_params=comm_params(1),
    )(*ins.values())
    return results[: len(outs)]


def finish_kernel(
    output, ginputs, own_w, own_e, own_l, rgate, igate, gains, tail,
    output_o, ginputs_o, gate, up, down, out, gate_proj, lift_proj, rgate_o, igate_o, taps, *flat
):
    output_o[...] = output[...]
    ginputs_o[...] = ginputs[...]
    side = out.shape[0]
    for blk in range(MLP_BLOCKS):
        lanes = slice(blk * LANES, (blk + 1) * LANES)
        for i, target in enumerate((gate, up)):
            at = (3 * blk + i) * LANES
            target[:, lanes] = own_w[:, at : at + LANES].astype(F32)
        at = (3 * blk + 2) * LANES
        down[lanes] = own_w[:, at : at + LANES].T.astype(F32)
    out[...] = own_e[0:side].astype(F32)
    gate_proj[...] = own_e[side:].astype(F32)
    lift_proj[...] = own_l[0:side].astype(F32)
    rgate_o[...] = rgate[...]
    igate_o[...] = igate[...]
    vectors = tail[:, 0:side].astype(F32)
    taps[...] = vectors[2:6]
    for i in range(3):
        flat[i][...] = gains[i : i + 1]
    for i, row in enumerate((0, 1, 6, 7, 8, 9)):
        flat[3 + i][...] = vectors[row : row + 1]


def finish(output, ginputs, own_w, own_e, own_l, rgate, igate, gains):
    steps = 4
    width = own_w.shape[0]
    hidden = own_w.shape[1] // 3
    side = own_e.shape[0] // 2
    sd = jax.ShapeDtypeStruct

    def by_rows(shape):
        return pl.BlockSpec((shape[0] // steps,) + shape[1:], lambda i: (i,) + (0,) * (len(shape) - 1))

    def by_columns(shape):
        return pl.BlockSpec((shape[0], shape[1] // steps), lambda i: (0, i))

    def once(shape):
        return pl.BlockSpec(shape, lambda i: (0,) * len(shape))

    inward, outward, square = (width, hidden), (hidden, width), (side, width)
    tail = pl.BlockSpec((16, own_l.shape[1]), lambda i: (side // 16, 0))
    flat = [(1, gains.shape[1])] * 3 + [(1, side)] * 6
    outs = (
        [(sd(v.shape, v.dtype), by_rows(v.shape)) for v in (output, ginputs)]
        + [(sd(inward, F32), by_rows(inward))] * 2
        + [(sd(outward, F32), by_columns(outward))]
        + [(sd(square, F32), by_columns(square))] * 3
        + [(sd(v.shape, v.dtype), by_rows(v.shape)) for v in (rgate, igate)]
        + [(sd((4, side), F32), once((4, side)))]
        + [(sd(shape, F32), once(shape)) for shape in flat]
    )
    return pl.pallas_call(
        finish_kernel,
        name="finish",
        grid=(steps,),
        in_specs=[by_rows(output.shape), by_rows(ginputs.shape), by_rows(own_w.shape),
                  by_columns(own_e.shape), by_columns(own_l.shape), by_rows(rgate.shape),
                  by_rows(igate.shape), once(gains.shape), tail],
        out_specs=[o[1] for o in outs],
        out_shape=[o[0] for o in outs],
        compiler_params=pltpu.CompilerParams(vmem_limit_bytes=VMEM_BYTES),
    )(output, ginputs, own_w, own_e, own_l, rgate, igate, gains, own_l)


def split_body(
    inputs, mix_gain, gate_proj, gate_bias, lift_proj, lift_bias, conv_taps, conv_bias,
    recur_gate, recur_bias, input_gate, input_bias, decay_param, out_proj, out_bias, mlp_gain,
    mlp_gate, mlp_up, mlp_down, doc_starts, cotangent,
):
    row = lambda v: v[None]
    vectors = (gate_bias, lift_bias, conv_bias, recur_bias, input_bias, decay_param)
    output, grad_inputs, own_w, own_e, own_l, rgate_o, igate_o, gains = block(
        dict(
            inputs=inputs, cot=cotangent, mix_gain=row(mix_gain), out_bias=row(out_bias),
            mlp_gain=row(mlp_gain), **{name: v.reshape(-1, LANES) for name, v in zip(VECTORS, vectors)}, conv_taps=conv_taps, starts=doc_starts,
            rgate_all=recur_gate, igate_all=input_gate, gp=gate_proj.T, lp=lift_proj.T, op=out_proj,
            mg=mlp_gate, mu=mlp_up, md=mlp_down,
        )
    )
    (output, grad_inputs, grad_gate, grad_up, grad_down, grad_out, grad_gate_proj, grad_lift_proj,
     rgate_o, igate_o, taps, *flat) = finish(
        output, grad_inputs, own_w, own_e, own_l, rgate_o, igate_o, gains
    )
    flat = [v.reshape(v.shape[1]) for v in flat]
    return (
        output, grad_inputs, flat[0],
        grad_gate_proj.T, flat[3], grad_lift_proj.T, flat[4], taps, flat[5],
        rgate_o, flat[6], igate_o, flat[7], flat[8],
        grad_out, flat[2], flat[1],
        grad_gate, grad_up, grad_down,
    )


def solution(mesh):
    in_specs = (
        P(("rows", "chan"), None),
        P(),
        P(None, "chan"),
        P(),
        P(None, "chan"),
        P(),
        P(),
        P(),
        P(),
        P(),
        P(),
        P(),
        P(),
        P("chan", None),
        P(),
        P(),
        P(None, "chan"),
        P(None, "chan"),
        P("chan", None),
        P("rows", None),
        P(("rows", "chan"), None),
    )
    out_specs = (
        P(("rows", "chan"), None),
        P(("rows", "chan"), None),
        P("chan"),
        P(None, "chan"),
        P("chan"),
        P(None, "chan"),
        P("chan"),
        P(None, "chan"),
        P("chan"),
        P(None, "chan", None),
        P("chan"),
        P(None, "chan", None),
        P("chan"),
        P("chan"),
        P("chan", None),
        P("chan"),
        P("chan"),
        P(None, "chan"),
        P(None, "chan"),
        P("chan", None),
    )
    split = mesh.shape["rows"] == 4 and mesh.shape["chan"] == HEADS
    return jax.shard_map(split_body if split else body, mesh=mesh, in_specs=in_specs, out_specs=out_specs, check_vma=False)
```

```python
from functools import partial
import math

import jax
import jax.numpy as jnp
from jax import lax
from jax.experimental import pallas as pl
from jax.experimental.pallas import tpu as pltpu
from jax.sharding import PartitionSpec as P

D = 1024
LRU = 1536
FF = 3072
HEADS = 8
GB = 192


EPSILON = 1e-06
precise = lax.Precision.HIGHEST


def from_behind(block, axis, distance):
    devices = range(lax.axis_size(axis))
    route = [(i - distance, i) for i in devices if i - distance in devices]
    return lax.ppermute(block, axis, route)


def prefix(value, axis, join, neutral, backward):
    count, mine = (lax.axis_size(axis), lax.axis_index(axis))
    pieces = jax.tree.map(lambda part: lax.all_gather(part, axis), value)
    if backward:
        pieces = jax.tree.map(lambda part: part[::-1], pieces)
        mine = count - 1 - mine
    subtotal = jax.tree.map(
        lambda part, zero: jnp.full_like(part, 0) + jnp.asarray(zero, part.dtype), value, neutral
    )

    def hop(position, subtotal):
        longer = join(subtotal, jax.tree.map(lambda part: part[position], pieces))
        return jax.tree.map(lambda new, old: jnp.where(position < mine, new, old), longer, subtotal)

    return lax.fori_loop(0, count - 1, hop, subtotal)


def rms_scale(values, gain_vec):
    return (
        values * lax.rsqrt(jnp.mean(values * values, axis=-1, keepdims=True) + EPSILON) * gain_vec
    )


def gated_unit(gate_pre, up_vals):
    return jax.nn.gelu(gate_pre) * up_vals


def affine(earlier, later_map):
    return (earlier[0] * later_map[0], later_map[0] * earlier[1] + later_map[1])


def segment_ids(starts, start_pos, pos_count, seq_len):
    where_at = start_pos + jnp.arange(pos_count, dtype=jnp.int32)
    seq_of = jnp.floor_divide(where_at, seq_len)
    within = where_at - seq_of * seq_len
    owner = seq_of[:, None] == jnp.arange(starts.shape[0], dtype=jnp.int32)[None, :]
    passed = starts[None, :, :] <= within[:, None, None]
    doc_tally = jnp.sum(jnp.logical_and(owner[:, :, None], passed).astype(jnp.int32), axis=(1, 2))
    return seq_of * (starts.shape[1] + 1) + doc_tally


def project(normed, weights, first_bias, second_bias):
    product = jnp.einsum("td,dc->ct", normed, weights, preferred_element_type=jnp.float32)
    channels = first_bias.shape[0]
    return (product[:channels] + first_bias[:, None], product[channels:] + second_bias[:, None])


def conv_forward(lifted, tail_rows, segments, tap_vals, bias_vec):
    length = lifted.shape[1]
    extended = jnp.concatenate([tail_rows, lifted], axis=1)
    own_seg = segments[3 : 3 + length]
    result = bias_vec[:, None] + tap_vals[0][:, None] * lifted
    for offset in range(1, 4):
        same_doc = (segments[3 - offset : 3 - offset + length] == own_seg).astype(jnp.float32)
        result = (
            result
            + tap_vals[offset][:, None]
            * extended[:, 3 - offset : 3 - offset + length]
            * same_doc[None, :]
        )
    return result


def conv_backward(grad_conv, head_rows, segments, lifted, tail_rows, tap_vals):
    length = grad_conv.shape[1]
    ahead_grad = jnp.concatenate([grad_conv, head_rows], axis=1)
    behind = jnp.concatenate([tail_rows, lifted], axis=1)
    own_seg = segments[3 : 3 + length]
    grad_lifted = tap_vals[0][:, None] * grad_conv
    tap_grads = [jnp.sum(grad_conv * lifted, axis=1)]
    for offset in range(1, 4):
        later_same = (segments[3 + offset : 3 + offset + length] == own_seg).astype(jnp.float32)
        grad_lifted = (
            grad_lifted
            + tap_vals[offset][:, None]
            * ahead_grad[:, offset : offset + length]
            * later_same[None, :]
        )
        earlier = (segments[3 - offset : 3 - offset + length] == own_seg).astype(jnp.float32)
        tap_grads.append(
            jnp.sum(
                grad_conv * behind[:, 3 - offset : 3 - offset + length] * earlier[None, :], axis=1
            )
        )
    return (grad_lifted, jnp.stack(tap_grads, axis=1), jnp.sum(grad_conv, axis=1))


def coefficients(is_reset, conv_out, recur_gate, recur_bias, input_gate, input_bias, decay_param):
    channels, length = conv_out.shape
    gate_block = recur_gate.shape[1]
    grouped = conv_out.reshape(channels // gate_block, gate_block, length)
    recurrence = jax.nn.sigmoid(
        jnp.einsum("hit,hio->hot", grouped, recur_gate, precision=precise).reshape(channels, length)
        + recur_bias[:, None]
    )
    opening = jax.nn.sigmoid(
        jnp.einsum("hit,hio->hot", grouped, input_gate, precision=precise).reshape(channels, length)
        + input_bias[:, None]
    )
    log_decay = -8.0 * recurrence * jax.nn.softplus(-decay_param)[:, None]
    decay_rate = jnp.where(is_reset[None, :], 0.0, jnp.exp(log_decay))
    scaling = jnp.where(is_reset[None, :], 1.0, jnp.sqrt(-jnp.expm1(2.0 * log_decay)))
    return (decay_rate, scaling * opening * conv_out)


def reverse_local(decay_rate, grad_state):
    ones_col = jnp.ones_like(decay_rate[:, :1])
    factor = jnp.flip(jnp.concatenate([decay_rate[:, 1:], ones_col], axis=1), axis=1)
    product, carried = lax.associative_scan(affine, (factor, jnp.flip(grad_state, axis=1)), axis=1)
    return (jnp.flip(product, axis=1), jnp.flip(carried, axis=1))


def finish_state(lru_state, start_state, carried, pull_coef):
    previous = jnp.concatenate([start_state[:, None], lru_state[:, :-1]], axis=1)
    return pull_coef((carried * previous, carried))


def flatten_rows(pieces, row_count):
    return jnp.concatenate([source.reshape(row_count, -1) for source in pieces], axis=1)


def body(
    inputs,
    mix_gain,
    gate_proj,
    gate_bias,
    lift_proj,
    lift_bias,
    conv_taps,
    conv_bias,
    recur_gate,
    recur_bias,
    input_gate,
    input_bias,
    decay_param,
    out_proj,
    out_bias,
    mlp_gain,
    mlp_gate,
    mlp_up,
    mlp_down,
    doc_starts,
    cotangent,
):
    chan_count = lax.axis_size("chan")
    chan_place = lax.axis_index("chan")
    local_rows = inputs.shape[0]
    seq_length = local_rows * chan_count
    rows_f32 = inputs.astype(jnp.float32)
    cot_f32 = cotangent.astype(jnp.float32)
    normed, pull_norm = jax.vjp(rms_scale, rows_f32, mix_gain)
    normed_low = normed.astype(jnp.bfloat16)
    gate_full, lift_full, out_full, mlp_gate_full, mlp_up_full, mlp_down_full = (
        lax.all_gather(gate_proj, "chan", axis=1, tiled=True),
        lax.all_gather(lift_proj, "chan", axis=1, tiled=True),
        lax.all_gather(out_proj, "chan", axis=0, tiled=True),
        lax.all_gather(mlp_gate, "chan", axis=1, tiled=True),
        lax.all_gather(mlp_up, "chan", axis=1, tiled=True),
        lax.all_gather(mlp_down, "chan", axis=0, tiled=True),
    )
    channels = LRU
    hidden_cut = FF
    segments = segment_ids(doc_starts, chan_place * local_rows - 3, local_rows + 6, seq_length)
    mix_proj = jnp.concatenate([gate_full, lift_full], axis=1)
    gate_pre, lifted = project(normed_low, mix_proj, gate_bias, lift_bias)
    tail_rows = from_behind(lifted[:, -3:], "chan", 1)
    conv_out = conv_forward(lifted, tail_rows, segments, conv_taps, conv_bias)
    is_reset = segments[3 : 3 + local_rows] != segments[2 : 2 + local_rows]
    (decay_rate, lru_input), pull_coef = jax.vjp(
        partial(coefficients, is_reset),
        conv_out,
        recur_gate,
        recur_bias,
        input_gate,
        input_bias,
        decay_param,
    )
    running, local_state = lax.associative_scan(affine, (decay_rate, lru_input), axis=1)
    ones_vec = jnp.ones((channels,), jnp.float32)
    zeros_vec = jnp.zeros((channels,), jnp.float32)
    _, start_state = prefix(
        (running[:, -1], local_state[:, -1]), "chan", affine, (ones_vec, zeros_vec), False
    )
    lru_state = local_state + running * start_state[:, None]
    gate_val, pull_gelu = jax.vjp(jax.nn.gelu, gate_pre)
    mixed_out = (lru_state * gate_val).astype(jnp.bfloat16)
    resid = (
        rows_f32
        + jnp.einsum("ct,cd->td", mixed_out, out_full, preferred_element_type=jnp.float32)
        + out_bias
    )
    normed2, pull_norm2 = jax.vjp(rms_scale, resid, mlp_gain)
    normed2_low = normed2.astype(jnp.bfloat16)
    mlp_proj = jnp.concatenate([mlp_gate_full, mlp_up_full], axis=1)
    mlp_pre = jnp.einsum("td,df->ft", normed2_low, mlp_proj, preferred_element_type=jnp.float32)
    hidden, pull_mlp = jax.vjp(gated_unit, mlp_pre[:hidden_cut], mlp_pre[hidden_cut:])
    hidden_low = hidden.astype(jnp.bfloat16)
    output = (
        resid
        + jnp.einsum("ft,fd->td", hidden_low, mlp_down_full, preferred_element_type=jnp.float32)
    ).astype(jnp.bfloat16)
    grad_down = jnp.einsum("ft,td->fd", hidden_low, cotangent, preferred_element_type=jnp.float32)
    grad_gate_m, grad_up_m = pull_mlp(
        jnp.einsum("td,fd->ft", cotangent, mlp_down_full, preferred_element_type=jnp.float32)
    )
    grad_pre = jnp.concatenate([grad_gate_m, grad_up_m], axis=0).astype(jnp.bfloat16)
    grad_mlp_in = jnp.einsum("ft,td->fd", grad_pre, normed2_low, preferred_element_type=jnp.float32)
    grad_resid_part, grad_gain2 = pull_norm2(
        jnp.einsum("ft,df->td", grad_pre, mlp_proj, preferred_element_type=jnp.float32)
    )
    grad_resid = cot_f32 + grad_resid_part
    grad_branch = grad_resid.astype(jnp.bfloat16)
    grad_out_proj = jnp.einsum(
        "ct,td->cd", mixed_out, grad_branch, preferred_element_type=jnp.float32
    )
    grad_mixed = jnp.einsum("td,cd->ct", grad_branch, out_full, preferred_element_type=jnp.float32)
    product, carried = reverse_local(decay_rate, grad_mixed * gate_val)
    _, incoming = prefix(
        (decay_rate[:, 0] * product[:, 0], decay_rate[:, 0] * carried[:, 0]),
        "chan",
        affine,
        (ones_vec, zeros_vec),
        True,
    )
    carried = carried + product * incoming[:, None]
    coef_grads = finish_state(lru_state, start_state, carried, pull_coef)
    head_rows = from_behind(coef_grads[0][:, :3], "chan", -1)
    grad_lifted, grad_taps, grad_conv_bias = conv_backward(
        coef_grads[0], head_rows, segments, lifted, tail_rows, conv_taps
    )
    (grad_gate_pre,) = pull_gelu(grad_mixed * lru_state)
    grad_front = jnp.concatenate([grad_gate_pre, grad_lifted], axis=0).astype(jnp.bfloat16)
    grad_mix_proj = jnp.einsum(
        "ct,td->cd", grad_front, normed_low, preferred_element_type=jnp.float32
    )
    grad_normed = jnp.einsum("ct,dc->td", grad_front, mix_proj, preferred_element_type=jnp.float32)
    grad_x_part, grad_gain1 = pull_norm(grad_normed)
    grad_inputs = (grad_resid + grad_x_part).astype(jnp.bfloat16)
    grad_out_bias = jnp.sum(grad_resid, axis=0)
    pieces = [
        grad_mix_proj[:channels],
        grad_mix_proj[channels:],
        jnp.sum(grad_gate_pre, axis=1),
        jnp.sum(grad_lifted, axis=1),
        grad_taps,
        grad_conv_bias,
        jnp.transpose(coef_grads[1], (1, 0, 2)),
        coef_grads[2],
        jnp.transpose(coef_grads[3], (1, 0, 2)),
        coef_grads[4],
        coef_grads[5],
        grad_out_proj,
        grad_mlp_in[:hidden_cut],
        grad_mlp_in[hidden_cut:],
        grad_down,
        grad_gain1,
        grad_out_bias,
        grad_gain2,
    ]
    spread = flatten_rows(pieces, chan_count)
    shared = lax.psum_scatter(spread, "chan", scatter_dimension=0, tiled=True)
    summed = lax.psum(shared.reshape(-1), "rows")
    channels_dev = LRU // chan_count
    hidden_dev = FF // chan_count
    width_dev = D // chan_count
    block_dev = GB // chan_count
    shapes = [
        (channels_dev, D),
        (channels_dev, D),
        (channels_dev,),
        (channels_dev,),
        (channels_dev, 4),
        (channels_dev,),
        (block_dev, HEADS, GB),
        (channels_dev,),
        (block_dev, HEADS, GB),
        (channels_dev,),
        (channels_dev,),
        (channels_dev, D),
        (hidden_dev, D),
        (hidden_dev, D),
        (hidden_dev, D),
        (width_dev,),
        (width_dev,),
        (width_dev,),
    ]
    unpacked = []
    offset = 0
    for piece_shape in shapes:
        piece_size = math.prod(piece_shape)
        unpacked.append(summed[offset : offset + piece_size].reshape(piece_shape))
        offset = offset + piece_size
    return (
        output,
        grad_inputs,
        unpacked[15],
        unpacked[0].T,
        unpacked[2],
        unpacked[1].T,
        unpacked[3],
        unpacked[4].T,
        unpacked[5],
        jnp.transpose(unpacked[6], (1, 0, 2)),
        unpacked[7],
        jnp.transpose(unpacked[8], (1, 0, 2)),
        unpacked[9],
        unpacked[10],
        unpacked[11],
        unpacked[16],
        unpacked[17],
        unpacked[12].T,
        unpacked[13].T,
        unpacked[14],
    )


MESH = pl.DeviceIdType.MESH
LOW = jnp.bfloat16
F32 = jnp.float32
VMEM_BYTES = 63 * 2**20
TILE = 8
GELU_A = math.sqrt(2.0 / math.pi)
GELU_B = 0.044715


def nt(left, right):
    return lax.dot_general(left, right, (((1,), (1,)), ((), ())), preferred_element_type=F32)


def nn(left, right):
    return lax.dot_general(left, right, (((1,), (0,)), ((), ())), preferred_element_type=F32)


def tn(left, right):
    return lax.dot_general(left, right, (((0,), (0,)), ((), ())), preferred_element_type=F32)


def gelu_pair(values):
    squared = values * values
    bend = jnp.tanh(GELU_A * values * (1.0 + GELU_B * squared))
    half = 0.5 * (1.0 + bend)
    slope = half + 0.5 * values * (1.0 - bend * bend) * GELU_A * (1.0 + 3.0 * GELU_B * squared)
    return values * half, slope


class Spot:
    def __init__(self):
        self.r = lax.axis_index("rows")
        self.c = lax.axis_index("chan")
        self.z = lax.div(self.c, 2)
        self.y = lax.rem(self.c, 2)
        self.r_core = self.r + 1 - 2 * lax.rem(self.r, 2)
        self.r_x = lax.rem(self.r + 2, 4)
        self.core = (self.r_core, self.c)
        self.x = (self.r_x, self.c)
        self.c_y = self.c + 1 - 2 * self.y
        self.ymate = (self.r, self.c_y)
        self.up = (self.r, lax.rem(self.c + 2, 8))
        self.dn = (self.r, lax.rem(self.c + 6, 8))


def greet(always, maybe=()):
    barrier = pltpu.get_barrier_semaphore()
    count = len(always)
    for device in always:
        pl.semaphore_signal(barrier, inc=1, device_id=device, device_id_type=MESH)
    for device, there in maybe:

        @pl.when(there)
        def _(device=device):
            pl.semaphore_signal(barrier, inc=1, device_id=device, device_id_type=MESH)

        count = count + jnp.where(there, 1, 0)
    pl.semaphore_wait(barrier, count)


def push(source, target, sems, index, device):
    return pltpu.make_async_remote_copy(
        src_ref=source,
        dst_ref=target,
        send_sem=sems[0].at[index],
        recv_sem=sems[1].at[index],
        device_id=device,
        device_id_type=MESH,
    )


def landed(me, target, sems, index):
    push(target, target, sems, index, me.ymate).wait_recv()


def sem_pair(count):
    return [pltpu.SemaphoreType.DMA((count,)), pltpu.SemaphoreType.DMA((count,))]


def comm_params(collective_id):
    return pltpu.CompilerParams(
        collective_id=collective_id, has_side_effects=True, vmem_limit_bytes=VMEM_BYTES
    )


ANYWHERE = pl.BlockSpec(memory_space=pl.ANY)
IN_VMEM = pl.BlockSpec(memory_space=pltpu.VMEM)


def decay_terms(rec, softplus_row, reset):
    log_decay = -8.0 * rec * softplus_row
    decay = jnp.exp(log_decay)
    twice = 2.0 * log_decay
    series = twice * (
        1.0
        + twice * (1 / 2 + twice * (1 / 6 + twice * (1 / 24 + twice * (1 / 120 + twice * (1 / 720)))))
    )
    gap = jnp.where(twice > -0.25, -series, 1.0 - jnp.exp(twice))
    return decay, jnp.where(reset, 1.0, jnp.sqrt(gap))


def fill_tallies(tallies, starts_row, first, length, seq_length):
    position = first - 8 + lax.broadcasted_iota(jnp.int32, (length + 16, 1), 0)
    begun = jnp.sum((starts_row <= position).astype(F32), axis=1, keepdims=True)
    inside = jnp.logical_and(position >= 0, position < seq_length)
    tallies[...] = jnp.broadcast_to(jnp.where(inside, begun, -1.0), tallies.shape)


def same_document(tallies, length, shift, wide):
    own = tallies[pl.ds(8, length)]
    other = tallies[pl.ds(8 + shift, length)]
    same = (own == other).astype(F32)
    return jnp.concatenate([same] * (wide // same.shape[1]), axis=1)


def pair_diagonal(target, blocks):
    side = blocks.shape[1]
    target[...] = jnp.zeros_like(target)
    target[0:side, 0:side] = blocks[0].astype(target.dtype)
    target[side : 2 * side, side : 2 * side] = blocks[1].astype(target.dtype)


def tile_scan(a, b, backward):
    row = lax.broadcasted_iota(jnp.int32, a.shape, 1)
    for step in (1, 2, 4):
        shift = TILE - step if backward else step
        there = row < TILE - step if backward else row >= step
        b = b + a * jnp.where(there, pltpu.roll(b, shift, 1), 0.0)
        a = a * jnp.where(there, pltpu.roll(a, shift, 1), 1.0)
    return a, b


def carry_start(me, backward, totals, slots, sems):
    sign = -1 if backward else 1
    steps = me.c if backward else 7 - me.c
    copies = [
        push(totals, slots.at[d], sems, d, (me.r, lax.rem(me.c + 8 + sign * d, 8)))
        for d in range(1, 8)
    ]
    for d in range(1, 8):

        @pl.when(d <= steps)
        def _(d=d):
            copies[d - 1].start()

    return copies


def carry_join(me, backward, slots, start, sems):
    behind = 7 - me.c if backward else me.c
    start[...] = jnp.zeros_like(start)
    for d in range(7, 0, -1):

        @pl.when(d <= behind)
        def _(d=d):
            landed(me, slots.at[d], sems, d)
            start[...] = slots[d, :, 0] * start[...] + slots[d, :, 1]


def carry_sent(me, backward, copies):
    steps = me.c if backward else 7 - me.c
    for d in range(1, 8):

        @pl.when(d <= steps)
        def _(d=d):
            copies[d - 1].wait_send()


def peers_of(me):
    return [(me.r, lax.rem(me.c + d, 8)) for d in range(1, 8)]


class Spread:
    def __init__(self, me, slabs, pieces, sems):
        self.me, self.slabs, self.pieces, self.sems = me, slabs, pieces, sems
        self.go_up = jnp.logical_and(me.z >= me.r, me.z < 3)
        self.go_dn = jnp.logical_and(me.z <= me.r, me.z > 0)
        self.source = me.z == me.r
        self.hop = jnp.where(me.z < me.r, me.r - me.z, me.z - me.r)

    def copies(self, k):
        me, found = self.me, []
        for i, slab in enumerate(self.slabs):
            piece = slab(k, me.y)
            ys, yr, us, ds, zr = self.sems[5 * i : 5 * i + 5]
            found.append(
                (
                    push(piece, piece, (ys, yr), k, me.ymate),
                    push(piece, piece, (us, zr), k, me.up),
                    push(piece, piece, (ds, zr), k, me.dn),
                )
            )
        return found

    def send(self, k):
        found = self.copies(k)
        for copies in found:
            copies[0].start()

        @pl.when(self.go_up)
        def _():
            for copies in found:
                copies[1].start()

        @pl.when(self.go_dn)
        def _():
            for copies in found:
                copies[2].start()

    def follow(self, k):
        for i, slab in enumerate(self.slabs):
            us, zr = self.sems[5 * i + 2], self.sems[5 * i + 4]
            landed(self.me, slab(k, self.me.y), (us, zr), k)
        self.send(k)

    def step(self, q):
        n = self.pieces

        def at(k, also, action):
            there = jnp.logical_and(k >= 0, k < n)

            @pl.when(jnp.logical_and(there, also))
            def _():
                action(lax.rem(k + 8 * n, n))

        at(q + SPREAD_AHEAD, self.source, self.send)
        at(q - SPREAD_LAG * (self.hop - 1), jnp.logical_not(self.source), self.follow)

    def reach(self):
        return -SPREAD_AHEAD, self.pieces + 2 * SPREAD_LAG

    def arrived(self):
        @pl.loop(0, self.pieces)
        def _(k):
            for i, slab in enumerate(self.slabs):
                ys, yr = self.sems[5 * i], self.sems[5 * i + 1]
                landed(self.me, slab(k, 1 - self.me.y), (ys, yr), k)

    def close(self):
        @pl.loop(0, self.pieces)
        def _(k):
            found = self.copies(k)
            for copies in found:
                copies[0].wait_send()

            @pl.when(self.go_up)
            def _():
                for copies in found:
                    copies[1].wait_send()

            @pl.when(self.go_dn)
            def _():
                for copies in found:
                    copies[2].wait_send()


SPREAD_AHEAD = 4
SPREAD_LAG = 1


def spread_sems(arrays, pieces):
    return [pltpu.SemaphoreType.DMA((pieces,))] * (5 * arrays)


AHEAD = 3
LAGS = (3, 8, 14)
LATE_LAGS = (2, 7, 9)


class Reduce:
    def __init__(self, me, parts, mine, from_y, from_z, own, pieces, sems, ahead=AHEAD, lags=LAGS):
        self.me, self.parts, self.mine = me, parts, mine
        self.from_y, self.from_z, self.own = from_y, from_z, own
        self.pieces, self.sems, self.ahead, self.lags = pieces, sems, ahead, lags
        self.hop = jnp.where(me.z < me.r, me.z, 3 - me.z)
        self.owner = me.z == me.r
        self.relays = me.z == me.r_x

    def rows(self, i, k):
        size = self.mine[i].shape[0] // self.pieces
        return pl.ds(pl.multiple_of(k * size, 16), size)

    def each(self, k):
        for i in range(len(self.mine)):
            yield i, self.rows(i, k), self.sems[11 * i : 11 * i + 11]

    def y_copies(self, k):
        me = self.me
        return [
            push(self.parts[i].at[1 - me.y, rows], self.from_y[i].at[rows], sems[0:2], k, me.ymate)
            for i, rows, sems in self.each(k)
        ]

    def y_send(self, k):
        for copy in self.y_copies(k):
            copy.start()

    def add(self, i, rows, other):
        total = self.mine[i][rows].astype(F32) + other[i][rows].astype(F32)
        self.mine[i][rows] = total.astype(LOW)

    def join(self, k):
        for i, rows, sems in self.each(k):
            landed(self.me, self.from_y[i].at[rows], sems[0:2], k)
            self.add(i, rows, self.from_y)

    def z_copies(self, k, way):
        found = []
        for i, rows, sems in self.each(k):
            target = self.own if way == 2 else self.from_z
            pair = ((sems[2], sems[4]), (sems[3], sems[4]), (sems[3], sems[5]))[way]
            found.append(
                push(self.mine[i].at[rows], target[i].at[rows], pair, k,
                     self.me.up if way == 0 else self.me.dn)
            )
        return found

    def z_way(self, action):
        me = self.me
        for way, there in enumerate(
            (me.z < me.r, me.z > me.r + 1, me.z == me.r + 1)
        ):

            @pl.when(there)
            def _(way=way):
                action(way)

    def chain(self, k):
        @pl.when(self.hop > 0)
        def _():
            for i, rows, sems in self.each(k):
                landed(self.me, self.from_z[i].at[rows], (sems[2], sems[4]), k)
                self.add(i, rows, self.from_z)

        def start(way):
            for copy in self.z_copies(k, way):
                copy.start()

        self.z_way(start)

    def out_copies(self, k, device, pair):
        return [
            push(self.own[i].at[rows], self.own[i].at[rows], sems[pair : pair + 2], k, device)
            for i, rows, sems in self.each(k)
        ]

    def finish(self, k):
        @pl.when(self.me.z > 0)
        def _():
            for i, rows, sems in self.each(k):
                landed(self.me, self.from_z[i].at[rows], (sems[2], sems[4]), k)
                self.add(i, rows, self.from_z)

        @pl.when(self.me.z < 3)
        def _():
            for i, rows, sems in self.each(k):
                landed(self.me, self.own[i].at[rows], (sems[3], sems[5]), k)
                self.add(i, rows, self.own)

        for i, rows, sems in self.each(k):
            self.own[i][rows] = self.mine[i][rows]
        for copy in self.out_copies(k, self.me.x, 6) + self.out_copies(k, self.me.core, 8):
            copy.start()

    def relay(self, k):
        for copy in self.out_copies(k, self.me.x, 6):
            copy.wait_recv()
        for copy in self.out_copies(k, self.me.core, 8):
            copy.start()

    def step(self, q):
        n = self.pieces

        def at(k, also, action):
            there = jnp.logical_and(k >= 0, k < n)

            @pl.when(there if also is None else jnp.logical_and(there, also))
            def _():
                action(lax.rem(k + 8 * n, n))

        hop_lag, end_lag, relay_lag = self.lags
        if self.ahead:
            at(q + self.ahead, None, self.y_send)
        at(q, None, self.join)
        at(q - hop_lag * self.hop, jnp.logical_not(self.owner), self.chain)
        at(q - end_lag, self.owner, self.finish)
        at(q - relay_lag, self.relays, self.relay)

    def reach(self):
        return -self.ahead, self.pieces + self.lags[2]

    def close(self):
        others = jnp.logical_not(jnp.logical_or(self.owner, self.relays))

        @pl.loop(0, self.pieces)
        def _(k):
            for copy in self.y_copies(k):
                copy.wait_send()

            def sent(way):
                for copy in self.z_copies(k, way):
                    copy.wait_send()

            self.z_way(sent)

            @pl.when(self.owner)
            def _():
                for copy in self.out_copies(k, self.me.x, 6) + self.out_copies(k, self.me.core, 8):
                    copy.wait_send()

            @pl.when(self.relays)
            def _():
                for copy in self.out_copies(k, self.me.core, 8):
                    copy.wait_send()

            @pl.when(others)
            def _():
                for copy in self.out_copies(k, self.me.core, 8):
                    copy.wait_recv()


class Line:
    def __init__(self, reduces, offsets):
        self.reduces, self.offsets = reduces, offsets
        self.done = reduces[0].reach()[0]

    def position(self, p, low, high):
        for one, offset in zip(self.reduces, self.offsets):
            first, last = one.reach()
            if offset + first < high and low < offset + last:
                one.step(p - offset)

    def advance(self, high):
        low, self.done = self.done, max(self.done, high)
        if high > low + 1:

            @pl.loop(low, high)
            def _(p):
                self.position(p, low, high)

        elif high > low:
            self.position(low, low, high)

    def ready(self, i):
        assert self.done <= self.offsets[i] + self.reduces[i].reach()[0]

    def during(self, begin, end, action):
        low, self.done = self.done, self.done + end - begin

        @pl.loop(begin, end)
        def _(s):
            action(s)
            self.position(low - begin + s, low, low + end - begin)

    def last(self):
        return max(offset + one.reach()[1] for offset, one in zip(self.offsets, self.reduces))

    def close(self):
        for one in self.reduces:
            one.close()


def reduce_sems(arrays, pieces):
    return [pltpu.SemaphoreType.DMA((pieces,))] * (11 * arrays)


RS_CHUNKS = 4


class RowsSum:
    def __init__(self, me, part, mate, out_x, in_x, core_sems, x_sems):
        self.me, self.part, self.mate, self.out_x, self.in_x = me, part, mate, out_x, in_x
        self.size = part.shape[1] // RS_CHUNKS
        far = lax.rem(me.r_core + 2, 4)
        self.to_core = [
            [
                push(part.at[owner, self.rows(k)], mate.at[block, self.rows(k)], core_sems,
                     block * RS_CHUNKS + k, me.core)
                for k in range(RS_CHUNKS)
            ]
            for block, owner in enumerate((far, me.r_core))
        ]
        self.to_x = [
            push(out_x.at[self.rows(k)], in_x.at[self.rows(k)], x_sems, k, me.x)
            for k in range(RS_CHUNKS)
        ]

    def rows(self, k):
        return pl.ds(k * self.size, self.size)

    def start(self, block, chunks=range(RS_CHUNKS)):
        for k in chunks:
            self.to_core[block][k].start()

    def cross(self, chunks=range(RS_CHUNKS)):
        for k in chunks:
            rows = self.rows(k)
            self.to_core[0][k].wait_recv()
            total = self.part[self.me.r_x, rows].astype(F32) + self.mate[0, rows].astype(F32)
            self.out_x[rows] = total.astype(LOW)
            self.to_x[k].start()

    def total(self, k):
        rows = self.rows(k)
        self.to_core[1][k].wait_recv()
        self.to_x[k].wait_recv()
        return (
            self.part[self.me.r, rows].astype(F32) + self.mate[1, rows].astype(F32)
            + self.in_x[rows].astype(F32)
        )

    def close(self):
        for copy in self.to_core[0] + self.to_core[1] + self.to_x:
            copy.wait_send()


class Share:
    def __init__(self, me, array, x_sems, core_sems):
        size = array.shape[1] // RS_CHUNKS

        def piece(row, k):
            return array.at[row, pl.ds(k * size, size)]

        self.to_x = [
            push(piece(me.r, k), piece(me.r, k), x_sems, k, me.x) for k in range(RS_CHUNKS)
        ]
        self.to_core = [
            push(piece(me.r, k), piece(me.r, k), core_sems, k, me.core) for k in range(RS_CHUNKS)
        ]
        self.passed = [
            push(piece(me.r_x, k), piece(me.r_x, k), core_sems, RS_CHUNKS + k, me.core)
            for k in range(RS_CHUNKS)
        ]

    def send(self, k):
        self.to_x[k].start()
        self.to_core[k].start()

    def relay(self, k):
        self.to_x[k].wait_recv()
        self.passed[k].start()

    def arrived(self, k):
        self.to_core[k].wait_recv()
        self.passed[k].wait_recv()

    def close(self):
        for copy in self.to_x + self.to_core + self.passed:
            copy.wait_send()


def finish_sends(copies):
    for copy in copies:
        copy.wait_send()


class Bag:
    def __init__(self, names, refs):
        self.__dict__.update(zip(names, refs))


MLP_BLOCKS = 3
VECTORS = ("gate_bias", "lift_bias", "conv_bias", "recur_bias", "input_bias", "decay_param")
LANES = 128


def block_kernel(names, *refs):
    R = Bag(names, refs)
    me = Spot()
    r, c, z, y = me.r, me.c, me.z, me.y
    length, width = R.inputs.shape
    seq_length = length * 8
    wide = 2 * R.gp.shape[0]
    side = wide // 2
    step = length // RS_CHUNKS
    tokens_all = 4 * length
    tiles = (length // TILE, TILE, wide)
    diag = (me.r_x + 1 - 2 * lax.rem(me.r_x, 2), c)
    row_peers = (me.core, me.x, diag)
    chan_peers = peers_of(me)
    x_place, core_place = lax.div(r, 2), lax.rem(r, 2)

    def far_first(i):
        return 2 * lax.rem(x_place + 1 + lax.div(i, 2), 2) + lax.rem(core_place + 1 + lax.rem(i, 2), 2)

    vec, taps = R.vec, R.taps
    keep = dict(gate_pre=R.gate_h, lext=R.lext_h, conv=R.conv_h, rec=R.rec_h, opening=R.open_h,
                state=R.state_h, mixed_t=R.mixed_h)

    def tallies_of(s):
        fill_tallies(R.tallies, R.starts_all[s, 0:1], c * length, length, seq_length)

    def same(shift):
        return same_document(R.tallies, length, shift, wide)


    mixer_pieces = (4, 6, 4)

    def mixer_slab(m):
        size = side // mixer_pieces[m]
        return lambda k, half: R.wq.at[m, half, pl.ds(pl.multiple_of(k * size, 16), size)]

    glo = [
        Spread(me, [mixer_slab(m)], mixer_pieces[m], R.spread[5 * m : 5 * m + 5]) for m in range(3)
    ]

    def mlp_slab(b):
        size = width // 8

        def slab(k, half):
            rows = pl.ds(pl.multiple_of(k * size, 16), size)
            return R.w.at[b, rows, pl.ds(pl.multiple_of(half * 3 * LANES, LANES), 3 * LANES)]

        return slab

    mlp_w = [
        Spread(me, [mlp_slab(b)], 8, R.spread[15 + 5 * b : 20 + 5 * b]) for b in range(MLP_BLOCKS)
    ]
    sline = Line([glo[0], glo[2]] + mlp_w, (0, 4, 8, 16, 24))

    part = R.opart
    sum1 = RowsSum(me, part, R.mate, R.out_x, R.in_x, (R.ms, R.mr), (R.rxs, R.rxr))

    def forward(gate_pre, lext, conv, rec, opening, a, b, mixed_t, rg32, ig32, md_v):
        barrier = pltpu.get_barrier_semaphore()
        always = list(row_peers) + chan_peers
        for device in always:
            pl.semaphore_signal(barrier, inc=1, device_id=device, device_id_type=MESH)
        count = len(always)
        for there, place in ((c < 7, lax.rem(c + 1, 8)), (c > 0, lax.rem(c + 7, 8))):
            for i in (1, 2, 3):

                @pl.when(there)
                def _(i=i, place=place):
                    pl.semaphore_signal(
                        barrier, inc=1, device_id=(lax.rem(r + i, 4), place), device_id_type=MESH
                    )

            count = count + jnp.where(there, 3, 0)
        own = [
            pltpu.make_async_copy(R.gp, R.wq.at[0, y], R.loc.at[12]),
            pltpu.make_async_copy(R.lp, R.wq.at[1, y], R.loc.at[13]),
            pltpu.make_async_copy(R.op, R.wq.at[2, y], R.loc.at[0]),
            pltpu.make_async_copy(R.md, md_v, R.loc.at[14]),
        ]
        for blk in range(MLP_BLOCKS):
            lanes = pl.ds(blk * LANES, LANES)
            for i, (source, at) in enumerate(
                ((R.mg, 4 * y), (R.mu, 4 * y + 1))
            ):
                column = pl.ds(pl.multiple_of(at * LANES, LANES), LANES)
                own.append(
                    pltpu.make_async_copy(
                        source.at[:, lanes], R.w.at[blk, :, column], R.loc.at[1 + 2 * blk + i]
                    )
                )

        @pl.when(z == r)
        def _():
            for copy in own:
                copy.start()

        heads = [
            pltpu.make_async_copy(R.rgate_all.at[pl.ds(2 * r, 2)], rg32, R.loc.at[10]),
            pltpu.make_async_copy(R.igate_all.at[pl.ds(2 * r, 2)], ig32, R.loc.at[11]),
        ]
        for copy in heads:
            copy.start()
        pl.semaphore_wait(barrier, count)

        @pl.when(z == r)
        def _():
            for copy in own[:2]:
                copy.wait()
            for k in range(mixer_pieces[1]):
                glo[1].send(k)

        R.call[r] = R.cot[...]
        vals = R.inputs[...].astype(F32)
        scale = lax.rsqrt(jnp.mean(vals * vals, axis=-1, keepdims=True) + EPSILON)
        R.nall[r] = (vals * scale * R.mix_gain[...]).astype(LOW)
        R.starts_all[r] = jnp.full(R.starts_all.shape[1:], jnp.iinfo(jnp.int32).max, jnp.int32)
        R.starts_all[r, 0:1, 0 : R.starts.shape[1]] = R.starts[...]

        mine_n, mine_c = R.nall.at[r], R.call.at[r]
        theirs_n, theirs_c = R.nall.at[me.r_x], R.call.at[me.r_x]
        x_n = push(mine_n, mine_n, (R.xs, R.xr), 0, me.x)
        c_n = push(mine_n, mine_n, (R.cs, R.cr), 0, me.core)
        c_c = push(mine_c, mine_c, (R.cs, R.cr), 1, me.core)
        x_c = push(mine_c, mine_c, (R.xs, R.xr), 1, me.x)
        fwd_n = push(theirs_n, theirs_n, (R.cs, R.cr), 2, me.core)
        fwd_c = push(theirs_c, theirs_c, (R.cs, R.cr), 3, me.core)
        s_copies = [
            push(R.starts_all.at[r], R.starts_all.at[r], (R.ss, R.sr), i, device)
            for i, device in enumerate(row_peers)
        ]
        tail = R.nall.at[r, pl.ds(length - 16, 16)]
        halo_copies = [
            push(tail, R.halo.at[r], (R.hs, R.hr), i, (lax.rem(r + i, 4), lax.rem(c + 1, 8)))
            for i in range(4)
        ]
        x_n.start()
        for copy in s_copies:
            copy.start()

        @pl.when(c < 7)
        def _():
            for copy in halo_copies:
                copy.start()

        c_n.start()
        c_c.start()

        @pl.when(c == 0)
        def _():
            R.halo[...] = jnp.zeros_like(R.halo)

        mine = pl.ds(pl.multiple_of(r * wide, LANES), wide)
        count_rows = wide // LANES
        for i, name in enumerate(VECTORS):
            for k in range(count_rows):
                place = pl.ds(r * count_rows + k, 1)
                vec[i : i + 1, k * LANES : (k + 1) * LANES] = getattr(R, name)[place]
        decay = vec[5:6]
        vec[5:6] = jnp.log1p(jnp.exp(-decay))
        vec[6:7] = jax.nn.sigmoid(-decay)
        taps[...] = R.conv_taps[:, mine]

        for copy in heads:
            copy.wait()
        pair_diagonal(R.rgate, rg32)
        pair_diagonal(R.igate, ig32)
        for k in range(mixer_pieces[1]):

            @pl.when(z != r)
            def _(k=k):
                glo[1].follow(k)

        x_n.wait_recv()
        fwd_n.start()
        x_c.start()

        @pl.when(z == r)
        def _():
            for copy in own[2:]:
                copy.wait()
            column = pl.ds(pl.multiple_of((2 + y) * LANES, LANES), LANES)
            for blk in range(MLP_BLOCKS):
                R.w[blk, :, column] = md_v[blk * LANES : (blk + 1) * LANES].T

        sline.advance(0)
        glo[1].arrived()
        c_n.wait_recv()
        fwd_n.wait_recv()
        for copy in s_copies:
            copy.wait_recv()

        @pl.when(c > 0)
        def _():
            for i in range(4):
                landed(me, R.halo.at[i], (R.hs, R.hr), i)

        def mixer_one(s):
            tallies_of(s)
            tokens = R.nall[s]
            wlift = R.wq[1].reshape(wide, width)
            lifted = nt(tokens, wlift) + vec[1:2]
            lext[s, 0:8] = (nt(R.halo[s], wlift) + vec[1:2])[8:16]
            lext[s, pl.ds(8, length)] = lifted
            out = vec[2:3] + taps[0:1] * lifted
            for k in range(1, 4):
                out = out + taps[k : k + 1] * lext[s, pl.ds(8 - k, length)] * same(-k)
            conv[s] = out
            low = out.astype(LOW)
            recur = jax.nn.sigmoid(nn(low, R.rgate[...]) + vec[3:4])
            opened = jax.nn.sigmoid(nn(low, R.igate[...]) + vec[4:5])
            rec[s] = recur
            opening[s] = opened
            reset = same(-1) < 0.5
            decay, scaling = decay_terms(recur, vec[5:6], reset)
            decay = jnp.where(reset, 0.0, decay)
            a_scan, b_scan = tile_scan(
                decay.reshape(tiles), (scaling * opened * out).reshape(tiles), False
            )
            a[s] = a_scan.reshape(length, wide)
            b[s] = b_scan.reshape(length, wide)
            product = jnp.ones((1, wide), F32)
            state = jnp.zeros((1, wide), F32)
            for t in range(length // TILE):
                last = t * TILE + TILE - 1
                a_last = a[s, last : last + 1]
                state = b[s, last : last + 1] + a_last * state
                product = product * a_last
            R.tot[s, 0:1] = product
            R.tot[s, 1:2] = state

        sline.during(0, 4, mixer_one)
        carry_copies = carry_start(me, False, R.tot, R.slots, (R.ps, R.pr))
        local = dict(gate_pre=gate_pre, lext=lext, conv=conv, rec=rec, opening=opening, state=b,
                     mixed_t=mixed_t)
        saved = {
            name: pltpu.make_async_copy(local[name], keep[name], R.outs.at[i])
            for i, name in enumerate(keep)
        }
        for name in ("lext", "conv", "rec", "opening"):
            saved[name].start()
        sline.advance(4 + 2 * SPREAD_LAG)
        glo[0].arrived()

        def gate_part(s):
            gate_pre[s] = nt(R.nall[s], R.wq[0].reshape(wide, width)) + vec[0:1]

        sline.during(0, 4, gate_part)
        saved["gate_pre"].start()
        carry_join(me, False, R.slots, R.start, (R.ps, R.pr))
        sline.advance(8 + 2 * SPREAD_LAG)
        glo[2].arrived()

        def mixer_two(i):
            s = far_first(i)
            state = R.start[pl.ds(s, 1)]
            for t in range(length // TILE):
                tile = pl.ds(t * TILE, TILE)
                now = b[s, tile] + a[s, tile] * state
                b[s, tile] = now
                state = now[TILE - 1 : TILE]
            gate_val, _ = gelu_pair(gate_pre[s])
            mix = (b[s] * gate_val).astype(LOW)
            mixed_t[:, pl.ds(pl.multiple_of(s * length, LANES), length)] = mix.T
            part[s] = nn(mix, R.wq[2].reshape(wide, width)).astype(LOW)

        sline.during(0, 2, mixer_two)
        sum1.start(0)
        sline.during(2, 3, mixer_two)
        sum1.start(1)
        sum1.cross((0, 1, 2))
        sline.during(3, 4, mixer_two)
        x_c.wait_recv()
        fwd_c.start()
        for name in ("state", "mixed_t"):
            saved[name].start()
        for m in range(3):
            glo[m].close()
        for copy in (x_n, x_c, c_n, fwd_n):
            copy.wait_send()
        c_c.wait()
        fwd_c.wait()
        finish_sends(s_copies)

        @pl.when(c < 7)
        def _():
            finish_sends(halo_copies)

        carry_sent(me, False, carry_copies)
        for copy in saved.values():
            copy.wait()

    tall = pltpu.VMEM((4, length, wide), F32)
    ext = pltpu.VMEM((4, length + TILE, wide), F32)
    low_t = pltpu.VMEM((wide, tokens_all), LOW)
    pl.run_scoped(
        forward, gate_pre=tall, lext=ext, conv=tall, rec=tall, opening=tall, a=tall, b=tall,
        mixed_t=low_t, rg32=pltpu.VMEM((2, GB, GB), F32),
        ig32=pltpu.VMEM((2, GB, GB), F32), md_v=pltpu.VMEM(R.md.shape, LOW),
    )


    groups = [R.reduce[11 * i : 11 * i + 11] for i in range(MLP_BLOCKS)]
    rest = R.reduce[11 * MLP_BLOCKS :]
    line = Line(
        [
            Reduce(
                me, [R.grad.at[blk]], [R.grad.at[blk, y]], [R.y_w.at[blk]], [R.z_w.at[blk]],
                [R.own_w.at[:, pl.ds(blk * 3 * LANES, 3 * LANES)]], 8, groups[blk],
            )
            for blk in range(MLP_BLOCKS)
        ]
        + [
            Reduce(me, [R.early], [R.early.at[y]], [R.y_e], [R.z_e], [R.own_e], 8, rest[:11]),
            Reduce(me, [R.late], [R.late.at[y]], [R.y_l], [R.z_l], [R.own_l], 7, rest[11:], 0,
                   LATE_LAGS),
        ],
        (0, 8, 16, 24, 33),
    )
    half = length // 2

    def mlp(acc_out, acc_in, n2_t, hid, low_a, low_b, gpart):
        share1 = Share(me, R.n2all, (R.ax, R.bx), (R.ac, R.bc))

        def norm_chunk(k):
            rows = pl.ds(k * step, step)
            res = R.inputs[rows].astype(F32) + sum1.total(k) + R.out_bias[...]
            R.resid[rows] = res
            scale = lax.rsqrt(jnp.mean(res * res, axis=-1, keepdims=True) + EPSILON)
            R.n2all[r, rows] = (res * scale * R.mlp_gain[...]).astype(LOW)
            share1.send(k)

        def turn(h):
            @pl.loop(0, 4)
            def _(s):
                at = pl.ds(pl.multiple_of(s * length + h * half, LANES), half)
                n2_t[:, at] = R.n2all[s, pl.ds(h * half, half)].T

        def mlp_tokens(blk, h, i):
            pair = pl.ds(2 * lax.rem(x_place + 1 + i, 2), 2)
            rows = pl.ds(h * half, half)
            fold = lambda v: v.reshape(2, half, v.shape[1])
            flat = lambda v: v.reshape(2 * half, v.shape[2])
            tokens, cot = flat(R.n2all[pair, rows]), flat(R.call[pair, rows])
            sides = (slice(0, 2 * LANES), slice(4 * LANES, 6 * LANES))
            across = slice(2 * LANES, 4 * LANES)
            first, second = [nn(tokens, R.w[blk, :, side_of]) for side_of in sides]
            gate = jnp.concatenate([first[:, :LANES], second[:, :LANES]], axis=1)
            up = jnp.concatenate([first[:, LANES:], second[:, LANES:]], axis=1)
            grad_hidden = nn(cot, R.w[blk, :, across])
            gate_val, slope = gelu_pair(gate)
            hidden = (gate_val * up).astype(LOW)
            grad_gate = (grad_hidden * up * slope).astype(LOW)
            grad_up = (grad_hidden * gate_val).astype(LOW)
            kept = blk % 2
            hid[kept, pair, rows] = fold(hidden)
            lows = [
                jnp.concatenate([grad_gate[:, at], grad_up[:, at]], axis=1)
                for at in (slice(0, LANES), slice(LANES, 2 * LANES))
            ]
            low_a[kept, pair, rows] = fold(lows[0])
            low_b[kept, pair, rows] = fold(lows[1])
            out = fold(nt(hidden, R.w[blk, :, across]))
            back = fold(nt(lows[0], R.w[blk, :, sides[0]]) + nt(lows[1], R.w[blk, :, sides[1]]))
            if blk == 0:
                acc_out[pair, rows] = out
                acc_in[pair, rows] = back
            elif blk < MLP_BLOCKS - 1:
                acc_out[pair, rows] += out
                acc_in[pair, rows] += back
            else:
                R.opart[pair, rows] = (acc_out[pair, rows] + out).astype(LOW)
                gpart[pair, rows] = (acc_in[pair, rows] + back).astype(LOW)

        def mlp_weights(blk):
            kept = blk % 2
            columns = lambda i: pl.ds(pl.multiple_of(i * 256, 256), 256)
            flat = lambda v: v.reshape(tokens_all, v.shape[2])
            hid_t = flat(hid[kept]).T

            @pl.loop(0, width // 256)
            def _(i):
                at = columns(i)
                down = nn(hid_t, flat(R.call[:, :, at])).astype(LOW).T
                for j, low in enumerate((low_a, low_b)):
                    R.grad[blk, j, at, 0 : 2 * LANES] = nn(n2_t[at], flat(low[kept])).astype(LOW)
                    R.grad[blk, j, at, 2 * LANES :] = down[:, j * LANES : (j + 1) * LANES]

        def weights_here(blk):
            sline.advance(max(sline.done, sline.offsets[2 + blk] + 8 + 2 * SPREAD_LAG))
            mlp_w[blk].arrived()

        norm_chunk(0)
        sline.advance(17)
        norm_chunk(1)
        sum1.cross((3,))
        sline.advance(19)
        norm_chunk(2)
        for k in range(2):
            share1.relay(k)
            sline.advance(20 + k)
        for k in range(2):
            share1.arrived(k)
        weights_here(0)
        turn(0)
        sline.during(0, 2, lambda i: mlp_tokens(0, 0, i))
        norm_chunk(3)
        share1.relay(2)
        weights_here(1)
        sline.during(0, 2, lambda i: mlp_tokens(1, 0, i))
        share1.relay(3)
        for k in range(2, RS_CHUNKS):
            share1.arrived(k)
        turn(1)
        sline.during(0, 2, lambda i: mlp_tokens(0, 1, i))
        sline.during(0, 2, lambda i: mlp_tokens(1, 1, i))
        mlp_weights(0)
        sline.advance(max(sline.done, sline.offsets[4] + 8 + 2 * SPREAD_LAG))
        mlp_weights(1)
        weights_here(2)
        line.ready(1)
        line.advance(0)
        sum1.close()
        share1.close()
        sum2 = RowsSum(me, gpart, R.mate, R.out_x, R.in_x, (R.m2s, R.m2r), (R.rx2s, R.rx2r))
        line.during(0, 2, lambda i: mlp_tokens(2, 0, i))
        for block in range(2):
            sum2.start(block, (0, 1))
        line.during(0, 1, lambda i: mlp_tokens(2, 1, i))
        sum2.cross((0, 1))
        line.during(1, 2, lambda i: mlp_tokens(2, 1, i))
        for block in range(2):
            sum2.start(block, (2, 3))
        mlp_weights(2)
        line.ready(2)
        line.advance(5)
        sum2.cross((2, 3))
        ball = R.n2all
        share2 = Share(me, ball, (R.a2x, R.b2x), (R.a2c, R.b2c))
        gain_sum = 0.0
        bias_sum = 0.0
        for k in range(RS_CHUNKS):
            rows = pl.ds(k * step, step)
            grad = sum2.total(k)
            res = R.resid[rows]
            scale = lax.rsqrt(jnp.mean(res * res, axis=-1, keepdims=True) + EPSILON)
            gain_sum = gain_sum + jnp.sum(grad * res * scale, axis=0, keepdims=True)
            pulled = grad * R.mlp_gain[...]
            inner = jnp.mean(pulled * res, axis=-1, keepdims=True)
            total = R.cot[rows].astype(F32) + scale * pulled - res * (scale * scale * scale * inner)
            bias_sum = bias_sum + jnp.sum(total, axis=0, keepdims=True)
            R.gresid[rows] = total
            ball[r, rows] = total.astype(LOW)
            share2.send(k)
            line.advance(6 + k)
        R.gain_keep[0:1] = gain_sum
        R.gain_keep[1:2] = bias_sum
        for k in range(RS_CHUNKS):
            share2.relay(k)
            line.advance(10 + k)
        for k in range(RS_CHUNKS):
            share2.arrived(k)
        share2.close()
        sum2.close()

    kept = pltpu.VMEM((2, 4, length, 2 * LANES), LOW)
    pl.run_scoped(
        mlp, acc_out=pltpu.VMEM((4, length, width), F32), acc_in=pltpu.VMEM((4, length, width), F32),
        n2_t=pltpu.VMEM((width, tokens_all), LOW), hid=kept, low_a=kept, low_b=kept,
        gpart=pltpu.VMEM((4, length, width), LOW),
    )
    for one in mlp_w:
        one.close()


    def backward(gate_pre, conv, rec, opening, state, a, b, gconv, gate_low, gate_t, mixed_t, acc_r,
                 acc_i, prev_ext):
        local = dict(gate_pre=gate_pre, conv=conv, rec=rec, opening=opening, state=state,
                     mixed_t=mixed_t)
        loads = {
            name: pltpu.make_async_copy(keep[name], ref, R.outs.at[i])
            for i, (name, ref) in enumerate(local.items())
        }
        soon = ("gate_pre", "state", "rec")
        later = ("mixed_t", "conv", "opening")
        for name in soon + later:
            loads[name].start()
        ball = R.n2all
        sum3 = RowsSum(me, R.opart, R.o_mate, R.o_out, R.o_in, (R.oms, R.omr), (R.oxs, R.oxr))
        for block in range(2):
            sum3.start(block)
        for name in soon:
            loads[name].wait()
        acc_r[...] = jnp.zeros_like(acc_r)
        acc_i[...] = jnp.zeros_like(acc_i)
        R.sums[...] = jnp.zeros_like(R.sums)

        def reset_of(s):
            tallies_of(s)
            return same(-1) < 0.5

        def mixer_three(s):
            grad_mixed = nt(ball[s], R.wq[2].reshape(wide, width))
            gate_val, slope = gelu_pair(gate_pre[s])
            grad_gate = grad_mixed * state[s] * slope
            low = grad_gate.astype(LOW)
            gate_low[s] = low
            gate_t[:, pl.ds(pl.multiple_of(s * length, LANES), length)] = low.T
            R.sums[0:1] += jnp.sum(grad_gate, axis=0, keepdims=True)
            grad_state = grad_mixed * gate_val
            gate_pre[s] = grad_state
            decay = jnp.where(reset_of(s), 0.0, jnp.exp(-8.0 * rec[s] * vec[5:6]))
            a_scan, b_scan = tile_scan(
                decay.reshape(tiles), (decay * grad_state).reshape(tiles), True
            )
            a[s, 0:length] = a_scan.reshape(length, wide)
            b[s] = b_scan.reshape(length, wide)
            product = jnp.ones((1, wide), F32)
            carried = jnp.zeros((1, wide), F32)
            for t in range(length // TILE - 1, -1, -1):
                head = t * TILE
                a_head = a[s, head : head + 1]
                carried = b[s, head : head + 1] + a_head * carried
                product = product * a_head
            R.tot[s, 0:1] = product
            R.tot[s, 1:2] = carried

        line.during(0, 4, mixer_three)
        carry_copies = carry_start(me, True, R.tot, R.slots2, (R.p2s, R.p2r))
        for name in later:
            loads[name].wait()
        columns = lambda i: pl.ds(pl.multiple_of(i * 256, 256), 256)

        def weight_grad(target, at, left_t, right):
            @pl.loop(0, width // 256)
            def _(i):
                product = nn(left_t[...], right[:, :, columns(i)].reshape(tokens_all, 256)).astype(LOW)
                for j in range(2):
                    target[j, at : at + side, columns(i)] = product[j * side : (j + 1) * side]

        weight_grad(R.early, 0, mixed_t, ball)
        weight_grad(R.early, side, gate_t, R.nall)
        line.ready(3)
        sum3.cross()
        line.advance(20)
        carry_join(me, True, R.slots2, R.carry, (R.p2s, R.p2r))

        def mixer_four(s):
            now = R.carry[pl.ds(s, 1)]
            gconv[s, pl.ds(length, TILE)] = jnp.broadcast_to(now, (TILE, wide))
            for t in range(length // TILE - 1, -1, -1):
                rows = pl.ds(t * TILE, TILE)
                moved = b[s, rows] + a[s, rows] * now
                gconv[s, rows] = moved
                now = moved[0:1]
            carried = gate_pre[s] + gconv[s, pl.ds(1, length)]
            prev_ext[0:TILE] = jnp.broadcast_to(R.start[pl.ds(s, 1)], (TILE, wide))
            prev_ext[pl.ds(TILE, length)] = state[s]
            previous = prev_ext[pl.ds(TILE - 1, length)]
            recur, opened, conv_s = rec[s], opening[s], conv[s]
            reset = reset_of(s)
            decay, scaling = decay_terms(recur, vec[5:6], reset)
            pulled = carried * scaling
            grad_opening = pulled * conv_s
            grad_log = carried * (previous * decay - opened * conv_s * (decay * decay / scaling))
            grad_log = jnp.where(reset, 0.0, grad_log)
            grad_rec = grad_log * (-8.0 * vec[5:6])
            grad_rpre = grad_rec * recur * (1.0 - recur)
            grad_opre = grad_opening * opened * (1.0 - opened)
            r_low, o_low, conv_low = grad_rpre.astype(LOW), grad_opre.astype(LOW), conv_s.astype(LOW)
            total = pulled * opened + nt(r_low, R.rgate[...]) + nt(o_low, R.igate[...])
            gconv[s, 0:length] = total
            acc_r[...] += tn(conv_low, r_low)
            acc_i[...] += tn(conv_low, o_low)
            R.sums[7:8] += jnp.sum(grad_rpre, axis=0, keepdims=True)
            R.sums[8:9] += jnp.sum(grad_opre, axis=0, keepdims=True)
            R.sums[9:10] += jnp.sum(grad_log * recur, axis=0, keepdims=True) * (8.0 * vec[6:7])
            R.sums[6:7] += jnp.sum(total, axis=0, keepdims=True)

        line.during(0, 4, mixer_four)
        lext = a
        load_lext = pltpu.make_async_copy(keep["lext"], lext, R.outs.at[6])
        load_lext.start()
        heads = [
            push(gconv.at[s, pl.ds(0, TILE)], R.heads_in.at[s], (R.h2s, R.h2r), s,
                 (r, lax.rem(c + 7, 8)))
            for s in range(4)
        ]

        @pl.when(c > 0)
        def _():
            for copy in heads:
                copy.start()

        @pl.when(c == 7)
        def _():
            R.heads_in[...] = jnp.zeros_like(R.heads_in)

        cut = side // 8
        for k in range(8):
            at = k * cut
            R.gate_send[k] = jnp.concatenate(
                [m[j * side + at : j * side + at + cut, j * side : (j + 1) * side]
                 for m in (acc_r, acc_i) for j in range(2)], axis=0
            ).astype(LOW)
        gate_copies = [
            push(R.gate_send.at[lax.rem(c + d, 8)], R.gate_slots.at[d], (R.qs, R.qr), d,
                 chan_peers[d - 1])
            for d in range(1, 8)
        ]
        for copy in gate_copies:
            copy.start()
        for k in range(RS_CHUNKS):
            rows = pl.ds(k * step, step)
            R.output[rows] = (R.resid[rows] + sum3.total(k)).astype(LOW)
        line.advance(26)
        load_lext.wait()

        @pl.when(c < 7)
        def _():
            for s in range(4):
                landed(me, R.heads_in.at[s], (R.h2s, R.h2r), s)

        lift_t = mixed_t
        gpart1 = R.call

        def mixer_five(i):
            s = far_first(i)
            tallies_of(s)
            grad = gconv[s, 0:length]
            prev_ext[0:length] = grad
            prev_ext[pl.ds(length, TILE)] = R.heads_in[s]
            grad_lifted = taps[0:1] * grad
            R.sums[2:3] += jnp.sum(grad * lext[s, pl.ds(TILE, length)], axis=0, keepdims=True)
            for k in range(1, 4):
                ahead = prev_ext[pl.ds(k, length)] * same(k)
                grad_lifted = grad_lifted + taps[k : k + 1] * ahead
                behind = lext[s, pl.ds(TILE - k, length)] * same(-k)
                R.sums[2 + k : 3 + k] += jnp.sum(grad * behind, axis=0, keepdims=True)
            R.sums[1:2] += jnp.sum(grad_lifted, axis=0, keepdims=True)
            lift_low = grad_lifted.astype(LOW)
            lift_t[:, pl.ds(pl.multiple_of(s * length, LANES), length)] = lift_low.T
            gpart1[s] = (
                nn(gate_low[s], R.wq[0].reshape(wide, width))
                + nn(lift_low, R.wq[1].reshape(wide, width))
            ).astype(LOW)

        sum4 = RowsSum(me, gpart1, R.mate, R.out_x, R.in_x, (R.m3s, R.m3r), (R.rx3s, R.rx3r))
        line.during(0, 2, mixer_five)
        sum4.start(0)
        line.during(2, 3, mixer_five)
        sum4.start(1)
        sum4.cross()
        line.during(3, 4, mixer_five)
        R.late[...] = jnp.zeros_like(R.late)
        weight_grad(R.late, 0, lift_t, R.nall)
        for j in range(2):
            R.late[j, side : side + 16, 0:side] = R.sums[:, j * side : (j + 1) * side].astype(LOW)
        line.ready(4)
        for k in range(7):
            line.reduces[4].y_send(k)
        line.advance(32)
        gain_sum = 0.0
        for k in range(RS_CHUNKS):
            rows = pl.ds(k * step, step)
            grad = sum4.total(k)
            vals = R.inputs[rows].astype(F32)
            scale = lax.rsqrt(jnp.mean(vals * vals, axis=-1, keepdims=True) + EPSILON)
            gain_sum = gain_sum + jnp.sum(grad * vals * scale, axis=0, keepdims=True)
            pulled = grad * R.mix_gain[...]
            inner = jnp.mean(pulled * vals, axis=-1, keepdims=True)
            R.ginputs[rows] = (
                R.gresid[rows] + scale * pulled - vals * (scale * scale * scale * inner)
            ).astype(LOW)
            line.advance(34 + 2 * k)
        for k in range(8):
            lanes = slice(k * LANES, (k + 1) * LANES)
            R.gain_slots[0, k] = jnp.concatenate(
                [gain_sum[:, lanes], R.gain_keep[0:1, lanes], R.gain_keep[1:2, lanes],
                 jnp.zeros((5, LANES), F32)], 0
            )
        gain_copies = [
            push(R.gain_slots.at[0, lax.rem(c + d, 8)], R.gain_slots.at[1, d], (R.ggs, R.ggr), d,
                 chan_peers[d - 1])
            for d in range(1, 8)
        ]
        for copy in gain_copies:
            copy.start()
        line.advance(42)
        gate_total = R.gate_send[c].astype(F32)
        for d in range(1, 8):
            gate_copies[d - 1].wait_recv()
            gate_total = gate_total + R.gate_slots[d].astype(F32)
        R.gates_all[r] = gate_total.astype(LOW)
        gate_rows = [
            push(R.gates_all.at[r], R.gates_all.at[r], (R.ts, R.tr), i, device)
            for i, device in enumerate(row_peers)
        ]
        for copy in gate_rows:
            copy.start()
        shared = R.gain_slots[0, c]
        for d in range(1, 8):
            gain_copies[d - 1].wait_recv()
            shared = shared + R.gain_slots[1, d]
        R.gain_sums[0] = shared
        row_copies = [
            push(R.gain_sums.at[0], R.gain_sums.at[1 + i], (R.ghs, R.ghr), i, device)
            for i, device in enumerate(row_peers)
        ]
        for copy in row_copies:
            copy.start()
        line.advance(line.last())
        for copy in row_copies + gate_rows:
            copy.wait()
        for row in range(4):
            found = R.gates_all[row].astype(F32)
            for head in range(2):
                R.rgate_o[2 * row + head] = found[head * cut : (head + 1) * cut]
                R.igate_o[2 * row + head] = found[(2 + head) * cut : (3 + head) * cut]
        R.gains_all[...] = R.gain_sums[0] + R.gain_sums[1] + R.gain_sums[2] + R.gain_sums[3]

        @pl.when(c > 0)
        def _():
            finish_sends(heads)

        finish_sends(gain_copies + gate_copies)
        sum3.close()
        sum4.close()
        carry_sent(me, True, carry_copies)
        line.close()

    square = pltpu.VMEM((wide, wide), F32)
    pl.run_scoped(
        backward, gate_pre=tall, conv=tall, rec=tall, opening=tall, state=tall, a=ext, b=tall,
        gconv=ext, gate_low=pltpu.VMEM((4, length, wide), LOW), gate_t=low_t, mixed_t=low_t,
        acc_r=square, acc_i=square, prev_ext=pltpu.VMEM((length + TILE, wide), F32),
    )


def block(ins):
    far = ("rgate_all", "igate_all", "gp", "lp", "op", "mg", "mu", "md")
    inputs, starts, mg = ins["inputs"], ins["starts"], ins["mg"]
    length, width = inputs.shape
    side = ins["gp"].shape[0]
    wide = 2 * side
    hidden = mg.shape[1]
    sd, vmem = jax.ShapeDtypeStruct, pltpu.VMEM
    blocks = hidden // LANES
    tall = sd((4, length, wide), F32)
    tokens = (4, length, width)
    outs = dict(
        output=sd(inputs.shape, LOW), ginputs=sd(inputs.shape, LOW),
        own_w=sd((width, 3 * hidden), LOW),
        own_e=sd((2 * side, width), LOW), own_l=sd((side + 32, width), LOW),
        rgate_o=sd((8, side // 8, side), F32), igate_o=sd((8, side // 8, side), F32),
        gains_all=sd((8, LANES), F32),
    )
    saved = dict(
        gate_h=tall, lext_h=sd((4, length + TILE, wide), F32), conv_h=tall, rec_h=tall, open_h=tall,
        state_h=tall, mixed_h=sd((wide, 4 * length), LOW),
    )
    scratch = dict(
        wq=vmem((3, 2, side, width), LOW), nall=vmem(tokens, LOW), halo=vmem((4, 16, width), LOW),
        starts_all=vmem((4, 8, LANES), starts.dtype), vec=vmem((8, wide), F32), taps=vmem((4, wide), F32),
        gates_all=vmem((4, side // 2, side), LOW),
        w=vmem((blocks, width, 6 * LANES), LOW),
        call=vmem(tokens, LOW), n2all=vmem(tokens, LOW), opart=vmem(tokens, LOW),
        rgate=vmem((wide, wide), LOW), igate=vmem((wide, wide), LOW),
        tallies=vmem((length + 16, LANES), F32), start=vmem((4, wide), F32), carry=vmem((4, wide), F32),
        tot=vmem((4, 2, wide), F32), slots=vmem((8, 4, 2, wide), F32), slots2=vmem((8, 4, 2, wide), F32),
        resid=vmem((length, width), F32), gresid=vmem((length, width), F32),
        mate=vmem((2, length, width), LOW), out_x=vmem((length, width), LOW),
        in_x=vmem((length, width), LOW),
        o_mate=vmem((2, length, width), LOW), o_out=vmem((length, width), LOW),
        o_in=vmem((length, width), LOW),
        grad=vmem((blocks, 2, width, 3 * LANES), LOW),
        early=vmem((2, 2 * side, width), LOW), late=vmem((2, side + 32, width), LOW),
        heads_in=vmem((4, TILE, wide), F32), sums=vmem((16, wide), F32),
        gate_send=vmem((8, side // 2, side), LOW), gate_slots=vmem((8, side // 2, side), LOW),
        gain_keep=vmem((8, width), F32), gain_slots=vmem((2, 8, 8, LANES), F32), gain_sums=vmem((4, 8, LANES), F32),
    )
    for way in "yz":
        scratch.update(
            {
                way + "_w": vmem((blocks, width, 3 * LANES), LOW),
                way + "_e": vmem((2 * side, width), LOW),
                way + "_l": vmem((side + 32, width), LOW),
            }
        )
    dma = pltpu.SemaphoreType.DMA
    counts = dict(
        loc=15, outs=7, xs=2, xr=2, cs=4, cr=4, hs=4, hr=4, ss=3, sr=3, ps=8, pr=8, p2s=8, p2r=8,
        h2s=4, h2r=4, qs=8, qr=8, ts=3, tr=3, ggs=8, ggr=8, ghs=3, ghr=3,
    )
    for name in ("m", "m2", "m3", "om"):
        counts.update({name + "s": 2 * RS_CHUNKS, name + "r": 2 * RS_CHUNKS})
    for name in ("rx", "rx2", "rx3", "ox"):
        counts.update({name + "s": RS_CHUNKS, name + "r": RS_CHUNKS})
    for name in ("", "2"):
        counts.update({f"a{name}x": RS_CHUNKS, f"b{name}x": RS_CHUNKS})
        counts.update({f"a{name}c": 2 * RS_CHUNKS, f"b{name}c": 2 * RS_CHUNKS})
    scratch.update({name: dma((count,)) for name, count in counts.items()})
    names = list(ins) + list(outs) + list(saved) + list(scratch)
    spread = spread_sems(1, 4) + spread_sems(1, 6) + spread_sems(1, 4) + spread_sems(1, 8) * blocks
    reduce = reduce_sems(1, 8) * blocks + reduce_sems(1, 8) + reduce_sems(1, 7)

    def kernel(*refs):
        n, m = len(names), len(spread)
        block_kernel(names + ["spread", "reduce"], *refs[:n], refs[n : n + m], refs[n + m :])

    results = pl.pallas_call(
        kernel,
        name="block",
        out_shape=list(outs.values()) + list(saved.values()),
        in_specs=[ANYWHERE if name in far else IN_VMEM for name in ins],
        out_specs=[IN_VMEM] * len(outs) + [ANYWHERE] * len(saved),
        scratch_shapes=list(scratch.values()) + spread + reduce,
        compiler_params=comm_params(1),
    )(*ins.values())
    return results[: len(outs)]


def finish_kernel(
    output, ginputs, own_w, own_e, own_l, rgate, igate, gains, tail,
    output_o, ginputs_o, gate, up, down, out, gate_proj, lift_proj, rgate_o, igate_o, taps, *flat
):
    output_o[...] = output[...]
    ginputs_o[...] = ginputs[...]
    side = out.shape[0]
    for blk in range(MLP_BLOCKS):
        lanes = slice(blk * LANES, (blk + 1) * LANES)
        for i, target in enumerate((gate, up)):
            at = (3 * blk + i) * LANES
            target[:, lanes] = own_w[:, at : at + LANES].astype(F32)
        at = (3 * blk + 2) * LANES
        down[lanes] = own_w[:, at : at + LANES].T.astype(F32)
    out[...] = own_e[0:side].astype(F32)
    gate_proj[...] = own_e[side:].astype(F32)
    lift_proj[...] = own_l[0:side].astype(F32)
    rgate_o[...] = rgate[...]
    igate_o[...] = igate[...]
    vectors = tail[:, 0:side].astype(F32)
    taps[...] = vectors[2:6]
    for i in range(3):
        flat[i][...] = gains[i : i + 1]
    for i, row in enumerate((0, 1, 6, 7, 8, 9)):
        flat[3 + i][...] = vectors[row : row + 1]


def finish(output, ginputs, own_w, own_e, own_l, rgate, igate, gains):
    steps = 2
    width = own_w.shape[0]
    hidden = own_w.shape[1] // 3
    side = own_e.shape[0] // 2
    sd = jax.ShapeDtypeStruct

    def by_rows(shape):
        return pl.BlockSpec((shape[0] // steps,) + shape[1:], lambda i: (i,) + (0,) * (len(shape) - 1))

    def by_columns(shape):
        return pl.BlockSpec((shape[0], shape[1] // steps), lambda i: (0, i))

    def once(shape):
        return pl.BlockSpec(shape, lambda i: (0,) * len(shape))

    inward, outward, square = (width, hidden), (hidden, width), (side, width)
    tail = pl.BlockSpec((16, own_l.shape[1]), lambda i: (side // 16, 0))
    flat = [(1, gains.shape[1])] * 3 + [(1, side)] * 6
    outs = (
        [(sd(v.shape, v.dtype), by_rows(v.shape)) for v in (output, ginputs)]
        + [(sd(inward, F32), by_rows(inward))] * 2
        + [(sd(outward, F32), by_columns(outward))]
        + [(sd(square, F32), by_columns(square))] * 3
        + [(sd(v.shape, v.dtype), by_rows(v.shape)) for v in (rgate, igate)]
        + [(sd((4, side), F32), once((4, side)))]
        + [(sd(shape, F32), once(shape)) for shape in flat]
    )
    return pl.pallas_call(
        finish_kernel,
        name="finish",
        grid=(steps,),
        in_specs=[by_rows(output.shape), by_rows(ginputs.shape), by_rows(own_w.shape),
                  by_columns(own_e.shape), by_columns(own_l.shape), by_rows(rgate.shape),
                  by_rows(igate.shape), once(gains.shape), tail],
        out_specs=[o[1] for o in outs],
        out_shape=[o[0] for o in outs],
        compiler_params=pltpu.CompilerParams(vmem_limit_bytes=VMEM_BYTES),
    )(output, ginputs, own_w, own_e, own_l, rgate, igate, gains, own_l)


def split_body(
    inputs, mix_gain, gate_proj, gate_bias, lift_proj, lift_bias, conv_taps, conv_bias,
    recur_gate, recur_bias, input_gate, input_bias, decay_param, out_proj, out_bias, mlp_gain,
    mlp_gate, mlp_up, mlp_down, doc_starts, cotangent,
):
    row = lambda v: v[None]
    vectors = (gate_bias, lift_bias, conv_bias, recur_bias, input_bias, decay_param)
    output, grad_inputs, own_w, own_e, own_l, rgate_o, igate_o, gains = block(
        dict(
            inputs=inputs, cot=cotangent, mix_gain=row(mix_gain), out_bias=row(out_bias),
            mlp_gain=row(mlp_gain), **{name: v.reshape(-1, LANES) for name, v in zip(VECTORS, vectors)}, conv_taps=conv_taps, starts=doc_starts,
            rgate_all=recur_gate, igate_all=input_gate, gp=gate_proj.T, lp=lift_proj.T, op=out_proj,
            mg=mlp_gate, mu=mlp_up, md=mlp_down,
        )
    )
    (output, grad_inputs, grad_gate, grad_up, grad_down, grad_out, grad_gate_proj, grad_lift_proj,
     rgate_o, igate_o, taps, *flat) = finish(
        output, grad_inputs, own_w, own_e, own_l, rgate_o, igate_o, gains
    )
    flat = [v.reshape(v.shape[1]) for v in flat]
    return (
        output, grad_inputs, flat[0],
        grad_gate_proj.T, flat[3], grad_lift_proj.T, flat[4], taps, flat[5],
        rgate_o, flat[6], igate_o, flat[7], flat[8],
        grad_out, flat[2], flat[1],
        grad_gate, grad_up, grad_down,
    )


def solution(mesh):
    in_specs = (
        P(("rows", "chan"), None),
        P(),
        P(None, "chan"),
        P(),
        P(None, "chan"),
        P(),
        P(),
        P(),
        P(),
        P(),
        P(),
        P(),
        P(),
        P("chan", None),
        P(),
        P(),
        P(None, "chan"),
        P(None, "chan"),
        P("chan", None),
        P("rows", None),
        P(("rows", "chan"), None),
    )
    out_specs = (
        P(("rows", "chan"), None),
        P(("rows", "chan"), None),
        P("chan"),
        P(None, "chan"),
        P("chan"),
        P(None, "chan"),
        P("chan"),
        P(None, "chan"),
        P("chan"),
        P(None, "chan", None),
        P("chan"),
        P(None, "chan", None),
        P("chan"),
        P("chan"),
        P("chan", None),
        P("chan"),
        P("chan"),
        P(None, "chan"),
        P(None, "chan"),
        P("chan", None),
    )
    split = mesh.shape["rows"] == 4 and mesh.shape["chan"] == HEADS
    return jax.shard_map(split_body if split else body, mesh=mesh, in_specs=in_specs, out_specs=out_specs, check_vma=False)
```

```python
from functools import partial
import math

import jax
import jax.numpy as jnp
from jax import lax
from jax.experimental import pallas as pl
from jax.experimental.pallas import tpu as pltpu
from jax.sharding import PartitionSpec as P

D = 1024
LRU = 1536
FF = 3072
HEADS = 8
GB = 192


EPSILON = 1e-06
precise = lax.Precision.HIGHEST


def from_behind(block, axis, distance):
    devices = range(lax.axis_size(axis))
    route = [(i - distance, i) for i in devices if i - distance in devices]
    return lax.ppermute(block, axis, route)


def prefix(value, axis, join, neutral, backward):
    count, mine = (lax.axis_size(axis), lax.axis_index(axis))
    pieces = jax.tree.map(lambda part: lax.all_gather(part, axis), value)
    if backward:
        pieces = jax.tree.map(lambda part: part[::-1], pieces)
        mine = count - 1 - mine
    subtotal = jax.tree.map(
        lambda part, zero: jnp.full_like(part, 0) + jnp.asarray(zero, part.dtype), value, neutral
    )

    def hop(position, subtotal):
        longer = join(subtotal, jax.tree.map(lambda part: part[position], pieces))
        return jax.tree.map(lambda new, old: jnp.where(position < mine, new, old), longer, subtotal)

    return lax.fori_loop(0, count - 1, hop, subtotal)


def rms_scale(values, gain_vec):
    return (
        values * lax.rsqrt(jnp.mean(values * values, axis=-1, keepdims=True) + EPSILON) * gain_vec
    )


def gated_unit(gate_pre, up_vals):
    return jax.nn.gelu(gate_pre) * up_vals


def affine(earlier, later_map):
    return (earlier[0] * later_map[0], later_map[0] * earlier[1] + later_map[1])


def segment_ids(starts, start_pos, pos_count, seq_len):
    where_at = start_pos + jnp.arange(pos_count, dtype=jnp.int32)
    seq_of = jnp.floor_divide(where_at, seq_len)
    within = where_at - seq_of * seq_len
    owner = seq_of[:, None] == jnp.arange(starts.shape[0], dtype=jnp.int32)[None, :]
    passed = starts[None, :, :] <= within[:, None, None]
    doc_tally = jnp.sum(jnp.logical_and(owner[:, :, None], passed).astype(jnp.int32), axis=(1, 2))
    return seq_of * (starts.shape[1] + 1) + doc_tally


def project(normed, weights, first_bias, second_bias):
    product = jnp.einsum("td,dc->ct", normed, weights, preferred_element_type=jnp.float32)
    channels = first_bias.shape[0]
    return (product[:channels] + first_bias[:, None], product[channels:] + second_bias[:, None])


def conv_forward(lifted, tail_rows, segments, tap_vals, bias_vec):
    length = lifted.shape[1]
    extended = jnp.concatenate([tail_rows, lifted], axis=1)
    own_seg = segments[3 : 3 + length]
    result = bias_vec[:, None] + tap_vals[0][:, None] * lifted
    for offset in range(1, 4):
        same_doc = (segments[3 - offset : 3 - offset + length] == own_seg).astype(jnp.float32)
        result = (
            result
            + tap_vals[offset][:, None]
            * extended[:, 3 - offset : 3 - offset + length]
            * same_doc[None, :]
        )
    return result


def conv_backward(grad_conv, head_rows, segments, lifted, tail_rows, tap_vals):
    length = grad_conv.shape[1]
    ahead_grad = jnp.concatenate([grad_conv, head_rows], axis=1)
    behind = jnp.concatenate([tail_rows, lifted], axis=1)
    own_seg = segments[3 : 3 + length]
    grad_lifted = tap_vals[0][:, None] * grad_conv
    tap_grads = [jnp.sum(grad_conv * lifted, axis=1)]
    for offset in range(1, 4):
        later_same = (segments[3 + offset : 3 + offset + length] == own_seg).astype(jnp.float32)
        grad_lifted = (
            grad_lifted
            + tap_vals[offset][:, None]
            * ahead_grad[:, offset : offset + length]
            * later_same[None, :]
        )
        earlier = (segments[3 - offset : 3 - offset + length] == own_seg).astype(jnp.float32)
        tap_grads.append(
            jnp.sum(
                grad_conv * behind[:, 3 - offset : 3 - offset + length] * earlier[None, :], axis=1
            )
        )
    return (grad_lifted, jnp.stack(tap_grads, axis=1), jnp.sum(grad_conv, axis=1))


def coefficients(is_reset, conv_out, recur_gate, recur_bias, input_gate, input_bias, decay_param):
    channels, length = conv_out.shape
    gate_block = recur_gate.shape[1]
    grouped = conv_out.reshape(channels // gate_block, gate_block, length)
    recurrence = jax.nn.sigmoid(
        jnp.einsum("hit,hio->hot", grouped, recur_gate, precision=precise).reshape(channels, length)
        + recur_bias[:, None]
    )
    opening = jax.nn.sigmoid(
        jnp.einsum("hit,hio->hot", grouped, input_gate, precision=precise).reshape(channels, length)
        + input_bias[:, None]
    )
    log_decay = -8.0 * recurrence * jax.nn.softplus(-decay_param)[:, None]
    decay_rate = jnp.where(is_reset[None, :], 0.0, jnp.exp(log_decay))
    scaling = jnp.where(is_reset[None, :], 1.0, jnp.sqrt(-jnp.expm1(2.0 * log_decay)))
    return (decay_rate, scaling * opening * conv_out)


def reverse_local(decay_rate, grad_state):
    ones_col = jnp.ones_like(decay_rate[:, :1])
    factor = jnp.flip(jnp.concatenate([decay_rate[:, 1:], ones_col], axis=1), axis=1)
    product, carried = lax.associative_scan(affine, (factor, jnp.flip(grad_state, axis=1)), axis=1)
    return (jnp.flip(product, axis=1), jnp.flip(carried, axis=1))


def finish_state(lru_state, start_state, carried, pull_coef):
    previous = jnp.concatenate([start_state[:, None], lru_state[:, :-1]], axis=1)
    return pull_coef((carried * previous, carried))


def flatten_rows(pieces, row_count):
    return jnp.concatenate([source.reshape(row_count, -1) for source in pieces], axis=1)


def body(
    inputs,
    mix_gain,
    gate_proj,
    gate_bias,
    lift_proj,
    lift_bias,
    conv_taps,
    conv_bias,
    recur_gate,
    recur_bias,
    input_gate,
    input_bias,
    decay_param,
    out_proj,
    out_bias,
    mlp_gain,
    mlp_gate,
    mlp_up,
    mlp_down,
    doc_starts,
    cotangent,
):
    chan_count = lax.axis_size("chan")
    chan_place = lax.axis_index("chan")
    local_rows = inputs.shape[0]
    seq_length = local_rows * chan_count
    rows_f32 = inputs.astype(jnp.float32)
    cot_f32 = cotangent.astype(jnp.float32)
    normed, pull_norm = jax.vjp(rms_scale, rows_f32, mix_gain)
    normed_low = normed.astype(jnp.bfloat16)
    gate_full, lift_full, out_full, mlp_gate_full, mlp_up_full, mlp_down_full = (
        lax.all_gather(gate_proj, "chan", axis=1, tiled=True),
        lax.all_gather(lift_proj, "chan", axis=1, tiled=True),
        lax.all_gather(out_proj, "chan", axis=0, tiled=True),
        lax.all_gather(mlp_gate, "chan", axis=1, tiled=True),
        lax.all_gather(mlp_up, "chan", axis=1, tiled=True),
        lax.all_gather(mlp_down, "chan", axis=0, tiled=True),
    )
    channels = LRU
    hidden_cut = FF
    segments = segment_ids(doc_starts, chan_place * local_rows - 3, local_rows + 6, seq_length)
    mix_proj = jnp.concatenate([gate_full, lift_full], axis=1)
    gate_pre, lifted = project(normed_low, mix_proj, gate_bias, lift_bias)
    tail_rows = from_behind(lifted[:, -3:], "chan", 1)
    conv_out = conv_forward(lifted, tail_rows, segments, conv_taps, conv_bias)
    is_reset = segments[3 : 3 + local_rows] != segments[2 : 2 + local_rows]
    (decay_rate, lru_input), pull_coef = jax.vjp(
        partial(coefficients, is_reset),
        conv_out,
        recur_gate,
        recur_bias,
        input_gate,
        input_bias,
        decay_param,
    )
    running, local_state = lax.associative_scan(affine, (decay_rate, lru_input), axis=1)
    ones_vec = jnp.ones((channels,), jnp.float32)
    zeros_vec = jnp.zeros((channels,), jnp.float32)
    _, start_state = prefix(
        (running[:, -1], local_state[:, -1]), "chan", affine, (ones_vec, zeros_vec), False
    )
    lru_state = local_state + running * start_state[:, None]
    gate_val, pull_gelu = jax.vjp(jax.nn.gelu, gate_pre)
    mixed_out = (lru_state * gate_val).astype(jnp.bfloat16)
    resid = (
        rows_f32
        + jnp.einsum("ct,cd->td", mixed_out, out_full, preferred_element_type=jnp.float32)
        + out_bias
    )
    normed2, pull_norm2 = jax.vjp(rms_scale, resid, mlp_gain)
    normed2_low = normed2.astype(jnp.bfloat16)
    mlp_proj = jnp.concatenate([mlp_gate_full, mlp_up_full], axis=1)
    mlp_pre = jnp.einsum("td,df->ft", normed2_low, mlp_proj, preferred_element_type=jnp.float32)
    hidden, pull_mlp = jax.vjp(gated_unit, mlp_pre[:hidden_cut], mlp_pre[hidden_cut:])
    hidden_low = hidden.astype(jnp.bfloat16)
    output = (
        resid
        + jnp.einsum("ft,fd->td", hidden_low, mlp_down_full, preferred_element_type=jnp.float32)
    ).astype(jnp.bfloat16)
    grad_down = jnp.einsum("ft,td->fd", hidden_low, cotangent, preferred_element_type=jnp.float32)
    grad_gate_m, grad_up_m = pull_mlp(
        jnp.einsum("td,fd->ft", cotangent, mlp_down_full, preferred_element_type=jnp.float32)
    )
    grad_pre = jnp.concatenate([grad_gate_m, grad_up_m], axis=0).astype(jnp.bfloat16)
    grad_mlp_in = jnp.einsum("ft,td->fd", grad_pre, normed2_low, preferred_element_type=jnp.float32)
    grad_resid_part, grad_gain2 = pull_norm2(
        jnp.einsum("ft,df->td", grad_pre, mlp_proj, preferred_element_type=jnp.float32)
    )
    grad_resid = cot_f32 + grad_resid_part
    grad_branch = grad_resid.astype(jnp.bfloat16)
    grad_out_proj = jnp.einsum(
        "ct,td->cd", mixed_out, grad_branch, preferred_element_type=jnp.float32
    )
    grad_mixed = jnp.einsum("td,cd->ct", grad_branch, out_full, preferred_element_type=jnp.float32)
    product, carried = reverse_local(decay_rate, grad_mixed * gate_val)
    _, incoming = prefix(
        (decay_rate[:, 0] * product[:, 0], decay_rate[:, 0] * carried[:, 0]),
        "chan",
        affine,
        (ones_vec, zeros_vec),
        True,
    )
    carried = carried + product * incoming[:, None]
    coef_grads = finish_state(lru_state, start_state, carried, pull_coef)
    head_rows = from_behind(coef_grads[0][:, :3], "chan", -1)
    grad_lifted, grad_taps, grad_conv_bias = conv_backward(
        coef_grads[0], head_rows, segments, lifted, tail_rows, conv_taps
    )
    (grad_gate_pre,) = pull_gelu(grad_mixed * lru_state)
    grad_front = jnp.concatenate([grad_gate_pre, grad_lifted], axis=0).astype(jnp.bfloat16)
    grad_mix_proj = jnp.einsum(
        "ct,td->cd", grad_front, normed_low, preferred_element_type=jnp.float32
    )
    grad_normed = jnp.einsum("ct,dc->td", grad_front, mix_proj, preferred_element_type=jnp.float32)
    grad_x_part, grad_gain1 = pull_norm(grad_normed)
    grad_inputs = (grad_resid + grad_x_part).astype(jnp.bfloat16)
    grad_out_bias = jnp.sum(grad_resid, axis=0)
    pieces = [
        grad_mix_proj[:channels],
        grad_mix_proj[channels:],
        jnp.sum(grad_gate_pre, axis=1),
        jnp.sum(grad_lifted, axis=1),
        grad_taps,
        grad_conv_bias,
        jnp.transpose(coef_grads[1], (1, 0, 2)),
        coef_grads[2],
        jnp.transpose(coef_grads[3], (1, 0, 2)),
        coef_grads[4],
        coef_grads[5],
        grad_out_proj,
        grad_mlp_in[:hidden_cut],
        grad_mlp_in[hidden_cut:],
        grad_down,
        grad_gain1,
        grad_out_bias,
        grad_gain2,
    ]
    spread = flatten_rows(pieces, chan_count)
    shared = lax.psum_scatter(spread, "chan", scatter_dimension=0, tiled=True)
    summed = lax.psum(shared.reshape(-1), "rows")
    channels_dev = LRU // chan_count
    hidden_dev = FF // chan_count
    width_dev = D // chan_count
    block_dev = GB // chan_count
    shapes = [
        (channels_dev, D),
        (channels_dev, D),
        (channels_dev,),
        (channels_dev,),
        (channels_dev, 4),
        (channels_dev,),
        (block_dev, HEADS, GB),
        (channels_dev,),
        (block_dev, HEADS, GB),
        (channels_dev,),
        (channels_dev,),
        (channels_dev, D),
        (hidden_dev, D),
        (hidden_dev, D),
        (hidden_dev, D),
        (width_dev,),
        (width_dev,),
        (width_dev,),
    ]
    unpacked = []
    offset = 0
    for piece_shape in shapes:
        piece_size = math.prod(piece_shape)
        unpacked.append(summed[offset : offset + piece_size].reshape(piece_shape))
        offset = offset + piece_size
    return (
        output,
        grad_inputs,
        unpacked[15],
        unpacked[0].T,
        unpacked[2],
        unpacked[1].T,
        unpacked[3],
        unpacked[4].T,
        unpacked[5],
        jnp.transpose(unpacked[6], (1, 0, 2)),
        unpacked[7],
        jnp.transpose(unpacked[8], (1, 0, 2)),
        unpacked[9],
        unpacked[10],
        unpacked[11],
        unpacked[16],
        unpacked[17],
        unpacked[12].T,
        unpacked[13].T,
        unpacked[14],
    )


MESH = pl.DeviceIdType.MESH
LOW = jnp.bfloat16
F32 = jnp.float32
VMEM_BYTES = 63 * 2**20
TILE = 8
GELU_A = math.sqrt(2.0 / math.pi)
GELU_B = 0.044715


def nt(left, right):
    return lax.dot_general(left, right, (((1,), (1,)), ((), ())), preferred_element_type=F32)


def nn(left, right):
    return lax.dot_general(left, right, (((1,), (0,)), ((), ())), preferred_element_type=F32)


def tn(left, right):
    return lax.dot_general(left, right, (((0,), (0,)), ((), ())), preferred_element_type=F32)


def gelu_pair(values):
    squared = values * values
    bend = jnp.tanh(GELU_A * values * (1.0 + GELU_B * squared))
    half = 0.5 * (1.0 + bend)
    slope = half + 0.5 * values * (1.0 - bend * bend) * GELU_A * (1.0 + 3.0 * GELU_B * squared)
    return values * half, slope


class Spot:
    def __init__(self):
        self.r = lax.axis_index("rows")
        self.c = lax.axis_index("chan")
        self.z = lax.div(self.c, 2)
        self.y = lax.rem(self.c, 2)
        self.r_core = self.r + 1 - 2 * lax.rem(self.r, 2)
        self.r_x = lax.rem(self.r + 2, 4)
        self.core = (self.r_core, self.c)
        self.x = (self.r_x, self.c)
        self.c_y = self.c + 1 - 2 * self.y
        self.ymate = (self.r, self.c_y)
        self.up = (self.r, lax.rem(self.c + 2, 8))
        self.dn = (self.r, lax.rem(self.c + 6, 8))


def greet(always, maybe=()):
    barrier = pltpu.get_barrier_semaphore()
    count = len(always)
    for device in always:
        pl.semaphore_signal(barrier, inc=1, device_id=device, device_id_type=MESH)
    for device, there in maybe:

        @pl.when(there)
        def _(device=device):
            pl.semaphore_signal(barrier, inc=1, device_id=device, device_id_type=MESH)

        count = count + jnp.where(there, 1, 0)
    pl.semaphore_wait(barrier, count)


def push(source, target, sems, index, device):
    return pltpu.make_async_remote_copy(
        src_ref=source,
        dst_ref=target,
        send_sem=sems[0].at[index],
        recv_sem=sems[1].at[index],
        device_id=device,
        device_id_type=MESH,
    )


def landed(me, target, sems, index):
    push(target, target, sems, index, me.ymate).wait_recv()


def sem_pair(count):
    return [pltpu.SemaphoreType.DMA((count,)), pltpu.SemaphoreType.DMA((count,))]


def comm_params(collective_id):
    return pltpu.CompilerParams(
        collective_id=collective_id, has_side_effects=True, vmem_limit_bytes=VMEM_BYTES
    )


ANYWHERE = pl.BlockSpec(memory_space=pl.ANY)
IN_VMEM = pl.BlockSpec(memory_space=pltpu.VMEM)


def decay_terms(rec, softplus_row, reset):
    log_decay = -8.0 * rec * softplus_row
    decay = jnp.exp(log_decay)
    twice = 2.0 * log_decay
    series = twice * (
        1.0
        + twice * (1 / 2 + twice * (1 / 6 + twice * (1 / 24 + twice * (1 / 120 + twice * (1 / 720)))))
    )
    gap = jnp.where(twice > -0.25, -series, 1.0 - jnp.exp(twice))
    return decay, jnp.where(reset, 1.0, jnp.sqrt(gap))


def fill_tallies(tallies, starts_row, first, length, seq_length):
    position = first - 8 + lax.broadcasted_iota(jnp.int32, (length + 16, 1), 0)
    begun = jnp.sum((starts_row <= position).astype(F32), axis=1, keepdims=True)
    inside = jnp.logical_and(position >= 0, position < seq_length)
    tallies[...] = jnp.broadcast_to(jnp.where(inside, begun, -1.0), tallies.shape)


def same_document(tallies, length, shift, wide):
    own = tallies[pl.ds(8, length)]
    other = tallies[pl.ds(8 + shift, length)]
    same = (own == other).astype(F32)
    return jnp.concatenate([same] * (wide // same.shape[1]), axis=1)


def pair_diagonal(target, blocks):
    side = blocks.shape[1]
    target[...] = jnp.zeros_like(target)
    target[0:side, 0:side] = blocks[0].astype(target.dtype)
    target[side : 2 * side, side : 2 * side] = blocks[1].astype(target.dtype)


def tile_scan(a, b, backward):
    row = lax.broadcasted_iota(jnp.int32, a.shape, 1)
    for step in (1, 2, 4):
        shift = TILE - step if backward else step
        there = row < TILE - step if backward else row >= step
        b = b + a * jnp.where(there, pltpu.roll(b, shift, 1), 0.0)
        a = a * jnp.where(there, pltpu.roll(a, shift, 1), 1.0)
    return a, b


def carry_start(me, backward, totals, slots, sems):
    sign = -1 if backward else 1
    steps = me.c if backward else 7 - me.c
    copies = [
        push(totals, slots.at[d], sems, d, (me.r, lax.rem(me.c + 8 + sign * d, 8)))
        for d in range(1, 8)
    ]
    for d in range(1, 8):

        @pl.when(d <= steps)
        def _(d=d):
            copies[d - 1].start()

    return copies


def carry_join(me, backward, slots, start, sems):
    behind = 7 - me.c if backward else me.c
    start[...] = jnp.zeros_like(start)
    for d in range(7, 0, -1):

        @pl.when(d <= behind)
        def _(d=d):
            landed(me, slots.at[d], sems, d)
            start[...] = slots[d, :, 0] * start[...] + slots[d, :, 1]


def carry_sent(me, backward, copies):
    steps = me.c if backward else 7 - me.c
    for d in range(1, 8):

        @pl.when(d <= steps)
        def _(d=d):
            copies[d - 1].wait_send()


def peers_of(me):
    return [(me.r, lax.rem(me.c + d, 8)) for d in range(1, 8)]


class Spread:
    def __init__(self, me, slabs, pieces, sems):
        self.me, self.slabs, self.pieces, self.sems = me, slabs, pieces, sems
        self.go_up = jnp.logical_and(me.z >= me.r, me.z < 3)
        self.go_dn = jnp.logical_and(me.z <= me.r, me.z > 0)
        self.source = me.z == me.r
        self.hop = jnp.where(me.z < me.r, me.r - me.z, me.z - me.r)

    def copies(self, k):
        me, found = self.me, []
        for i, slab in enumerate(self.slabs):
            piece = slab(k, me.y)
            ys, yr, us, ds, zr = self.sems[5 * i : 5 * i + 5]
            found.append(
                (
                    push(piece, piece, (ys, yr), k, me.ymate),
                    push(piece, piece, (us, zr), k, me.up),
                    push(piece, piece, (ds, zr), k, me.dn),
                )
            )
        return found

    def send(self, k):
        found = self.copies(k)
        for copies in found:
            copies[0].start()

        @pl.when(self.go_up)
        def _():
            for copies in found:
                copies[1].start()

        @pl.when(self.go_dn)
        def _():
            for copies in found:
                copies[2].start()

    def follow(self, k):
        for i, slab in enumerate(self.slabs):
            us, zr = self.sems[5 * i + 2], self.sems[5 * i + 4]
            landed(self.me, slab(k, self.me.y), (us, zr), k)
        self.send(k)

    def step(self, q):
        n = self.pieces

        def at(k, also, action):
            there = jnp.logical_and(k >= 0, k < n)

            @pl.when(jnp.logical_and(there, also))
            def _():
                action(lax.rem(k + 8 * n, n))

        at(q + SPREAD_AHEAD, self.source, self.send)
        at(q - SPREAD_LAG * (self.hop - 1), jnp.logical_not(self.source), self.follow)

    def reach(self):
        return -SPREAD_AHEAD, self.pieces + 2 * SPREAD_LAG

    def arrived(self):
        @pl.loop(0, self.pieces)
        def _(k):
            for i, slab in enumerate(self.slabs):
                ys, yr = self.sems[5 * i], self.sems[5 * i + 1]
                landed(self.me, slab(k, 1 - self.me.y), (ys, yr), k)

    def close(self):
        @pl.loop(0, self.pieces)
        def _(k):
            found = self.copies(k)
            for copies in found:
                copies[0].wait_send()

            @pl.when(self.go_up)
            def _():
                for copies in found:
                    copies[1].wait_send()

            @pl.when(self.go_dn)
            def _():
                for copies in found:
                    copies[2].wait_send()


SPREAD_AHEAD = 4
SPREAD_LAG = 1


def spread_sems(arrays, pieces):
    return [pltpu.SemaphoreType.DMA((pieces,))] * (5 * arrays)


AHEAD = 3
LAGS = (3, 8, 14)
LATE_LAGS = (2, 7, 9)


class Reduce:
    def __init__(self, me, parts, mine, from_y, from_z, own, pieces, sems, ahead=AHEAD, lags=LAGS):
        self.me, self.parts, self.mine = me, parts, mine
        self.from_y, self.from_z, self.own = from_y, from_z, own
        self.pieces, self.sems, self.ahead, self.lags = pieces, sems, ahead, lags
        self.hop = jnp.where(me.z < me.r, me.z, 3 - me.z)
        self.owner = me.z == me.r
        self.relays = me.z == me.r_x

    def rows(self, i, k):
        size = self.mine[i].shape[0] // self.pieces
        return pl.ds(pl.multiple_of(k * size, 16), size)

    def each(self, k):
        for i in range(len(self.mine)):
            yield i, self.rows(i, k), self.sems[11 * i : 11 * i + 11]

    def y_copies(self, k):
        me = self.me
        return [
            push(self.parts[i].at[1 - me.y, rows], self.from_y[i].at[rows], sems[0:2], k, me.ymate)
            for i, rows, sems in self.each(k)
        ]

    def y_send(self, k):
        for copy in self.y_copies(k):
            copy.start()

    def add(self, i, rows, other):
        total = self.mine[i][rows].astype(F32) + other[i][rows].astype(F32)
        self.mine[i][rows] = total.astype(LOW)

    def join(self, k):
        for i, rows, sems in self.each(k):
            landed(self.me, self.from_y[i].at[rows], sems[0:2], k)
            self.add(i, rows, self.from_y)

    def z_copies(self, k, way):
        found = []
        for i, rows, sems in self.each(k):
            target = self.own if way == 2 else self.from_z
            pair = ((sems[2], sems[4]), (sems[3], sems[4]), (sems[3], sems[5]))[way]
            found.append(
                push(self.mine[i].at[rows], target[i].at[rows], pair, k,
                     self.me.up if way == 0 else self.me.dn)
            )
        return found

    def z_way(self, action):
        me = self.me
        for way, there in enumerate(
            (me.z < me.r, me.z > me.r + 1, me.z == me.r + 1)
        ):

            @pl.when(there)
            def _(way=way):
                action(way)

    def chain(self, k):
        @pl.when(self.hop > 0)
        def _():
            for i, rows, sems in self.each(k):
                landed(self.me, self.from_z[i].at[rows], (sems[2], sems[4]), k)
                self.add(i, rows, self.from_z)

        def start(way):
            for copy in self.z_copies(k, way):
                copy.start()

        self.z_way(start)

    def out_copies(self, k, device, pair):
        return [
            push(self.own[i].at[rows], self.own[i].at[rows], sems[pair : pair + 2], k, device)
            for i, rows, sems in self.each(k)
        ]

    def finish(self, k):
        @pl.when(self.me.z > 0)
        def _():
            for i, rows, sems in self.each(k):
                landed(self.me, self.from_z[i].at[rows], (sems[2], sems[4]), k)
                self.add(i, rows, self.from_z)

        @pl.when(self.me.z < 3)
        def _():
            for i, rows, sems in self.each(k):
                landed(self.me, self.own[i].at[rows], (sems[3], sems[5]), k)
                self.add(i, rows, self.own)

        for i, rows, sems in self.each(k):
            self.own[i][rows] = self.mine[i][rows]
        for copy in self.out_copies(k, self.me.x, 6) + self.out_copies(k, self.me.core, 8):
            copy.start()

    def relay(self, k):
        for copy in self.out_copies(k, self.me.x, 6):
            copy.wait_recv()
        for copy in self.out_copies(k, self.me.core, 8):
            copy.start()

    def step(self, q):
        n = self.pieces

        def at(k, also, action):
            there = jnp.logical_and(k >= 0, k < n)

            @pl.when(there if also is None else jnp.logical_and(there, also))
            def _():
                action(lax.rem(k + 8 * n, n))

        hop_lag, end_lag, relay_lag = self.lags
        if self.ahead:
            at(q + self.ahead, None, self.y_send)
        at(q, None, self.join)
        at(q - hop_lag * self.hop, jnp.logical_not(self.owner), self.chain)
        at(q - end_lag, self.owner, self.finish)
        at(q - relay_lag, self.relays, self.relay)

    def reach(self):
        return -self.ahead, self.pieces + self.lags[2]

    def close(self):
        others = jnp.logical_not(jnp.logical_or(self.owner, self.relays))

        @pl.loop(0, self.pieces)
        def _(k):
            for copy in self.y_copies(k):
                copy.wait_send()

            def sent(way):
                for copy in self.z_copies(k, way):
                    copy.wait_send()

            self.z_way(sent)

            @pl.when(self.owner)
            def _():
                for copy in self.out_copies(k, self.me.x, 6) + self.out_copies(k, self.me.core, 8):
                    copy.wait_send()

            @pl.when(self.relays)
            def _():
                for copy in self.out_copies(k, self.me.core, 8):
                    copy.wait_send()

            @pl.when(others)
            def _():
                for copy in self.out_copies(k, self.me.core, 8):
                    copy.wait_recv()


class Line:
    def __init__(self, reduces, offsets):
        self.reduces, self.offsets = reduces, offsets
        self.done = reduces[0].reach()[0]

    def position(self, p, low, high):
        for one, offset in zip(self.reduces, self.offsets):
            first, last = one.reach()
            if offset + first < high and low < offset + last:
                one.step(p - offset)

    def advance(self, high):
        low, self.done = self.done, max(self.done, high)
        if high > low + 1:

            @pl.loop(low, high)
            def _(p):
                self.position(p, low, high)

        elif high > low:
            self.position(low, low, high)

    def ready(self, i):
        assert self.done <= self.offsets[i] + self.reduces[i].reach()[0]

    def during(self, begin, end, action):
        low, self.done = self.done, self.done + end - begin

        @pl.loop(begin, end)
        def _(s):
            action(s)
            self.position(low - begin + s, low, low + end - begin)

    def last(self):
        return max(offset + one.reach()[1] for offset, one in zip(self.offsets, self.reduces))

    def close(self):
        for one in self.reduces:
            one.close()


def reduce_sems(arrays, pieces):
    return [pltpu.SemaphoreType.DMA((pieces,))] * (11 * arrays)


RS_CHUNKS = 4


class RowsSum:
    def __init__(self, me, part, mate, out_x, in_x, core_sems, x_sems):
        self.me, self.part, self.mate, self.out_x, self.in_x = me, part, mate, out_x, in_x
        self.size = part.shape[1] // RS_CHUNKS
        far = lax.rem(me.r_core + 2, 4)
        self.to_core = [
            [
                push(part.at[owner, self.rows(k)], mate.at[block, self.rows(k)], core_sems,
                     block * RS_CHUNKS + k, me.core)
                for k in range(RS_CHUNKS)
            ]
            for block, owner in enumerate((far, me.r_core))
        ]
        self.to_x = [
            push(out_x.at[self.rows(k)], in_x.at[self.rows(k)], x_sems, k, me.x)
            for k in range(RS_CHUNKS)
        ]

    def rows(self, k):
        return pl.ds(k * self.size, self.size)

    def start(self, block, chunks=range(RS_CHUNKS)):
        for k in chunks:
            self.to_core[block][k].start()

    def cross(self, chunks=range(RS_CHUNKS)):
        for k in chunks:
            rows = self.rows(k)
            self.to_core[0][k].wait_recv()
            total = self.part[self.me.r_x, rows].astype(F32) + self.mate[0, rows].astype(F32)
            self.out_x[rows] = total.astype(LOW)
            self.to_x[k].start()

    def total(self, k):
        rows = self.rows(k)
        self.to_core[1][k].wait_recv()
        self.to_x[k].wait_recv()
        return (
            self.part[self.me.r, rows].astype(F32) + self.mate[1, rows].astype(F32)
            + self.in_x[rows].astype(F32)
        )

    def close(self):
        for copy in self.to_core[0] + self.to_core[1] + self.to_x:
            copy.wait_send()


class Share:
    def __init__(self, me, array, x_sems, core_sems):
        size = array.shape[1] // RS_CHUNKS

        def piece(row, k):
            return array.at[row, pl.ds(k * size, size)]

        self.to_x = [
            push(piece(me.r, k), piece(me.r, k), x_sems, k, me.x) for k in range(RS_CHUNKS)
        ]
        self.to_core = [
            push(piece(me.r, k), piece(me.r, k), core_sems, k, me.core) for k in range(RS_CHUNKS)
        ]
        self.passed = [
            push(piece(me.r_x, k), piece(me.r_x, k), core_sems, RS_CHUNKS + k, me.core)
            for k in range(RS_CHUNKS)
        ]

    def send(self, k):
        self.to_x[k].start()
        self.to_core[k].start()

    def relay(self, k):
        self.to_x[k].wait_recv()
        self.passed[k].start()

    def arrived(self, k):
        self.to_core[k].wait_recv()
        self.passed[k].wait_recv()

    def close(self):
        for copy in self.to_x + self.to_core + self.passed:
            copy.wait_send()


def finish_sends(copies):
    for copy in copies:
        copy.wait_send()


class Bag:
    def __init__(self, names, refs):
        self.__dict__.update(zip(names, refs))


MLP_BLOCKS = 3
VECTORS = ("gate_bias", "lift_bias", "conv_bias", "recur_bias", "input_bias", "decay_param")
LANES = 128


def block_kernel(names, *refs):
    R = Bag(names, refs)
    me = Spot()
    r, c, z, y = me.r, me.c, me.z, me.y
    length, width = R.inputs.shape
    seq_length = length * 8
    wide = 2 * R.gp.shape[0]
    side = wide // 2
    step = length // RS_CHUNKS
    tokens_all = 4 * length
    tiles = (length // TILE, TILE, wide)
    diag = (me.r_x + 1 - 2 * lax.rem(me.r_x, 2), c)
    row_peers = (me.core, me.x, diag)
    chan_peers = peers_of(me)
    x_place, core_place = lax.div(r, 2), lax.rem(r, 2)

    def far_first(i):
        return 2 * lax.rem(x_place + 1 + lax.div(i, 2), 2) + lax.rem(core_place + 1 + lax.rem(i, 2), 2)

    vec, taps = R.vec, R.taps
    keep = dict(gate_pre=R.gate_h, lext=R.lext_h, conv=R.conv_h, rec=R.rec_h, opening=R.open_h,
                state=R.state_h, mixed_t=R.mixed_h)

    def tallies_of(s):
        fill_tallies(R.tallies, R.starts_all[s, 0:1], c * length, length, seq_length)

    def same(shift):
        return same_document(R.tallies, length, shift, wide)


    mixer_pieces = (4, 6, 4)

    def mixer_slab(m):
        size = side // mixer_pieces[m]
        return lambda k, half: R.wq.at[m, half, pl.ds(pl.multiple_of(k * size, 16), size)]

    glo = [
        Spread(me, [mixer_slab(m)], mixer_pieces[m], R.spread[5 * m : 5 * m + 5]) for m in range(3)
    ]

    def mlp_slab(b):
        size = width // 8

        def slab(k, half):
            rows = pl.ds(pl.multiple_of(k * size, 16), size)
            return R.w.at[b, rows, pl.ds(pl.multiple_of(half * 3 * LANES, LANES), 3 * LANES)]

        return slab

    mlp_w = [
        Spread(me, [mlp_slab(b)], 8, R.spread[15 + 5 * b : 20 + 5 * b]) for b in range(MLP_BLOCKS)
    ]
    sline = Line([glo[0], glo[2]] + mlp_w, (0, 4, 8, 16, 24))

    part = R.opart
    sum1 = RowsSum(me, part, R.mate, R.out_x, R.in_x, (R.ms, R.mr), (R.rxs, R.rxr))

    def forward(gate_pre, lext, conv, rec, opening, a, b, mixed_t, rg32, ig32, md_v):
        barrier = pltpu.get_barrier_semaphore()
        always = list(row_peers) + chan_peers
        for device in always:
            pl.semaphore_signal(barrier, inc=1, device_id=device, device_id_type=MESH)
        count = len(always)
        for there, place in ((c < 7, lax.rem(c + 1, 8)), (c > 0, lax.rem(c + 7, 8))):
            for i in (1, 2, 3):

                @pl.when(there)
                def _(i=i, place=place):
                    pl.semaphore_signal(
                        barrier, inc=1, device_id=(lax.rem(r + i, 4), place), device_id_type=MESH
                    )

            count = count + jnp.where(there, 3, 0)
        own = [
            pltpu.make_async_copy(R.gp, R.wq.at[0, y], R.loc.at[12]),
            pltpu.make_async_copy(R.lp, R.wq.at[1, y], R.loc.at[13]),
            pltpu.make_async_copy(R.op, R.wq.at[2, y], R.loc.at[0]),
            pltpu.make_async_copy(R.md, md_v, R.loc.at[14]),
        ]
        for blk in range(MLP_BLOCKS):
            lanes = pl.ds(blk * LANES, LANES)
            for i, (source, at) in enumerate(
                ((R.mg, 4 * y), (R.mu, 4 * y + 1))
            ):
                column = pl.ds(pl.multiple_of(at * LANES, LANES), LANES)
                own.append(
                    pltpu.make_async_copy(
                        source.at[:, lanes], R.w.at[blk, :, column], R.loc.at[1 + 2 * blk + i]
                    )
                )

        @pl.when(z == r)
        def _():
            for copy in own:
                copy.start()

        heads = [
            pltpu.make_async_copy(R.rgate_all.at[pl.ds(2 * r, 2)], rg32, R.loc.at[10]),
            pltpu.make_async_copy(R.igate_all.at[pl.ds(2 * r, 2)], ig32, R.loc.at[11]),
        ]
        for copy in heads:
            copy.start()
        pl.semaphore_wait(barrier, count)

        @pl.when(z == r)
        def _():
            for copy in own[:2]:
                copy.wait()
            for k in range(mixer_pieces[1]):
                glo[1].send(k)

        R.call[r] = R.cot[...]
        vals = R.inputs[...].astype(F32)
        scale = lax.rsqrt(jnp.mean(vals * vals, axis=-1, keepdims=True) + EPSILON)
        R.nall[r] = (vals * scale * R.mix_gain[...]).astype(LOW)
        R.starts_all[r] = jnp.full(R.starts_all.shape[1:], jnp.iinfo(jnp.int32).max, jnp.int32)
        R.starts_all[r, 0:1, 0 : R.starts.shape[1]] = R.starts[...]

        mine_n, mine_c = R.nall.at[r], R.call.at[r]
        theirs_n, theirs_c = R.nall.at[me.r_x], R.call.at[me.r_x]
        x_n = push(mine_n, mine_n, (R.xs, R.xr), 0, me.x)
        c_n = push(mine_n, mine_n, (R.cs, R.cr), 0, me.core)
        c_c = push(mine_c, mine_c, (R.cs, R.cr), 1, me.core)
        x_c = push(mine_c, mine_c, (R.xs, R.xr), 1, me.x)
        fwd_n = push(theirs_n, theirs_n, (R.cs, R.cr), 2, me.core)
        fwd_c = push(theirs_c, theirs_c, (R.cs, R.cr), 3, me.core)
        s_copies = [
            push(R.starts_all.at[r], R.starts_all.at[r], (R.ss, R.sr), i, device)
            for i, device in enumerate(row_peers)
        ]
        tail = R.nall.at[r, pl.ds(length - 16, 16)]
        halo_copies = [
            push(tail, R.halo.at[r], (R.hs, R.hr), i, (lax.rem(r + i, 4), lax.rem(c + 1, 8)))
            for i in range(4)
        ]
        x_n.start()
        for copy in s_copies:
            copy.start()

        @pl.when(c < 7)
        def _():
            for copy in halo_copies:
                copy.start()

        c_n.start()
        c_c.start()

        @pl.when(c == 0)
        def _():
            R.halo[...] = jnp.zeros_like(R.halo)

        mine = pl.ds(pl.multiple_of(r * wide, LANES), wide)
        count_rows = wide // LANES
        for i, name in enumerate(VECTORS):
            for k in range(count_rows):
                place = pl.ds(r * count_rows + k, 1)
                vec[i : i + 1, k * LANES : (k + 1) * LANES] = getattr(R, name)[place]
        decay = vec[5:6]
        vec[5:6] = jnp.log1p(jnp.exp(-decay))
        vec[6:7] = jax.nn.sigmoid(-decay)
        taps[...] = R.conv_taps[:, mine]

        for copy in heads:
            copy.wait()
        pair_diagonal(R.rgate, rg32)
        pair_diagonal(R.igate, ig32)
        for k in range(mixer_pieces[1]):

            @pl.when(z != r)
            def _(k=k):
                glo[1].follow(k)

        x_n.wait_recv()
        fwd_n.start()
        x_c.start()

        @pl.when(z == r)
        def _():
            for copy in own[2:]:
                copy.wait()
            column = pl.ds(pl.multiple_of((2 + y) * LANES, LANES), LANES)
            for blk in range(MLP_BLOCKS):
                R.w[blk, :, column] = md_v[blk * LANES : (blk + 1) * LANES].T

        sline.advance(0)
        glo[1].arrived()
        c_n.wait_recv()
        fwd_n.wait_recv()
        for copy in s_copies:
            copy.wait_recv()

        @pl.when(c > 0)
        def _():
            for i in range(4):
                landed(me, R.halo.at[i], (R.hs, R.hr), i)

        def mixer_one(s):
            tallies_of(s)
            tokens = R.nall[s]
            wlift = R.wq[1].reshape(wide, width)
            lifted = nt(tokens, wlift) + vec[1:2]
            lext[s, 0:8] = (nt(R.halo[s], wlift) + vec[1:2])[8:16]
            lext[s, pl.ds(8, length)] = lifted
            out = vec[2:3] + taps[0:1] * lifted
            for k in range(1, 4):
                out = out + taps[k : k + 1] * lext[s, pl.ds(8 - k, length)] * same(-k)
            conv[s] = out
            low = out.astype(LOW)
            recur = jax.nn.sigmoid(nn(low, R.rgate[...]) + vec[3:4])
            opened = jax.nn.sigmoid(nn(low, R.igate[...]) + vec[4:5])
            rec[s] = recur
            opening[s] = opened
            reset = same(-1) < 0.5
            decay, scaling = decay_terms(recur, vec[5:6], reset)
            decay = jnp.where(reset, 0.0, decay)
            a_scan, b_scan = tile_scan(
                decay.reshape(tiles), (scaling * opened * out).reshape(tiles), False
            )
            a[s] = a_scan.reshape(length, wide)
            b[s] = b_scan.reshape(length, wide)
            product = jnp.ones((1, wide), F32)
            state = jnp.zeros((1, wide), F32)
            for t in range(length // TILE):
                last = t * TILE + TILE - 1
                a_last = a[s, last : last + 1]
                state = b[s, last : last + 1] + a_last * state
                product = product * a_last
            R.tot[s, 0:1] = product
            R.tot[s, 1:2] = state

        sline.during(0, 4, mixer_one)
        carry_copies = carry_start(me, False, R.tot, R.slots, (R.ps, R.pr))
        local = dict(gate_pre=gate_pre, lext=lext, conv=conv, rec=rec, opening=opening, state=b,
                     mixed_t=mixed_t)
        saved = {
            name: pltpu.make_async_copy(local[name], keep[name], R.outs.at[i])
            for i, name in enumerate(keep)
        }
        for name in ("lext", "conv", "rec", "opening"):
            saved[name].start()
        sline.advance(4 + 2 * SPREAD_LAG)
        glo[0].arrived()

        def gate_part(s):
            gate_pre[s] = nt(R.nall[s], R.wq[0].reshape(wide, width)) + vec[0:1]

        sline.during(0, 4, gate_part)
        saved["gate_pre"].start()
        carry_join(me, False, R.slots, R.start, (R.ps, R.pr))
        sline.advance(8 + 2 * SPREAD_LAG)
        glo[2].arrived()

        def mixer_two(i):
            s = far_first(i)
            state = R.start[pl.ds(s, 1)]
            for t in range(length // TILE):
                tile = pl.ds(t * TILE, TILE)
                now = b[s, tile] + a[s, tile] * state
                b[s, tile] = now
                state = now[TILE - 1 : TILE]
            gate_val, _ = gelu_pair(gate_pre[s])
            mix = (b[s] * gate_val).astype(LOW)
            mixed_t[:, pl.ds(pl.multiple_of(s * length, LANES), length)] = mix.T
            part[s] = nn(mix, R.wq[2].reshape(wide, width)).astype(LOW)

        sline.during(0, 2, mixer_two)
        sum1.start(0)
        sline.during(2, 3, mixer_two)
        sum1.start(1)
        sum1.cross((0, 1, 2))
        sline.during(3, 4, mixer_two)
        x_c.wait_recv()
        fwd_c.start()
        for name in ("state", "mixed_t"):
            saved[name].start()
        for m in range(3):
            glo[m].close()
        for copy in (x_n, x_c, c_n, fwd_n):
            copy.wait_send()
        c_c.wait()
        fwd_c.wait()
        finish_sends(s_copies)

        @pl.when(c < 7)
        def _():
            finish_sends(halo_copies)

        carry_sent(me, False, carry_copies)
        for copy in saved.values():
            copy.wait()

    tall = pltpu.VMEM((4, length, wide), F32)
    ext = pltpu.VMEM((4, length + TILE, wide), F32)
    low_t = pltpu.VMEM((wide, tokens_all), LOW)
    pl.run_scoped(
        forward, gate_pre=tall, lext=ext, conv=tall, rec=tall, opening=tall, a=tall, b=tall,
        mixed_t=low_t, rg32=pltpu.VMEM((2, GB, GB), F32),
        ig32=pltpu.VMEM((2, GB, GB), F32), md_v=pltpu.VMEM(R.md.shape, LOW),
    )


    groups = [R.reduce[11 * i : 11 * i + 11] for i in range(MLP_BLOCKS)]
    rest = R.reduce[11 * MLP_BLOCKS :]
    line = Line(
        [
            Reduce(
                me, [R.grad.at[blk]], [R.grad.at[blk, y]], [R.y_w.at[blk]], [R.z_w.at[blk]],
                [R.own_w.at[:, pl.ds(blk * 3 * LANES, 3 * LANES)]], 8, groups[blk],
            )
            for blk in range(MLP_BLOCKS)
        ]
        + [
            Reduce(me, [R.early], [R.early.at[y]], [R.y_e], [R.z_e], [R.own_e], 8, rest[:11]),
            Reduce(me, [R.late], [R.late.at[y]], [R.y_l], [R.z_l], [R.own_l], 7, rest[11:], 0,
                   LATE_LAGS),
        ],
        (0, 8, 16, 24, 33),
    )
    half = length // 2

    def mlp(acc_out, acc_in, n2_t, hid, low_a, low_b, gpart):
        share1 = Share(me, R.n2all, (R.ax, R.bx), (R.ac, R.bc))

        def norm_chunk(k):
            rows = pl.ds(k * step, step)
            res = R.inputs[rows].astype(F32) + sum1.total(k) + R.out_bias[...]
            R.resid[rows] = res
            scale = lax.rsqrt(jnp.mean(res * res, axis=-1, keepdims=True) + EPSILON)
            R.n2all[r, rows] = (res * scale * R.mlp_gain[...]).astype(LOW)
            share1.send(k)

        def turn(h):
            @pl.loop(0, 4)
            def _(s):
                at = pl.ds(pl.multiple_of(s * length + h * half, LANES), half)
                n2_t[:, at] = R.n2all[s, pl.ds(h * half, half)].T

        def mlp_tokens(blk, h, i):
            pair = pl.ds(2 * lax.rem(x_place + 1 + i, 2), 2)
            rows = pl.ds(h * half, half)
            fold = lambda v: v.reshape(2, half, v.shape[1])
            flat = lambda v: v.reshape(2 * half, v.shape[2])
            tokens, cot = flat(R.n2all[pair, rows]), flat(R.call[pair, rows])
            sides = (slice(0, 2 * LANES), slice(4 * LANES, 6 * LANES))
            across = slice(2 * LANES, 4 * LANES)
            first, second = [nn(tokens, R.w[blk, :, side_of]) for side_of in sides]
            gate = jnp.concatenate([first[:, :LANES], second[:, :LANES]], axis=1)
            up = jnp.concatenate([first[:, LANES:], second[:, LANES:]], axis=1)
            grad_hidden = nn(cot, R.w[blk, :, across])
            gate_val, slope = gelu_pair(gate)
            hidden = (gate_val * up).astype(LOW)
            grad_gate = (grad_hidden * up * slope).astype(LOW)
            grad_up = (grad_hidden * gate_val).astype(LOW)
            kept = blk % 2
            hid[kept, pair, rows] = fold(hidden)
            lows = [
                jnp.concatenate([grad_gate[:, at], grad_up[:, at]], axis=1)
                for at in (slice(0, LANES), slice(LANES, 2 * LANES))
            ]
            low_a[kept, pair, rows] = fold(lows[0])
            low_b[kept, pair, rows] = fold(lows[1])
            out = fold(nt(hidden, R.w[blk, :, across]))
            back = fold(nt(lows[0], R.w[blk, :, sides[0]]) + nt(lows[1], R.w[blk, :, sides[1]]))
            if blk == 0:
                acc_out[pair, rows] = out
                acc_in[pair, rows] = back
            elif blk < MLP_BLOCKS - 1:
                acc_out[pair, rows] += out
                acc_in[pair, rows] += back
            else:
                R.opart[pair, rows] = (acc_out[pair, rows] + out).astype(LOW)
                gpart[pair, rows] = (acc_in[pair, rows] + back).astype(LOW)

        def mlp_weights(blk):
            kept = blk % 2
            columns = lambda i: pl.ds(pl.multiple_of(i * 256, 256), 256)
            flat = lambda v: v.reshape(tokens_all, v.shape[2])
            hid_t = flat(hid[kept]).T

            @pl.loop(0, width // 256)
            def _(i):
                at = columns(i)
                down = nn(hid_t, flat(R.call[:, :, at])).astype(LOW).T
                for j, low in enumerate((low_a, low_b)):
                    R.grad[blk, j, at, 0 : 2 * LANES] = nn(n2_t[at], flat(low[kept])).astype(LOW)
                    R.grad[blk, j, at, 2 * LANES :] = down[:, j * LANES : (j + 1) * LANES]

        def weights_here(blk):
            sline.advance(max(sline.done, sline.offsets[2 + blk] + 8 + 2 * SPREAD_LAG))
            mlp_w[blk].arrived()

        norm_chunk(0)
        sline.advance(17)
        norm_chunk(1)
        sum1.cross((3,))
        sline.advance(19)
        norm_chunk(2)
        for k in range(2):
            share1.relay(k)
            sline.advance(20 + k)
        for k in range(2):
            share1.arrived(k)
        weights_here(0)
        turn(0)
        sline.during(0, 2, lambda i: mlp_tokens(0, 0, i))
        norm_chunk(3)
        share1.relay(2)
        weights_here(1)
        sline.during(0, 2, lambda i: mlp_tokens(1, 0, i))
        share1.relay(3)
        for k in range(2, RS_CHUNKS):
            share1.arrived(k)
        turn(1)
        sline.during(0, 2, lambda i: mlp_tokens(0, 1, i))
        sline.during(0, 2, lambda i: mlp_tokens(1, 1, i))
        mlp_weights(0)
        sline.advance(max(sline.done, sline.offsets[4] + 8 + 2 * SPREAD_LAG))
        mlp_weights(1)
        weights_here(2)
        line.ready(1)
        line.advance(0)
        sum1.close()
        share1.close()
        sum2 = RowsSum(me, gpart, R.mate, R.out_x, R.in_x, (R.m2s, R.m2r), (R.rx2s, R.rx2r))
        line.during(0, 2, lambda i: mlp_tokens(2, 0, i))
        for block in range(2):
            sum2.start(block, (0, 1))
        line.during(0, 1, lambda i: mlp_tokens(2, 1, i))
        sum2.cross((0, 1))
        line.during(1, 2, lambda i: mlp_tokens(2, 1, i))
        for block in range(2):
            sum2.start(block, (2, 3))
        mlp_weights(2)
        line.ready(2)
        line.advance(5)
        sum2.cross((2, 3))
        ball = R.n2all
        share2 = Share(me, ball, (R.a2x, R.b2x), (R.a2c, R.b2c))
        gain_sum = 0.0
        bias_sum = 0.0
        for k in range(RS_CHUNKS):
            rows = pl.ds(k * step, step)
            grad = sum2.total(k)
            res = R.resid[rows]
            scale = lax.rsqrt(jnp.mean(res * res, axis=-1, keepdims=True) + EPSILON)
            gain_sum = gain_sum + jnp.sum(grad * res * scale, axis=0, keepdims=True)
            pulled = grad * R.mlp_gain[...]
            inner = jnp.mean(pulled * res, axis=-1, keepdims=True)
            total = R.cot[rows].astype(F32) + scale * pulled - res * (scale * scale * scale * inner)
            bias_sum = bias_sum + jnp.sum(total, axis=0, keepdims=True)
            R.gresid[rows] = total
            ball[r, rows] = total.astype(LOW)
            share2.send(k)
            line.advance(6 + k)
        R.gain_keep[0:1] = gain_sum
        R.gain_keep[1:2] = bias_sum
        for k in range(RS_CHUNKS):
            share2.relay(k)
            line.advance(10 + k)
        for k in range(RS_CHUNKS):
            share2.arrived(k)
        share2.close()
        sum2.close()

    kept = pltpu.VMEM((2, 4, length, 2 * LANES), LOW)
    pl.run_scoped(
        mlp, acc_out=pltpu.VMEM((4, length, width), F32), acc_in=pltpu.VMEM((4, length, width), F32),
        n2_t=pltpu.VMEM((width, tokens_all), LOW), hid=kept, low_a=kept, low_b=kept,
        gpart=pltpu.VMEM((4, length, width), LOW),
    )
    for one in mlp_w:
        one.close()


    def backward(gate_pre, conv, rec, opening, state, a, b, gconv, gate_low, gate_t, mixed_t, acc_r,
                 acc_i, prev_ext):
        local = dict(gate_pre=gate_pre, conv=conv, rec=rec, opening=opening, state=state,
                     mixed_t=mixed_t)
        loads = {
            name: pltpu.make_async_copy(keep[name], ref, R.outs.at[i])
            for i, (name, ref) in enumerate(local.items())
        }
        soon = ("gate_pre", "state", "rec")
        later = ("mixed_t", "conv", "opening")
        for name in soon + later:
            loads[name].start()
        ball = R.n2all
        sum3 = RowsSum(me, R.opart, R.o_mate, R.o_out, R.o_in, (R.oms, R.omr), (R.oxs, R.oxr))
        for block in range(2):
            sum3.start(block)
        for name in soon:
            loads[name].wait()
        acc_r[...] = jnp.zeros_like(acc_r)
        acc_i[...] = jnp.zeros_like(acc_i)
        R.sums[...] = jnp.zeros_like(R.sums)

        def reset_of(s):
            tallies_of(s)
            return same(-1) < 0.5

        def mixer_three(s):
            grad_mixed = nt(ball[s], R.wq[2].reshape(wide, width))
            gate_val, slope = gelu_pair(gate_pre[s])
            grad_gate = grad_mixed * state[s] * slope
            low = grad_gate.astype(LOW)
            gate_low[s] = low
            gate_t[:, pl.ds(pl.multiple_of(s * length, LANES), length)] = low.T
            R.sums[0:1] += jnp.sum(grad_gate, axis=0, keepdims=True)
            grad_state = grad_mixed * gate_val
            gate_pre[s] = grad_state
            decay = jnp.where(reset_of(s), 0.0, jnp.exp(-8.0 * rec[s] * vec[5:6]))
            a_scan, b_scan = tile_scan(
                decay.reshape(tiles), (decay * grad_state).reshape(tiles), True
            )
            a[s, 0:length] = a_scan.reshape(length, wide)
            b[s] = b_scan.reshape(length, wide)
            product = jnp.ones((1, wide), F32)
            carried = jnp.zeros((1, wide), F32)
            for t in range(length // TILE - 1, -1, -1):
                head = t * TILE
                a_head = a[s, head : head + 1]
                carried = b[s, head : head + 1] + a_head * carried
                product = product * a_head
            R.tot[s, 0:1] = product
            R.tot[s, 1:2] = carried

        line.during(0, 1, mixer_three)
        sum3.cross()
        line.during(1, 4, mixer_three)
        carry_copies = carry_start(me, True, R.tot, R.slots2, (R.p2s, R.p2r))
        for name in later:
            loads[name].wait()
        columns = lambda i: pl.ds(pl.multiple_of(i * 256, 256), 256)

        def weight_grad(target, at, left_t, right):
            @pl.loop(0, width // 256)
            def _(i):
                product = nn(left_t[...], right[:, :, columns(i)].reshape(tokens_all, 256)).astype(LOW)
                for j in range(2):
                    target[j, at : at + side, columns(i)] = product[j * side : (j + 1) * side]

        weight_grad(R.early, 0, mixed_t, ball)
        weight_grad(R.early, side, gate_t, R.nall)
        line.ready(3)
        line.advance(20)
        carry_join(me, True, R.slots2, R.carry, (R.p2s, R.p2r))

        def mixer_four(s):
            now = R.carry[pl.ds(s, 1)]
            gconv[s, pl.ds(length, TILE)] = jnp.broadcast_to(now, (TILE, wide))
            for t in range(length // TILE - 1, -1, -1):
                rows = pl.ds(t * TILE, TILE)
                moved = b[s, rows] + a[s, rows] * now
                gconv[s, rows] = moved
                now = moved[0:1]
            carried = gate_pre[s] + gconv[s, pl.ds(1, length)]
            prev_ext[0:TILE] = jnp.broadcast_to(R.start[pl.ds(s, 1)], (TILE, wide))
            prev_ext[pl.ds(TILE, length)] = state[s]
            previous = prev_ext[pl.ds(TILE - 1, length)]
            recur, opened, conv_s = rec[s], opening[s], conv[s]
            reset = reset_of(s)
            decay, scaling = decay_terms(recur, vec[5:6], reset)
            pulled = carried * scaling
            grad_opening = pulled * conv_s
            grad_log = carried * (previous * decay - opened * conv_s * (decay * decay / scaling))
            grad_log = jnp.where(reset, 0.0, grad_log)
            grad_rec = grad_log * (-8.0 * vec[5:6])
            grad_rpre = grad_rec * recur * (1.0 - recur)
            grad_opre = grad_opening * opened * (1.0 - opened)
            r_low, o_low, conv_low = grad_rpre.astype(LOW), grad_opre.astype(LOW), conv_s.astype(LOW)
            total = pulled * opened + nt(r_low, R.rgate[...]) + nt(o_low, R.igate[...])
            gconv[s, 0:length] = total
            acc_r[...] += tn(conv_low, r_low)
            acc_i[...] += tn(conv_low, o_low)
            R.sums[7:8] += jnp.sum(grad_rpre, axis=0, keepdims=True)
            R.sums[8:9] += jnp.sum(grad_opre, axis=0, keepdims=True)
            R.sums[9:10] += jnp.sum(grad_log * recur, axis=0, keepdims=True) * (8.0 * vec[6:7])
            R.sums[6:7] += jnp.sum(total, axis=0, keepdims=True)

        line.during(0, 4, mixer_four)
        lext = a
        load_lext = pltpu.make_async_copy(keep["lext"], lext, R.outs.at[6])
        load_lext.start()
        heads = [
            push(gconv.at[s, pl.ds(0, TILE)], R.heads_in.at[s], (R.h2s, R.h2r), s,
                 (r, lax.rem(c + 7, 8)))
            for s in range(4)
        ]

        @pl.when(c > 0)
        def _():
            for copy in heads:
                copy.start()

        @pl.when(c == 7)
        def _():
            R.heads_in[...] = jnp.zeros_like(R.heads_in)

        cut = side // 8
        for k in range(8):
            at = k * cut
            R.gate_send[k] = jnp.concatenate(
                [m[j * side + at : j * side + at + cut, j * side : (j + 1) * side]
                 for m in (acc_r, acc_i) for j in range(2)], axis=0
            ).astype(LOW)
        gate_copies = [
            push(R.gate_send.at[lax.rem(c + d, 8)], R.gate_slots.at[d], (R.qs, R.qr), d,
                 chan_peers[d - 1])
            for d in range(1, 8)
        ]
        for copy in gate_copies:
            copy.start()
        for k in range(RS_CHUNKS):
            rows = pl.ds(k * step, step)
            R.output[rows] = (R.resid[rows] + sum3.total(k)).astype(LOW)
        line.advance(26)
        load_lext.wait()

        @pl.when(c < 7)
        def _():
            for s in range(4):
                landed(me, R.heads_in.at[s], (R.h2s, R.h2r), s)

        lift_t = mixed_t
        gpart1 = R.call

        def mixer_five(i):
            s = far_first(i)
            tallies_of(s)
            grad = gconv[s, 0:length]
            prev_ext[0:length] = grad
            prev_ext[pl.ds(length, TILE)] = R.heads_in[s]
            grad_lifted = taps[0:1] * grad
            R.sums[2:3] += jnp.sum(grad * lext[s, pl.ds(TILE, length)], axis=0, keepdims=True)
            for k in range(1, 4):
                ahead = prev_ext[pl.ds(k, length)] * same(k)
                grad_lifted = grad_lifted + taps[k : k + 1] * ahead
                behind = lext[s, pl.ds(TILE - k, length)] * same(-k)
                R.sums[2 + k : 3 + k] += jnp.sum(grad * behind, axis=0, keepdims=True)
            R.sums[1:2] += jnp.sum(grad_lifted, axis=0, keepdims=True)
            lift_low = grad_lifted.astype(LOW)
            lift_t[:, pl.ds(pl.multiple_of(s * length, LANES), length)] = lift_low.T
            gpart1[s] = (
                nn(gate_low[s], R.wq[0].reshape(wide, width))
                + nn(lift_low, R.wq[1].reshape(wide, width))
            ).astype(LOW)

        sum4 = RowsSum(me, gpart1, R.mate, R.out_x, R.in_x, (R.m3s, R.m3r), (R.rx3s, R.rx3r))
        line.during(0, 2, mixer_five)
        sum4.start(0)
        line.during(2, 3, mixer_five)
        sum4.start(1)
        sum4.cross()
        line.during(3, 4, mixer_five)
        R.late[...] = jnp.zeros_like(R.late)
        weight_grad(R.late, 0, lift_t, R.nall)
        for j in range(2):
            R.late[j, side : side + 16, 0:side] = R.sums[:, j * side : (j + 1) * side].astype(LOW)
        line.ready(4)
        for k in range(7):
            line.reduces[4].y_send(k)
        line.advance(32)
        gain_sum = 0.0
        for k in range(RS_CHUNKS):
            rows = pl.ds(k * step, step)
            grad = sum4.total(k)
            vals = R.inputs[rows].astype(F32)
            scale = lax.rsqrt(jnp.mean(vals * vals, axis=-1, keepdims=True) + EPSILON)
            gain_sum = gain_sum + jnp.sum(grad * vals * scale, axis=0, keepdims=True)
            pulled = grad * R.mix_gain[...]
            inner = jnp.mean(pulled * vals, axis=-1, keepdims=True)
            R.ginputs[rows] = (
                R.gresid[rows] + scale * pulled - vals * (scale * scale * scale * inner)
            ).astype(LOW)
            line.advance(34 + 2 * k)
        for k in range(8):
            lanes = slice(k * LANES, (k + 1) * LANES)
            R.gain_slots[0, k] = jnp.concatenate(
                [gain_sum[:, lanes], R.gain_keep[0:1, lanes], R.gain_keep[1:2, lanes],
                 jnp.zeros((5, LANES), F32)], 0
            )
        gain_copies = [
            push(R.gain_slots.at[0, lax.rem(c + d, 8)], R.gain_slots.at[1, d], (R.ggs, R.ggr), d,
                 chan_peers[d - 1])
            for d in range(1, 8)
        ]
        for copy in gain_copies:
            copy.start()
        line.advance(42)
        gate_total = R.gate_send[c].astype(F32)
        for d in range(1, 8):
            gate_copies[d - 1].wait_recv()
            gate_total = gate_total + R.gate_slots[d].astype(F32)
        R.gates_all[r] = gate_total.astype(LOW)
        gate_rows = [
            push(R.gates_all.at[r], R.gates_all.at[r], (R.ts, R.tr), i, device)
            for i, device in enumerate(row_peers)
        ]
        for copy in gate_rows:
            copy.start()
        shared = R.gain_slots[0, c]
        for d in range(1, 8):
            gain_copies[d - 1].wait_recv()
            shared = shared + R.gain_slots[1, d]
        R.gain_sums[0] = shared
        row_copies = [
            push(R.gain_sums.at[0], R.gain_sums.at[1 + i], (R.ghs, R.ghr), i, device)
            for i, device in enumerate(row_peers)
        ]
        for copy in row_copies:
            copy.start()
        line.advance(line.last())
        for copy in row_copies + gate_rows:
            copy.wait()
        for row in range(4):
            found = R.gates_all[row].astype(F32)
            for head in range(2):
                R.rgate_o[2 * row + head] = found[head * cut : (head + 1) * cut]
                R.igate_o[2 * row + head] = found[(2 + head) * cut : (3 + head) * cut]
        R.gains_all[...] = R.gain_sums[0] + R.gain_sums[1] + R.gain_sums[2] + R.gain_sums[3]

        @pl.when(c > 0)
        def _():
            finish_sends(heads)

        finish_sends(gain_copies + gate_copies)
        sum3.close()
        sum4.close()
        carry_sent(me, True, carry_copies)
        line.close()

    square = pltpu.VMEM((wide, wide), F32)
    pl.run_scoped(
        backward, gate_pre=tall, conv=tall, rec=tall, opening=tall, state=tall, a=ext, b=tall,
        gconv=ext, gate_low=pltpu.VMEM((4, length, wide), LOW), gate_t=low_t, mixed_t=low_t,
        acc_r=square, acc_i=square, prev_ext=pltpu.VMEM((length + TILE, wide), F32),
    )


def block(ins):
    far = ("rgate_all", "igate_all", "gp", "lp", "op", "mg", "mu", "md")
    inputs, starts, mg = ins["inputs"], ins["starts"], ins["mg"]
    length, width = inputs.shape
    side = ins["gp"].shape[0]
    wide = 2 * side
    hidden = mg.shape[1]
    sd, vmem = jax.ShapeDtypeStruct, pltpu.VMEM
    blocks = hidden // LANES
    tall = sd((4, length, wide), F32)
    tokens = (4, length, width)
    outs = dict(
        output=sd(inputs.shape, LOW), ginputs=sd(inputs.shape, LOW),
        own_w=sd((width, 3 * hidden), LOW),
        own_e=sd((2 * side, width), LOW), own_l=sd((side + 32, width), LOW),
        rgate_o=sd((8, side // 8, side), F32), igate_o=sd((8, side // 8, side), F32),
        gains_all=sd((8, LANES), F32),
    )
    saved = dict(
        gate_h=tall, lext_h=sd((4, length + TILE, wide), F32), conv_h=tall, rec_h=tall, open_h=tall,
        state_h=tall, mixed_h=sd((wide, 4 * length), LOW),
    )
    scratch = dict(
        wq=vmem((3, 2, side, width), LOW), nall=vmem(tokens, LOW), halo=vmem((4, 16, width), LOW),
        starts_all=vmem((4, 8, LANES), starts.dtype), vec=vmem((8, wide), F32), taps=vmem((4, wide), F32),
        gates_all=vmem((4, side // 2, side), LOW),
        w=vmem((blocks, width, 6 * LANES), LOW),
        call=vmem(tokens, LOW), n2all=vmem(tokens, LOW), opart=vmem(tokens, LOW),
        rgate=vmem((wide, wide), LOW), igate=vmem((wide, wide), LOW),
        tallies=vmem((length + 16, LANES), F32), start=vmem((4, wide), F32), carry=vmem((4, wide), F32),
        tot=vmem((4, 2, wide), F32), slots=vmem((8, 4, 2, wide), F32), slots2=vmem((8, 4, 2, wide), F32),
        resid=vmem((length, width), F32), gresid=vmem((length, width), F32),
        mate=vmem((2, length, width), LOW), out_x=vmem((length, width), LOW),
        in_x=vmem((length, width), LOW),
        o_mate=vmem((2, length, width), LOW), o_out=vmem((length, width), LOW),
        o_in=vmem((length, width), LOW),
        grad=vmem((blocks, 2, width, 3 * LANES), LOW),
        early=vmem((2, 2 * side, width), LOW), late=vmem((2, side + 32, width), LOW),
        heads_in=vmem((4, TILE, wide), F32), sums=vmem((16, wide), F32),
        gate_send=vmem((8, side // 2, side), LOW), gate_slots=vmem((8, side // 2, side), LOW),
        gain_keep=vmem((8, width), F32), gain_slots=vmem((2, 8, 8, LANES), F32), gain_sums=vmem((4, 8, LANES), F32),
    )
    for way in "yz":
        scratch.update(
            {
                way + "_w": vmem((blocks, width, 3 * LANES), LOW),
                way + "_e": vmem((2 * side, width), LOW),
                way + "_l": vmem((side + 32, width), LOW),
            }
        )
    dma = pltpu.SemaphoreType.DMA
    counts = dict(
        loc=15, outs=7, xs=2, xr=2, cs=4, cr=4, hs=4, hr=4, ss=3, sr=3, ps=8, pr=8, p2s=8, p2r=8,
        h2s=4, h2r=4, qs=8, qr=8, ts=3, tr=3, ggs=8, ggr=8, ghs=3, ghr=3,
    )
    for name in ("m", "m2", "m3", "om"):
        counts.update({name + "s": 2 * RS_CHUNKS, name + "r": 2 * RS_CHUNKS})
    for name in ("rx", "rx2", "rx3", "ox"):
        counts.update({name + "s": RS_CHUNKS, name + "r": RS_CHUNKS})
    for name in ("", "2"):
        counts.update({f"a{name}x": RS_CHUNKS, f"b{name}x": RS_CHUNKS})
        counts.update({f"a{name}c": 2 * RS_CHUNKS, f"b{name}c": 2 * RS_CHUNKS})
    scratch.update({name: dma((count,)) for name, count in counts.items()})
    names = list(ins) + list(outs) + list(saved) + list(scratch)
    spread = spread_sems(1, 4) + spread_sems(1, 6) + spread_sems(1, 4) + spread_sems(1, 8) * blocks
    reduce = reduce_sems(1, 8) * blocks + reduce_sems(1, 8) + reduce_sems(1, 7)

    def kernel(*refs):
        n, m = len(names), len(spread)
        block_kernel(names + ["spread", "reduce"], *refs[:n], refs[n : n + m], refs[n + m :])

    results = pl.pallas_call(
        kernel,
        name="block",
        out_shape=list(outs.values()) + list(saved.values()),
        in_specs=[ANYWHERE if name in far else IN_VMEM for name in ins],
        out_specs=[IN_VMEM] * len(outs) + [ANYWHERE] * len(saved),
        scratch_shapes=list(scratch.values()) + spread + reduce,
        compiler_params=comm_params(1),
    )(*ins.values())
    return results[: len(outs)]


def finish_kernel(
    output, ginputs, own_w, own_e, own_l, rgate, igate, gains, tail,
    output_o, ginputs_o, gate, up, down, out, gate_proj, lift_proj, rgate_o, igate_o, taps, *flat
):
    output_o[...] = output[...]
    ginputs_o[...] = ginputs[...]
    side = out.shape[0]
    for blk in range(MLP_BLOCKS):
        lanes = slice(blk * LANES, (blk + 1) * LANES)
        for i, target in enumerate((gate, up)):
            at = (3 * blk + i) * LANES
            target[:, lanes] = own_w[:, at : at + LANES].astype(F32)
        at = (3 * blk + 2) * LANES
        down[lanes] = own_w[:, at : at + LANES].T.astype(F32)
    out[...] = own_e[0:side].astype(F32)
    gate_proj[...] = own_e[side:].astype(F32)
    lift_proj[...] = own_l[0:side].astype(F32)
    rgate_o[...] = rgate[...]
    igate_o[...] = igate[...]
    vectors = tail[:, 0:side].astype(F32)
    taps[...] = vectors[2:6]
    for i in range(3):
        flat[i][...] = gains[i : i + 1]
    for i, row in enumerate((0, 1, 6, 7, 8, 9)):
        flat[3 + i][...] = vectors[row : row + 1]


def finish(output, ginputs, own_w, own_e, own_l, rgate, igate, gains):
    steps = 2
    width = own_w.shape[0]
    hidden = own_w.shape[1] // 3
    side = own_e.shape[0] // 2
    sd = jax.ShapeDtypeStruct

    def by_rows(shape):
        return pl.BlockSpec((shape[0] // steps,) + shape[1:], lambda i: (i,) + (0,) * (len(shape) - 1))

    def by_columns(shape):
        return pl.BlockSpec((shape[0], shape[1] // steps), lambda i: (0, i))

    def once(shape):
        return pl.BlockSpec(shape, lambda i: (0,) * len(shape))

    inward, outward, square = (width, hidden), (hidden, width), (side, width)
    tail = pl.BlockSpec((16, own_l.shape[1]), lambda i: (side // 16, 0))
    flat = [(1, gains.shape[1])] * 3 + [(1, side)] * 6
    outs = (
        [(sd(v.shape, v.dtype), by_rows(v.shape)) for v in (output, ginputs)]
        + [(sd(inward, F32), by_rows(inward))] * 2
        + [(sd(outward, F32), by_columns(outward))]
        + [(sd(square, F32), by_columns(square))] * 3
        + [(sd(v.shape, v.dtype), by_rows(v.shape)) for v in (rgate, igate)]
        + [(sd((4, side), F32), once((4, side)))]
        + [(sd(shape, F32), once(shape)) for shape in flat]
    )
    return pl.pallas_call(
        finish_kernel,
        name="finish",
        grid=(steps,),
        in_specs=[by_rows(output.shape), by_rows(ginputs.shape), by_rows(own_w.shape),
                  by_columns(own_e.shape), by_columns(own_l.shape), by_rows(rgate.shape),
                  by_rows(igate.shape), once(gains.shape), tail],
        out_specs=[o[1] for o in outs],
        out_shape=[o[0] for o in outs],
        compiler_params=pltpu.CompilerParams(vmem_limit_bytes=VMEM_BYTES),
    )(output, ginputs, own_w, own_e, own_l, rgate, igate, gains, own_l)


def split_body(
    inputs, mix_gain, gate_proj, gate_bias, lift_proj, lift_bias, conv_taps, conv_bias,
    recur_gate, recur_bias, input_gate, input_bias, decay_param, out_proj, out_bias, mlp_gain,
    mlp_gate, mlp_up, mlp_down, doc_starts, cotangent,
):
    row = lambda v: v[None]
    vectors = (gate_bias, lift_bias, conv_bias, recur_bias, input_bias, decay_param)
    output, grad_inputs, own_w, own_e, own_l, rgate_o, igate_o, gains = block(
        dict(
            inputs=inputs, cot=cotangent, mix_gain=row(mix_gain), out_bias=row(out_bias),
            mlp_gain=row(mlp_gain), **{name: v.reshape(-1, LANES) for name, v in zip(VECTORS, vectors)}, conv_taps=conv_taps, starts=doc_starts,
            rgate_all=recur_gate, igate_all=input_gate, gp=gate_proj.T, lp=lift_proj.T, op=out_proj,
            mg=mlp_gate, mu=mlp_up, md=mlp_down,
        )
    )
    (output, grad_inputs, grad_gate, grad_up, grad_down, grad_out, grad_gate_proj, grad_lift_proj,
     rgate_o, igate_o, taps, *flat) = finish(
        output, grad_inputs, own_w, own_e, own_l, rgate_o, igate_o, gains
    )
    flat = [v.reshape(v.shape[1]) for v in flat]
    return (
        output, grad_inputs, flat[0],
        grad_gate_proj.T, flat[3], grad_lift_proj.T, flat[4], taps, flat[5],
        rgate_o, flat[6], igate_o, flat[7], flat[8],
        grad_out, flat[2], flat[1],
        grad_gate, grad_up, grad_down,
    )


def solution(mesh):
    in_specs = (
        P(("rows", "chan"), None),
        P(),
        P(None, "chan"),
        P(),
        P(None, "chan"),
        P(),
        P(),
        P(),
        P(),
        P(),
        P(),
        P(),
        P(),
        P("chan", None),
        P(),
        P(),
        P(None, "chan"),
        P(None, "chan"),
        P("chan", None),
        P("rows", None),
        P(("rows", "chan"), None),
    )
    out_specs = (
        P(("rows", "chan"), None),
        P(("rows", "chan"), None),
        P("chan"),
        P(None, "chan"),
        P("chan"),
        P(None, "chan"),
        P("chan"),
        P(None, "chan"),
        P("chan"),
        P(None, "chan", None),
        P("chan"),
        P(None, "chan", None),
        P("chan"),
        P("chan"),
        P("chan", None),
        P("chan"),
        P("chan"),
        P(None, "chan"),
        P(None, "chan"),
        P("chan", None),
    )
    split = mesh.shape["rows"] == 4 and mesh.shape["chan"] == HEADS
    return jax.shard_map(split_body if split else body, mesh=mesh, in_specs=in_specs, out_specs=out_specs, check_vma=False)
```
